32 devices in a mesh: cand: 2 (over y), gx: 4 (over z), gy: 2 (over x), wa: 2 (over core).
Axes of the slice: x: 2, y: 2, z: 4, core: 2. Of those that a mesh axis runs over, the one named last changes fastest.
Arguments:
- field: bfloat16 [4, 4, 2, 4, 4, 128, 128], P('wa', 'cand', None, 'gx', None, 'gy'), parts along dimension 1, may hold values from -6 to 6
- active_rows: int32 [4, 4], P('gx'), may hold values from 0 to 128, as said below
- kern: bfloat16 [4, 2, 4, 64, 128], P('wa'), may hold values from -0.25 to 0.25
- target: float32 [4, 64, 64], P('wa'), may hold values from 0 to 3
Outputs:
- design_grad: float32 [4, 8, 128, 128], P('gx', 'cand', 'gy'), parts along dimension 1
- intensity: float32 [4, 128, 64], P('wa', 'cand'), parts along dimension 1
The draws below stay inside these ranges and needn't reach their ends.
There are 2 independent parts, one for each index of `cand`. The reference program is written for one: setup_inputs(seed, part) draws one part's arguments, and reference() takes and returns one part's arrays. A program takes and returns all parts, laid end to end along the dimension named above; an argument that names none is the same for every part. Nothing has to cross between parts.
Inputs may be any that keep to these rules, and one draw needn't show every extreme that they name: `active_rows`: live rows are counted from a tile's first cell row; tiles near the aperture's centre are full and its corners empty.
All inputs are finite; a program needn't handle non-finite values.
Results may differ from the reference program's by a relative error of at most 0.0075.
Values may be sent and summed in bfloat16 or wider, within the bound.
No kernel may reach another device: no remote copies, remote signals or barrier semaphores. Data moves between devices by JAX's collectives and lax.ppermute only.
A program may use at most 128 MiB of HBM per device.

```python
import jax
import jax.numpy as jnp
from jax import lax

WL = 4
POL = 2
CELLS = 128
FP = 64
G = 4


def draw_active_rows(key, part):
    index = jnp.arange(G, dtype=jnp.int32)
    centred = 2 * index - (G - 1)
    radius = centred[:, None] * centred[:, None] + centred[None, :] * centred[None, :]
    border = jax.random.randint(key, (G, G), 1, CELLS, dtype=jnp.int32)
    inside = 4 * radius <= G * G
    outside = radius > G * G
    full = jnp.full((G, G), CELLS, jnp.int32)
    empty = jnp.zeros((G, G), jnp.int32)
    return jnp.where(inside, full, jnp.where(outside, empty, border)).astype(jnp.int32)


def level_of(stream_key, dims, cuts, low, top_value):
    factor_of, own = 1.0, jax.random.fold_in(stream_key, 6)
    for dim, shards_of in cuts:
        draws = jnp.exp(jax.random.uniform(jax.random.fold_in(own, dim), (shards_of,), jnp.float32, low / len(cuts), top_value / len(cuts)))
        factor_of = factor_of * jnp.repeat(draws, dims[dim] // shards_of).reshape([-1 if axis == dim else 1 for axis in range(len(dims))])
    return factor_of


def bell_draw(key, shape, scale, bound, shards=(), held_as=jnp.bfloat16):
    loudness = level_of(key, shape, shards, -0.22, 0.18) if shards else 1.0
    drawn = jax.random.normal(key, shape, jnp.float32) * scale * loudness
    return jnp.minimum(jnp.maximum(drawn, -bound), bound).astype(held_as)


def setup_inputs(seed: int = 0, part: int = 0) -> dict:
    key_of = jax.random.split(jax.random.key(seed), 5)
    own_keys = jax.random.split(jax.random.fold_in(key_of[4], part), 5)
    return {
        "field": bell_draw(own_keys[0], (WL, POL, 2, G, G, CELLS, CELLS), 1.0, 6.0, ((0, 2), (3, 4), (5, 2))),
        "active_rows": draw_active_rows(jax.random.fold_in(key_of[4], 71), part),
        "kern": bell_draw(key_of[2], (WL, 2, G, FP, CELLS), (G * CELLS) ** -0.5, 0.25, ((0, 2),)),
        "target": jnp.clip(3.0 * jax.random.uniform(key_of[3], (WL, FP, FP), jnp.float32) ** level_of(key_of[3], (WL, FP, FP), ((0, 2),), -0.2, 0.2), 0.0, 3.0),
    }


def one_wave(masked_wave, kern_wave, target_wave):
    tiles = masked_wave.shape[2]
    side = masked_wave.shape[4]
    width = tiles * side
    stack_real = kern_wave[0].transpose(0, 2, 1).reshape(width, FP)
    stack_imag = kern_wave[1].transpose(0, 2, 1).reshape(width, FP)
    left_real = kern_wave[0].transpose(1, 0, 2).reshape(FP, width).astype(jnp.float32)
    left_imag = kern_wave[1].transpose(1, 0, 2).reshape(FP, width).astype(jnp.float32)
    high = lax.Precision.HIGHEST
    planes = []
    focals = []
    for polar in range(POL):
        plane_real = masked_wave[polar, 0].transpose(0, 2, 1, 3).reshape(width, width)
        plane_imag = masked_wave[polar, 1].transpose(0, 2, 1, 3).reshape(width, width)
        inner_real = jnp.dot(plane_real, stack_real, preferred_element_type=jnp.float32) - jnp.dot(plane_imag, stack_imag, preferred_element_type=jnp.float32)
        inner_imag = jnp.dot(plane_real, stack_imag, preferred_element_type=jnp.float32) + jnp.dot(plane_imag, stack_real, preferred_element_type=jnp.float32)
        focal_real = jnp.dot(left_real, inner_real, precision=high) - jnp.dot(left_imag, inner_imag, precision=high)
        focal_imag = jnp.dot(left_real, inner_imag, precision=high) + jnp.dot(left_imag, inner_real, precision=high)
        planes.append((plane_real, plane_imag))
        focals.append((focal_real, focal_imag))
    inten = jnp.zeros((FP, FP), jnp.float32)
    for focal_real, focal_imag in focals:
        inten = inten + focal_real * focal_real + focal_imag * focal_imag
    excess = inten - target_wave
    partial_value = jnp.zeros((width, width), jnp.float32)
    for polar in range(POL):
        focal_real, focal_imag = focals[polar]
        plane_real, plane_imag = planes[polar]
        source_real = excess * focal_real
        source_imag = excess * focal_imag
        row_real = (jnp.dot(left_real.T, source_real, precision=high) + jnp.dot(left_imag.T, source_imag, precision=high)).astype(jnp.bfloat16)
        row_imag = (jnp.dot(left_real.T, source_imag, precision=high) - jnp.dot(left_imag.T, source_real, precision=high)).astype(jnp.bfloat16)
        back_real = jnp.dot(row_real, stack_real.T, preferred_element_type=jnp.float32) + jnp.dot(row_imag, stack_imag.T, preferred_element_type=jnp.float32)
        back_imag = jnp.dot(row_imag, stack_real.T, preferred_element_type=jnp.float32) - jnp.dot(row_real, stack_imag.T, preferred_element_type=jnp.float32)
        partial_value = partial_value + back_real * plane_real.astype(jnp.float32) + back_imag * plane_imag.astype(jnp.float32)
    return partial_value, inten


def reference(field, active_rows, kern, target):
    tiles = field.shape[3]
    side = field.shape[5]
    cell_rows = jnp.arange(side, dtype=jnp.int32)
    live = cell_rows[None, None, :, None] < active_rows[:, :, None, None]
    masked = jnp.where(live, field, jnp.zeros((), field.dtype)).astype(jnp.bfloat16)

    def step(items):
        return one_wave(items[0], items[1], items[2])

    partials, inten = lax.map(step, (masked, kern, target))
    scale = jnp.float32(tiles * side / FP)
    total = jnp.sum(partials, axis=0) * scale
    total = total.reshape(tiles, side, tiles, side).transpose(0, 2, 1, 3)
    design_grad = 0.5 * (total + total.transpose(1, 0, 3, 2))
    return design_grad, inten
```

```python
import jax
import jax.numpy as jnp
from jax import lax
from jax.sharding import PartitionSpec as P

DIRECT = 8


def product(form, first, second):
    return jnp.einsum(form, first, second, preferred_element_type=jnp.float32)


def precise(form, first, second):
    return jnp.einsum(
        form, first, second, precision=lax.Precision.HIGHEST, preferred_element_type=jnp.float32
    )


def pairs(count, distance):
    return [(device, device ^ distance) for device in range(count)]


def exchange(pieces, axes, count, me):
    if count > DIRECT:
        return lax.all_to_all(pieces, axes, split_axis=0, concat_axis=0, tiled=True), None
    came = [lax.dynamic_index_in_dim(pieces, me, axis=0, keepdims=False)]
    for distance in range(1, count):
        piece = lax.dynamic_index_in_dim(pieces, me ^ distance, axis=0, keepdims=False)
        came.append(lax.ppermute(piece, axes, pairs(count, distance)))
    return jnp.stack(came), me


def in_order(came, me):
    if me is None:
        return came
    count = came.shape[0]
    rest = came.shape[1:]
    bit = 1
    while bit < count:
        split = came.reshape((count // (2 * bit), 2, bit) + rest)
        came = jnp.where((me & bit) != 0, split[:, ::-1], split).reshape((count,) + rest)
        bit *= 2
    return came


def gather(piece, axes, count, me):
    if count > DIRECT:
        return lax.all_gather(piece, axes, axis=0, tiled=False)
    came = [piece]
    for distance in range(1, count):
        came.append(lax.ppermute(piece, axes, pairs(count, distance)))
    return in_order(jnp.stack(came), me)


def make(mesh):
    count_x = mesh.shape["gx"]
    count_y = mesh.shape["gy"]
    count = count_x * count_y
    axes = ("gx", "gy")

    def on_device(field, active_rows, kern, target):
        tile_row = lax.axis_index("gx")
        block = lax.axis_index("gy")
        me = tile_row * count_y + block
        waves, polars = field.shape[0], field.shape[1]
        tiles = field.shape[4]
        rows_dev = field.shape[5]
        side = field.shape[6]
        focus = kern.shape[3]
        first_row = block * rows_dev
        local_rows = first_row + jnp.arange(rows_dev, dtype=jnp.int32)
        live = local_rows[None, :, None] < active_rows[0][:, None, None]
        masked = jnp.where(live, field[:, :, :, 0], jnp.zeros((), field.dtype))
        plane_real = masked[:, :, 0]
        plane_imag = masked[:, :, 1]
        kern_real = kern[:, 0]
        kern_imag = kern[:, 1]
        inner_real = product("lsjuv,ljqv->lsuq", plane_real, kern_real) - product(
            "lsjuv,ljqv->lsuq", plane_imag, kern_imag
        )
        inner_imag = product("lsjuv,ljqv->lsuq", plane_real, kern_imag) + product(
            "lsjuv,ljqv->lsuq", plane_imag, kern_real
        )
        own_kern = lax.dynamic_index_in_dim(kern, tile_row, axis=2, keepdims=False)
        own_kern = lax.dynamic_slice_in_dim(own_kern, first_row, rows_dev, axis=3)
        own_real = own_kern[:, 0].astype(jnp.float32)
        own_imag = own_kern[:, 1].astype(jnp.float32)
        focal_real = precise("lpu,lsuq->lspq", own_real, inner_real) - precise(
            "lpu,lsuq->lspq", own_imag, inner_imag
        )
        focal_imag = precise("lpu,lsuq->lspq", own_real, inner_imag) + precise(
            "lpu,lsuq->lspq", own_imag, inner_real
        )
        focal = jnp.stack([focal_real, focal_imag]).astype(jnp.bfloat16)
        points = focus * focus // count
        pieces = focal.reshape(2, waves, polars, count, points).transpose(3, 0, 1, 2, 4)
        came, _ = exchange(pieces, axes, count, me)
        focal = jnp.sum(came.astype(jnp.float32), axis=0)
        part = jnp.sum(focal * focal, axis=(0, 2))
        own_target = lax.dynamic_slice_in_dim(
            target.reshape(waves, focus * focus), me * points, points, axis=1
        )
        excess = part - own_target
        source = excess[None, :, None] * focal
        bundle = jnp.concatenate([source.reshape(2 * waves * polars, points), part])
        bundle = gather(bundle.astype(jnp.bfloat16), axes, count, me)
        bundle = bundle.transpose(1, 0, 2).reshape(-1, focus, focus).astype(jnp.float32)
        source = bundle[: 2 * waves * polars].reshape(2, waves, polars, focus, focus)
        intensity = bundle[2 * waves * polars :]
        source_real = source[0]
        source_imag = source[1]
        scale = jnp.float32(tiles * side / focus)
        row_real = (
            precise("lpu,lspq->lsuq", own_real, source_real)
            + precise("lpu,lspq->lsuq", own_imag, source_imag)
        ).astype(jnp.bfloat16)
        row_imag = (
            precise("lpu,lspq->lsuq", own_real, source_imag)
            - precise("lpu,lspq->lsuq", own_imag, source_real)
        ).astype(jnp.bfloat16)
        back_real = product("lsuq,ljqv->lsjuv", row_real, kern_real) + product(
            "lsuq,ljqv->lsjuv", row_imag, kern_imag
        )
        back_imag = product("lsuq,ljqv->lsjuv", row_imag, kern_real) - product(
            "lsuq,ljqv->lsjuv", row_real, kern_imag
        )
        own_terms = back_real * plane_real.astype(jnp.float32) + back_imag * plane_imag.astype(
            jnp.float32
        )
        partial_value = lax.reduce_precision(scale * jnp.sum(own_terms, axis=(0, 1)), 8, 7)
        other = lax.ppermute(partial_value.astype(jnp.bfloat16), "wa", pairs(2, 1))
        summed = partial_value + other.astype(jnp.float32)
        blocks = summed.astype(jnp.bfloat16).reshape(count_x, rows_dev, count_y, rows_dev)
        blocks = blocks.transpose(0, 2, 1, 3).reshape(count, rows_dev, rows_dev)
        came, order = exchange(blocks, axes, count, me)
        came = in_order(came, order).reshape(count_x, count_y, rows_dev, rows_dev)
        partner = came.transpose(0, 3, 1, 2).reshape(tiles, rows_dev, side)
        design_grad = 0.5 * (summed + partner.astype(jnp.float32))
        return (design_grad[None], intensity)

    return on_device


def solution(mesh):
    placed = (
        P("wa", "cand", None, "gx", None, "gy", None),
        P("gx", None),
        P("wa", None, None, None, None),
        P("wa", None, None),
    )
    return jax.shard_map(
        make(mesh),
        mesh=mesh,
        in_specs=placed,
        out_specs=(P("gx", "cand", "gy", None), P("wa", "cand", None)),
        check_vma=False,
    )
```

```python
import jax
import jax.numpy as jnp
from jax import lax
from jax.sharding import PartitionSpec as P

def product(form, first, second):
    return jnp.einsum(form, first, second, preferred_element_type=jnp.float32)


def precise(form, first, second):
    return jnp.einsum(
        form, first, second, precision=lax.Precision.HIGHEST, preferred_element_type=jnp.float32
    )


def pairs(count, distance):
    return [(device, device ^ distance) for device in range(count)]


def partners(value, axis, count):
    came = {d: lax.ppermute(value(d), axis, pairs(count, d)) for d in range(count - 1, 0, -1)}
    return [came[d] for d in range(1, count)]


def total(terms):
    while len(terms) > 1:
        terms = [first + second for first, second in zip(terms[::2], terms[1::2])]
    return terms[0]


def rounded(value):
    return lax.reduce_precision(value, 8, 7)


def add_up(value, axis, count):
    narrow = value.astype(jnp.bfloat16)
    came = partners(lambda d: narrow, axis, count)
    return total([rounded(value)] + [term.astype(jnp.float32) for term in came])


def in_order(came, me):
    count = came.shape[0]
    rest = came.shape[1:]
    bit = 1
    while bit < count:
        split = came.reshape((count // (2 * bit), 2, bit) + rest)
        came = jnp.where((me & bit) != 0, split[:, ::-1], split).reshape((count,) + rest)
        bit *= 2
    return came


def make(mesh):
    count_x = mesh.shape["gx"]
    count_y = mesh.shape["gy"]

    def on_device(field, active_rows, kern, target):
        tile_row = lax.axis_index("gx")
        block = lax.axis_index("gy")
        waves, polars = field.shape[0], field.shape[1]
        tiles = field.shape[4]
        rows_dev = field.shape[5]
        side = field.shape[6]
        focus = kern.shape[3]
        first_row = block * rows_dev
        local_rows = first_row + jnp.arange(rows_dev, dtype=jnp.int32)
        live = local_rows[None, :, None] < active_rows[0][:, None, None]
        masked = jnp.where(live, field[:, :, :, 0], jnp.zeros((), field.dtype))
        plane_real = masked[:, :, 0]
        plane_imag = masked[:, :, 1]
        kern_real = kern[:, 0]
        kern_imag = kern[:, 1]
        inner_real = product("lsjuv,ljqv->lsuq", plane_real, kern_real) - product(
            "lsjuv,ljqv->lsuq", plane_imag, kern_imag
        )
        inner_imag = product("lsjuv,ljqv->lsuq", plane_real, kern_imag) + product(
            "lsjuv,ljqv->lsuq", plane_imag, kern_real
        )
        own_kern = lax.dynamic_index_in_dim(kern, tile_row, axis=2, keepdims=False)
        own_kern = lax.dynamic_slice_in_dim(own_kern, first_row, rows_dev, axis=3)
        own_real = own_kern[:, 0].astype(jnp.float32)
        own_imag = own_kern[:, 1].astype(jnp.float32)
        focal_real = precise("lpu,lsuq->lspq", own_real, inner_real) - precise(
            "lpu,lsuq->lspq", own_imag, inner_imag
        )
        focal_imag = precise("lpu,lsuq->lspq", own_real, inner_imag) + precise(
            "lpu,lsuq->lspq", own_imag, inner_real
        )
        focal = jnp.concatenate([focal_real, focal_imag], axis=3)
        focal = add_up(focal, "gy", count_y)
        focal = add_up(focal, "gx", count_x)
        focal_real, focal_imag = focal[..., :focus], focal[..., focus:]
        intensity = jnp.sum(focal_real * focal_real + focal_imag * focal_imag, axis=1)
        excess = (intensity - target)[:, None]
        source_real = excess * focal_real
        source_imag = excess * focal_imag
        scale = jnp.float32(tiles * side / focus)
        row_real = (
            precise("lpu,lspq->lsuq", own_real, source_real)
            + precise("lpu,lspq->lsuq", own_imag, source_imag)
        ).astype(jnp.bfloat16)
        row_imag = (
            precise("lpu,lspq->lsuq", own_real, source_imag)
            - precise("lpu,lspq->lsuq", own_imag, source_real)
        ).astype(jnp.bfloat16)
        back_real = product("lsuq,ljqv->lsjuv", row_real, kern_real) + product(
            "lsuq,ljqv->lsjuv", row_imag, kern_imag
        )
        back_imag = product("lsuq,ljqv->lsjuv", row_imag, kern_real) - product(
            "lsuq,ljqv->lsjuv", row_real, kern_imag
        )
        own_terms = back_real * plane_real.astype(jnp.float32) + back_imag * plane_imag.astype(
            jnp.float32
        )
        partial_value = scale * jnp.sum(own_terms, axis=(0, 1))
        summed = partial_value + lax.ppermute(partial_value, "wa", pairs(2, 1))
        narrow = in_order(summed.astype(jnp.bfloat16), tile_row)
        came = jnp.stack([narrow[0]] + partners(lambda d: narrow[d], "gx", count_x))

        def columns(of):
            return lax.dynamic_slice_in_dim(came, of * rows_dev, rows_dev, axis=2)

        def paired(d):
            half = columns(block ^ d)
            return jnp.concatenate([half[: tiles // 2], half[tiles // 2 :]], axis=2)

        others = [
            jnp.concatenate([term[:, :, :rows_dev], term[:, :, rows_dev:]], axis=0)
            for term in partners(paired, "gy", count_y)
        ]
        halves = in_order(jnp.stack([columns(block)] + others), block)
        partner = halves.transpose(1, 3, 0, 2).reshape(tiles, rows_dev, side)
        partner = in_order(partner, tile_row)
        design_grad = 0.5 * (summed + partner.astype(jnp.float32))
        return (design_grad[None], intensity)

    return on_device


def solution(mesh):
    placed = (
        P("wa", "cand", None, "gx", None, "gy", None),
        P("gx", None),
        P("wa", None, None, None, None),
        P("wa", None, None),
    )
    return jax.shard_map(
        make(mesh),
        mesh=mesh,
        in_specs=placed,
        out_specs=(P("gx", "cand", "gy", None), P("wa", "cand", None)),
        check_vma=False,
    )
```

```python
import functools

import jax
import jax.numpy as jnp
from jax import lax
from jax.experimental import pallas as pl
from jax.experimental.pallas import tpu as pltpu
from jax.sharding import PartitionSpec as P

VMEM = 16 * 2**20


def two_terms(value):
    high = value.astype(jnp.bfloat16)
    return high, (value - high.astype(jnp.float32)).astype(jnp.bfloat16)


def dot(first, second, over):
    return lax.dot_general(
        first, second, ((over[:1], over[1:]), ((), ())), preferred_element_type=jnp.float32
    )


def swapped(value, focus, left, right):
    lane = lax.broadcasted_iota(jnp.int32, value.shape, 1)
    sign = jnp.where(lane < focus, jnp.float32(left), jnp.float32(right))
    return pltpu.roll(value, focus, 1) * sign


def tile_kern(kern, wave, tile):
    real, imag = kern[wave, 0, tile], kern[wave, 1, tile]
    return jnp.concatenate([real, imag], axis=0), jnp.concatenate([-imag, real], axis=0)


def over_tiles(tiles, body, init):
    return lax.fori_loop(0, tiles, body, init, unroll=tiles <= 8)


def live_rows(rows, tile, shape):
    height = shape[-2]
    row = lax.axis_index("gy") * height + lax.broadcasted_iota(jnp.int32, shape, len(shape) - 2)
    return row < rows[0, tile]


def share_kernel(rows, field, kern, share, spread):
    waves, polars, _, _, tiles, height, side = field.shape
    focus = kern.shape[3]
    tile_row = lax.axis_index("gx")
    first = pl.multiple_of(lax.axis_index("gy") * height, height)
    spread[...] = jnp.zeros_like(spread)
    for wave in range(waves):

        def add_tile(tile, inner):
            live = live_rows(rows, tile, (polars, height, side))
            planes = [
                jnp.where(live, field[wave, :, part, 0, tile], jnp.zeros((), field.dtype))
                for part in range(2)
            ]
            planes = [plane.reshape(polars * height, side) for plane in planes]
            return inner + dot(
                jnp.concatenate(planes, axis=1),
                jnp.concatenate(tile_kern(kern, wave, tile), axis=1),
                (1, 1),
            )

        inner = over_tiles(tiles, add_tile, jnp.zeros((polars * height, 2 * focus), jnp.float32))
        for polar in range(polars):
            lanes = pl.ds(polar * 2 * focus, 2 * focus)
            terms = two_terms(inner[polar * height : (polar + 1) * height])
            for index, term in enumerate(terms):
                spread[wave, pl.ds(index * side + first, height), lanes] = term
        own = tile_kern(kern, wave, tile_row)[0]
        both = dot(jnp.concatenate([own, own], axis=1), spread[wave], (1, 0))
        for polar in range(polars):
            lanes = slice(polar * 2 * focus, (polar + 1) * 2 * focus)
            straight, crossed = both[:focus, lanes], both[focus:, lanes]
            share[wave, polar] = (straight + swapped(crossed, focus, -1, 1)).astype(share.dtype)


def gradient_kernel(scale, rows, field, kern, target, *refs):
    shares, (intensity, gradient, rowside) = refs[:-3], refs[-3:]
    waves, polars, _, _, tiles, height, side = field.shape
    focus = kern.shape[3]
    tile_row = lax.axis_index("gx")
    first = pl.multiple_of(lax.axis_index("gy") * height, height)
    sides = []
    for wave in range(waves):
        focal = [
            total([share[wave, polar].astype(jnp.float32) for share in shares])
            for polar in range(polars)
        ]
        power = sum(value * value for value in focal)
        power = power + pltpu.roll(power, focus, 1)
        intensity[wave] = power[:, :focus]
        goal = target[wave]
        excess = power - jnp.concatenate([goal, goal], axis=1)
        source = jnp.concatenate([excess * value for value in focal], axis=1)
        own = jnp.concatenate([kern[wave, 0, tile_row], kern[wave, 1, tile_row]], axis=1)
        rowside[...] = dot(
            jnp.concatenate([own, own], axis=0),
            jnp.concatenate(two_terms(source), axis=0),
            (0, 0),
        )
        parts = []
        for polar in range(polars):
            lanes = pl.ds(polar * 2 * focus, 2 * focus)
            straight = rowside[pl.ds(first, height), lanes]
            crossed = rowside[pl.ds(side + first, height), lanes]
            parts.append(straight + swapped(crossed, focus, 1, -1))
        sides.append(jnp.concatenate(parts, axis=0).astype(jnp.bfloat16))

    def add_tile(distance, carry):
        tile = tile_row ^ distance
        term = jnp.zeros((height, side), jnp.float32)
        for wave in range(waves):
            back = dot(
                sides[wave], jnp.concatenate(tile_kern(kern, wave, tile), axis=1), (1, 0)
            ).reshape(polars, height, 2 * side)
            for polar in range(polars):
                for part in range(2):
                    plane = field[wave, polar, part, 0, tile].astype(jnp.float32)
                    term += back[polar, :, part * side : (part + 1) * side] * plane
        live = live_rows(rows, tile, (height, side))
        gradient[distance] = jnp.where(live, term * scale, 0.0)
        return carry

    over_tiles(tiles, add_tile, 0)


def call(kernel, out_shape, scratch, args):
    in_vmem = pl.BlockSpec(memory_space=pltpu.VMEM)
    return pl.pallas_call(
        kernel,
        out_shape=out_shape,
        in_specs=[pl.BlockSpec(memory_space=pltpu.SMEM)] + [in_vmem] * (len(args) - 1),
        out_specs=[in_vmem] * len(out_shape),
        scratch_shapes=scratch,
        compiler_params=pltpu.CompilerParams(vmem_limit_bytes=VMEM),
    )(*args)


def pairs(count, distance):
    return [(device, device ^ distance) for device in range(count)]


def partners(value, axis, count):
    came = {d: lax.ppermute(value(d), axis, pairs(count, d)) for d in range(count - 1, 0, -1)}
    return [came[d] for d in range(1, count)]


def total(terms):
    while len(terms) > 1:
        terms = [first + second for first, second in zip(terms[::2], terms[1::2])]
    return terms[0]


def in_order(came, me):
    count = came.shape[0]
    rest = came.shape[1:]
    bit = 1
    while bit < count:
        split = came.reshape((count // (2 * bit), 2, bit) + rest)
        came = jnp.where((me & bit) != 0, split[:, ::-1], split).reshape((count,) + rest)
        bit *= 2
    return came


def make(mesh):
    count_x = mesh.shape["gx"]
    count_y = mesh.shape["gy"]

    def on_device(field, active_rows, kern, target):
        tile_row = lax.axis_index("gx")
        block = lax.axis_index("gy")
        waves, polars = field.shape[0], field.shape[1]
        tiles = field.shape[4]
        rows_dev = field.shape[5]
        side = field.shape[6]
        focus = kern.shape[3]
        shape = (waves, polars, focus, 2 * focus)
        (share,) = call(
            share_kernel,
            [jax.ShapeDtypeStruct(shape, jnp.bfloat16)],
            [pltpu.VMEM((waves, 2 * side, polars * 2 * focus), jnp.bfloat16)],
            (active_rows, field, kern),
        )
        shares = [share] + partners(lambda d: share, "gy", count_y)
        share = total([term.astype(jnp.float32) for term in shares]).astype(jnp.bfloat16)
        shares = [share] + partners(lambda d: share, "gx", count_x)
        intensity, gradient = call(
            functools.partial(gradient_kernel, tiles * side / focus),
            [
                jax.ShapeDtypeStruct((waves, focus, focus), jnp.float32),
                jax.ShapeDtypeStruct((tiles, rows_dev, side), jnp.float32),
            ],
            [pltpu.VMEM((2 * side, polars * 2 * focus), jnp.float32)],
            (active_rows, field, kern, target, *shares),
        )
        summed = gradient + lax.ppermute(gradient, "wa", pairs(2, 1))
        narrow = summed.astype(jnp.bfloat16)
        came = jnp.stack([narrow[0]] + partners(lambda d: narrow[d], "gx", count_x))

        def columns(of):
            return lax.dynamic_slice_in_dim(came, of * rows_dev, rows_dev, axis=2)

        def paired(d):
            half = columns(block ^ d)
            return jnp.concatenate([half[: tiles // 2], half[tiles // 2 :]], axis=2)

        others = [
            jnp.concatenate([term[:, :, :rows_dev], term[:, :, rows_dev:]], axis=0)
            for term in partners(paired, "gy", count_y)
        ]
        halves = in_order(jnp.stack([columns(block)] + others), block)
        partner = halves.transpose(1, 3, 0, 2).reshape(tiles, rows_dev, side)
        design_grad = in_order(0.5 * (summed + partner.astype(jnp.float32)), tile_row)
        return (design_grad[None], intensity)

    return on_device


def solution(mesh):
    placed = (
        P("wa", "cand", None, "gx", None, "gy", None),
        P("gx", None),
        P("wa", None, None, None, None),
        P("wa", None, None),
    )
    return jax.shard_map(
        make(mesh),
        mesh=mesh,
        in_specs=placed,
        out_specs=(P("gx", "cand", "gy", None), P("wa", "cand", None)),
        check_vma=False,
    )
```

```python
import functools

import jax
import jax.numpy as jnp
from jax import lax
from jax.experimental import pallas as pl
from jax.experimental.pallas import tpu as pltpu
from jax.sharding import PartitionSpec as P

VMEM = 16 * 2**20


def two_terms(value):
    high = value.astype(jnp.bfloat16)
    return high, (value - high.astype(jnp.float32)).astype(jnp.bfloat16)


def dot(first, second, over):
    return lax.dot_general(
        first, second, ((over[:1], over[1:]), ((), ())), preferred_element_type=jnp.float32
    )


def swapped(value, focus, left, right):
    lane = lax.broadcasted_iota(jnp.int32, value.shape, 1)
    sign = jnp.where(lane < focus, jnp.float32(left), jnp.float32(right))
    return pltpu.roll(value, focus, 1) * sign


def tile_kern(kern, wave, tile):
    real, imag = kern[wave, 0, tile], kern[wave, 1, tile]
    return jnp.concatenate([real, imag], axis=0), jnp.concatenate([-imag, real], axis=0)


def over_tiles(tiles, body, init):
    return lax.fori_loop(0, tiles, body, init, unroll=tiles <= 8)


def live_rows(rows, tile, shape):
    height = shape[-2]
    row = lax.axis_index("gy") * height + lax.broadcasted_iota(jnp.int32, shape, len(shape) - 2)
    return row < rows[0, tile]


def share_kernel(rows_far, field_far, kern_far, share, field, kern, rows, spread, arrived):
    waves, polars, _, tiles, height, side = field.shape
    focus = kern.shape[3]
    copies = [pltpu.make_async_copy(rows_far, rows, arrived.at[2 * waves])]
    for wave in range(waves):
        copies += [
            pltpu.make_async_copy(kern_far.at[wave], kern.at[wave], arrived.at[2 * wave]),
            pltpu.make_async_copy(
                field_far.at[wave, :, :, 0], field.at[wave], arrived.at[2 * wave + 1]
            ),
        ]
    for copy in copies:
        copy.start()
    tile_row = lax.axis_index("gx")
    first = pl.multiple_of(lax.axis_index("gy") * height, height)
    spread[...] = jnp.zeros_like(spread)
    copies[0].wait()
    for wave in range(waves):
        copies[2 * wave + 1].wait()
        copies[2 * wave + 2].wait()

        def add_tile(tile, inner):
            live = live_rows(rows, tile, (polars, height, side))
            planes = [
                jnp.where(live, field[wave, :, part, tile], jnp.zeros((), field.dtype))
                for part in range(2)
            ]
            for part in range(2):
                field[wave, :, part, tile] = planes[part]
            planes = [plane.reshape(polars * height, side) for plane in planes]
            return inner + dot(
                jnp.concatenate(planes, axis=1),
                jnp.concatenate(tile_kern(kern, wave, tile), axis=1),
                (1, 1),
            )

        inner = over_tiles(tiles, add_tile, jnp.zeros((polars * height, 2 * focus), jnp.float32))
        for polar in range(polars):
            lanes = pl.ds(polar * 2 * focus, 2 * focus)
            terms = two_terms(inner[polar * height : (polar + 1) * height])
            for index, term in enumerate(terms):
                spread[wave, pl.ds(index * side + first, height), lanes] = term
        own = tile_kern(kern, wave, tile_row)[0]
        both = dot(jnp.concatenate([own, own], axis=1), spread[wave], (1, 0))
        for polar in range(polars):
            lanes = slice(polar * 2 * focus, (polar + 1) * 2 * focus)
            straight, crossed = both[:focus, lanes], both[focus:, lanes]
            share[wave, polar] = (straight + swapped(crossed, focus, -1, 1)).astype(share.dtype)


def gradient_kernel(scale, field, kern, target, *refs):
    shares, (intensity, gradient, rowside) = refs[:-3], refs[-3:]
    waves, polars, _, tiles, height, side = field.shape
    focus = kern.shape[3]
    tile_row = lax.axis_index("gx")
    first = pl.multiple_of(lax.axis_index("gy") * height, height)
    sides = []
    for wave in range(waves):
        focal = [
            total([share[wave, polar].astype(jnp.float32) for share in shares])
            for polar in range(polars)
        ]
        power = sum(value * value for value in focal)
        power = power + pltpu.roll(power, focus, 1)
        intensity[wave] = power[:, :focus]
        goal = target[wave]
        excess = power - jnp.concatenate([goal, goal], axis=1)
        source = jnp.concatenate([excess * value for value in focal], axis=1)
        own = jnp.concatenate([kern[wave, 0, tile_row], kern[wave, 1, tile_row]], axis=1)
        rowside[...] = dot(
            jnp.concatenate([own, own], axis=0),
            jnp.concatenate(two_terms(source), axis=0),
            (0, 0),
        )
        parts = []
        for polar in range(polars):
            lanes = pl.ds(polar * 2 * focus, 2 * focus)
            straight = rowside[pl.ds(first, height), lanes]
            crossed = rowside[pl.ds(side + first, height), lanes]
            parts.append(straight + swapped(crossed, focus, 1, -1))
        sides.append(jnp.concatenate(parts, axis=0).astype(jnp.bfloat16))

    def add_tile(distance, carry):
        tile = tile_row ^ distance
        term = jnp.zeros((height, side), jnp.float32)
        for wave in range(waves):
            back = dot(
                sides[wave], jnp.concatenate(tile_kern(kern, wave, tile), axis=1), (1, 0)
            ).reshape(polars, height, 2 * side)
            for polar in range(polars):
                for part in range(2):
                    plane = field[wave, polar, part, tile].astype(jnp.float32)
                    term += back[polar, :, part * side : (part + 1) * side] * plane
        gradient[distance] = term * scale
        return carry

    over_tiles(tiles, add_tile, 0)


def call(kernel, out_shape, scratch, args, spaces):
    return pl.pallas_call(
        kernel,
        out_shape=out_shape,
        in_specs=[pl.BlockSpec(memory_space=space) for space in spaces],
        out_specs=[pl.BlockSpec(memory_space=pltpu.VMEM)] * len(out_shape),
        scratch_shapes=scratch,
        compiler_params=pltpu.CompilerParams(vmem_limit_bytes=VMEM),
    )(*args)


def pairs(count, distance):
    return [(device, device ^ distance) for device in range(count)]


def partners(value, axis, count):
    came = {d: lax.ppermute(value(d), axis, pairs(count, d)) for d in range(count - 1, 0, -1)}
    return [came[d] for d in range(1, count)]


def total(terms):
    while len(terms) > 1:
        terms = [first + second for first, second in zip(terms[::2], terms[1::2])]
    return terms[0]


def in_order(came, me):
    count = came.shape[0]
    rest = came.shape[1:]
    bit = 1
    while bit < count:
        split = came.reshape((count // (2 * bit), 2, bit) + rest)
        came = jnp.where((me & bit) != 0, split[:, ::-1], split).reshape((count,) + rest)
        bit *= 2
    return came


def make(mesh):
    count_x = mesh.shape["gx"]
    count_y = mesh.shape["gy"]

    def on_device(field, active_rows, kern, target):
        tile_row = lax.axis_index("gx")
        block = lax.axis_index("gy")
        waves, polars = field.shape[0], field.shape[1]
        tiles = field.shape[4]
        rows_dev = field.shape[5]
        side = field.shape[6]
        focus = kern.shape[3]
        shape = (waves, polars, focus, 2 * focus)
        share, near_field, near_kern = call(
            share_kernel,
            [
                jax.ShapeDtypeStruct(shape, jnp.bfloat16),
                jax.ShapeDtypeStruct(field.shape[:3] + field.shape[4:], field.dtype),
                jax.ShapeDtypeStruct(kern.shape, kern.dtype),
            ],
            [
                pltpu.SMEM(active_rows.shape, jnp.int32),
                pltpu.VMEM((waves, 2 * side, polars * 2 * focus), jnp.bfloat16),
                pltpu.SemaphoreType.DMA((2 * waves + 1,)),
            ],
            [
                pltpu.with_memory_space_constraint(operand, pltpu.HBM)
                for operand in (active_rows, field, kern)
            ],
            [pltpu.HBM] * 3,
        )
        shares = [share] + partners(lambda d: share, "gy", count_y)
        share = total([term.astype(jnp.float32) for term in shares]).astype(jnp.bfloat16)
        shares = [share] + partners(lambda d: share, "gx", count_x)
        intensity, gradient = call(
            functools.partial(gradient_kernel, tiles * side / focus),
            [
                jax.ShapeDtypeStruct((waves, focus, focus), jnp.float32),
                jax.ShapeDtypeStruct((tiles, rows_dev, side), jnp.float32),
            ],
            [pltpu.VMEM((2 * side, polars * 2 * focus), jnp.float32)],
            (near_field, near_kern, target, *shares),
            [pltpu.VMEM] * (3 + count_x),
        )
        summed = gradient + lax.ppermute(gradient, "wa", pairs(2, 1))
        narrow = summed.astype(jnp.bfloat16)
        came = jnp.stack([narrow[0]] + partners(lambda d: narrow[d], "gx", count_x))

        def columns(of):
            return lax.dynamic_slice_in_dim(came, of * rows_dev, rows_dev, axis=2)

        def paired(d):
            half = columns(block ^ d)
            return jnp.concatenate([half[: tiles // 2], half[tiles // 2 :]], axis=2)

        others = [
            jnp.concatenate([term[:, :, :rows_dev], term[:, :, rows_dev:]], axis=0)
            for term in partners(paired, "gy", count_y)
        ]
        halves = in_order(jnp.stack([columns(block)] + others), block)
        partner = halves.transpose(1, 3, 0, 2).reshape(tiles, rows_dev, side)
        design_grad = in_order(0.5 * (summed + partner.astype(jnp.float32)), tile_row)
        return (design_grad[None], intensity)

    return on_device


def solution(mesh):
    placed = (
        P("wa", "cand", None, "gx", None, "gy", None),
        P("gx", None),
        P("wa", None, None, None, None),
        P("wa", None, None),
    )
    return jax.shard_map(
        make(mesh),
        mesh=mesh,
        in_specs=placed,
        out_specs=(P("gx", "cand", "gy", None), P("wa", "cand", None)),
        check_vma=False,
    )
```

```python
import functools

import jax
import jax.numpy as jnp
from jax import lax
from jax.experimental import pallas as pl
from jax.experimental.pallas import tpu as pltpu
from jax.sharding import PartitionSpec as P

VMEM = 16 * 2**20


def two_terms(value):
    high = value.astype(jnp.bfloat16)
    return high, (value - high.astype(jnp.float32)).astype(jnp.bfloat16)


def dot(first, second, over):
    return lax.dot_general(
        first, second, ((over[:1], over[1:]), ((), ())), preferred_element_type=jnp.float32
    )


def swapped(value, focus, left, right):
    lane = lax.broadcasted_iota(jnp.int32, value.shape, 1)
    sign = jnp.where(lane < focus, jnp.float32(left), jnp.float32(right))
    return pltpu.roll(value, focus, 1) * sign


def tile_kern(kern, wave, tile):
    real, imag = kern[wave, 0, tile], kern[wave, 1, tile]
    return jnp.concatenate([real, imag], axis=0), jnp.concatenate([-imag, real], axis=0)


def in_block(shape, block, width):
    lane = lax.broadcasted_iota(jnp.int32, shape, len(shape) - 1)
    return (lane >= block * width) & (lane < (block + 1) * width)


def side_by_side(first, second, block, blocks):
    width = first.shape[-1] // blocks
    first, second = first.astype(jnp.float32), second.astype(jnp.float32)
    beside = in_block(first.shape, lax.rem(block + 1, blocks), width)
    moved = jnp.where(beside, pltpu.roll(second, width, first.ndim - 1), 0.0)
    return jnp.where(in_block(first.shape, block, width), first, moved).astype(jnp.bfloat16)


def over_tiles(tiles, body, init):
    return lax.fori_loop(0, tiles, body, init, unroll=tiles <= 8)


def live_rows(rows, tile, shape):
    height = shape[-2]
    row = lax.axis_index("gy") * height + lax.broadcasted_iota(jnp.int32, shape, len(shape) - 2)
    return row < rows[0, tile]


def share_kernel(rows_far, field_far, kern_far, share, field, kern, rows, spread, arrived):
    waves, polars, _, tiles, height, side = field.shape
    focus = kern.shape[3]
    copies = [pltpu.make_async_copy(rows_far, rows, arrived.at[2 * waves])]
    for wave in range(waves):
        copies += [
            pltpu.make_async_copy(kern_far.at[wave], kern.at[wave], arrived.at[2 * wave]),
            pltpu.make_async_copy(
                field_far.at[wave, :, :, 0], field.at[wave], arrived.at[2 * wave + 1]
            ),
        ]
    for copy in copies:
        copy.start()
    tile_row = lax.axis_index("gx")
    first = pl.multiple_of(lax.axis_index("gy") * height, height)
    spread[...] = jnp.zeros_like(spread)
    copies[0].wait()
    for wave in range(waves):
        copies[2 * wave + 1].wait()
        copies[2 * wave + 2].wait()

        def add_tile(tile, inner):
            live = live_rows(rows, tile, (polars, height, side))
            planes = [
                jnp.where(live, field[wave, :, part, tile], jnp.zeros((), field.dtype))
                for part in range(2)
            ]
            for part in range(2):
                field[wave, :, part, tile] = planes[part]
            planes = [plane.reshape(polars * height, side) for plane in planes]
            return inner + dot(
                jnp.concatenate(planes, axis=1),
                jnp.concatenate(tile_kern(kern, wave, tile), axis=1),
                (1, 1),
            )

        inner = over_tiles(tiles, add_tile, jnp.zeros((polars * height, 2 * focus), jnp.float32))
        for polar in range(polars):
            lanes = pl.ds(polar * 2 * focus, 2 * focus)
            terms = two_terms(inner[polar * height : (polar + 1) * height])
            for index, term in enumerate(terms):
                spread[wave, pl.ds(index * side + first, height), lanes] = term
        own = tile_kern(kern, wave, tile_row)[0]
        both = dot(jnp.concatenate([own, own], axis=1), spread[wave], (1, 0))
        for polar in range(polars):
            lanes = slice(polar * 2 * focus, (polar + 1) * 2 * focus)
            straight, crossed = both[:focus, lanes], both[focus:, lanes]
            share[wave, polar] = (straight + swapped(crossed, focus, -1, 1)).astype(share.dtype)


def strip_kernel(field, kern, strip_kern, *strips):
    waves, polars, _, tiles, height, side = field.shape
    blocks = side // height
    block = lax.axis_index("gy")

    def one_tile(tile, carry):
        for wave in range(waves):
            strip_kern[wave, tile] = side_by_side(*tile_kern(kern, wave, tile), block, blocks)
            for polar in range(polars):
                for distance, strip in enumerate(strips, 1):
                    strip[wave, polar, tile] = side_by_side(
                        field[wave, polar, 0, tile],
                        field[wave, polar, 1, tile],
                        block ^ distance,
                        blocks,
                    )
        return carry

    over_tiles(tiles, one_tile, 0)


def gradient_kernel(scale, blocks, field, kern, strip_kern, target, *refs):
    strips, refs = refs[: blocks - 1], refs[blocks - 1 :]
    shares, (intensity, gradient, crossed, rowside, whole, turned) = refs[:-6], refs[-6:]
    waves, polars, _, tiles, height, side = field.shape
    focus = kern.shape[3]
    tile_row = lax.axis_index("gx")
    block = lax.axis_index("gy")
    sides = []
    for wave in range(waves):
        focal = [
            total([share[wave, polar].astype(jnp.float32) for share in shares])
            for polar in range(polars)
        ]
        power = sum(value * value for value in focal)
        power = power + pltpu.roll(power, focus, 1)
        intensity[wave] = power[:, :focus]
        goal = target[wave]
        excess = power - jnp.concatenate([goal, goal], axis=1)
        source = jnp.concatenate([excess * value for value in focal], axis=1)
        own = jnp.concatenate([kern[wave, 0, tile_row], kern[wave, 1, tile_row]], axis=1)
        rowside[...] = dot(
            jnp.concatenate([own, own], axis=0),
            jnp.concatenate(two_terms(source), axis=0),
            (0, 0),
        )
        near = []
        for distance in range(blocks):
            first = pl.multiple_of((block ^ distance) * height, height)
            parts = []
            for polar in range(polars):
                lanes = pl.ds(polar * 2 * focus, 2 * focus)
                straight = rowside[pl.ds(first, height), lanes]
                across = rowside[pl.ds(side + first, height), lanes]
                parts.append(straight + swapped(across, focus, 1, -1))
            terms = two_terms(jnp.concatenate(parts, axis=0))
            near.append(jnp.concatenate(terms, axis=1))
        sides.append(near)

    def twice(value):
        return jnp.concatenate([value, value], axis=0)

    def add_tile(distance, carry):
        tile = tile_row ^ distance
        term = jnp.zeros((height, side), jnp.float32)
        others = [jnp.zeros((height, side), jnp.float32) for _ in strips]
        for wave in range(waves):
            both = jnp.concatenate(tile_kern(kern, wave, tile), axis=1)
            back = dot(sides[wave][0], twice(both), (1, 0)).reshape(polars, height, 2 * side)
            for polar in range(polars):
                for part in range(2):
                    plane = field[wave, polar, part, tile].astype(jnp.float32)
                    term += back[polar, :, part * side : (part + 1) * side] * plane
            for index, strip in enumerate(strips):
                back = dot(sides[wave][index + 1], twice(strip_kern[wave, tile]), (1, 0))
                back = back.reshape(polars, height, side)
                for polar in range(polars):
                    others[index] += back[polar] * strip[wave, polar, tile].astype(jnp.float32)
        gradient[distance] = term * scale
        whole[pl.ds(pl.multiple_of(block * height, height), height)] = term * scale
        for index, other in enumerate(others):
            first = pl.multiple_of((block ^ (index + 1)) * height, height)
            whole[pl.ds(first, height)] = (other + pltpu.roll(other, side - height, 1)) * scale
        turned[...] = whole[...].T
        own = turned[pl.ds(pl.multiple_of(block * height, height), height)]
        crossed[distance] = own.astype(crossed.dtype)
        return carry

    over_tiles(tiles, add_tile, 0)


def call(kernel, out_shape, scratch, args, spaces):
    return pl.pallas_call(
        kernel,
        out_shape=out_shape,
        in_specs=[pl.BlockSpec(memory_space=space) for space in spaces],
        out_specs=[pl.BlockSpec(memory_space=pltpu.VMEM)] * len(out_shape),
        scratch_shapes=scratch,
        compiler_params=pltpu.CompilerParams(vmem_limit_bytes=VMEM),
    )(*args)


def pairs(count, distance):
    return [(device, device ^ distance) for device in range(count)]


def partners(value, axis, count):
    came = {d: lax.ppermute(value(d), axis, pairs(count, d)) for d in range(count - 1, 0, -1)}
    return [came[d] for d in range(1, count)]


def total(terms):
    while len(terms) > 1:
        terms = [first + second for first, second in zip(terms[::2], terms[1::2])]
    return terms[0]


def in_order(came, me):
    count = came.shape[0]
    rest = came.shape[1:]
    bit = 1
    while bit < count:
        split = came.reshape((count // (2 * bit), 2, bit) + rest)
        came = jnp.where((me & bit) != 0, split[:, ::-1], split).reshape((count,) + rest)
        bit *= 2
    return came


def make(mesh):
    count_x = mesh.shape["gx"]
    count_y = mesh.shape["gy"]

    def on_device(field, active_rows, kern, target):
        tile_row = lax.axis_index("gx")
        waves, polars = field.shape[0], field.shape[1]
        tiles = field.shape[4]
        rows_dev = field.shape[5]
        side = field.shape[6]
        focus = kern.shape[3]
        shape = (waves, polars, focus, 2 * focus)
        share, near_field, near_kern = call(
            share_kernel,
            [
                jax.ShapeDtypeStruct(shape, jnp.bfloat16),
                jax.ShapeDtypeStruct(field.shape[:3] + field.shape[4:], field.dtype),
                jax.ShapeDtypeStruct(kern.shape, kern.dtype),
            ],
            [
                pltpu.SMEM(active_rows.shape, jnp.int32),
                pltpu.VMEM((waves, 2 * side, polars * 2 * focus), jnp.bfloat16),
                pltpu.SemaphoreType.DMA((2 * waves + 1,)),
            ],
            [
                pltpu.with_memory_space_constraint(operand, pltpu.HBM)
                for operand in (active_rows, field, kern)
            ],
            [pltpu.HBM] * 3,
        )
        shares = [share] + partners(lambda d: share, "gy", count_y)
        share = total([term.astype(jnp.float32) for term in shares]).astype(jnp.bfloat16)
        strip_shape = (waves, polars, tiles, rows_dev, side)
        strip_kern, *strips = call(
            strip_kernel,
            [jax.ShapeDtypeStruct((waves, tiles, 2 * focus, side), kern.dtype)]
            + [jax.ShapeDtypeStruct(strip_shape, field.dtype)] * (count_y - 1),
            [],
            (near_field, near_kern),
            [pltpu.VMEM] * 2,
        )
        strips = partners(lambda d: strips[d - 1], "gy", count_y)
        shares = [share] + partners(lambda d: share, "gx", count_x)
        shape = (tiles, rows_dev, side)
        intensity, gradient, crossed = call(
            functools.partial(gradient_kernel, tiles * side / focus, count_y),
            [
                jax.ShapeDtypeStruct((waves, focus, focus), jnp.float32),
                jax.ShapeDtypeStruct(shape, jnp.float32),
                jax.ShapeDtypeStruct(shape, jnp.bfloat16),
            ],
            [pltpu.VMEM((2 * side, polars * 2 * focus), jnp.float32)]
            + [pltpu.VMEM((side, side), jnp.float32)] * 2,
            (near_field, near_kern, strip_kern, target, *strips, *shares),
            [pltpu.VMEM] * (3 + count_x + count_y),
        )
        partner = crossed.astype(jnp.float32) + lax.ppermute(crossed, "wa", pairs(2, 1)).astype(
            jnp.float32
        )
        narrow = partner.astype(jnp.bfloat16)
        came = [narrow[0]] + partners(lambda d: narrow[d], "gx", count_x)
        summed = gradient + lax.ppermute(gradient, "wa", pairs(2, 1))
        design_grad = in_order(0.5 * (summed + jnp.stack(came).astype(jnp.float32)), tile_row)
        return (design_grad[None], intensity)

    return on_device


def solution(mesh):
    placed = (
        P("wa", "cand", None, "gx", None, "gy", None),
        P("gx", None),
        P("wa", None, None, None, None),
        P("wa", None, None),
    )
    return jax.shard_map(
        make(mesh),
        mesh=mesh,
        in_specs=placed,
        out_specs=(P("gx", "cand", "gy", None), P("wa", "cand", None)),
        check_vma=False,
    )
```

```python
import functools

import jax
import jax.numpy as jnp
from jax import lax
from jax.experimental import pallas as pl
from jax.experimental.pallas import tpu as pltpu
from jax.sharding import PartitionSpec as P

VMEM = 16 * 2**20


def two_terms(value):
    high = value.astype(jnp.bfloat16)
    return high, (value - high.astype(jnp.float32)).astype(jnp.bfloat16)


def dot(first, second, over):
    return lax.dot_general(
        first, second, ((over[:1], over[1:]), ((), ())), preferred_element_type=jnp.float32
    )


def swapped(value, focus, left, right):
    lane = lax.broadcasted_iota(jnp.int32, value.shape, 1)
    sign = jnp.where(lane < focus, jnp.float32(left), jnp.float32(right))
    return pltpu.roll(value, focus, 1) * sign


def tile_kern(kern, wave, tile):
    real, imag = kern[wave, 0, tile], kern[wave, 1, tile]
    return jnp.concatenate([real, imag], axis=0), jnp.concatenate([-imag, real], axis=0)


def in_block(shape, block, width):
    lane = lax.broadcasted_iota(jnp.int32, shape, len(shape) - 1)
    return (lane >= block * width) & (lane < (block + 1) * width)


def side_by_side(first, second, block, blocks):
    width = first.shape[-1] // blocks
    first, second = first.astype(jnp.float32), second.astype(jnp.float32)
    beside = in_block(first.shape, lax.rem(block + 1, blocks), width)
    moved = jnp.where(beside, pltpu.roll(second, width, first.ndim - 1), 0.0)
    return jnp.where(in_block(first.shape, block, width), first, moved).astype(jnp.bfloat16)


def over_tiles(tiles, body, init):
    return lax.fori_loop(0, tiles, body, init, unroll=tiles <= 8)


def live_rows(rows, tile, shape):
    height = shape[-2]
    row = lax.axis_index("gy") * height + lax.broadcasted_iota(jnp.int32, shape, len(shape) - 2)
    return row < rows[0, tile]


def share_kernel(rows_far, field_far, kern_far, share, field, kern, rows, spread, arrived):
    waves, polars, _, tiles, height, side = field.shape
    focus = kern.shape[3]
    copies = [pltpu.make_async_copy(rows_far, rows, arrived.at[2 * waves])]
    for wave in range(waves):
        copies += [
            pltpu.make_async_copy(kern_far.at[wave], kern.at[wave], arrived.at[2 * wave]),
            pltpu.make_async_copy(
                field_far.at[wave, :, :, 0], field.at[wave], arrived.at[2 * wave + 1]
            ),
        ]
    for copy in copies:
        copy.start()
    tile_row = lax.axis_index("gx")
    first = pl.multiple_of(lax.axis_index("gy") * height, height)
    spread[...] = jnp.zeros_like(spread)
    copies[0].wait()
    inner = []
    for wave in range(waves):
        copies[2 * wave + 1].wait()
        copies[2 * wave + 2].wait()

        def add_tile(tile, value):
            live = live_rows(rows, tile, (polars, height, side))
            planes = [
                jnp.where(live, field[wave, :, part, tile], jnp.zeros((), field.dtype))
                for part in range(2)
            ]
            for part in range(2):
                field[wave, :, part, tile] = planes[part]
            planes = [plane.reshape(polars * height, side) for plane in planes]
            return value + dot(
                jnp.concatenate(planes, axis=1),
                jnp.concatenate(tile_kern(kern, wave, tile), axis=1),
                (1, 1),
            )

        zero = jnp.zeros((polars * height, 2 * focus), jnp.float32)
        inner.append(over_tiles(tiles, add_tile, zero))
    for wave in range(waves):
        for polar in range(polars):
            lanes = pl.ds(polar * 2 * focus, 2 * focus)
            terms = two_terms(inner[wave][polar * height : (polar + 1) * height])
            for index, term in enumerate(terms):
                spread[wave, pl.ds(index * side + first, height), lanes] = term
        own = tile_kern(kern, wave, tile_row)[0]
        both = dot(jnp.concatenate([own, own], axis=1), spread[wave], (1, 0))
        for polar in range(polars):
            lanes = slice(polar * 2 * focus, (polar + 1) * 2 * focus)
            straight, crossed = both[:focus, lanes], both[focus:, lanes]
            share[wave, polar] = (straight + swapped(crossed, focus, -1, 1)).astype(share.dtype)


def strip_kernel(field, kern, own_kern, both_kern, strip_kern, *strips):
    waves, polars, _, tiles, height, side = field.shape
    blocks = side // height
    block = lax.axis_index("gy")
    tile_row = lax.axis_index("gx")
    for wave in range(waves):
        for part in range(2):
            turned = kern[wave, part, tile_row].astype(jnp.float32).T.astype(kern.dtype)
            own_kern[wave, pl.ds(part * side, side)] = jnp.concatenate([turned, turned], axis=1)

    def one_tile(tile, carry):
        for wave in range(waves):
            parts = tile_kern(kern, wave, tile)
            both_kern[wave, tile] = jnp.concatenate(parts, axis=1)
            strip_kern[wave, tile] = side_by_side(*parts, block, blocks)
            for polar in range(polars):
                for distance, strip in enumerate(strips, 1):
                    strip[wave, polar, tile] = side_by_side(
                        field[wave, polar, 0, tile],
                        field[wave, polar, 1, tile],
                        block ^ distance,
                        blocks,
                    )
        return carry

    over_tiles(tiles, one_tile, 0)


def gradient_kernel(scale, blocks, field, own_kern, both_kern, strip_kern, target, *refs):
    strips, refs = refs[: blocks - 1], refs[blocks - 1 :]
    shares, (intensity, gradient, crossed, rowside, whole, turned) = refs[:-6], refs[-6:]
    waves, polars, _, tiles, height, side = field.shape
    focus = target.shape[1]
    tile_row = lax.axis_index("gx")
    block = lax.axis_index("gy")
    sides = []
    for wave in range(waves):
        focal = [
            total([share[wave, polar].astype(jnp.float32) for share in shares])
            for polar in range(polars)
        ]
        power = sum(value * value for value in focal)
        power = power + pltpu.roll(power, focus, 1)
        intensity[wave] = power[:, :focus]
        goal = target[wave]
        excess = power - jnp.concatenate([goal, goal], axis=1)
        source = jnp.concatenate([excess * value for value in focal], axis=1)
        terms = jnp.concatenate(two_terms(source), axis=0)
        rowside[wave] = dot(own_kern[wave], terms, (1, 0))
    for wave in range(waves):
        near = []
        for distance in range(blocks):
            first = pl.multiple_of((block ^ distance) * height, height)
            parts = []
            for polar in range(polars):
                lanes = pl.ds(polar * 2 * focus, 2 * focus)
                straight = rowside[wave, pl.ds(first, height), lanes]
                across = rowside[wave, pl.ds(side + first, height), lanes]
                parts.append(straight + swapped(across, focus, 1, -1))
            terms = two_terms(jnp.concatenate(parts, axis=0))
            near.append(jnp.concatenate(terms, axis=1))
        sides.append(near)

    def twice(value):
        return jnp.concatenate([value, value], axis=0)

    def add_tile(distance, carry):
        tile = tile_row ^ distance
        term = jnp.zeros((height, side), jnp.float32)
        others = [jnp.zeros((height, side), jnp.float32) for _ in strips]
        for wave in range(waves):
            back = dot(sides[wave][0], twice(both_kern[wave, tile]), (1, 0)).reshape(polars, height, 2 * side)
            for polar in range(polars):
                for part in range(2):
                    plane = field[wave, polar, part, tile].astype(jnp.float32)
                    term += back[polar, :, part * side : (part + 1) * side] * plane
            for index, strip in enumerate(strips):
                back = dot(sides[wave][index + 1], twice(strip_kern[wave, tile]), (1, 0))
                back = back.reshape(polars, height, side)
                for polar in range(polars):
                    others[index] += back[polar] * strip[wave, polar, tile].astype(jnp.float32)
        gradient[distance] = term * scale
        whole[pl.ds(pl.multiple_of(block * height, height), height)] = term * scale
        for index, other in enumerate(others):
            first = pl.multiple_of((block ^ (index + 1)) * height, height)
            whole[pl.ds(first, height)] = (other + pltpu.roll(other, side - height, 1)) * scale
        turned[...] = whole[...].T
        own = turned[pl.ds(pl.multiple_of(block * height, height), height)]
        crossed[distance] = own.astype(crossed.dtype)
        return carry

    over_tiles(tiles, add_tile, 0)


def call(kernel, out_shape, scratch, args, spaces):
    return pl.pallas_call(
        kernel,
        out_shape=out_shape,
        in_specs=[pl.BlockSpec(memory_space=space) for space in spaces],
        out_specs=[pl.BlockSpec(memory_space=pltpu.VMEM)] * len(out_shape),
        scratch_shapes=scratch,
        compiler_params=pltpu.CompilerParams(vmem_limit_bytes=VMEM),
    )(*args)


def pairs(count, distance):
    return [(device, device ^ distance) for device in range(count)]


def partners(value, axis, count):
    came = {d: lax.ppermute(value(d), axis, pairs(count, d)) for d in range(count - 1, 0, -1)}
    return [came[d] for d in range(1, count)]


def total(terms):
    while len(terms) > 1:
        terms = [first + second for first, second in zip(terms[::2], terms[1::2])]
    return terms[0]


def in_order(came, me):
    count = came.shape[0]
    rest = came.shape[1:]
    bit = 1
    while bit < count:
        split = came.reshape((count // (2 * bit), 2, bit) + rest)
        came = jnp.where((me & bit) != 0, split[:, ::-1], split).reshape((count,) + rest)
        bit *= 2
    return came


def make(mesh):
    count_x = mesh.shape["gx"]
    count_y = mesh.shape["gy"]

    def on_device(field, active_rows, kern, target):
        tile_row = lax.axis_index("gx")
        waves, polars = field.shape[0], field.shape[1]
        tiles = field.shape[4]
        rows_dev = field.shape[5]
        side = field.shape[6]
        focus = kern.shape[3]
        shape = (waves, polars, focus, 2 * focus)
        share, near_field, near_kern = call(
            share_kernel,
            [
                jax.ShapeDtypeStruct(shape, jnp.bfloat16),
                jax.ShapeDtypeStruct(field.shape[:3] + field.shape[4:], field.dtype),
                jax.ShapeDtypeStruct(kern.shape, kern.dtype),
            ],
            [
                pltpu.SMEM(active_rows.shape, jnp.int32),
                pltpu.VMEM((waves, 2 * side, polars * 2 * focus), jnp.bfloat16),
                pltpu.SemaphoreType.DMA((2 * waves + 1,)),
            ],
            [
                pltpu.with_memory_space_constraint(operand, pltpu.HBM)
                for operand in (active_rows, field, kern)
            ],
            [pltpu.HBM] * 3,
        )
        shares = [share] + partners(lambda d: share, "gy", count_y)
        share = total([term.astype(jnp.float32) for term in shares]).astype(jnp.bfloat16)
        strip_shape = (waves, polars, tiles, rows_dev, side)
        own_kern, both_kern, strip_kern, *strips = call(
            strip_kernel,
            [
                jax.ShapeDtypeStruct((waves, 2 * side, 2 * focus), kern.dtype),
                jax.ShapeDtypeStruct((waves, tiles, 2 * focus, 2 * side), kern.dtype),
                jax.ShapeDtypeStruct((waves, tiles, 2 * focus, side), kern.dtype),
            ]
            + [jax.ShapeDtypeStruct(strip_shape, field.dtype)] * (count_y - 1),
            [],
            (near_field, near_kern),
            [pltpu.VMEM] * 2,
        )
        strips = partners(lambda d: strips[d - 1], "gy", count_y)
        shares = [share] + partners(lambda d: share, "gx", count_x)
        shape = (tiles, rows_dev, side)
        intensity, gradient, crossed = call(
            functools.partial(gradient_kernel, tiles * side / focus, count_y),
            [
                jax.ShapeDtypeStruct((waves, focus, focus), jnp.float32),
                jax.ShapeDtypeStruct(shape, jnp.float32),
                jax.ShapeDtypeStruct(shape, jnp.bfloat16),
            ],
            [pltpu.VMEM((waves, 2 * side, polars * 2 * focus), jnp.float32)]
            + [pltpu.VMEM((side, side), jnp.float32)] * 2,
            (near_field, own_kern, both_kern, strip_kern, target, *strips, *shares),
            [pltpu.VMEM] * (4 + count_x + count_y),
        )
        partner = crossed.astype(jnp.float32) + lax.ppermute(crossed, "wa", pairs(2, 1)).astype(
            jnp.float32
        )
        narrow = partner.astype(jnp.bfloat16)
        came = [narrow[0]] + partners(lambda d: narrow[d], "gx", count_x)
        summed = gradient + lax.ppermute(gradient, "wa", pairs(2, 1))
        design_grad = in_order(0.5 * (summed + jnp.stack(came).astype(jnp.float32)), tile_row)
        return (design_grad[None], intensity)

    return on_device


def solution(mesh):
    placed = (
        P("wa", "cand", None, "gx", None, "gy", None),
        P("gx", None),
        P("wa", None, None, None, None),
        P("wa", None, None),
    )
    return jax.shard_map(
        make(mesh),
        mesh=mesh,
        in_specs=placed,
        out_specs=(P("gx", "cand", "gy", None), P("wa", "cand", None)),
        check_vma=False,
    )
```

```python
import functools

import jax
import jax.numpy as jnp
from jax import lax
from jax.experimental import pallas as pl
from jax.experimental.pallas import tpu as pltpu
from jax.sharding import PartitionSpec as P

VMEM = 16 * 2**20


def two_terms(value):
    high = value.astype(jnp.bfloat16)
    return high, (value - high.astype(jnp.float32)).astype(jnp.bfloat16)


def dot(first, second, over):
    return lax.dot_general(
        first, second, ((over[:1], over[1:]), ((), ())), preferred_element_type=jnp.float32
    )


def swapped(value, focus, left, right):
    lane = lax.broadcasted_iota(jnp.int32, value.shape, 1)
    sign = jnp.where(lane < focus, jnp.float32(left), jnp.float32(right))
    return pltpu.roll(value, focus, 1) * sign


def tile_kern(kern, wave, tile):
    real, imag = kern[wave, 0, tile], kern[wave, 1, tile]
    return jnp.concatenate([real, imag], axis=0), jnp.concatenate([-imag, real], axis=0)


def in_block(shape, block, width):
    lane = lax.broadcasted_iota(jnp.int32, shape, len(shape) - 1)
    return (lane >= block * width) & (lane < (block + 1) * width)


def side_by_side(first, second, block, blocks):
    width = first.shape[-1] // blocks
    first, second = first.astype(jnp.float32), second.astype(jnp.float32)
    beside = in_block(first.shape, lax.rem(block + 1, blocks), width)
    moved = jnp.where(beside, pltpu.roll(second, width, first.ndim - 1), 0.0)
    return jnp.where(in_block(first.shape, block, width), first, moved).astype(jnp.bfloat16)


def over_tiles(tiles, body, init):
    return lax.fori_loop(0, tiles, body, init, unroll=tiles <= 8)


def live_rows(rows, tile, shape):
    height = shape[-2]
    row = lax.axis_index("gy") * height + lax.broadcasted_iota(jnp.int32, shape, len(shape) - 2)
    return row < rows[0, tile]


def share_kernel(rows_far, field_far, kern_far, share, field, kern, rows, spread, arrived):
    waves, polars, _, tiles, height, side = field.shape
    focus = kern.shape[3]
    copies = [pltpu.make_async_copy(rows_far, rows, arrived.at[2 * waves])]
    for wave in range(waves):
        copies += [
            pltpu.make_async_copy(kern_far.at[wave], kern.at[wave], arrived.at[2 * wave]),
            pltpu.make_async_copy(
                field_far.at[wave, :, :, 0], field.at[wave], arrived.at[2 * wave + 1]
            ),
        ]
    for copy in copies:
        copy.start()
    tile_row = lax.axis_index("gx")
    first = pl.multiple_of(lax.axis_index("gy") * height, height)
    spread[...] = jnp.zeros_like(spread)
    copies[0].wait()
    inner = []
    for wave in range(waves):
        copies[2 * wave + 1].wait()
        copies[2 * wave + 2].wait()

        def add_tile(tile, value):
            live = live_rows(rows, tile, (polars, height, side))
            planes = [
                jnp.where(live, field[wave, :, part, tile], jnp.zeros((), field.dtype))
                for part in range(2)
            ]
            for part in range(2):
                field[wave, :, part, tile] = planes[part]
            planes = [plane.reshape(polars * height, side) for plane in planes]
            return value + dot(
                jnp.concatenate(planes, axis=1),
                jnp.concatenate(tile_kern(kern, wave, tile), axis=1),
                (1, 1),
            )

        zero = jnp.zeros((polars * height, 2 * focus), jnp.float32)
        inner.append(over_tiles(tiles, add_tile, zero))
    for wave in range(waves):
        for polar in range(polars):
            lanes = pl.ds(polar * 2 * focus, 2 * focus)
            terms = two_terms(inner[wave][polar * height : (polar + 1) * height])
            for index, term in enumerate(terms):
                spread[wave, pl.ds(index * side + first, height), lanes] = term
        own = tile_kern(kern, wave, tile_row)[0]
        both = dot(jnp.concatenate([own, own], axis=1), spread[wave], (1, 0))
        for polar in range(polars):
            lanes = slice(polar * 2 * focus, (polar + 1) * 2 * focus)
            straight, crossed = both[:focus, lanes], both[focus:, lanes]
            share[wave, polar] = (straight + swapped(crossed, focus, -1, 1)).astype(share.dtype)


def strip_kernel(field, kern, own_kern, both_kern, strip_kern, *strips):
    waves, polars, _, tiles, height, side = field.shape
    blocks = side // height
    block = lax.axis_index("gy")
    tile_row = lax.axis_index("gx")
    for wave in range(waves):
        for part in range(2):
            turned = kern[wave, part, tile_row].astype(jnp.float32).T.astype(kern.dtype)
            own_kern[wave, pl.ds(part * side, side)] = jnp.concatenate([turned, turned], axis=1)

    def one_tile(tile, carry):
        for wave in range(waves):
            parts = tile_kern(kern, wave, tile)
            both_kern[wave, tile] = jnp.concatenate(parts, axis=1)
            strip_kern[wave, tile] = side_by_side(*parts, block, blocks)
            for polar in range(polars):
                for distance, strip in enumerate(strips, 1):
                    strip[wave, polar, tile] = side_by_side(
                        field[wave, polar, 0, tile],
                        field[wave, polar, 1, tile],
                        block ^ distance,
                        blocks,
                    )
        return carry

    over_tiles(tiles, one_tile, 0)


def gradient_kernel(scale, blocks, field, own_kern, both_kern, strip_kern, target, *refs):
    strips, refs = refs[: blocks - 1], refs[blocks - 1 :]
    shares, (intensity, gradient, crossed, rowside, whole, turned) = refs[:-6], refs[-6:]
    waves, polars, _, tiles, height, side = field.shape
    focus = target.shape[1]
    tile_row = lax.axis_index("gx")
    block = lax.axis_index("gy")
    sides = []
    for wave in range(waves):
        focal = [
            total([share[wave, polar].astype(jnp.float32) for share in shares])
            for polar in range(polars)
        ]
        power = sum(value * value for value in focal)
        power = power + pltpu.roll(power, focus, 1)
        intensity[wave] = power[:, :focus]
        goal = target[wave]
        excess = power - jnp.concatenate([goal, goal], axis=1)
        source = jnp.concatenate([excess * value for value in focal], axis=1)
        terms = jnp.concatenate(two_terms(source), axis=0)
        rowside[wave] = dot(own_kern[wave], terms, (1, 0))
    for wave in range(waves):
        near = []
        for distance in range(blocks):
            first = pl.multiple_of((block ^ distance) * height, height)
            parts = []
            for polar in range(polars):
                lanes = pl.ds(polar * 2 * focus, 2 * focus)
                straight = rowside[wave, pl.ds(first, height), lanes]
                across = rowside[wave, pl.ds(side + first, height), lanes]
                parts.append(straight + swapped(across, focus, 1, -1))
            terms = two_terms(jnp.concatenate(parts, axis=0))
            near.append(jnp.concatenate(terms, axis=1))
        sides.append(near)

    def twice(value):
        return jnp.concatenate([value, value], axis=0)

    def add_tile(distance, carry):
        tile = tile_row ^ distance
        term = jnp.zeros((height, side), jnp.float32)
        others = [jnp.zeros((height, side), jnp.float32) for _ in strips]
        for wave in range(waves):
            back = dot(sides[wave][0], twice(both_kern[wave, tile]), (1, 0)).reshape(polars, height, 2 * side)
            for polar in range(polars):
                for part in range(2):
                    plane = field[wave, polar, part, tile].astype(jnp.float32)
                    term += back[polar, :, part * side : (part + 1) * side] * plane
            for index, strip in enumerate(strips):
                back = dot(sides[wave][index + 1], twice(strip_kern[wave, tile]), (1, 0))
                back = back.reshape(polars, height, side)
                for polar in range(polars):
                    others[index] += back[polar] * strip[wave, polar, tile].astype(jnp.float32)
        gradient[distance] = term * scale
        whole[pl.ds(pl.multiple_of(block * height, height), height)] = term * scale
        for index, other in enumerate(others):
            first = pl.multiple_of((block ^ (index + 1)) * height, height)
            whole[pl.ds(first, height)] = (other + pltpu.roll(other, side - height, 1)) * scale
        turned[...] = whole[...].T
        own = turned[pl.ds(pl.multiple_of(block * height, height), height)]
        crossed[distance] = own.astype(crossed.dtype)
        return carry

    over_tiles(tiles, add_tile, 0)


def call(kernel, out_shape, scratch, args, spaces):
    return pl.pallas_call(
        kernel,
        out_shape=out_shape,
        in_specs=[pl.BlockSpec(memory_space=space) for space in spaces],
        out_specs=[pl.BlockSpec(memory_space=pltpu.VMEM)] * len(out_shape),
        scratch_shapes=scratch,
        compiler_params=pltpu.CompilerParams(vmem_limit_bytes=VMEM),
    )(*args)


def pairs(count, distance):
    return [(device, device ^ distance) for device in range(count)]


def partners(value, axis, count):
    came = {d: lax.ppermute(value(d), axis, pairs(count, d)) for d in range(count - 1, 0, -1)}
    return [came[d] for d in range(1, count)]


def total(terms):
    while len(terms) > 1:
        terms = [first + second for first, second in zip(terms[::2], terms[1::2])]
    return terms[0]


def in_order(came, me):
    count = came.shape[0]
    rest = came.shape[1:]
    bit = 1
    while bit < count:
        split = came.reshape((count // (2 * bit), 2, bit) + rest)
        came = jnp.where((me & bit) != 0, split[:, ::-1], split).reshape((count,) + rest)
        bit *= 2
    return came


def make(mesh):
    count_x = mesh.shape["gx"]
    count_y = mesh.shape["gy"]

    def on_device(field, active_rows, kern, target):
        tile_row = lax.axis_index("gx")
        waves, polars = field.shape[0], field.shape[1]
        tiles = field.shape[4]
        rows_dev = field.shape[5]
        side = field.shape[6]
        focus = kern.shape[3]
        shape = (waves, polars, focus, 2 * focus)
        share, near_field, near_kern = call(
            share_kernel,
            [
                jax.ShapeDtypeStruct(shape, jnp.bfloat16),
                jax.ShapeDtypeStruct(field.shape[:3] + field.shape[4:], field.dtype),
                jax.ShapeDtypeStruct(kern.shape, kern.dtype),
            ],
            [
                pltpu.SMEM(active_rows.shape, jnp.int32),
                pltpu.VMEM((waves, 2 * side, polars * 2 * focus), jnp.bfloat16),
                pltpu.SemaphoreType.DMA((2 * waves + 1,)),
            ],
            [
                pltpu.with_memory_space_constraint(operand, pltpu.HBM)
                for operand in (active_rows, field, kern)
            ],
            [pltpu.HBM] * 3,
        )
        shares = [share] + partners(lambda d: share, "gy", count_y)
        share = total([term.astype(jnp.float32) for term in shares]).astype(jnp.bfloat16)
        strip_shape = (waves, polars, tiles, rows_dev, side)
        own_kern, both_kern, strip_kern, *strips = call(
            strip_kernel,
            [
                jax.ShapeDtypeStruct((waves, 2 * side, 2 * focus), kern.dtype),
                jax.ShapeDtypeStruct((waves, tiles, 2 * focus, 2 * side), kern.dtype),
                jax.ShapeDtypeStruct((waves, tiles, 2 * focus, side), kern.dtype),
            ]
            + [jax.ShapeDtypeStruct(strip_shape, field.dtype)] * (count_y - 1),
            [],
            (near_field, near_kern),
            [pltpu.VMEM] * 2,
        )
        strips = partners(lambda d: strips[d - 1], "gy", count_y)
        shares = [share] + partners(lambda d: share, "gx", count_x)
        shares = shares[::-1]
        shape = (tiles, rows_dev, side)
        intensity, gradient, crossed = call(
            functools.partial(gradient_kernel, tiles * side / focus, count_y),
            [
                jax.ShapeDtypeStruct((waves, focus, focus), jnp.float32),
                jax.ShapeDtypeStruct(shape, jnp.float32),
                jax.ShapeDtypeStruct(shape, jnp.bfloat16),
            ],
            [pltpu.VMEM((waves, 2 * side, polars * 2 * focus), jnp.float32)]
            + [pltpu.VMEM((side, side), jnp.float32)] * 2,
            (near_field, own_kern, both_kern, strip_kern, target, *strips, *shares),
            [pltpu.VMEM] * (4 + count_x + count_y),
        )
        partner = crossed.astype(jnp.float32) + lax.ppermute(crossed, "wa", pairs(2, 1)).astype(
            jnp.float32
        )
        narrow = partner.astype(jnp.bfloat16)
        came = [narrow[0]] + partners(lambda d: narrow[d], "gx", count_x)
        summed = gradient + lax.ppermute(gradient, "wa", pairs(2, 1))
        design_grad = in_order(0.5 * (summed + jnp.stack(came).astype(jnp.float32)), tile_row)
        return (design_grad[None], intensity)

    return on_device


def solution(mesh):
    placed = (
        P("wa", "cand", None, "gx", None, "gy", None),
        P("gx", None),
        P("wa", None, None, None, None),
        P("wa", None, None),
    )
    return jax.shard_map(
        make(mesh),
        mesh=mesh,
        in_specs=placed,
        out_specs=(P("gx", "cand", "gy", None), P("wa", "cand", None)),
        check_vma=False,
    )
```

```python
import functools

import jax
import jax.numpy as jnp
from jax import lax
from jax.experimental import pallas as pl
from jax.experimental.pallas import tpu as pltpu
from jax.sharding import PartitionSpec as P

VMEM = 16 * 2**20


def two_terms(value):
    high = value.astype(jnp.bfloat16)
    return high, (value - high.astype(jnp.float32)).astype(jnp.bfloat16)


def dot(first, second, over):
    return lax.dot_general(
        first, second, ((over[:1], over[1:]), ((), ())), preferred_element_type=jnp.float32
    )


def swapped(value, focus, left, right):
    lane = lax.broadcasted_iota(jnp.int32, value.shape, 1)
    sign = jnp.where(lane < focus, jnp.float32(left), jnp.float32(right))
    return pltpu.roll(value, focus, 1) * sign


def tile_kern(kern, wave, tile):
    real, imag = kern[wave, 0, tile], kern[wave, 1, tile]
    return jnp.concatenate([real, imag], axis=0), jnp.concatenate([-imag, real], axis=0)


def in_block(shape, block, width):
    lane = lax.broadcasted_iota(jnp.int32, shape, len(shape) - 1)
    return (lane >= block * width) & (lane < (block + 1) * width)


def side_by_side(first, second, block, blocks):
    width = first.shape[-1] // blocks
    first, second = first.astype(jnp.float32), second.astype(jnp.float32)
    beside = in_block(first.shape, lax.rem(block + 1, blocks), width)
    moved = jnp.where(beside, pltpu.roll(second, width, first.ndim - 1), 0.0)
    return jnp.where(in_block(first.shape, block, width), first, moved).astype(jnp.bfloat16)


def over_tiles(tiles, body, init):
    return lax.fori_loop(0, tiles, body, init, unroll=tiles <= 8)


def live_rows(rows, tile, shape):
    height = shape[-2]
    row = lax.axis_index("gy") * height + lax.broadcasted_iota(jnp.int32, shape, len(shape) - 2)
    return row < rows[0, tile]


def share_kernel(rows_far, field_far, kern_far, share, field, kern, rows, spread, arrived):
    waves, polars, _, tiles, height, side = field.shape
    focus = kern.shape[3]
    copies = [pltpu.make_async_copy(rows_far, rows, arrived.at[2 * waves])]
    for wave in range(waves):
        copies += [
            pltpu.make_async_copy(kern_far.at[wave], kern.at[wave], arrived.at[2 * wave]),
            pltpu.make_async_copy(
                field_far.at[wave, :, :, 0], field.at[wave], arrived.at[2 * wave + 1]
            ),
        ]
    for copy in copies:
        copy.start()
    tile_row = lax.axis_index("gx")
    first = pl.multiple_of(lax.axis_index("gy") * height, height)
    spread[...] = jnp.zeros_like(spread)
    copies[0].wait()
    inner = []
    for wave in range(waves):
        copies[2 * wave + 1].wait()
        copies[2 * wave + 2].wait()

        def add_tile(tile, value):
            live = live_rows(rows, tile, (polars, height, side))
            planes = [
                jnp.where(live, field[wave, :, part, tile], jnp.zeros((), field.dtype))
                for part in range(2)
            ]
            for part in range(2):
                field[wave, :, part, tile] = planes[part]
            planes = [plane.reshape(polars * height, side) for plane in planes]
            return value + dot(
                jnp.concatenate(planes, axis=1),
                jnp.concatenate(tile_kern(kern, wave, tile), axis=1),
                (1, 1),
            )

        zero = jnp.zeros((polars * height, 2 * focus), jnp.float32)
        inner.append(over_tiles(tiles, add_tile, zero))
    for wave in range(waves):
        for polar in range(polars):
            lanes = pl.ds(polar * 2 * focus, 2 * focus)
            terms = two_terms(inner[wave][polar * height : (polar + 1) * height])
            for index, term in enumerate(terms):
                spread[wave, pl.ds(index * side + first, height), lanes] = term
        own = tile_kern(kern, wave, tile_row)[0]
        both = dot(jnp.concatenate([own, own], axis=1), spread[wave], (1, 0))
        for polar in range(polars):
            lanes = slice(polar * 2 * focus, (polar + 1) * 2 * focus)
            straight, crossed = both[:focus, lanes], both[focus:, lanes]
            share[wave, polar] = (straight + swapped(crossed, focus, -1, 1)).astype(share.dtype)


def strip_kernel(field, kern, own_kern, both_kern, strip_kern, *strips):
    waves, polars, _, tiles, height, side = field.shape
    blocks = side // height
    block = lax.axis_index("gy")
    tile_row = lax.axis_index("gx")
    for wave in range(waves):
        for part in range(2):
            turned = kern[wave, part, tile_row].astype(jnp.float32).T.astype(kern.dtype)
            own_kern[wave, pl.ds(part * side, side)] = jnp.concatenate([turned, turned], axis=1)

    def one_tile(tile, carry):
        for wave in range(waves):
            parts = tile_kern(kern, wave, tile)
            both_kern[wave, tile] = jnp.concatenate(parts, axis=1)
            strip_kern[wave, tile] = side_by_side(*parts, block, blocks)
            for polar in range(polars):
                for distance, strip in enumerate(strips, 1):
                    strip[wave, polar, tile] = side_by_side(
                        field[wave, polar, 0, tile],
                        field[wave, polar, 1, tile],
                        block ^ distance,
                        blocks,
                    )
        return carry

    over_tiles(tiles, one_tile, 0)


def gradient_kernel(scale, blocks, field, own_kern, both_kern, strip_kern, target, *refs):
    strips, refs = refs[: blocks - 1], refs[blocks - 1 :]
    shares, (intensity, gradient, crossed, rowside, whole, turned) = refs[:-6], refs[-6:]
    waves, polars, _, tiles, height, side = field.shape
    focus = target.shape[1]
    tile_row = lax.axis_index("gx")
    block = lax.axis_index("gy")
    sides = []
    for wave in range(waves):
        focal = [
            total([share[wave, polar].astype(jnp.float32) for share in shares])
            for polar in range(polars)
        ]
        power = sum(value * value for value in focal)
        power = power + pltpu.roll(power, focus, 1)
        intensity[wave] = power[:, :focus]
        goal = target[wave]
        excess = power - jnp.concatenate([goal, goal], axis=1)
        source = jnp.concatenate([excess * value for value in focal], axis=1)
        terms = jnp.concatenate(two_terms(source), axis=0)
        rowside[wave] = dot(own_kern[wave], terms, (1, 0))
    for wave in range(waves):
        near = []
        for distance in range(blocks):
            first = pl.multiple_of((block ^ distance) * height, height)
            parts = []
            for polar in range(polars):
                lanes = pl.ds(polar * 2 * focus, 2 * focus)
                straight = rowside[wave, pl.ds(first, height), lanes]
                across = rowside[wave, pl.ds(side + first, height), lanes]
                parts.append(straight + swapped(across, focus, 1, -1))
            terms = two_terms(jnp.concatenate(parts, axis=0))
            near.append(jnp.concatenate(terms, axis=1))
        sides.append(near)

    def twice(value):
        return jnp.concatenate([value, value], axis=0)

    def add_tile(distance, carry):
        tile = tile_row ^ distance
        term = jnp.zeros((height, side), jnp.float32)
        others = [jnp.zeros((height, side), jnp.float32) for _ in strips]
        for wave in range(waves):
            back = dot(sides[wave][0], twice(both_kern[wave, tile]), (1, 0)).reshape(polars, height, 2 * side)
            for polar in range(polars):
                for part in range(2):
                    plane = field[wave, polar, part, tile].astype(jnp.float32)
                    term += back[polar, :, part * side : (part + 1) * side] * plane
            for index, strip in enumerate(strips):
                back = dot(sides[wave][index + 1], twice(strip_kern[wave, tile]), (1, 0))
                back = back.reshape(polars, height, side)
                for polar in range(polars):
                    others[index] += back[polar] * strip[wave, polar, tile].astype(jnp.float32)
        gradient[distance] = term * scale
        whole[pl.ds(pl.multiple_of(block * height, height), height)] = term * scale
        for index, other in enumerate(others):
            first = pl.multiple_of((block ^ (index + 1)) * height, height)
            whole[pl.ds(first, height)] = (other + pltpu.roll(other, side - height, 1)) * scale
        turned[...] = whole[...].T
        own = turned[pl.ds(pl.multiple_of(block * height, height), height)]
        crossed[distance] = own.astype(crossed.dtype)
        return carry

    over_tiles(tiles, add_tile, 0)


def call(kernel, out_shape, scratch, args, spaces):
    return pl.pallas_call(
        kernel,
        out_shape=out_shape,
        in_specs=[pl.BlockSpec(memory_space=space) for space in spaces],
        out_specs=[pl.BlockSpec(memory_space=pltpu.VMEM)] * len(out_shape),
        scratch_shapes=scratch,
        compiler_params=pltpu.CompilerParams(vmem_limit_bytes=VMEM),
    )(*args)


def pairs(count, distance):
    return [(device, device ^ distance) for device in range(count)]


def partners(value, axis, count):
    came = {d: lax.ppermute(value(d), axis, pairs(count, d)) for d in range(count - 1, 0, -1)}
    return [came[d] for d in range(1, count)]


def total(terms):
    while len(terms) > 1:
        terms = [first + second for first, second in zip(terms[::2], terms[1::2])]
    return terms[0]


def in_order(came, me):
    count = came.shape[0]
    rest = came.shape[1:]
    bit = 1
    while bit < count:
        split = came.reshape((count // (2 * bit), 2, bit) + rest)
        came = jnp.where((me & bit) != 0, split[:, ::-1], split).reshape((count,) + rest)
        bit *= 2
    return came


def make(mesh):
    count_x = mesh.shape["gx"]
    count_y = mesh.shape["gy"]

    def on_device(field, active_rows, kern, target):
        tile_row = lax.axis_index("gx")
        waves, polars = field.shape[0], field.shape[1]
        tiles = field.shape[4]
        rows_dev = field.shape[5]
        side = field.shape[6]
        focus = kern.shape[3]
        shape = (waves, polars, focus, 2 * focus)
        share, near_field, near_kern = call(
            share_kernel,
            [
                jax.ShapeDtypeStruct(shape, jnp.bfloat16),
                jax.ShapeDtypeStruct(field.shape[:3] + field.shape[4:], field.dtype),
                jax.ShapeDtypeStruct(kern.shape, kern.dtype),
            ],
            [
                pltpu.SMEM(active_rows.shape, jnp.int32),
                pltpu.VMEM((waves, 2 * side, polars * 2 * focus), jnp.bfloat16),
                pltpu.SemaphoreType.DMA((2 * waves + 1,)),
            ],
            [
                pltpu.with_memory_space_constraint(operand, pltpu.HBM)
                for operand in (active_rows, field, kern)
            ],
            [pltpu.HBM] * 3,
        )
        shares = [share] + partners(lambda d: share, "gx", count_x)
        share = total([term.astype(jnp.float32) for term in shares]).astype(jnp.bfloat16)
        strip_shape = (waves, polars, tiles, rows_dev, side)
        own_kern, both_kern, strip_kern, *strips = call(
            strip_kernel,
            [
                jax.ShapeDtypeStruct((waves, 2 * side, 2 * focus), kern.dtype),
                jax.ShapeDtypeStruct((waves, tiles, 2 * focus, 2 * side), kern.dtype),
                jax.ShapeDtypeStruct((waves, tiles, 2 * focus, side), kern.dtype),
            ]
            + [jax.ShapeDtypeStruct(strip_shape, field.dtype)] * (count_y - 1),
            [],
            (near_field, near_kern),
            [pltpu.VMEM] * 2,
        )
        strips = partners(lambda d: strips[d - 1], "gy", count_y)
        shares = [share] + partners(lambda d: share, "gy", count_y)
        shape = (tiles, rows_dev, side)
        intensity, gradient, crossed = call(
            functools.partial(gradient_kernel, tiles * side / focus, count_y),
            [
                jax.ShapeDtypeStruct((waves, focus, focus), jnp.float32),
                jax.ShapeDtypeStruct(shape, jnp.float32),
                jax.ShapeDtypeStruct(shape, jnp.bfloat16),
            ],
            [pltpu.VMEM((waves, 2 * side, polars * 2 * focus), jnp.float32)]
            + [pltpu.VMEM((side, side), jnp.float32)] * 2,
            (near_field, own_kern, both_kern, strip_kern, target, *strips, *shares),
            [pltpu.VMEM] * (4 + 2 * count_y),
        )
        partner = crossed.astype(jnp.float32) + lax.ppermute(crossed, "wa", pairs(2, 1)).astype(
            jnp.float32
        )
        narrow = partner.astype(jnp.bfloat16)
        came = [narrow[0]] + partners(lambda d: narrow[d], "gx", count_x)
        summed = gradient + lax.ppermute(gradient, "wa", pairs(2, 1))
        design_grad = in_order(0.5 * (summed + jnp.stack(came).astype(jnp.float32)), tile_row)
        return (design_grad[None], intensity)

    return on_device


def solution(mesh):
    placed = (
        P("wa", "cand", None, "gx", None, "gy", None),
        P("gx", None),
        P("wa", None, None, None, None),
        P("wa", None, None),
    )
    return jax.shard_map(
        make(mesh),
        mesh=mesh,
        in_specs=placed,
        out_specs=(P("gx", "cand", "gy", None), P("wa", "cand", None)),
        check_vma=False,
    )
```

```python
import functools

import jax
import jax.numpy as jnp
from jax import lax
from jax.experimental import pallas as pl
from jax.experimental.pallas import tpu as pltpu
from jax.sharding import PartitionSpec as P

VMEM = 16 * 2**20


def two_terms(value):
    high = value.astype(jnp.bfloat16)
    return high, (value - high.astype(jnp.float32)).astype(jnp.bfloat16)


def dot(first, second, over):
    return lax.dot_general(
        first, second, ((over[:1], over[1:]), ((), ())), preferred_element_type=jnp.float32
    )


def swapped(value, focus, left, right):
    lane = lax.broadcasted_iota(jnp.int32, value.shape, 1)
    sign = jnp.where(lane < focus, jnp.float32(left), jnp.float32(right))
    return pltpu.roll(value, focus, 1) * sign


def tile_kern(kern, wave, tile):
    real, imag = kern[wave, 0, tile], kern[wave, 1, tile]
    return jnp.concatenate([real, imag], axis=0), jnp.concatenate([-imag, real], axis=0)


def in_block(shape, block, width):
    lane = lax.broadcasted_iota(jnp.int32, shape, len(shape) - 1)
    return (lane >= block * width) & (lane < (block + 1) * width)


def side_by_side(first, second, block, blocks):
    width = first.shape[-1] // blocks
    first, second = first.astype(jnp.float32), second.astype(jnp.float32)
    beside = in_block(first.shape, lax.rem(block + 1, blocks), width)
    moved = jnp.where(beside, pltpu.roll(second, width, first.ndim - 1), 0.0)
    return jnp.where(in_block(first.shape, block, width), first, moved).astype(jnp.bfloat16)


def over_tiles(tiles, body, init):
    return lax.fori_loop(0, tiles, body, init, unroll=tiles <= 8)


def live_rows(rows, tile, shape):
    height = shape[-2]
    row = lax.axis_index("gy") * height + lax.broadcasted_iota(jnp.int32, shape, len(shape) - 2)
    return row < rows[0, tile]


def share_kernel(rows_far, field_far, kern_far, share, field, kern, rows, spread, arrived):
    waves, polars, _, tiles, height, side = field.shape
    focus = kern.shape[3]
    copies = [pltpu.make_async_copy(rows_far, rows, arrived.at[2 * waves])]
    for wave in range(waves):
        copies += [
            pltpu.make_async_copy(kern_far.at[wave], kern.at[wave], arrived.at[2 * wave]),
            pltpu.make_async_copy(
                field_far.at[wave, :, :, 0], field.at[wave], arrived.at[2 * wave + 1]
            ),
        ]
    for copy in copies:
        copy.start()
    tile_row = lax.axis_index("gx")
    first = pl.multiple_of(lax.axis_index("gy") * height, height)
    spread[...] = jnp.zeros_like(spread)
    copies[0].wait()
    inner = []
    for wave in range(waves):
        copies[2 * wave + 1].wait()
        copies[2 * wave + 2].wait()

        def add_tile(tile, value):
            live = live_rows(rows, tile, (polars, height, side))
            planes = [
                jnp.where(live, field[wave, :, part, tile], jnp.zeros((), field.dtype))
                for part in range(2)
            ]
            for part in range(2):
                field[wave, :, part, tile] = planes[part]
            planes = [plane.reshape(polars * height, side) for plane in planes]
            return value + dot(
                jnp.concatenate(planes, axis=1),
                jnp.concatenate(tile_kern(kern, wave, tile), axis=1),
                (1, 1),
            )

        zero = jnp.zeros((polars * height, 2 * focus), jnp.float32)
        inner.append(over_tiles(tiles, add_tile, zero))
    for wave in range(waves):
        for polar in range(polars):
            lanes = pl.ds(polar * 2 * focus, 2 * focus)
            terms = two_terms(inner[wave][polar * height : (polar + 1) * height])
            for index, term in enumerate(terms):
                spread[wave, pl.ds(index * side + first, height), lanes] = term
        own = tile_kern(kern, wave, tile_row)[0]
        both = dot(jnp.concatenate([own, own], axis=1), spread[wave], (1, 0))
        for polar in range(polars):
            lanes = slice(polar * 2 * focus, (polar + 1) * 2 * focus)
            straight, crossed = both[:focus, lanes], both[focus:, lanes]
            share[wave, polar] = (straight + swapped(crossed, focus, -1, 1)).astype(share.dtype)


def strip_kernel(field, kern, own_kern, both_kern, strip_kern, *strips):
    waves, polars, _, tiles, height, side = field.shape
    blocks = side // height
    block = lax.axis_index("gy")
    tile_row = lax.axis_index("gx")
    for wave in range(waves):
        for part in range(2):
            turned = kern[wave, part, tile_row].astype(jnp.float32).T.astype(kern.dtype)
            own_kern[wave, pl.ds(part * side, side)] = jnp.concatenate([turned, turned], axis=1)

    def one_tile(tile, carry):
        for wave in range(waves):
            parts = tile_kern(kern, wave, tile)
            both_kern[wave, tile] = jnp.concatenate(parts, axis=1)
            strip_kern[wave, tile] = side_by_side(*parts, block, blocks)
            for polar in range(polars):
                for distance, strip in enumerate(strips, 1):
                    strip[wave, polar, tile] = side_by_side(
                        field[wave, polar, 0, tile],
                        field[wave, polar, 1, tile],
                        block ^ distance,
                        blocks,
                    )
        return carry

    over_tiles(tiles, one_tile, 0)


def gradient_kernel(scale, blocks, field, own_kern, both_kern, strip_kern, target, *refs):
    strips, refs = refs[: blocks - 1], refs[blocks - 1 :]
    shares, (intensity, gradient, crossed, rowside, whole, turned) = refs[:-6], refs[-6:]
    waves, polars, _, tiles, height, side = field.shape
    focus = target.shape[1]
    tile_row = lax.axis_index("gx")
    block = lax.axis_index("gy")
    sides = []
    for wave in range(waves):
        focal = [
            total([share[wave, polar].astype(jnp.float32) for share in shares])
            for polar in range(polars)
        ]
        power = sum(value * value for value in focal)
        power = power + pltpu.roll(power, focus, 1)
        intensity[wave] = power[:, :focus]
        goal = target[wave]
        excess = power - jnp.concatenate([goal, goal], axis=1)
        source = jnp.concatenate([excess * value for value in focal], axis=1)
        terms = jnp.concatenate(two_terms(source), axis=0)
        rowside[wave] = dot(own_kern[wave], terms, (1, 0))
    for wave in range(waves):
        near = []
        for distance in range(blocks):
            first = pl.multiple_of((block ^ distance) * height, height)
            parts = []
            for polar in range(polars):
                lanes = pl.ds(polar * 2 * focus, 2 * focus)
                straight = rowside[wave, pl.ds(first, height), lanes]
                across = rowside[wave, pl.ds(side + first, height), lanes]
                parts.append(straight + swapped(across, focus, 1, -1))
            terms = two_terms(jnp.concatenate(parts, axis=0))
            near.append(jnp.concatenate(terms, axis=1))
        sides.append(near)

    def twice(value):
        return jnp.concatenate([value, value], axis=0)

    def add_tile(distance, carry):
        tile = tile_row ^ distance
        term = jnp.zeros((height, side), jnp.float32)
        others = [jnp.zeros((height, side), jnp.float32) for _ in strips]
        for wave in range(waves):
            back = dot(sides[wave][0], twice(both_kern[wave, tile]), (1, 0)).reshape(polars, height, 2 * side)
            for polar in range(polars):
                for part in range(2):
                    plane = field[wave, polar, part, tile].astype(jnp.float32)
                    term += back[polar, :, part * side : (part + 1) * side] * plane
            for index, strip in enumerate(strips):
                back = dot(sides[wave][index + 1], twice(strip_kern[wave, tile]), (1, 0))
                back = back.reshape(polars, height, side)
                for polar in range(polars):
                    others[index] += back[polar] * strip[wave, polar, tile].astype(jnp.float32)
        gradient[distance] = term * scale
        whole[pl.ds(pl.multiple_of(block * height, height), height)] = term * scale
        for index, other in enumerate(others):
            first = pl.multiple_of((block ^ (index + 1)) * height, height)
            whole[pl.ds(first, height)] = (other + pltpu.roll(other, side - height, 1)) * scale
        turned[...] = whole[...].T
        own = turned[pl.ds(pl.multiple_of(block * height, height), height)]
        crossed[distance] = own.astype(crossed.dtype)
        return carry

    over_tiles(tiles, add_tile, 0)


def call(kernel, out_shape, scratch, args, spaces):
    return pl.pallas_call(
        kernel,
        out_shape=out_shape,
        in_specs=[pl.BlockSpec(memory_space=space) for space in spaces],
        out_specs=[pl.BlockSpec(memory_space=pltpu.VMEM)] * len(out_shape),
        scratch_shapes=scratch,
        compiler_params=pltpu.CompilerParams(vmem_limit_bytes=VMEM),
    )(*args)


def pairs(count, distance):
    return [(device, device ^ distance) for device in range(count)]


def partners(value, axis, count):
    came = {d: lax.ppermute(value(d), axis, pairs(count, d)) for d in range(count - 1, 0, -1)}
    return [came[d] for d in range(1, count)]


def add_partners(straight, tiles, mesh):
    count, cores = mesh.shape["gx"], mesh.shape["wa"]
    core = lax.axis_index("wa")
    turns = count // cores
    asked = [
        sorted(((index * turns + turn) % count for turn in range(1, turns + 1)), reverse=True)
        for index in range(cores)
    ]

    def own(values):
        picked = [values[distance] for distance in values_of]
        chosen = picked[0]
        for index in range(1, cores):
            chosen = jnp.where(core == index, picked[index], chosen)
        return chosen

    sums = []
    for values_of in zip(*asked):
        routes = [
            (device * cores + index, (device ^ distance) * cores + index)
            for index, distance in enumerate(values_of)
            for device in range(count)
            if distance
        ]
        mine = own(tiles)
        came = lax.ppermute(mine, ("gx", "wa"), routes)
        if 0 in values_of:
            came = jnp.where(core == values_of.index(0), mine, came)
        sums.append(own(straight) + came.astype(straight.dtype))
    sums = jnp.stack(sums)
    other = lax.ppermute(sums, "wa", pairs(cores, 1))
    found = [None] * count
    for index in range(cores):
        held = jnp.where(core == index, sums, other)
        for turn, distance in enumerate(asked[index]):
            found[distance] = held[turn]
    return jnp.stack(found)


def total(terms):
    while len(terms) > 1:
        terms = [first + second for first, second in zip(terms[::2], terms[1::2])]
    return terms[0]


def in_order(came, me):
    count = came.shape[0]
    rest = came.shape[1:]
    bit = 1
    while bit < count:
        split = came.reshape((count // (2 * bit), 2, bit) + rest)
        came = jnp.where((me & bit) != 0, split[:, ::-1], split).reshape((count,) + rest)
        bit *= 2
    return came


def make(mesh):
    count_x = mesh.shape["gx"]
    count_y = mesh.shape["gy"]

    def on_device(field, active_rows, kern, target):
        tile_row = lax.axis_index("gx")
        waves, polars = field.shape[0], field.shape[1]
        tiles = field.shape[4]
        rows_dev = field.shape[5]
        side = field.shape[6]
        focus = kern.shape[3]
        shape = (waves, polars, focus, 2 * focus)
        share, near_field, near_kern = call(
            share_kernel,
            [
                jax.ShapeDtypeStruct(shape, jnp.bfloat16),
                jax.ShapeDtypeStruct(field.shape[:3] + field.shape[4:], field.dtype),
                jax.ShapeDtypeStruct(kern.shape, kern.dtype),
            ],
            [
                pltpu.SMEM(active_rows.shape, jnp.int32),
                pltpu.VMEM((waves, 2 * side, polars * 2 * focus), jnp.bfloat16),
                pltpu.SemaphoreType.DMA((2 * waves + 1,)),
            ],
            [
                pltpu.with_memory_space_constraint(operand, pltpu.HBM)
                for operand in (active_rows, field, kern)
            ],
            [pltpu.HBM] * 3,
        )
        shares = [share] + partners(lambda d: share, "gy", count_y)
        share = total([term.astype(jnp.float32) for term in shares]).astype(jnp.bfloat16)
        strip_shape = (waves, polars, tiles, rows_dev, side)
        own_kern, both_kern, strip_kern, *strips = call(
            strip_kernel,
            [
                jax.ShapeDtypeStruct((waves, 2 * side, 2 * focus), kern.dtype),
                jax.ShapeDtypeStruct((waves, tiles, 2 * focus, 2 * side), kern.dtype),
                jax.ShapeDtypeStruct((waves, tiles, 2 * focus, side), kern.dtype),
            ]
            + [jax.ShapeDtypeStruct(strip_shape, field.dtype)] * (count_y - 1),
            [],
            (near_field, near_kern),
            [pltpu.VMEM] * 2,
        )
        strips = partners(lambda d: strips[d - 1], "gy", count_y)
        shares = [share] + partners(lambda d: share, "gx", count_x)
        shares = shares[::-1]
        shape = (tiles, rows_dev, side)
        intensity, gradient, crossed = call(
            functools.partial(gradient_kernel, tiles * side / focus, count_y),
            [
                jax.ShapeDtypeStruct((waves, focus, focus), jnp.float32),
                jax.ShapeDtypeStruct(shape, jnp.float32),
                jax.ShapeDtypeStruct(shape, jnp.bfloat16),
            ],
            [pltpu.VMEM((waves, 2 * side, polars * 2 * focus), jnp.float32)]
            + [pltpu.VMEM((side, side), jnp.float32)] * 2,
            (near_field, own_kern, both_kern, strip_kern, target, *strips, *shares),
            [pltpu.VMEM] * (4 + count_x + count_y),
        )
        partner = crossed.astype(jnp.float32) + lax.ppermute(crossed, "wa", pairs(2, 1)).astype(
            jnp.float32
        )
        narrow = partner.astype(jnp.bfloat16)
        summed = gradient + lax.ppermute(gradient, "wa", pairs(2, 1))
        design_grad = in_order(0.5 * add_partners(summed, narrow, mesh), tile_row)
        return (design_grad[None], intensity)

    return on_device


def solution(mesh):
    placed = (
        P("wa", "cand", None, "gx", None, "gy", None),
        P("gx", None),
        P("wa", None, None, None, None),
        P("wa", None, None),
    )
    return jax.shard_map(
        make(mesh),
        mesh=mesh,
        in_specs=placed,
        out_specs=(P("gx", "cand", "gy", None), P("wa", "cand", None)),
        check_vma=False,
    )
```

```python
import functools

import jax
import jax.numpy as jnp
from jax import lax
from jax.experimental import pallas as pl
from jax.experimental.pallas import tpu as pltpu
from jax.sharding import PartitionSpec as P

VMEM = 16 * 2**20


def two_terms(value):
    high = value.astype(jnp.bfloat16)
    return high, (value - high.astype(jnp.float32)).astype(jnp.bfloat16)


def dot(first, second, over):
    return lax.dot_general(
        first, second, ((over[:1], over[1:]), ((), ())), preferred_element_type=jnp.float32
    )


def swapped(value, focus, left, right):
    lane = lax.broadcasted_iota(jnp.int32, value.shape, 1)
    sign = jnp.where(lane < focus, jnp.float32(left), jnp.float32(right))
    return pltpu.roll(value, focus, 1) * sign


def tile_kern(kern, wave, tile):
    real, imag = kern[wave, 0, tile], kern[wave, 1, tile]
    return jnp.concatenate([real, imag], axis=0), jnp.concatenate([-imag, real], axis=0)


def in_block(shape, block, width):
    lane = lax.broadcasted_iota(jnp.int32, shape, len(shape) - 1)
    return (lane >= block * width) & (lane < (block + 1) * width)


def side_by_side(first, second, block, blocks):
    width = first.shape[-1] // blocks
    first, second = first.astype(jnp.float32), second.astype(jnp.float32)
    beside = in_block(first.shape, lax.rem(block + 1, blocks), width)
    moved = jnp.where(beside, pltpu.roll(second, width, first.ndim - 1), 0.0)
    return jnp.where(in_block(first.shape, block, width), first, moved).astype(jnp.bfloat16)


def over_tiles(tiles, body, init):
    return lax.fori_loop(0, tiles, body, init, unroll=tiles <= 8)


def live_rows(count, shape):
    height = shape[-2]
    row = lax.axis_index("gy") * height + lax.broadcasted_iota(jnp.int32, shape, len(shape) - 2)
    return row < count


def share_kernel(rows_far, field_far, kern_far, share, field, kern, counts, rows, spread, arrived):
    waves, polars, _, tiles, height, side = field.shape
    focus = kern.shape[3]
    copies = [pltpu.make_async_copy(rows_far, rows, arrived.at[2 * waves])]
    for wave in range(waves):
        copies += [
            pltpu.make_async_copy(kern_far.at[wave], kern.at[wave], arrived.at[2 * wave]),
            pltpu.make_async_copy(
                field_far.at[wave, :, :, 0], field.at[wave], arrived.at[2 * wave + 1]
            ),
        ]
    for copy in copies:
        copy.start()
    tile_row = lax.axis_index("gx")
    first = pl.multiple_of(lax.axis_index("gy") * height, height)
    spread[...] = jnp.zeros_like(spread)
    copies[0].wait()
    inner = []
    for wave in range(waves):
        copies[2 * wave + 1].wait()
        copies[2 * wave + 2].wait()

        def add_tile(tile, value):
            live = live_rows(rows[0, tile], (polars, height, side))
            planes = [
                jnp.where(live, field[wave, :, part, tile], jnp.zeros((), field.dtype))
                for part in range(2)
            ]
            planes = [plane.reshape(polars * height, side) for plane in planes]
            return value + dot(
                jnp.concatenate(planes, axis=1),
                jnp.concatenate(tile_kern(kern, wave, tile), axis=1),
                (1, 1),
            )

        zero = jnp.zeros((polars * height, 2 * focus), jnp.float32)
        inner.append(over_tiles(tiles, add_tile, zero))
    for wave in range(waves):
        for polar in range(polars):
            lanes = pl.ds(polar * 2 * focus, 2 * focus)
            terms = two_terms(inner[wave][polar * height : (polar + 1) * height])
            for index, term in enumerate(terms):
                spread[wave, pl.ds(index * side + first, height), lanes] = term
        own = tile_kern(kern, wave, tile_row)[0]
        both = dot(jnp.concatenate([own, own], axis=1), spread[wave], (1, 0))
        for polar in range(polars):
            lanes = slice(polar * 2 * focus, (polar + 1) * 2 * focus)
            straight, crossed = both[:focus, lanes], both[focus:, lanes]
            share[wave, polar] = (straight + swapped(crossed, focus, -1, 1)).astype(share.dtype)

    def put_count(tile, carry):
        counts[tile] = jnp.full(counts.shape[1:], rows[0, tile], jnp.int32)
        return carry

    over_tiles(tiles, put_count, 0)


def strip_kernel(field, kern, counts, own_kern, both_kern, strip_kern, *strips):
    waves, polars, _, tiles, height, side = field.shape
    blocks = side // height
    block = lax.axis_index("gy")
    tile_row = lax.axis_index("gx")
    for wave in range(waves):
        for part in range(2):
            turned = kern[wave, part, tile_row].astype(jnp.float32).T.astype(kern.dtype)
            own_kern[wave, pl.ds(part * side, side)] = jnp.concatenate([turned, turned], axis=1)

    def one_tile(tile, carry):
        live = live_rows(counts[tile, :1], (height, side))
        for wave in range(waves):
            parts = tile_kern(kern, wave, tile)
            both_kern[wave, tile] = jnp.concatenate(parts, axis=1)
            strip_kern[wave, tile] = side_by_side(*parts, block, blocks)
            for polar in range(polars):
                for distance, strip in enumerate(strips):
                    both = side_by_side(
                        field[wave, polar, 0, tile],
                        field[wave, polar, 1, tile],
                        block ^ distance,
                        blocks,
                    )
                    strip[wave, polar, tile] = jnp.where(live, both, jnp.zeros((), both.dtype))
        return carry

    over_tiles(tiles, one_tile, 0)


def twice(value):
    return jnp.concatenate([value, value], axis=0)


def crossed_kernel(scale, blocks, own_kern, strip_kern, target, *refs):
    strips, refs = refs[:blocks], refs[blocks:]
    shares, (intensity, sides, crossed, rowside, whole, turned) = refs[:-6], refs[-6:]
    waves, polars, tiles, height, side = strips[0].shape
    focus = target.shape[1]
    block = lax.axis_index("gy")
    for wave in range(waves):
        focal = [
            total([share[wave, polar].astype(jnp.float32) for share in shares])
            for polar in range(polars)
        ]
        power = sum(value * value for value in focal)
        power = power + pltpu.roll(power, focus, 1)
        intensity[wave] = power[:, :focus]
        goal = target[wave]
        excess = power - jnp.concatenate([goal, goal], axis=1)
        source = jnp.concatenate([excess * value for value in focal], axis=1)
        terms = jnp.concatenate(two_terms(source), axis=0)
        rowside[wave] = dot(own_kern[wave], terms, (1, 0))
    near = []
    for wave in range(waves):
        near.append([])
        for distance in range(blocks):
            first = pl.multiple_of((block ^ distance) * height, height)
            parts = []
            for polar in range(polars):
                lanes = pl.ds(polar * 2 * focus, 2 * focus)
                straight = rowside[wave, pl.ds(first, height), lanes]
                across = rowside[wave, pl.ds(side + first, height), lanes]
                parts.append(straight + swapped(across, focus, 1, -1))
            terms = two_terms(jnp.concatenate(parts, axis=0))
            near[wave].append(jnp.concatenate(terms, axis=1))
        sides[wave] = near[wave][0]

    def add_tile(distance, carry):
        tile = lax.axis_index("gx") ^ distance
        for index, strip in enumerate(strips):
            value = jnp.zeros((height, side), jnp.float32)
            for wave in range(waves):
                back = dot(near[wave][index], twice(strip_kern[wave, tile]), (1, 0))
                back = back.reshape(polars, height, side)
                for polar in range(polars):
                    value += back[polar] * strip[wave, polar, tile].astype(jnp.float32)
            first = pl.multiple_of((block ^ index) * height, height)
            whole[distance, pl.ds(first, height)] = (
                value + pltpu.roll(value, side - height, 1)
            ) * scale
        turned[distance] = whole[distance].T
        own = turned[distance, pl.ds(pl.multiple_of(block * height, height), height)]
        crossed[distance] = own.astype(crossed.dtype)
        return carry

    over_tiles(tiles, add_tile, 0)


def straight_kernel(scale, field, counts, both_kern, sides, gradient):
    waves, polars, _, tiles, height, side = field.shape

    def add_tile(distance, carry):
        tile = lax.axis_index("gx") ^ distance
        term = jnp.zeros((height, side), jnp.float32)
        for wave in range(waves):
            back = dot(sides[wave], twice(both_kern[wave, tile]), (1, 0))
            back = back.reshape(polars, height, 2 * side)
            for polar in range(polars):
                for part in range(2):
                    plane = field[wave, polar, part, tile].astype(jnp.float32)
                    term += back[polar, :, part * side : (part + 1) * side] * plane
        live = live_rows(counts[tile, :1], (height, side))
        gradient[distance] = jnp.where(live, term * scale, 0.0)
        return carry

    over_tiles(tiles, add_tile, 0)


def call(kernel, out_shape, scratch, args, spaces):
    return pl.pallas_call(
        kernel,
        out_shape=out_shape,
        in_specs=[pl.BlockSpec(memory_space=space) for space in spaces],
        out_specs=[pl.BlockSpec(memory_space=pltpu.VMEM)] * len(out_shape),
        scratch_shapes=scratch,
        compiler_params=pltpu.CompilerParams(vmem_limit_bytes=VMEM),
    )(*args)


def pairs(count, distance):
    return [(device, device ^ distance) for device in range(count)]


def partners(value, axis, count):
    came = {d: lax.ppermute(value(d), axis, pairs(count, d)) for d in range(count - 1, 0, -1)}
    return [came[d] for d in range(1, count)]


def total(terms):
    while len(terms) > 1:
        terms = [first + second for first, second in zip(terms[::2], terms[1::2])]
    return terms[0]


def in_order(came, me):
    count = came.shape[0]
    rest = came.shape[1:]
    bit = 1
    while bit < count:
        split = came.reshape((count // (2 * bit), 2, bit) + rest)
        came = jnp.where((me & bit) != 0, split[:, ::-1], split).reshape((count,) + rest)
        bit *= 2
    return came


def make(mesh):
    count_x = mesh.shape["gx"]
    count_y = mesh.shape["gy"]

    def on_device(field, active_rows, kern, target):
        tile_row = lax.axis_index("gx")
        waves, polars = field.shape[0], field.shape[1]
        tiles = field.shape[4]
        rows_dev = field.shape[5]
        side = field.shape[6]
        focus = kern.shape[3]
        shape = (waves, polars, focus, 2 * focus)
        share, near_field, near_kern, counts = call(
            share_kernel,
            [
                jax.ShapeDtypeStruct(shape, jnp.bfloat16),
                jax.ShapeDtypeStruct(field.shape[:3] + field.shape[4:], field.dtype),
                jax.ShapeDtypeStruct(kern.shape, kern.dtype),
                jax.ShapeDtypeStruct((tiles, 8, side), jnp.int32),
            ],
            [
                pltpu.SMEM(active_rows.shape, jnp.int32),
                pltpu.VMEM((waves, 2 * side, polars * 2 * focus), jnp.bfloat16),
                pltpu.SemaphoreType.DMA((2 * waves + 1,)),
            ],
            [
                pltpu.with_memory_space_constraint(operand, pltpu.HBM)
                for operand in (active_rows, field, kern)
            ],
            [pltpu.HBM] * 3,
        )
        shares = [share] + partners(lambda d: share, "gy", count_y)
        share = total([term.astype(jnp.float32) for term in shares]).astype(jnp.bfloat16)
        strip_shape = (waves, polars, tiles, rows_dev, side)
        own_kern, both_kern, strip_kern, own_strip, *strips = call(
            strip_kernel,
            [
                jax.ShapeDtypeStruct((waves, 2 * side, 2 * focus), kern.dtype),
                jax.ShapeDtypeStruct((waves, tiles, 2 * focus, 2 * side), kern.dtype),
                jax.ShapeDtypeStruct((waves, tiles, 2 * focus, side), kern.dtype),
            ]
            + [jax.ShapeDtypeStruct(strip_shape, field.dtype)] * count_y,
            [],
            (near_field, near_kern, counts),
            [pltpu.VMEM] * 3,
        )
        strips = partners(lambda d: strips[d - 1], "gy", count_y)
        shares = [share] + partners(lambda d: share, "gx", count_x)
        shares = shares[::-1]
        shape = (tiles, rows_dev, side)
        scale = tiles * side / focus
        intensity, sides, crossed = call(
            functools.partial(crossed_kernel, scale, count_y),
            [
                jax.ShapeDtypeStruct((waves, focus, focus), jnp.float32),
                jax.ShapeDtypeStruct((waves, polars * rows_dev, 4 * focus), jnp.bfloat16),
                jax.ShapeDtypeStruct(shape, jnp.bfloat16),
            ],
            [pltpu.VMEM((waves, 2 * side, polars * 2 * focus), jnp.float32)]
            + [pltpu.VMEM((tiles, side, side), jnp.float32)] * 2,
            (own_kern, strip_kern, target, own_strip, *strips, *shares),
            [pltpu.VMEM] * (3 + count_x + count_y),
        )
        (gradient,) = call(
            functools.partial(straight_kernel, scale),
            [jax.ShapeDtypeStruct(shape, jnp.float32)],
            [],
            (near_field, counts, both_kern, sides),
            [pltpu.VMEM] * 4,
        )
        partner = crossed.astype(jnp.float32) + lax.ppermute(crossed, "wa", pairs(2, 1)).astype(
            jnp.float32
        )
        narrow = partner.astype(jnp.bfloat16)
        came = [narrow[0]] + partners(lambda d: narrow[d], "gx", count_x)
        summed = gradient + lax.ppermute(gradient, "wa", pairs(2, 1))
        design_grad = in_order(0.5 * (summed + jnp.stack(came).astype(jnp.float32)), tile_row)
        return (design_grad[None], intensity)

    return on_device


def solution(mesh):
    placed = (
        P("wa", "cand", None, "gx", None, "gy", None),
        P("gx", None),
        P("wa", None, None, None, None),
        P("wa", None, None),
    )
    return jax.shard_map(
        make(mesh),
        mesh=mesh,
        in_specs=placed,
        out_specs=(P("gx", "cand", "gy", None), P("wa", "cand", None)),
        check_vma=False,
    )
```

```python
import functools

import jax
import jax.numpy as jnp
from jax import lax
from jax.experimental import pallas as pl
from jax.experimental.pallas import tpu as pltpu
from jax.sharding import PartitionSpec as P

VMEM = 16 * 2**20


def two_terms(value):
    high = value.astype(jnp.bfloat16)
    return high, (value - high.astype(jnp.float32)).astype(jnp.bfloat16)


def dot(first, second, over):
    return lax.dot_general(
        first, second, ((over[:1], over[1:]), ((), ())), preferred_element_type=jnp.float32
    )


def swapped(value, focus, left, right):
    lane = lax.broadcasted_iota(jnp.int32, value.shape, 1)
    sign = jnp.where(lane < focus, jnp.float32(left), jnp.float32(right))
    return pltpu.roll(value, focus, 1) * sign


def tile_kern(kern, wave, tile):
    real, imag = kern[wave, 0, tile], kern[wave, 1, tile]
    return jnp.concatenate([real, imag], axis=0), jnp.concatenate([-imag, real], axis=0)


def in_block(shape, block, width):
    lane = lax.broadcasted_iota(jnp.int32, shape, len(shape) - 1)
    return (lane >= block * width) & (lane < (block + 1) * width)


def side_by_side(first, second, block, blocks):
    width = first.shape[-1] // blocks
    first, second = first.astype(jnp.float32), second.astype(jnp.float32)
    beside = in_block(first.shape, lax.rem(block + 1, blocks), width)
    moved = jnp.where(beside, pltpu.roll(second, width, first.ndim - 1), 0.0)
    return jnp.where(in_block(first.shape, block, width), first, moved).astype(jnp.bfloat16)


def over_tiles(tiles, body, init):
    return lax.fori_loop(0, tiles, body, init, unroll=tiles <= 8)


def live_rows(count, shape):
    height = shape[-2]
    row = lax.axis_index("gy") * height + lax.broadcasted_iota(jnp.int32, shape, len(shape) - 2)
    return row < count


def share_kernel(rows_far, field_far, kern_far, share, field, kern, counts, rows, spread, arrived):
    waves, polars, _, tiles, height, side = field.shape
    focus = kern.shape[3]
    copies = [pltpu.make_async_copy(rows_far, rows, arrived.at[2 * waves])]
    for wave in range(waves):
        copies += [
            pltpu.make_async_copy(kern_far.at[wave], kern.at[wave], arrived.at[2 * wave]),
            pltpu.make_async_copy(
                field_far.at[wave, :, :, 0], field.at[wave], arrived.at[2 * wave + 1]
            ),
        ]
    for copy in copies:
        copy.start()
    tile_row = lax.axis_index("gx")
    first = pl.multiple_of(lax.axis_index("gy") * height, height)
    spread[...] = jnp.zeros_like(spread)
    copies[0].wait()
    inner = []
    for wave in range(waves):
        copies[2 * wave + 1].wait()
        copies[2 * wave + 2].wait()

        def add_tile(tile, value):
            live = live_rows(rows[0, tile], (polars, height, side))
            planes = [
                jnp.where(live, field[wave, :, part, tile], jnp.zeros((), field.dtype))
                for part in range(2)
            ]
            planes = [plane.reshape(polars * height, side) for plane in planes]
            upright, turned = tile_kern(kern, wave, tile)
            pair = jnp.concatenate([upright, turned], axis=1)
            opposite = jnp.concatenate([turned, -upright], axis=1)
            return value + dot(
                jnp.concatenate(planes, axis=1),
                jnp.concatenate([pair, opposite], axis=0),
                (1, 1),
            )

        zero = jnp.zeros((polars * height, 4 * focus), jnp.float32)
        inner.append(over_tiles(tiles, add_tile, zero))
    for wave in range(waves):
        for polar in range(polars):
            lanes = pl.ds(polar * 2 * focus, 2 * focus)
            terms = two_terms(inner[wave][polar * height : (polar + 1) * height])
            for index, term in enumerate(terms):
                for part in range(2):
                    row = (2 * index + part) * side + first
                    piece = term[:, part * 2 * focus : (part + 1) * 2 * focus]
                    spread[wave, pl.ds(row, height), lanes] = piece
        own = [kern[wave, part, tile_row] for part in range(2)]
        both = dot(jnp.concatenate(own + own, axis=1), spread[wave], (1, 0))
        for polar in range(polars):
            lanes = slice(polar * 2 * focus, (polar + 1) * 2 * focus)
            share[wave, polar] = both[:, lanes].astype(share.dtype)

    def put_count(tile, carry):
        counts[tile] = jnp.full(counts.shape[1:], rows[0, tile], jnp.int32)
        return carry

    over_tiles(tiles, put_count, 0)


def strip_kernel(field, kern, counts, target, goal, own_kern, both_kern, strip_kern, *strips):
    waves, polars, _, tiles, height, side = field.shape
    blocks = side // height
    block = lax.axis_index("gy")
    tile_row = lax.axis_index("gx")
    for wave in range(waves):
        goal[wave] = jnp.concatenate([target[wave], target[wave]], axis=1)
        own = [kern[wave, part, tile_row].astype(jnp.float32).T for part in range(2)]
        own_kern[wave] = jnp.concatenate(own + own, axis=1).astype(kern.dtype)

    def one_tile(tile, carry):
        live = live_rows(counts[tile, :1], (height, side))
        for wave in range(waves):
            parts = tile_kern(kern, wave, tile)
            both_kern[wave, tile] = jnp.concatenate(parts, axis=1)
            strip_kern[wave, tile] = side_by_side(*parts, block, blocks)
            for polar in range(polars):
                for distance, strip in enumerate(strips):
                    both = side_by_side(
                        field[wave, polar, 0, tile],
                        field[wave, polar, 1, tile],
                        block ^ distance,
                        blocks,
                    )
                    strip[wave, polar, tile] = jnp.where(live, both, jnp.zeros((), both.dtype))
        return carry

    over_tiles(tiles, one_tile, 0)


def twice(value):
    return jnp.concatenate([value, value], axis=0)


def crossed_kernel(scale, blocks, own_kern, strip_kern, goal, *refs):
    strips, refs = refs[:blocks], refs[blocks:]
    shares, (intensity, sides, crossed) = refs[:-3], refs[-3:]
    waves, polars, tiles, height, side = strips[0].shape
    focus = goal.shape[1]
    block = lax.axis_index("gy")
    near = []
    for wave in range(waves):
        focal = [
            total([share[wave, polar].astype(jnp.float32) for share in shares])
            for polar in range(polars)
        ]
        power = sum(value * value for value in focal)
        power = power + pltpu.roll(power, focus, 1)
        intensity[wave] = power[:, :focus]
        excess = power - goal[wave]
        source = [excess * value for value in focal]
        upright = jnp.concatenate(source, axis=1)
        turned = jnp.concatenate([swapped(value, focus, 1, -1) for value in source], axis=1)
        terms = two_terms(jnp.concatenate([upright, turned], axis=0))
        rowside = dot(own_kern[wave], jnp.concatenate(terms, axis=0), (1, 0))
        near.append([])
        for index in range(blocks):
            rows = rowside[index * height : (index + 1) * height]
            rows = [
                rows[:, polar * 2 * focus : (polar + 1) * 2 * focus] for polar in range(polars)
            ]
            terms = two_terms(jnp.concatenate(rows, axis=0))
            near[wave].append(jnp.concatenate(terms, axis=1))
        own = near[wave][0]
        for index in range(1, blocks):
            own = jnp.where(block == index, near[wave][index], own)
        sides[wave] = own

    def add_tile(distance, carry):
        tile = lax.axis_index("gx") ^ distance
        values = []
        for index in range(blocks):
            value = jnp.zeros((height, side), jnp.float32)
            for wave in range(waves):
                back = dot(near[wave][index], twice(strip_kern[wave, tile]), (1, 0))
                back = back.reshape(polars, height, side)
                for polar in range(polars):
                    strip = strips[0][wave, polar, tile]
                    for apart in range(1, blocks):
                        other = strips[apart][wave, polar, tile]
                        strip = jnp.where((block ^ apart) == index, other, strip)
                    value += back[polar] * strip.astype(jnp.float32)
            values.append(value)
        turned = jnp.concatenate(values, axis=0).T
        rows = sum(turned[index * height : (index + 1) * height] for index in range(blocks))
        crossed[distance] = (rows * scale).astype(crossed.dtype)
        return carry

    over_tiles(tiles, add_tile, 0)


def straight_kernel(scale, field, counts, both_kern, sides, gradient):
    waves, polars, _, tiles, height, side = field.shape

    def add_tile(distance, carry):
        tile = lax.axis_index("gx") ^ distance
        term = jnp.zeros((height, side), jnp.float32)
        for wave in range(waves):
            back = dot(sides[wave], twice(both_kern[wave, tile]), (1, 0))
            back = back.reshape(polars, height, 2 * side)
            for polar in range(polars):
                for part in range(2):
                    plane = field[wave, polar, part, tile].astype(jnp.float32)
                    term += back[polar, :, part * side : (part + 1) * side] * plane
        live = live_rows(counts[tile, :1], (height, side))
        gradient[distance] = jnp.where(live, term * scale, 0.0)
        return carry

    over_tiles(tiles, add_tile, 0)


def call(kernel, out_shape, scratch, args, spaces):
    return pl.pallas_call(
        kernel,
        out_shape=out_shape,
        in_specs=[pl.BlockSpec(memory_space=space) for space in spaces],
        out_specs=[pl.BlockSpec(memory_space=pltpu.VMEM)] * len(out_shape),
        scratch_shapes=scratch,
        compiler_params=pltpu.CompilerParams(vmem_limit_bytes=VMEM),
    )(*args)


def pairs(count, distance):
    return [(device, device ^ distance) for device in range(count)]


def partners(value, axis, count):
    came = {d: lax.ppermute(value(d), axis, pairs(count, d)) for d in range(count - 1, 0, -1)}
    return [came[d] for d in range(1, count)]


def total(terms):
    while len(terms) > 1:
        terms = [first + second for first, second in zip(terms[::2], terms[1::2])]
    return terms[0]


def in_order(came, me):
    count = came.shape[0]
    rest = came.shape[1:]
    bit = 1
    while bit < count:
        split = came.reshape((count // (2 * bit), 2, bit) + rest)
        came = jnp.where((me & bit) != 0, split[:, ::-1], split).reshape((count,) + rest)
        bit *= 2
    return came


def make(mesh):
    count_x = mesh.shape["gx"]
    count_y = mesh.shape["gy"]

    def on_device(field, active_rows, kern, target):
        tile_row = lax.axis_index("gx")
        waves, polars = field.shape[0], field.shape[1]
        tiles = field.shape[4]
        rows_dev = field.shape[5]
        side = field.shape[6]
        focus = kern.shape[3]
        shape = (waves, polars, focus, 2 * focus)
        share, near_field, near_kern, counts = call(
            share_kernel,
            [
                jax.ShapeDtypeStruct(shape, jnp.bfloat16),
                jax.ShapeDtypeStruct(field.shape[:3] + field.shape[4:], field.dtype),
                jax.ShapeDtypeStruct(kern.shape, kern.dtype),
                jax.ShapeDtypeStruct((tiles, 8, side), jnp.int32),
            ],
            [
                pltpu.SMEM(active_rows.shape, jnp.int32),
                pltpu.VMEM((waves, 4 * side, polars * 2 * focus), jnp.bfloat16),
                pltpu.SemaphoreType.DMA((2 * waves + 1,)),
            ],
            [
                pltpu.with_memory_space_constraint(operand, pltpu.HBM)
                for operand in (active_rows, field, kern)
            ],
            [pltpu.HBM] * 3,
        )
        shares = [share] + partners(lambda d: share, "gy", count_y)
        share = total([term.astype(jnp.float32) for term in shares]).astype(jnp.bfloat16)
        strip_shape = (waves, polars, tiles, rows_dev, side)
        goal, own_kern, both_kern, strip_kern, own_strip, *strips = call(
            strip_kernel,
            [
                jax.ShapeDtypeStruct((waves, focus, 2 * focus), target.dtype),
                jax.ShapeDtypeStruct((waves, side, 4 * focus), kern.dtype),
                jax.ShapeDtypeStruct((waves, tiles, 2 * focus, 2 * side), kern.dtype),
                jax.ShapeDtypeStruct((waves, tiles, 2 * focus, side), kern.dtype),
            ]
            + [jax.ShapeDtypeStruct(strip_shape, field.dtype)] * count_y,
            [],
            (near_field, near_kern, counts, target),
            [pltpu.VMEM] * 4,
        )
        strips = partners(lambda d: strips[d - 1], "gy", count_y)
        shares = [share] + partners(lambda d: share, "gx", count_x)
        shares = shares[::-1]
        shape = (tiles, rows_dev, side)
        scale = tiles * side / focus
        intensity, sides, crossed = call(
            functools.partial(crossed_kernel, scale, count_y),
            [
                jax.ShapeDtypeStruct((waves, focus, focus), jnp.float32),
                jax.ShapeDtypeStruct((waves, polars * rows_dev, 4 * focus), jnp.bfloat16),
                jax.ShapeDtypeStruct(shape, jnp.bfloat16),
            ],
            [],
            (own_kern, strip_kern, goal, own_strip, *strips, *shares),
            [pltpu.VMEM] * (3 + count_x + count_y),
        )
        (gradient,) = call(
            functools.partial(straight_kernel, scale),
            [jax.ShapeDtypeStruct(shape, jnp.float32)],
            [],
            (near_field, counts, both_kern, sides),
            [pltpu.VMEM] * 4,
        )
        partner = crossed.astype(jnp.float32) + lax.ppermute(crossed, "wa", pairs(2, 1)).astype(
            jnp.float32
        )
        narrow = partner.astype(jnp.bfloat16)
        came = [narrow[0]] + partners(lambda d: narrow[d], "gx", count_x)
        summed = gradient + lax.ppermute(gradient, "wa", pairs(2, 1))
        design_grad = in_order(0.5 * (summed + jnp.stack(came).astype(jnp.float32)), tile_row)
        return (design_grad[None], intensity)

    return on_device


def solution(mesh):
    placed = (
        P("wa", "cand", None, "gx", None, "gy", None),
        P("gx", None),
        P("wa", None, None, None, None),
        P("wa", None, None),
    )
    return jax.shard_map(
        make(mesh),
        mesh=mesh,
        in_specs=placed,
        out_specs=(P("gx", "cand", "gy", None), P("wa", "cand", None)),
        check_vma=False,
    )
```

```python
import functools

import jax
import jax.numpy as jnp
from jax import lax
from jax.experimental import pallas as pl
from jax.experimental.pallas import tpu as pltpu
from jax.sharding import PartitionSpec as P

VMEM = 16 * 2**20


def two_terms(value):
    high = value.astype(jnp.bfloat16)
    return high, (value - high.astype(jnp.float32)).astype(jnp.bfloat16)


def dot(first, second, over):
    return lax.dot_general(
        first, second, ((over[:1], over[1:]), ((), ())), preferred_element_type=jnp.float32
    )


def tile_kern(kern, wave, tile):
    real, imag = kern[wave, 0, tile], kern[wave, 1, tile]
    return jnp.concatenate([real, imag], axis=0), jnp.concatenate([-imag, real], axis=0)


def one_block(value, block, blocks):
    width = value.shape[1] // blocks
    picked = value[:, :width]
    for index in range(1, blocks):
        picked = jnp.where(block == index, value[:, index * width : (index + 1) * width], picked)
    return picked


def twice(value, axis):
    return jnp.concatenate([value, value], axis=axis)


def diagonal(value, count):
    zero = jnp.zeros_like(value)
    rows = [
        jnp.concatenate([value if index == other else zero for other in range(count)], axis=1)
        for index in range(count)
    ]
    return jnp.concatenate(rows, axis=0)


def over_tiles(tiles, body, init):
    return lax.fori_loop(0, tiles, body, init, unroll=tiles <= 8)


def live_rows(count, shape):
    height = shape[-2]
    row = lax.axis_index("gy") * height + lax.broadcasted_iota(jnp.int32, shape, len(shape) - 2)
    return row < count


def share_kernel(rows_far, field_far, kern_far, share, field, kern, counts, rows, arrived):
    waves, polars, _, tiles, height, side = field.shape
    focus = kern.shape[3]
    copies = [pltpu.make_async_copy(rows_far, rows, arrived.at[2 * waves])]
    for wave in range(waves):
        copies += [
            pltpu.make_async_copy(kern_far.at[wave], kern.at[wave], arrived.at[2 * wave]),
            pltpu.make_async_copy(
                field_far.at[wave, :, :, 0], field.at[wave], arrived.at[2 * wave + 1]
            ),
        ]
    for copy in copies:
        copy.start()
    tile_row = lax.axis_index("gx")
    block = lax.axis_index("gy")
    copies[0].wait()
    inner = []
    own = []
    for wave in range(waves):
        copies[2 * wave + 1].wait()
        parts = []
        for part in range(2):
            value = kern[wave, part, tile_row].astype(jnp.float32)
            parts.append(diagonal(one_block(value, block, side // height), polars))
        own.append(twice(jnp.concatenate(parts, axis=0).astype(kern.dtype), 1))
        copies[2 * wave + 2].wait()

        def add_tile(tile, value):
            live = live_rows(rows[0, tile], (polars, height, side))
            planes = [
                jnp.where(live, field[wave, :, part, tile], jnp.zeros((), field.dtype))
                for part in range(2)
            ]
            planes = [plane.reshape(polars * height, side) for plane in planes]
            return value + dot(
                jnp.concatenate(tile_kern(kern, wave, tile), axis=1),
                jnp.concatenate(planes, axis=1),
                (1, 1),
            )

        zero = jnp.zeros((2 * focus, polars * height), jnp.float32)
        inner.append(over_tiles(tiles, add_tile, zero))
    for wave in range(waves):
        both = dot(jnp.concatenate(two_terms(inner[wave]), axis=1), own[wave], (1, 1))
        real, imag = both[:, : polars * focus], both[:, polars * focus :]
        focal = [real[:focus] - imag[focus:], real[focus:] + imag[:focus]]
        share[wave] = jnp.concatenate(focal, axis=0).astype(share.dtype)

    def put_count(tile, carry):
        counts[tile] = jnp.full(counts.shape[1:], rows[0, tile], jnp.int32)
        return carry

    over_tiles(tiles, put_count, 0)


def strip_kernel(field, kern, counts, target, goal, row_kern, turn_kern, both_kern, *strips):
    waves, polars, _, tiles, height, side = field.shape
    blocks = side // height
    block = lax.axis_index("gy")
    tile_row = lax.axis_index("gx")
    for wave in range(waves):
        goal[wave] = jnp.concatenate([target[wave].T] * polars, axis=1)
        for part in range(2):
            value = kern[wave, part, tile_row].astype(jnp.float32)
            columns = [
                diagonal(one_block(value, block ^ distance, blocks), polars)
                for distance in range(blocks)
            ]
            rows = pl.ds(part * polars * value.shape[0], polars * value.shape[0])
            row_kern[wave, rows] = jnp.concatenate(columns, axis=1).astype(kern.dtype)

    def one_tile(tile, carry):
        live = live_rows(counts[tile, :1], (height, side))
        for wave in range(waves):
            parts = tile_kern(kern, wave, tile)
            both_kern[wave, tile] = jnp.concatenate(parts, axis=1)
            parts = [one_block(part.astype(jnp.float32), block, blocks) for part in parts]
            turned = jnp.concatenate(parts, axis=1).T
            turn_kern[wave, tile] = twice(turned, 1).astype(kern.dtype)
            planes = [
                [
                    jnp.where(live, field[wave, polar, part, tile].astype(jnp.float32), 0.0)
                    for part in range(2)
                ]
                for polar in range(polars)
            ]
            for distance, strip in enumerate(strips):
                rows = [
                    jnp.concatenate(
                        [one_block(plane, block ^ distance, blocks) for plane in pair], axis=1
                    )
                    for pair in planes
                ]
                strip[wave, tile] = jnp.concatenate(rows, axis=0).T.astype(strip.dtype)
        return carry

    over_tiles(tiles, one_tile, 0)


def crossed_kernel(scale, blocks, row_kern, turn_kern, goal, *refs):
    strips, refs = refs[:blocks], refs[blocks:]
    shares, (intensity, near, crossed) = refs[:-3], refs[-3:]
    waves, tiles, height, width = strips[0].shape
    height = height // 2
    polars = width // height
    focus = goal.shape[1]
    block = lax.axis_index("gy")
    sides = []
    for wave in range(waves):
        focal = total([share[wave].astype(jnp.float32) for share in shares])
        real, imag = focal[:focus], focal[focus:]
        power = real * real + imag * imag
        power = sum(pltpu.roll(power, polar * focus, 1) for polar in range(polars))
        intensity[wave] = power
        excess = power - goal[wave]
        real, imag = excess * real, excess * imag
        upright = jnp.concatenate([real, imag], axis=0)
        turned = jnp.concatenate([imag, -real], axis=0)
        terms = two_terms(jnp.concatenate([upright, turned], axis=1))
        row = dot(jnp.concatenate(terms, axis=1), twice(row_kern[wave], 0), (1, 0))
        sides.append(jnp.concatenate(two_terms(row), axis=0))
        near[wave] = sides[wave]

    def add_tile(distance, carry):
        tile = lax.axis_index("gx") ^ distance
        value = jnp.zeros((2 * height, blocks * width), jnp.float32)
        for wave in range(waves):
            back = dot(turn_kern[wave, tile], sides[wave], (1, 0))
            strip = jnp.concatenate([strip[wave, tile] for strip in strips], axis=1)
            value += back * strip.astype(jnp.float32)
        value = (value[:height] + value[height:]) * scale
        parts = []
        for apart in range(blocks):
            part = value[:, apart * width : (apart + 1) * width]
            parts.append(sum(part[:, at * height : (at + 1) * height] for at in range(polars)))
        columns = []
        for index in range(blocks):
            column = parts[0]
            for apart in range(1, blocks):
                column = jnp.where((block ^ apart) == index, parts[apart], column)
            columns.append(column)
        crossed[distance] = jnp.concatenate(columns, axis=1).astype(crossed.dtype)
        return carry

    over_tiles(tiles, add_tile, 0)


def straight_kernel(scale, field, counts, both_kern, near, power, gradient, intensity):
    waves, polars, _, tiles, height, side = field.shape
    sides = []
    for wave in range(waves):
        intensity[wave] = power[wave].T[: intensity.shape[1]]
        sides.append(near[wave, :, : polars * height].T)

    def add_tile(distance, carry):
        tile = lax.axis_index("gx") ^ distance
        term = jnp.zeros((height, side), jnp.float32)
        for wave in range(waves):
            back = dot(sides[wave], twice(both_kern[wave, tile], 0), (1, 0))
            back = back.reshape(polars, height, 2 * side)
            for polar in range(polars):
                for part in range(2):
                    plane = field[wave, polar, part, tile].astype(jnp.float32)
                    term += back[polar, :, part * side : (part + 1) * side] * plane
        live = live_rows(counts[tile, :1], (height, side))
        gradient[distance] = jnp.where(live, term * scale, 0.0)
        return carry

    over_tiles(tiles, add_tile, 0)


def call(kernel, out_shape, scratch, args, spaces):
    return pl.pallas_call(
        kernel,
        out_shape=out_shape,
        in_specs=[pl.BlockSpec(memory_space=space) for space in spaces],
        out_specs=[pl.BlockSpec(memory_space=pltpu.VMEM)] * len(out_shape),
        scratch_shapes=scratch,
        compiler_params=pltpu.CompilerParams(vmem_limit_bytes=VMEM),
    )(*args)


def pairs(count, distance):
    return [(device, device ^ distance) for device in range(count)]


def partners(value, axis, count):
    came = {d: lax.ppermute(value(d), axis, pairs(count, d)) for d in range(count - 1, 0, -1)}
    return [came[d] for d in range(1, count)]


def total(terms):
    while len(terms) > 1:
        terms = [first + second for first, second in zip(terms[::2], terms[1::2])]
    return terms[0]


def in_order(came, me):
    count = came.shape[0]
    rest = came.shape[1:]
    bit = 1
    while bit < count:
        split = came.reshape((count // (2 * bit), 2, bit) + rest)
        came = jnp.where((me & bit) != 0, split[:, ::-1], split).reshape((count,) + rest)
        bit *= 2
    return came


def make(mesh):
    count_x = mesh.shape["gx"]
    count_y = mesh.shape["gy"]

    def on_device(field, active_rows, kern, target):
        tile_row = lax.axis_index("gx")
        waves, polars = field.shape[0], field.shape[1]
        tiles = field.shape[4]
        rows_dev = field.shape[5]
        side = field.shape[6]
        focus = kern.shape[3]
        shape = (waves, 2 * focus, polars * focus)
        share, near_field, near_kern, counts = call(
            share_kernel,
            [
                jax.ShapeDtypeStruct(shape, jnp.bfloat16),
                jax.ShapeDtypeStruct(field.shape[:3] + field.shape[4:], field.dtype),
                jax.ShapeDtypeStruct(kern.shape, kern.dtype),
                jax.ShapeDtypeStruct((tiles, 8, side), jnp.int32),
            ],
            [
                pltpu.SMEM(active_rows.shape, jnp.int32),
                pltpu.SemaphoreType.DMA((2 * waves + 1,)),
            ],
            [
                pltpu.with_memory_space_constraint(operand, pltpu.HBM)
                for operand in (active_rows, field, kern)
            ],
            [pltpu.HBM] * 3,
        )
        shares = [share] + partners(lambda d: share, "gy", count_y)
        share = total([term.astype(jnp.float32) for term in shares]).astype(jnp.bfloat16)
        strip_shape = (waves, tiles, 2 * rows_dev, polars * rows_dev)
        goal, row_kern, turn_kern, both_kern, own_strip, *strips = call(
            strip_kernel,
            [
                jax.ShapeDtypeStruct((waves, focus, polars * focus), target.dtype),
                jax.ShapeDtypeStruct((waves, 2 * polars * focus, polars * side), kern.dtype),
                jax.ShapeDtypeStruct((waves, tiles, 2 * rows_dev, 4 * focus), kern.dtype),
                jax.ShapeDtypeStruct((waves, tiles, 2 * focus, 2 * side), kern.dtype),
            ]
            + [jax.ShapeDtypeStruct(strip_shape, field.dtype)] * count_y,
            [],
            (near_field, near_kern, counts, target),
            [pltpu.VMEM] * 4,
        )
        strips = partners(lambda d: strips[d - 1], "gy", count_y)
        shares = [share] + partners(lambda d: share, "gx", count_x)
        shares = shares[::-1]
        shape = (tiles, rows_dev, side)
        scale = tiles * side / focus
        power, near, crossed = call(
            functools.partial(crossed_kernel, scale, count_y),
            [
                jax.ShapeDtypeStruct((waves, focus, polars * focus), jnp.float32),
                jax.ShapeDtypeStruct((waves, 4 * focus, polars * side), jnp.bfloat16),
                jax.ShapeDtypeStruct(shape, jnp.bfloat16),
            ],
            [],
            (row_kern, turn_kern, goal, own_strip, *strips, *shares),
            [pltpu.VMEM] * (3 + count_x + count_y),
        )
        gradient, intensity = call(
            functools.partial(straight_kernel, scale),
            [
                jax.ShapeDtypeStruct(shape, jnp.float32),
                jax.ShapeDtypeStruct((waves, focus, focus), jnp.float32),
            ],
            [],
            (near_field, counts, both_kern, near, power),
            [pltpu.VMEM] * 5,
        )
        partner = crossed.astype(jnp.float32) + lax.ppermute(crossed, "wa", pairs(2, 1)).astype(
            jnp.float32
        )
        narrow = partner.astype(jnp.bfloat16)
        came = [narrow[0]] + partners(lambda d: narrow[d], "gx", count_x)
        summed = gradient + lax.ppermute(gradient, "wa", pairs(2, 1))
        design_grad = in_order(0.5 * (summed + jnp.stack(came).astype(jnp.float32)), tile_row)
        return (design_grad[None], intensity)

    return on_device


def solution(mesh):
    placed = (
        P("wa", "cand", None, "gx", None, "gy", None),
        P("gx", None),
        P("wa", None, None, None, None),
        P("wa", None, None),
    )
    return jax.shard_map(
        make(mesh),
        mesh=mesh,
        in_specs=placed,
        out_specs=(P("gx", "cand", "gy", None), P("wa", "cand", None)),
        check_vma=False,
    )
```

```python
import functools

import jax
import jax.numpy as jnp
from jax import lax
from jax.experimental import pallas as pl
from jax.experimental.pallas import tpu as pltpu
from jax.sharding import PartitionSpec as P

VMEM = 16 * 2**20


def two_terms(value):
    high = value.astype(jnp.bfloat16)
    return high, (value - high.astype(jnp.float32)).astype(jnp.bfloat16)


def dot(first, second, over):
    return lax.dot_general(
        first, second, ((over[:1], over[1:]), ((), ())), preferred_element_type=jnp.float32
    )


def tile_kern(kern, wave, tile):
    real, imag = kern[wave, 0, tile], kern[wave, 1, tile]
    return jnp.concatenate([real, imag], axis=0), jnp.concatenate([-imag, real], axis=0)


def one_block(value, block, blocks):
    width = value.shape[1] // blocks
    picked = value[:, :width]
    for index in range(1, blocks):
        picked = jnp.where(block == index, value[:, index * width : (index + 1) * width], picked)
    return picked


def turn(value):
    width = value.shape[1]
    row = lax.broadcasted_iota(jnp.int32, (width, width), 0)
    column = lax.broadcasted_iota(jnp.int32, (width, width), 1)
    unit = jnp.where(row == column, 1.0, 0.0).astype(value.dtype)
    return dot(unit, value, (1, 1)).astype(value.dtype)


def twice(value, axis):
    return jnp.concatenate([value, value], axis=axis)


def diagonal(value, count):
    zero = jnp.zeros_like(value)
    rows = [
        jnp.concatenate([value if index == other else zero for other in range(count)], axis=1)
        for index in range(count)
    ]
    return jnp.concatenate(rows, axis=0)


def over_tiles(tiles, body, init):
    return lax.fori_loop(0, tiles, body, init, unroll=tiles <= 8)


def live_rows(count, shape):
    height = shape[-2]
    row = lax.axis_index("gy") * height + lax.broadcasted_iota(jnp.int32, shape, len(shape) - 2)
    return row < count


def share_kernel(rows_far, field_far, kern_far, share, field, kern, counts, rows, arrived):
    waves, polars, _, tiles, height, side = field.shape
    focus = kern.shape[3]
    copies = [pltpu.make_async_copy(rows_far, rows, arrived.at[2 * waves])]
    for wave in range(waves):
        copies += [
            pltpu.make_async_copy(kern_far.at[wave], kern.at[wave], arrived.at[2 * wave]),
            pltpu.make_async_copy(
                field_far.at[wave, :, :, 0], field.at[wave], arrived.at[2 * wave + 1]
            ),
        ]
    for copy in copies:
        copy.start()
    tile_row = lax.axis_index("gx")
    block = lax.axis_index("gy")
    copies[0].wait()
    inner = []
    own = []
    for wave in range(waves):
        copies[2 * wave + 1].wait()
        parts = []
        for part in range(2):
            value = kern[wave, part, tile_row].astype(jnp.float32)
            parts.append(diagonal(one_block(value, block, side // height), polars))
        own.append(twice(jnp.concatenate(parts, axis=0).astype(kern.dtype), 1))
        copies[2 * wave + 2].wait()

        def add_tile(tile, value):
            live = live_rows(rows[0, tile], (polars, height, side))
            planes = [
                jnp.where(live, field[wave, :, part, tile], jnp.zeros((), field.dtype))
                for part in range(2)
            ]
            planes = [plane.reshape(polars * height, side) for plane in planes]
            return value + dot(
                jnp.concatenate(tile_kern(kern, wave, tile), axis=1),
                jnp.concatenate(planes, axis=1),
                (1, 1),
            )

        zero = jnp.zeros((2 * focus, polars * height), jnp.float32)
        inner.append(over_tiles(tiles, add_tile, zero))
    for wave in range(waves):
        both = dot(jnp.concatenate(two_terms(inner[wave]), axis=1), own[wave], (1, 1))
        real, imag = both[:, : polars * focus], both[:, polars * focus :]
        focal = [real[:focus] - imag[focus:], real[focus:] + imag[:focus]]
        share[wave] = jnp.concatenate(focal, axis=0).astype(share.dtype)

    def put_count(tile, carry):
        counts[tile] = jnp.full(counts.shape[1:], rows[0, tile], jnp.int32)
        return carry

    over_tiles(tiles, put_count, 0)


def strip_kernel(field, kern, counts, target, goal, row_kern, turn_kern, both_kern, *strips):
    waves, polars, _, tiles, height, side = field.shape
    blocks = side // height
    block = lax.axis_index("gy")
    tile_row = lax.axis_index("gx")
    for wave in range(waves):
        goal[wave] = jnp.concatenate([target[wave].T] * polars, axis=1)
        for part in range(2):
            value = kern[wave, part, tile_row].astype(jnp.float32)
            columns = [
                diagonal(one_block(value, block ^ distance, blocks), polars)
                for distance in range(blocks)
            ]
            rows = pl.ds(part * polars * value.shape[0], polars * value.shape[0])
            row_kern[wave, rows] = jnp.concatenate(columns, axis=1).astype(kern.dtype)

    def one_tile(tile, carry):
        live = live_rows(counts[tile, :1], (height, side))
        for wave in range(waves):
            parts = tile_kern(kern, wave, tile)
            both_kern[wave, tile] = jnp.concatenate(parts, axis=1)
            parts = [one_block(part.astype(jnp.float32), block, blocks) for part in parts]
            turned = turn(jnp.concatenate(parts, axis=1).astype(kern.dtype))
            turn_kern[wave, tile] = twice(turned, 1)
            planes = [
                [
                    jnp.where(live, field[wave, polar, part, tile].astype(jnp.float32), 0.0)
                    for part in range(2)
                ]
                for polar in range(polars)
            ]
            for distance, strip in enumerate(strips):
                rows = [
                    jnp.concatenate(
                        [one_block(plane, block ^ distance, blocks) for plane in pair], axis=1
                    )
                    for pair in planes
                ]
                strip[wave, tile] = turn(jnp.concatenate(rows, axis=0).astype(strip.dtype))
        return carry

    over_tiles(tiles, one_tile, 0)


def crossed_kernel(scale, blocks, row_kern, turn_kern, goal, *refs):
    strips, refs = refs[:blocks], refs[blocks:]
    shares, (intensity, near, crossed) = refs[:-3], refs[-3:]
    waves, tiles, height, width = strips[0].shape
    height = height // 2
    polars = width // height
    focus = goal.shape[1]
    block = lax.axis_index("gy")
    sides = []
    for wave in range(waves):
        focal = total([share[wave].astype(jnp.float32) for share in shares])
        real, imag = focal[:focus], focal[focus:]
        power = real * real + imag * imag
        power = sum(pltpu.roll(power, polar * focus, 1) for polar in range(polars))
        intensity[wave] = power
        excess = power - goal[wave]
        real, imag = excess * real, excess * imag
        upright = jnp.concatenate([real, imag], axis=0)
        turned = jnp.concatenate([imag, -real], axis=0)
        terms = two_terms(jnp.concatenate([upright, turned], axis=1))
        row = dot(jnp.concatenate(terms, axis=1), twice(row_kern[wave], 0), (1, 0))
        sides.append(jnp.concatenate(two_terms(row), axis=0))
        near[wave] = sides[wave]

    def add_tile(distance, carry):
        tile = lax.axis_index("gx") ^ distance
        value = jnp.zeros((2 * height, blocks * width), jnp.float32)
        for wave in range(waves):
            back = dot(turn_kern[wave, tile], sides[wave], (1, 0))
            strip = jnp.concatenate([strip[wave, tile] for strip in strips], axis=1)
            value += back * strip.astype(jnp.float32)
        value = (value[:height] + value[height:]) * scale
        parts = []
        for apart in range(blocks):
            part = value[:, apart * width : (apart + 1) * width]
            parts.append(sum(part[:, at * height : (at + 1) * height] for at in range(polars)))
        columns = []
        for index in range(blocks):
            column = parts[0]
            for apart in range(1, blocks):
                column = jnp.where((block ^ apart) == index, parts[apart], column)
            columns.append(column)
        crossed[distance] = jnp.concatenate(columns, axis=1).astype(crossed.dtype)
        return carry

    over_tiles(tiles, add_tile, 0)


def straight_kernel(scale, field, counts, both_kern, near, gradient):
    waves, polars, _, tiles, height, side = field.shape
    sides = []
    for wave in range(waves):
        sides.append(turn(near[wave, :, : polars * height]))

    def add_tile(distance, carry):
        tile = lax.axis_index("gx") ^ distance
        term = jnp.zeros((height, side), jnp.float32)
        for wave in range(waves):
            back = dot(sides[wave], twice(both_kern[wave, tile], 0), (1, 0))
            back = back.reshape(polars, height, 2 * side)
            for polar in range(polars):
                for part in range(2):
                    plane = field[wave, polar, part, tile].astype(jnp.float32)
                    term += back[polar, :, part * side : (part + 1) * side] * plane
        live = live_rows(counts[tile, :1], (height, side))
        gradient[distance] = jnp.where(live, term * scale, 0.0)
        return carry

    over_tiles(tiles, add_tile, 0)


def call(kernel, out_shape, scratch, args, spaces):
    return pl.pallas_call(
        kernel,
        out_shape=out_shape,
        in_specs=[pl.BlockSpec(memory_space=space) for space in spaces],
        out_specs=[pl.BlockSpec(memory_space=pltpu.VMEM)] * len(out_shape),
        scratch_shapes=scratch,
        compiler_params=pltpu.CompilerParams(vmem_limit_bytes=VMEM),
    )(*args)


def pairs(count, distance):
    return [(device, device ^ distance) for device in range(count)]


def partners(value, axis, count):
    came = {d: lax.ppermute(value(d), axis, pairs(count, d)) for d in range(count - 1, 0, -1)}
    return [came[d] for d in range(1, count)]


def total(terms):
    while len(terms) > 1:
        terms = [first + second for first, second in zip(terms[::2], terms[1::2])]
    return terms[0]


def in_order(came, me):
    count = came.shape[0]
    rest = came.shape[1:]
    bit = 1
    while bit < count:
        split = came.reshape((count // (2 * bit), 2, bit) + rest)
        came = jnp.where((me & bit) != 0, split[:, ::-1], split).reshape((count,) + rest)
        bit *= 2
    return came


def make(mesh):
    count_x = mesh.shape["gx"]
    count_y = mesh.shape["gy"]

    def on_device(field, active_rows, kern, target):
        tile_row = lax.axis_index("gx")
        waves, polars = field.shape[0], field.shape[1]
        tiles = field.shape[4]
        rows_dev = field.shape[5]
        side = field.shape[6]
        focus = kern.shape[3]
        shape = (waves, 2 * focus, polars * focus)
        share, near_field, near_kern, counts = call(
            share_kernel,
            [
                jax.ShapeDtypeStruct(shape, jnp.bfloat16),
                jax.ShapeDtypeStruct(field.shape[:3] + field.shape[4:], field.dtype),
                jax.ShapeDtypeStruct(kern.shape, kern.dtype),
                jax.ShapeDtypeStruct((tiles, 8, side), jnp.int32),
            ],
            [
                pltpu.SMEM(active_rows.shape, jnp.int32),
                pltpu.SemaphoreType.DMA((2 * waves + 1,)),
            ],
            [
                pltpu.with_memory_space_constraint(operand, pltpu.HBM)
                for operand in (active_rows, field, kern)
            ],
            [pltpu.HBM] * 3,
        )
        shares = [share] + partners(lambda d: share, "gy", count_y)
        share = total([term.astype(jnp.float32) for term in shares]).astype(jnp.bfloat16)
        strip_shape = (waves, tiles, 2 * rows_dev, polars * rows_dev)
        goal, row_kern, turn_kern, both_kern, own_strip, *strips = call(
            strip_kernel,
            [
                jax.ShapeDtypeStruct((waves, focus, polars * focus), target.dtype),
                jax.ShapeDtypeStruct((waves, 2 * polars * focus, polars * side), kern.dtype),
                jax.ShapeDtypeStruct((waves, tiles, 2 * rows_dev, 4 * focus), kern.dtype),
                jax.ShapeDtypeStruct((waves, tiles, 2 * focus, 2 * side), kern.dtype),
            ]
            + [jax.ShapeDtypeStruct(strip_shape, field.dtype)] * count_y,
            [],
            (near_field, near_kern, counts, target),
            [pltpu.VMEM] * 4,
        )
        strips = partners(lambda d: strips[d - 1], "gy", count_y)
        shares = [share] + partners(lambda d: share, "gx", count_x)
        shares = shares[::-1]
        shape = (tiles, rows_dev, side)
        scale = tiles * side / focus
        power, near, crossed = call(
            functools.partial(crossed_kernel, scale, count_y),
            [
                jax.ShapeDtypeStruct((waves, focus, polars * focus), jnp.float32),
                jax.ShapeDtypeStruct((waves, 4 * focus, polars * side), jnp.bfloat16),
                jax.ShapeDtypeStruct(shape, jnp.bfloat16),
            ],
            [],
            (row_kern, turn_kern, goal, own_strip, *strips, *shares),
            [pltpu.VMEM] * (3 + count_x + count_y),
        )
        (gradient,) = call(
            functools.partial(straight_kernel, scale),
            [jax.ShapeDtypeStruct(shape, jnp.float32)],
            [],
            (near_field, counts, both_kern, near),
            [pltpu.VMEM] * 4,
        )
        partner = crossed.astype(jnp.float32) + lax.ppermute(crossed, "wa", pairs(2, 1)).astype(
            jnp.float32
        )
        narrow = partner.astype(jnp.bfloat16)
        came = [narrow[0]] + partners(lambda d: narrow[d], "gx", count_x)
        summed = gradient + lax.ppermute(gradient, "wa", pairs(2, 1))
        design_grad = in_order(0.5 * (summed + jnp.stack(came).astype(jnp.float32)), tile_row)
        intensity = jnp.swapaxes(power[:, :, :focus], 1, 2)
        return (design_grad[None], intensity)

    return on_device


def solution(mesh):
    placed = (
        P("wa", "cand", None, "gx", None, "gy", None),
        P("gx", None),
        P("wa", None, None, None, None),
        P("wa", None, None),
    )
    return jax.shard_map(
        make(mesh),
        mesh=mesh,
        in_specs=placed,
        out_specs=(P("gx", "cand", "gy", None), P("wa", "cand", None)),
        check_vma=False,
    )
```

```python
import functools

import jax
import jax.numpy as jnp
from jax import lax
from jax.experimental import pallas as pl
from jax.experimental.pallas import tpu as pltpu
from jax.sharding import PartitionSpec as P

VMEM = 16 * 2**20


def two_terms(value):
    high = value.astype(jnp.bfloat16)
    return high, (value - high.astype(jnp.float32)).astype(jnp.bfloat16)


def dot(first, second, over):
    return lax.dot_general(
        first, second, ((over[:1], over[1:]), ((), ())), preferred_element_type=jnp.float32
    )


def swapped(value, focus, left, right):
    lane = lax.broadcasted_iota(jnp.int32, value.shape, 1)
    sign = jnp.where(lane < focus, jnp.float32(left), jnp.float32(right))
    return pltpu.roll(value, focus, 1) * sign


def tile_kern(kern, wave, tile):
    real, imag = kern[wave, 0, tile], kern[wave, 1, tile]
    return jnp.concatenate([real, imag], axis=0), jnp.concatenate([-imag, real], axis=0)


def in_block(shape, block, width):
    lane = lax.broadcasted_iota(jnp.int32, shape, len(shape) - 1)
    return (lane >= block * width) & (lane < (block + 1) * width)


def side_by_side(first, second, block, blocks):
    width = first.shape[-1] // blocks
    first, second = first.astype(jnp.float32), second.astype(jnp.float32)
    beside = in_block(first.shape, lax.rem(block + 1, blocks), width)
    moved = jnp.where(beside, pltpu.roll(second, width, first.ndim - 1), 0.0)
    return jnp.where(in_block(first.shape, block, width), first, moved).astype(jnp.bfloat16)


def over_tiles(tiles, body, init):
    return lax.fori_loop(0, tiles, body, init, unroll=tiles <= 8)


def live_rows(count, shape):
    height = shape[-2]
    row = lax.axis_index("gy") * height + lax.broadcasted_iota(jnp.int32, shape, len(shape) - 2)
    return row < count


def share_kernel(rows_far, field_far, kern_far, share, field, kern, counts, rows, spread, arrived):
    waves, polars, _, tiles, height, side = field.shape
    focus = kern.shape[3]
    copies = [pltpu.make_async_copy(rows_far, rows, arrived.at[2 * waves])]
    for wave in range(waves):
        copies += [
            pltpu.make_async_copy(kern_far.at[wave], kern.at[wave], arrived.at[2 * wave]),
            pltpu.make_async_copy(
                field_far.at[wave, :, :, 0], field.at[wave], arrived.at[2 * wave + 1]
            ),
        ]
    for copy in copies:
        copy.start()
    tile_row = lax.axis_index("gx")
    first = pl.multiple_of(lax.axis_index("gy") * height, height)
    spread[...] = jnp.zeros_like(spread)
    copies[0].wait()
    inner = []
    for wave in range(waves):
        copies[2 * wave + 1].wait()
        copies[2 * wave + 2].wait()

        def add_tile(tile, value):
            live = live_rows(rows[0, tile], (polars, height, side))
            planes = [
                jnp.where(live, field[wave, :, part, tile], jnp.zeros((), field.dtype))
                for part in range(2)
            ]
            planes = [plane.reshape(polars * height, side) for plane in planes]
            return value + dot(
                jnp.concatenate(planes, axis=1),
                jnp.concatenate(tile_kern(kern, wave, tile), axis=1),
                (1, 1),
            )

        zero = jnp.zeros((polars * height, 2 * focus), jnp.float32)
        inner.append(over_tiles(tiles, add_tile, zero))
    for wave in range(waves):
        for polar in range(polars):
            lanes = pl.ds(polar * 2 * focus, 2 * focus)
            terms = two_terms(inner[wave][polar * height : (polar + 1) * height])
            for index, term in enumerate(terms):
                spread[wave, pl.ds(index * side + first, height), lanes] = term
        own = tile_kern(kern, wave, tile_row)[0]
        both = dot(jnp.concatenate([own, own], axis=1), spread[wave], (1, 0))
        for polar in range(polars):
            lanes = slice(polar * 2 * focus, (polar + 1) * 2 * focus)
            straight, crossed = both[:focus, lanes], both[focus:, lanes]
            share[wave, polar] = (straight + swapped(crossed, focus, -1, 1)).astype(share.dtype)

    def put_count(tile, carry):
        counts[tile] = jnp.full(counts.shape[1:], rows[0, tile], jnp.int32)
        return carry

    over_tiles(tiles, put_count, 0)


def strip_kernel(field, kern, counts, own_kern, both_kern, strip_kern, *strips):
    waves, polars, _, tiles, height, side = field.shape
    blocks = side // height
    block = lax.axis_index("gy")
    tile_row = lax.axis_index("gx")
    for wave in range(waves):
        for part in range(2):
            turned = kern[wave, part, tile_row].astype(jnp.float32).T.astype(kern.dtype)
            own_kern[wave, pl.ds(part * side, side)] = jnp.concatenate([turned, turned], axis=1)

    def one_tile(tile, carry):
        live = live_rows(counts[tile, :1], (height, side))
        for wave in range(waves):
            parts = tile_kern(kern, wave, tile)
            both_kern[wave, tile] = jnp.concatenate(parts, axis=1)
            strip_kern[wave, tile] = side_by_side(*parts, block, blocks)
            for polar in range(polars):
                for distance, strip in enumerate(strips):
                    both = side_by_side(
                        field[wave, polar, 0, tile],
                        field[wave, polar, 1, tile],
                        block ^ distance,
                        blocks,
                    )
                    strip[wave, polar, tile] = jnp.where(live, both, jnp.zeros((), both.dtype))
        return carry

    over_tiles(tiles, one_tile, 0)


def twice(value):
    return jnp.concatenate([value, value], axis=0)


def crossed_kernel(scale, blocks, own_kern, strip_kern, target, *refs):
    strips, refs = refs[:blocks], refs[blocks:]
    shares, (powers, sides, crossed, rowside, whole, turned) = refs[:-6], refs[-6:]
    waves, polars, tiles, height, side = strips[0].shape
    focus = target.shape[1]
    block = lax.axis_index("gy")
    for wave in range(waves):
        focal = [
            total([share[wave, polar].astype(jnp.float32) for share in shares])
            for polar in range(polars)
        ]
        power = sum(value * value for value in focal)
        powers[wave] = power
        power = power + pltpu.roll(power, focus, 1)
        goal = target[wave]
        excess = power - jnp.concatenate([goal, goal], axis=1)
        source = jnp.concatenate([excess * value for value in focal], axis=1)
        terms = jnp.concatenate(two_terms(source), axis=0)
        rowside[wave] = dot(own_kern[wave], terms, (1, 0))
    near = []
    for wave in range(waves):
        near.append([])
        for distance in range(blocks):
            first = pl.multiple_of((block ^ distance) * height, height)
            parts = []
            for polar in range(polars):
                lanes = pl.ds(polar * 2 * focus, 2 * focus)
                straight = rowside[wave, pl.ds(first, height), lanes]
                across = rowside[wave, pl.ds(side + first, height), lanes]
                parts.append(straight + swapped(across, focus, 1, -1))
            terms = two_terms(jnp.concatenate(parts, axis=0))
            near[wave].append(jnp.concatenate(terms, axis=1))
        sides[wave] = near[wave][0]

    def add_tile(distance, carry):
        tile = lax.axis_index("gx") ^ distance
        for index, strip in enumerate(strips):
            value = jnp.zeros((height, side), jnp.float32)
            for wave in range(waves):
                back = dot(near[wave][index], twice(strip_kern[wave, tile]), (1, 0))
                back = back.reshape(polars, height, side)
                for polar in range(polars):
                    value += back[polar] * strip[wave, polar, tile].astype(jnp.float32)
            first = pl.multiple_of((block ^ index) * height, height)
            whole[distance, pl.ds(first, height)] = (
                value + pltpu.roll(value, side - height, 1)
            ) * scale
        turned[distance] = whole[distance].T
        own = turned[distance, pl.ds(pl.multiple_of(block * height, height), height)]
        crossed[distance] = own.astype(crossed.dtype)
        return carry

    over_tiles(tiles, add_tile, 0)


def straight_kernel(scale, field, counts, both_kern, sides, gradient):
    waves, polars, _, tiles, height, side = field.shape

    def add_tile(distance, carry):
        tile = lax.axis_index("gx") ^ distance
        term = jnp.zeros((height, side), jnp.float32)
        for wave in range(waves):
            back = dot(sides[wave], twice(both_kern[wave, tile]), (1, 0))
            back = back.reshape(polars, height, 2 * side)
            for polar in range(polars):
                for part in range(2):
                    plane = field[wave, polar, part, tile].astype(jnp.float32)
                    term += back[polar, :, part * side : (part + 1) * side] * plane
        live = live_rows(counts[tile, :1], (height, side))
        gradient[distance] = jnp.where(live, term * scale, 0.0)
        return carry

    over_tiles(tiles, add_tile, 0)


def call(kernel, out_shape, scratch, args, spaces):
    return pl.pallas_call(
        kernel,
        out_shape=out_shape,
        in_specs=[pl.BlockSpec(memory_space=space) for space in spaces],
        out_specs=[pl.BlockSpec(memory_space=pltpu.VMEM)] * len(out_shape),
        scratch_shapes=scratch,
        compiler_params=pltpu.CompilerParams(vmem_limit_bytes=VMEM),
    )(*args)


def pairs(count, distance):
    return [(device, device ^ distance) for device in range(count)]


def partners(value, axis, count):
    came = {d: lax.ppermute(value(d), axis, pairs(count, d)) for d in range(count - 1, 0, -1)}
    return [came[d] for d in range(1, count)]


def total(terms):
    while len(terms) > 1:
        terms = [first + second for first, second in zip(terms[::2], terms[1::2])]
    return terms[0]


def in_order(came, me):
    count = came.shape[0]
    rest = came.shape[1:]
    bit = 1
    while bit < count:
        split = came.reshape((count // (2 * bit), 2, bit) + rest)
        came = jnp.where((me & bit) != 0, split[:, ::-1], split).reshape((count,) + rest)
        bit *= 2
    return came


def make(mesh):
    count_x = mesh.shape["gx"]
    count_y = mesh.shape["gy"]

    def on_device(field, active_rows, kern, target):
        tile_row = lax.axis_index("gx")
        waves, polars = field.shape[0], field.shape[1]
        tiles = field.shape[4]
        rows_dev = field.shape[5]
        side = field.shape[6]
        focus = kern.shape[3]
        shape = (waves, polars, focus, 2 * focus)
        share, near_field, near_kern, counts = call(
            share_kernel,
            [
                jax.ShapeDtypeStruct(shape, jnp.bfloat16),
                jax.ShapeDtypeStruct(field.shape[:3] + field.shape[4:], field.dtype),
                jax.ShapeDtypeStruct(kern.shape, kern.dtype),
                jax.ShapeDtypeStruct((tiles, 8, side), jnp.int32),
            ],
            [
                pltpu.SMEM(active_rows.shape, jnp.int32),
                pltpu.VMEM((waves, 2 * side, polars * 2 * focus), jnp.bfloat16),
                pltpu.SemaphoreType.DMA((2 * waves + 1,)),
            ],
            [
                pltpu.with_memory_space_constraint(operand, pltpu.HBM)
                for operand in (active_rows, field, kern)
            ],
            [pltpu.HBM] * 3,
        )
        shares = [share] + partners(lambda d: share, "gy", count_y)
        share = total([term.astype(jnp.float32) for term in shares]).astype(jnp.bfloat16)
        strip_shape = (waves, polars, tiles, rows_dev, side)
        own_kern, both_kern, strip_kern, own_strip, *strips = call(
            strip_kernel,
            [
                jax.ShapeDtypeStruct((waves, 2 * side, 2 * focus), kern.dtype),
                jax.ShapeDtypeStruct((waves, tiles, 2 * focus, 2 * side), kern.dtype),
                jax.ShapeDtypeStruct((waves, tiles, 2 * focus, side), kern.dtype),
            ]
            + [jax.ShapeDtypeStruct(strip_shape, field.dtype)] * count_y,
            [],
            (near_field, near_kern, counts),
            [pltpu.VMEM] * 3,
        )
        strips = partners(lambda d: strips[d - 1], "gy", count_y)
        shares = [share] + partners(lambda d: share, "gx", count_x)
        shares = shares[::-1]
        shape = (tiles, rows_dev, side)
        scale = tiles * side / focus
        powers, sides, crossed = call(
            functools.partial(crossed_kernel, scale, count_y),
            [
                jax.ShapeDtypeStruct((waves, focus, 2 * focus), jnp.float32),
                jax.ShapeDtypeStruct((waves, polars * rows_dev, 4 * focus), jnp.bfloat16),
                jax.ShapeDtypeStruct(shape, jnp.bfloat16),
            ],
            [pltpu.VMEM((waves, 2 * side, polars * 2 * focus), jnp.float32)]
            + [pltpu.VMEM((tiles, side, side), jnp.float32)] * 2,
            (own_kern, strip_kern, target, own_strip, *strips, *shares),
            [pltpu.VMEM] * (3 + count_x + count_y),
        )
        (gradient,) = call(
            functools.partial(straight_kernel, scale),
            [jax.ShapeDtypeStruct(shape, jnp.float32)],
            [],
            (near_field, counts, both_kern, sides),
            [pltpu.VMEM] * 4,
        )
        partner = crossed.astype(jnp.float32) + lax.ppermute(crossed, "wa", pairs(2, 1)).astype(
            jnp.float32
        )
        narrow = partner.astype(jnp.bfloat16)
        came = [narrow[0]] + partners(lambda d: narrow[d], "gx", count_x)
        summed = gradient + lax.ppermute(gradient, "wa", pairs(2, 1))
        design_grad = in_order(0.5 * (summed + jnp.stack(came).astype(jnp.float32)), tile_row)
        intensity = powers[:, :, :focus] + powers[:, :, focus:]
        return (design_grad[None], intensity)

    return on_device


def solution(mesh):
    placed = (
        P("wa", "cand", None, "gx", None, "gy", None),
        P("gx", None),
        P("wa", None, None, None, None),
        P("wa", None, None),
    )
    return jax.shard_map(
        make(mesh),
        mesh=mesh,
        in_specs=placed,
        out_specs=(P("gx", "cand", "gy", None), P("wa", "cand", None)),
        check_vma=False,
    )
```

```python
import functools

import jax
import jax.numpy as jnp
from jax import lax
from jax.experimental import pallas as pl
from jax.experimental.pallas import tpu as pltpu
from jax.sharding import PartitionSpec as P

VMEM = 16 * 2**20


def two_terms(value):
    high = value.astype(jnp.bfloat16)
    return high, (value - high.astype(jnp.float32)).astype(jnp.bfloat16)


def dot(first, second, over):
    return lax.dot_general(
        first, second, ((over[:1], over[1:]), ((), ())), preferred_element_type=jnp.float32
    )


def swapped(value, focus, left, right):
    lane = lax.broadcasted_iota(jnp.int32, value.shape, 1)
    sign = jnp.where(lane < focus, jnp.float32(left), jnp.float32(right))
    return pltpu.roll(value, focus, 1) * sign


def tile_kern(kern, wave, tile):
    real, imag = kern[wave, 0, tile], kern[wave, 1, tile]
    return jnp.concatenate([real, imag], axis=0), jnp.concatenate([-imag, real], axis=0)


def in_block(shape, block, width):
    lane = lax.broadcasted_iota(jnp.int32, shape, len(shape) - 1)
    return (lane >= block * width) & (lane < (block + 1) * width)


def side_by_side(first, second, block, blocks):
    width = first.shape[-1] // blocks
    first, second = first.astype(jnp.float32), second.astype(jnp.float32)
    beside = in_block(first.shape, lax.rem(block + 1, blocks), width)
    moved = jnp.where(beside, pltpu.roll(second, width, first.ndim - 1), 0.0)
    return jnp.where(in_block(first.shape, block, width), first, moved).astype(jnp.bfloat16)


def over_tiles(tiles, body, init):
    return lax.fori_loop(0, tiles, body, init, unroll=tiles <= 8)


def live_rows(count, shape):
    height = shape[-2]
    row = lax.axis_index("gy") * height + lax.broadcasted_iota(jnp.int32, shape, len(shape) - 2)
    return row < count


def share_kernel(rows_far, field_far, kern_far, share, field, kern, counts, rows, spread, arrived):
    waves, polars, _, tiles, height, side = field.shape
    focus = kern.shape[3]
    copies = [pltpu.make_async_copy(rows_far, rows, arrived.at[2 * waves])]
    for wave in range(waves):
        copies += [
            pltpu.make_async_copy(kern_far.at[wave], kern.at[wave], arrived.at[2 * wave]),
            pltpu.make_async_copy(
                field_far.at[wave, :, :, 0], field.at[wave], arrived.at[2 * wave + 1]
            ),
        ]
    for copy in copies:
        copy.start()
    tile_row = lax.axis_index("gx")
    first = pl.multiple_of(lax.axis_index("gy") * height, height)
    spread[...] = jnp.zeros_like(spread)
    copies[0].wait()
    inner = []
    for wave in range(waves):
        copies[2 * wave + 1].wait()
        copies[2 * wave + 2].wait()

        def add_tile(tile, value):
            live = live_rows(rows[0, tile], (polars, height, side))
            planes = [
                jnp.where(live, field[wave, :, part, tile], jnp.zeros((), field.dtype))
                for part in range(2)
            ]
            planes = [plane.reshape(polars * height, side) for plane in planes]
            return value + dot(
                jnp.concatenate(planes, axis=1),
                jnp.concatenate(tile_kern(kern, wave, tile), axis=1),
                (1, 1),
            )

        zero = jnp.zeros((polars * height, 2 * focus), jnp.float32)
        inner.append(over_tiles(tiles, add_tile, zero))
    for wave in range(waves):
        for polar in range(polars):
            lanes = pl.ds(polar * 2 * focus, 2 * focus)
            terms = two_terms(inner[wave][polar * height : (polar + 1) * height])
            for index, term in enumerate(terms):
                spread[wave, pl.ds(index * side + first, height), lanes] = term
        own = tile_kern(kern, wave, tile_row)[0]
        both = dot(jnp.concatenate([own, own], axis=1), spread[wave], (1, 0))
        for polar in range(polars):
            lanes = slice(polar * 2 * focus, (polar + 1) * 2 * focus)
            straight, crossed = both[:focus, lanes], both[focus:, lanes]
            share[wave, polar] = (straight + swapped(crossed, focus, -1, 1)).astype(share.dtype)

    def put_count(tile, carry):
        counts[tile] = jnp.full(counts.shape[1:], rows[0, tile], jnp.int32)
        return carry

    over_tiles(tiles, put_count, 0)


def strip_kernel(field, kern, counts, own_kern, both_kern, strip_kern, *strips):
    waves, polars, _, tiles, height, side = field.shape
    blocks = side // height
    block = lax.axis_index("gy")
    tile_row = lax.axis_index("gx")
    for wave in range(waves):
        for part in range(2):
            turned = kern[wave, part, tile_row].astype(jnp.float32).T.astype(kern.dtype)
            own_kern[wave, pl.ds(part * side, side)] = jnp.concatenate([turned, turned], axis=1)

    def one_tile(tile, carry):
        live = live_rows(counts[tile, :1], (height, side))
        for wave in range(waves):
            parts = tile_kern(kern, wave, tile)
            both_kern[wave, tile] = jnp.concatenate(parts, axis=1)
            strip_kern[wave, tile] = side_by_side(*parts, block, blocks)
            for polar in range(polars):
                for distance, strip in enumerate(strips):
                    both = side_by_side(
                        field[wave, polar, 0, tile],
                        field[wave, polar, 1, tile],
                        block ^ distance,
                        blocks,
                    )
                    strip[wave, polar, tile] = jnp.where(live, both, jnp.zeros((), both.dtype))
        return carry

    over_tiles(tiles, one_tile, 0)


def twice(value):
    return jnp.concatenate([value, value], axis=0)


def crossed_kernel(scale, blocks, own_kern, strip_kern, target, *refs):
    strips, refs = refs[:blocks], refs[blocks:]
    shares, (powers, sides, crossed, rowside, whole, turned) = refs[:-6], refs[-6:]
    waves, polars, tiles, height, side = strips[0].shape
    focus = target.shape[1]
    block = lax.axis_index("gy")
    for wave in range(waves):
        focal = [
            total([share[wave, polar].astype(jnp.float32) for share in shares])
            for polar in range(polars)
        ]
        power = sum(value * value for value in focal)
        powers[wave] = power
        power = power + pltpu.roll(power, focus, 1)
        goal = target[wave]
        excess = power - jnp.concatenate([goal, goal], axis=1)
        source = jnp.concatenate([excess * value for value in focal], axis=1)
        terms = jnp.concatenate(two_terms(source), axis=0)
        rowside[wave] = dot(own_kern[wave], terms, (1, 0))
    near = []
    for wave in range(waves):
        near.append([])
        for distance in range(blocks):
            first = pl.multiple_of((block ^ distance) * height, height)
            parts = []
            for polar in range(polars):
                lanes = pl.ds(polar * 2 * focus, 2 * focus)
                straight = rowside[wave, pl.ds(first, height), lanes]
                across = rowside[wave, pl.ds(side + first, height), lanes]
                parts.append(straight + swapped(across, focus, 1, -1))
            terms = two_terms(jnp.concatenate(parts, axis=0))
            near[wave].append(jnp.concatenate(terms, axis=1))
        sides[wave] = near[wave][0]

    def add_tile(distance, carry):
        tile = lax.axis_index("gx") ^ distance
        for index, strip in enumerate(strips):
            value = jnp.zeros((height, side), jnp.float32)
            for wave in range(waves):
                back = dot(near[wave][index], twice(strip_kern[wave, tile]), (1, 0))
                back = back.reshape(polars, height, side)
                for polar in range(polars):
                    value += back[polar] * strip[wave, polar, tile].astype(jnp.float32)
            first = pl.multiple_of((block ^ index) * height, height)
            whole[distance, pl.ds(first, height)] = (
                value + pltpu.roll(value, side - height, 1)
            ) * scale
        turned[distance] = whole[distance].T
        own = turned[distance, pl.ds(pl.multiple_of(block * height, height), height)]
        crossed[distance] = own.astype(crossed.dtype)
        return carry

    over_tiles(tiles, add_tile, 0)


def straight_kernel(scale, field, counts, both_kern, sides, gradient):
    waves, polars, _, tiles, height, side = field.shape

    def add_tile(distance, carry):
        tile = lax.axis_index("gx") ^ distance
        term = jnp.zeros((height, side), jnp.float32)
        for wave in range(waves):
            back = dot(sides[wave], twice(both_kern[wave, tile]), (1, 0))
            back = back.reshape(polars, height, 2 * side)
            for polar in range(polars):
                for part in range(2):
                    plane = field[wave, polar, part, tile].astype(jnp.float32)
                    term += back[polar, :, part * side : (part + 1) * side] * plane
        live = live_rows(counts[tile, :1], (height, side))
        gradient[distance] = jnp.where(live, term * scale, 0.0)
        return carry

    over_tiles(tiles, add_tile, 0)


def call(kernel, out_shape, scratch, args, spaces):
    return pl.pallas_call(
        kernel,
        out_shape=out_shape,
        in_specs=[pl.BlockSpec(memory_space=space) for space in spaces],
        out_specs=[pl.BlockSpec(memory_space=pltpu.VMEM)] * len(out_shape),
        scratch_shapes=scratch,
        compiler_params=pltpu.CompilerParams(vmem_limit_bytes=VMEM),
    )(*args)


def pairs(count, distance):
    return [(device, device ^ distance) for device in range(count)]


def partners(value, axis, count):
    came = {d: lax.ppermute(value(d), axis, pairs(count, d)) for d in range(count - 1, 0, -1)}
    return [came[d] for d in range(1, count)]


def total(terms):
    while len(terms) > 1:
        terms = [first + second for first, second in zip(terms[::2], terms[1::2])]
    return terms[0]


def rounded(value):
    return lax.reduce_precision(value, 8, 7)


def in_order(came, me):
    count = came.shape[0]
    rest = came.shape[1:]
    bit = 1
    while bit < count:
        split = came.reshape((count // (2 * bit), 2, bit) + rest)
        came = jnp.where((me & bit) != 0, split[:, ::-1], split).reshape((count,) + rest)
        bit *= 2
    return came


def make(mesh):
    count_x = mesh.shape["gx"]
    count_y = mesh.shape["gy"]

    def on_device(field, active_rows, kern, target):
        tile_row = lax.axis_index("gx")
        waves, polars = field.shape[0], field.shape[1]
        tiles = field.shape[4]
        rows_dev = field.shape[5]
        side = field.shape[6]
        focus = kern.shape[3]
        shape = (waves, polars, focus, 2 * focus)
        share, near_field, near_kern, counts = call(
            share_kernel,
            [
                jax.ShapeDtypeStruct(shape, jnp.bfloat16),
                jax.ShapeDtypeStruct(field.shape[:3] + field.shape[4:], field.dtype),
                jax.ShapeDtypeStruct(kern.shape, kern.dtype),
                jax.ShapeDtypeStruct((tiles, 8, side), jnp.int32),
            ],
            [
                pltpu.SMEM(active_rows.shape, jnp.int32),
                pltpu.VMEM((waves, 2 * side, polars * 2 * focus), jnp.bfloat16),
                pltpu.SemaphoreType.DMA((2 * waves + 1,)),
            ],
            [
                pltpu.with_memory_space_constraint(operand, pltpu.HBM)
                for operand in (active_rows, field, kern)
            ],
            [pltpu.HBM] * 3,
        )
        shares = [share] + partners(lambda d: share, "gy", count_y)
        share = total([term.astype(jnp.float32) for term in shares]).astype(jnp.bfloat16)
        strip_shape = (waves, polars, tiles, rows_dev, side)
        own_kern, both_kern, strip_kern, own_strip, *strips = call(
            strip_kernel,
            [
                jax.ShapeDtypeStruct((waves, 2 * side, 2 * focus), kern.dtype),
                jax.ShapeDtypeStruct((waves, tiles, 2 * focus, 2 * side), kern.dtype),
                jax.ShapeDtypeStruct((waves, tiles, 2 * focus, side), kern.dtype),
            ]
            + [jax.ShapeDtypeStruct(strip_shape, field.dtype)] * count_y,
            [],
            (near_field, near_kern, counts),
            [pltpu.VMEM] * 3,
        )
        strips = partners(lambda d: strips[d - 1], "gy", count_y)
        shares = [share] + partners(lambda d: share, "gx", count_x)
        shares = shares[::-1]
        shape = (tiles, rows_dev, side)
        scale = tiles * side / focus
        powers, sides, crossed = call(
            functools.partial(crossed_kernel, scale, count_y),
            [
                jax.ShapeDtypeStruct((waves, focus, 2 * focus), jnp.float32),
                jax.ShapeDtypeStruct((waves, polars * rows_dev, 4 * focus), jnp.bfloat16),
                jax.ShapeDtypeStruct(shape, jnp.bfloat16),
            ],
            [pltpu.VMEM((waves, 2 * side, polars * 2 * focus), jnp.float32)]
            + [pltpu.VMEM((tiles, side, side), jnp.float32)] * 2,
            (own_kern, strip_kern, target, own_strip, *strips, *shares),
            [pltpu.VMEM] * (3 + count_x + count_y),
        )
        (gradient,) = call(
            functools.partial(straight_kernel, scale),
            [jax.ShapeDtypeStruct(shape, jnp.float32)],
            [],
            (near_field, counts, both_kern, sides),
            [pltpu.VMEM] * 4,
        )
        came = [crossed[0]] + partners(lambda d: crossed[d], "gx", count_x)
        own = rounded(gradient + jnp.stack(came).astype(jnp.float32))
        other = lax.ppermute(own.astype(jnp.bfloat16), "wa", pairs(2, 1))
        design_grad = in_order(0.5 * (own + other.astype(jnp.float32)), tile_row)
        intensity = powers[:, :, :focus] + powers[:, :, focus:]
        return (design_grad[None], intensity)

    return on_device


def solution(mesh):
    placed = (
        P("wa", "cand", None, "gx", None, "gy", None),
        P("gx", None),
        P("wa", None, None, None, None),
        P("wa", None, None),
    )
    return jax.shard_map(
        make(mesh),
        mesh=mesh,
        in_specs=placed,
        out_specs=(P("gx", "cand", "gy", None), P("wa", "cand", None)),
        check_vma=False,
    )
```

```python
import functools

import jax
import jax.numpy as jnp
from jax import lax
from jax.experimental import pallas as pl
from jax.experimental.pallas import tpu as pltpu
from jax.sharding import PartitionSpec as P

VMEM = 16 * 2**20


def two_terms(value):
    high = value.astype(jnp.bfloat16)
    return high, (value - high.astype(jnp.float32)).astype(jnp.bfloat16)


def dot(first, second, over):
    return lax.dot_general(
        first, second, ((over[:1], over[1:]), ((), ())), preferred_element_type=jnp.float32
    )


def swapped(value, focus, left, right):
    lane = lax.broadcasted_iota(jnp.int32, value.shape, 1)
    sign = jnp.where(lane < focus, jnp.float32(left), jnp.float32(right))
    return pltpu.roll(value, focus, 1) * sign


def tile_kern(kern, wave, tile):
    real, imag = kern[wave, 0, tile], kern[wave, 1, tile]
    return jnp.concatenate([real, imag], axis=0), jnp.concatenate([-imag, real], axis=0)


def in_block(shape, block, width):
    lane = lax.broadcasted_iota(jnp.int32, shape, len(shape) - 1)
    return (lane >= block * width) & (lane < (block + 1) * width)


def side_by_side(first, second, block, blocks):
    width = first.shape[-1] // blocks
    first, second = first.astype(jnp.float32), second.astype(jnp.float32)
    beside = in_block(first.shape, lax.rem(block + 1, blocks), width)
    moved = jnp.where(beside, pltpu.roll(second, width, first.ndim - 1), 0.0)
    return jnp.where(in_block(first.shape, block, width), first, moved).astype(jnp.bfloat16)


def over_tiles(tiles, body, init):
    return lax.fori_loop(0, tiles, body, init, unroll=tiles <= 8)


def live_rows(count, shape):
    height = shape[-2]
    row = lax.axis_index("gy") * height + lax.broadcasted_iota(jnp.int32, shape, len(shape) - 2)
    return row < count


def share_kernel(rows_far, field_far, kern_far, share, field, kern, counts, rows, spread, arrived):
    waves, polars, _, tiles, height, side = field.shape
    focus = kern.shape[3]
    copies = [pltpu.make_async_copy(rows_far, rows, arrived.at[2 * waves])]
    for wave in range(waves):
        copies += [
            pltpu.make_async_copy(kern_far.at[wave], kern.at[wave], arrived.at[2 * wave]),
            pltpu.make_async_copy(
                field_far.at[wave, :, :, 0], field.at[wave], arrived.at[2 * wave + 1]
            ),
        ]
    for copy in copies:
        copy.start()
    tile_row = lax.axis_index("gx")
    first = pl.multiple_of(lax.axis_index("gy") * height, height)
    spread[...] = jnp.zeros_like(spread)
    copies[0].wait()
    inner = []
    for wave in range(waves):
        copies[2 * wave + 1].wait()
        copies[2 * wave + 2].wait()

        def add_tile(tile, value):
            live = live_rows(rows[0, tile], (polars, height, side))
            planes = [
                jnp.where(live, field[wave, :, part, tile], jnp.zeros((), field.dtype))
                for part in range(2)
            ]
            planes = [plane.reshape(polars * height, side) for plane in planes]
            return value + dot(
                jnp.concatenate(planes, axis=1),
                jnp.concatenate(tile_kern(kern, wave, tile), axis=1),
                (1, 1),
            )

        zero = jnp.zeros((polars * height, 2 * focus), jnp.float32)
        inner.append(over_tiles(tiles, add_tile, zero))
    for wave in range(waves):
        for polar in range(polars):
            lanes = pl.ds(polar * 2 * focus, 2 * focus)
            terms = two_terms(inner[wave][polar * height : (polar + 1) * height])
            for index, term in enumerate(terms):
                spread[wave, pl.ds(index * side + first, height), lanes] = term
        own = tile_kern(kern, wave, tile_row)[0]
        both = dot(jnp.concatenate([own, own], axis=1), spread[wave], (1, 0))
        for polar in range(polars):
            lanes = slice(polar * 2 * focus, (polar + 1) * 2 * focus)
            straight, crossed = both[:focus, lanes], both[focus:, lanes]
            share[wave, polar] = (straight + swapped(crossed, focus, -1, 1)).astype(share.dtype)

    def put_count(tile, carry):
        counts[tile] = jnp.full(counts.shape[1:], rows[0, tile], jnp.int32)
        return carry

    over_tiles(tiles, put_count, 0)


def strip_kernel(field, kern, counts, own_kern, both_kern, strip_kern, *strips):
    waves, polars, _, tiles, height, side = field.shape
    blocks = side // height
    block = lax.axis_index("gy")
    tile_row = lax.axis_index("gx")
    for wave in range(waves):
        for part in range(2):
            turned = kern[wave, part, tile_row].astype(jnp.float32).T.astype(kern.dtype)
            own_kern[wave, pl.ds(part * side, side)] = jnp.concatenate([turned, turned], axis=1)

    def one_tile(tile, carry):
        live = live_rows(counts[tile, :1], (height, side))
        for wave in range(waves):
            parts = tile_kern(kern, wave, tile)
            both_kern[wave, tile] = jnp.concatenate(parts, axis=1)
            strip_kern[wave, tile] = side_by_side(*parts, block, blocks)
            for polar in range(polars):
                for distance, strip in enumerate(strips):
                    both = side_by_side(
                        field[wave, polar, 0, tile],
                        field[wave, polar, 1, tile],
                        block ^ distance,
                        blocks,
                    )
                    strip[wave, polar, tile] = jnp.where(live, both, jnp.zeros((), both.dtype))
        return carry

    over_tiles(tiles, one_tile, 0)


def twice(value):
    return jnp.concatenate([value, value], axis=0)


def crossed_kernel(scale, blocks, own_kern, strip_kern, target, *refs):
    strips, refs = refs[:blocks], refs[blocks:]
    shares, (powers, sides, crossed, rowside, whole, turned) = refs[:-6], refs[-6:]
    waves, polars, tiles, height, side = strips[0].shape
    focus = target.shape[1]
    block = lax.axis_index("gy")
    for wave in range(waves):
        focal = [
            total([share[wave, polar].astype(jnp.float32) for share in shares])
            for polar in range(polars)
        ]
        power = sum(value * value for value in focal)
        powers[wave] = power
        power = power + pltpu.roll(power, focus, 1)
        goal = target[wave]
        excess = power - jnp.concatenate([goal, goal], axis=1)
        source = jnp.concatenate([excess * value for value in focal], axis=1)
        terms = jnp.concatenate(two_terms(source), axis=0)
        rowside[wave] = dot(own_kern[wave], terms, (1, 0))
    near = []
    for wave in range(waves):
        near.append([])
        for distance in range(blocks):
            first = pl.multiple_of((block ^ distance) * height, height)
            parts = []
            for polar in range(polars):
                lanes = pl.ds(polar * 2 * focus, 2 * focus)
                straight = rowside[wave, pl.ds(first, height), lanes]
                across = rowside[wave, pl.ds(side + first, height), lanes]
                parts.append(straight + swapped(across, focus, 1, -1))
            terms = two_terms(jnp.concatenate(parts, axis=0))
            near[wave].append(jnp.concatenate(terms, axis=1))
        sides[wave] = near[wave][0]

    def add_tile(distance, carry):
        tile = lax.axis_index("gx") ^ distance
        for index, strip in enumerate(strips):
            value = jnp.zeros((height, side), jnp.float32)
            for wave in range(waves):
                back = dot(near[wave][index], twice(strip_kern[wave, tile]), (1, 0))
                back = back.reshape(polars, height, side)
                for polar in range(polars):
                    value += back[polar] * strip[wave, polar, tile].astype(jnp.float32)
            first = pl.multiple_of((block ^ index) * height, height)
            whole[distance, pl.ds(first, height)] = (
                value + pltpu.roll(value, side - height, 1)
            ) * scale
        turned[distance] = whole[distance].T
        own = turned[distance, pl.ds(pl.multiple_of(block * height, height), height)]
        crossed[distance] = own.astype(crossed.dtype)
        return carry

    over_tiles(tiles, add_tile, 0)


def straight_kernel(scale, field, counts, both_kern, sides, gradient):
    waves, polars, _, tiles, height, side = field.shape

    def add_tile(distance, carry):
        tile = lax.axis_index("gx") ^ distance
        term = jnp.zeros((height, side), jnp.float32)
        for wave in range(waves):
            back = dot(sides[wave], twice(both_kern[wave, tile]), (1, 0))
            back = back.reshape(polars, height, 2 * side)
            for polar in range(polars):
                for part in range(2):
                    plane = field[wave, polar, part, tile].astype(jnp.float32)
                    term += back[polar, :, part * side : (part + 1) * side] * plane
        live = live_rows(counts[tile, :1], (height, side))
        gradient[distance] = jnp.where(live, term * scale, 0.0)
        return carry

    over_tiles(tiles, add_tile, 0)


def call(kernel, out_shape, scratch, args, spaces):
    return pl.pallas_call(
        kernel,
        out_shape=out_shape,
        in_specs=[pl.BlockSpec(memory_space=space) for space in spaces],
        out_specs=[pl.BlockSpec(memory_space=pltpu.VMEM)] * len(out_shape),
        scratch_shapes=scratch,
        compiler_params=pltpu.CompilerParams(vmem_limit_bytes=VMEM),
    )(*args)


def pairs(count, distance):
    return [(device, device ^ distance) for device in range(count)]


def partners(value, axis, count):
    came = {d: lax.ppermute(value(d), axis, pairs(count, d)) for d in range(count - 1, 0, -1)}
    return [came[d] for d in range(1, count)]


def last_core_partners(value, mesh):
    count, cores = mesh.shape["gx"], mesh.shape["wa"]

    def routes(distance):
        moved = [distance if core == cores - 1 else 0 for core in range(cores)]
        return [
            (device * cores + core, (device ^ moved[core]) * cores + core)
            for device in range(count)
            for core in range(cores)
        ]

    came = {d: lax.ppermute(value(d), ("gx", "wa"), routes(d)) for d in range(count - 1, 0, -1)}
    return [came[d] for d in range(1, count)]


def total(terms):
    while len(terms) > 1:
        terms = [first + second for first, second in zip(terms[::2], terms[1::2])]
    return terms[0]


def rounded(value):
    return lax.reduce_precision(value, 8, 7)


def in_order(came, me):
    count = came.shape[0]
    rest = came.shape[1:]
    bit = 1
    while bit < count:
        split = came.reshape((count // (2 * bit), 2, bit) + rest)
        came = jnp.where((me & bit) != 0, split[:, ::-1], split).reshape((count,) + rest)
        bit *= 2
    return came


def make(mesh):
    count_x = mesh.shape["gx"]
    count_y = mesh.shape["gy"]

    def on_device(field, active_rows, kern, target):
        tile_row = lax.axis_index("gx")
        waves, polars = field.shape[0], field.shape[1]
        tiles = field.shape[4]
        rows_dev = field.shape[5]
        side = field.shape[6]
        focus = kern.shape[3]
        shape = (waves, polars, focus, 2 * focus)
        share, near_field, near_kern, counts = call(
            share_kernel,
            [
                jax.ShapeDtypeStruct(shape, jnp.bfloat16),
                jax.ShapeDtypeStruct(field.shape[:3] + field.shape[4:], field.dtype),
                jax.ShapeDtypeStruct(kern.shape, kern.dtype),
                jax.ShapeDtypeStruct((tiles, 8, side), jnp.int32),
            ],
            [
                pltpu.SMEM(active_rows.shape, jnp.int32),
                pltpu.VMEM((waves, 2 * side, polars * 2 * focus), jnp.bfloat16),
                pltpu.SemaphoreType.DMA((2 * waves + 1,)),
            ],
            [
                pltpu.with_memory_space_constraint(operand, pltpu.HBM)
                for operand in (active_rows, field, kern)
            ],
            [pltpu.HBM] * 3,
        )
        shares = [share] + partners(lambda d: share, "gy", count_y)
        share = total([term.astype(jnp.float32) for term in shares]).astype(jnp.bfloat16)
        strip_shape = (waves, polars, tiles, rows_dev, side)
        own_kern, both_kern, strip_kern, own_strip, *strips = call(
            strip_kernel,
            [
                jax.ShapeDtypeStruct((waves, 2 * side, 2 * focus), kern.dtype),
                jax.ShapeDtypeStruct((waves, tiles, 2 * focus, 2 * side), kern.dtype),
                jax.ShapeDtypeStruct((waves, tiles, 2 * focus, side), kern.dtype),
            ]
            + [jax.ShapeDtypeStruct(strip_shape, field.dtype)] * count_y,
            [],
            (near_field, near_kern, counts),
            [pltpu.VMEM] * 3,
        )
        strips = partners(lambda d: strips[d - 1], "gy", count_y)
        shares = [share] + partners(lambda d: share, "gx", count_x)
        shares = shares[::-1]
        shape = (tiles, rows_dev, side)
        scale = tiles * side / focus
        powers, sides, crossed = call(
            functools.partial(crossed_kernel, scale, count_y),
            [
                jax.ShapeDtypeStruct((waves, focus, 2 * focus), jnp.float32),
                jax.ShapeDtypeStruct((waves, polars * rows_dev, 4 * focus), jnp.bfloat16),
                jax.ShapeDtypeStruct(shape, jnp.bfloat16),
            ],
            [pltpu.VMEM((waves, 2 * side, polars * 2 * focus), jnp.float32)]
            + [pltpu.VMEM((tiles, side, side), jnp.float32)] * 2,
            (own_kern, strip_kern, target, own_strip, *strips, *shares),
            [pltpu.VMEM] * (3 + count_x + count_y),
        )
        (gradient,) = call(
            functools.partial(straight_kernel, scale),
            [jax.ShapeDtypeStruct(shape, jnp.float32)],
            [],
            (near_field, counts, both_kern, sides),
            [pltpu.VMEM] * 4,
        )
        both = crossed.astype(jnp.float32) + lax.ppermute(crossed, "wa", pairs(2, 1)).astype(
            jnp.float32
        )
        narrow = both.astype(jnp.bfloat16)
        came = [narrow[0]] + last_core_partners(lambda d: narrow[d], mesh)
        came = jnp.where(lax.axis_index("wa") == mesh.shape["wa"] - 1, jnp.stack(came), 0)
        own = rounded(gradient + came.astype(jnp.float32))
        other = lax.ppermute(own.astype(jnp.bfloat16), "wa", pairs(2, 1))
        design_grad = in_order(0.5 * (own + other.astype(jnp.float32)), tile_row)
        intensity = powers[:, :, :focus] + powers[:, :, focus:]
        return (design_grad[None], intensity)

    return on_device


def solution(mesh):
    placed = (
        P("wa", "cand", None, "gx", None, "gy", None),
        P("gx", None),
        P("wa", None, None, None, None),
        P("wa", None, None),
    )
    return jax.shard_map(
        make(mesh),
        mesh=mesh,
        in_specs=placed,
        out_specs=(P("gx", "cand", "gy", None), P("wa", "cand", None)),
        check_vma=False,
    )
```

```python
import functools

import jax
import jax.numpy as jnp
from jax import lax
from jax.experimental import pallas as pl
from jax.experimental.pallas import tpu as pltpu
from jax.sharding import PartitionSpec as P

VMEM = 16 * 2**20


def two_terms(value):
    high = value.astype(jnp.bfloat16)
    return high, (value - high.astype(jnp.float32)).astype(jnp.bfloat16)


def dot(first, second, over):
    return lax.dot_general(
        first, second, ((over[:1], over[1:]), ((), ())), preferred_element_type=jnp.float32
    )


def swapped(value, focus, left, right):
    lane = lax.broadcasted_iota(jnp.int32, value.shape, 1)
    sign = jnp.where(lane < focus, jnp.float32(left), jnp.float32(right))
    return pltpu.roll(value, focus, 1) * sign


def tile_kern(kern, wave, tile):
    real, imag = kern[wave, 0, tile], kern[wave, 1, tile]
    return jnp.concatenate([real, imag], axis=0), jnp.concatenate([-imag, real], axis=0)


def in_block(shape, block, width):
    lane = lax.broadcasted_iota(jnp.int32, shape, len(shape) - 1)
    return (lane >= block * width) & (lane < (block + 1) * width)


def side_by_side(first, second, block, blocks):
    width = first.shape[-1] // blocks
    first, second = first.astype(jnp.float32), second.astype(jnp.float32)
    beside = in_block(first.shape, lax.rem(block + 1, blocks), width)
    moved = jnp.where(beside, pltpu.roll(second, width, first.ndim - 1), 0.0)
    return jnp.where(in_block(first.shape, block, width), first, moved).astype(jnp.bfloat16)


def over_tiles(tiles, body, init):
    return lax.fori_loop(0, tiles, body, init, unroll=tiles <= 8)


def live_rows(count, shape):
    height = shape[-2]
    row = lax.axis_index("gy") * height + lax.broadcasted_iota(jnp.int32, shape, len(shape) - 2)
    return row < count


def share_kernel(rows_far, field_far, kern_far, share, field, kern, counts, rows, spread, arrived):
    waves, polars, _, tiles, height, side = field.shape
    focus = kern.shape[3]
    copies = [pltpu.make_async_copy(rows_far, rows, arrived.at[2 * waves])]
    for wave in range(waves):
        copies += [
            pltpu.make_async_copy(kern_far.at[wave], kern.at[wave], arrived.at[2 * wave]),
            pltpu.make_async_copy(
                field_far.at[wave, :, :, 0], field.at[wave], arrived.at[2 * wave + 1]
            ),
        ]
    for copy in copies:
        copy.start()
    tile_row = lax.axis_index("gx")
    first = pl.multiple_of(lax.axis_index("gy") * height, height)
    spread[...] = jnp.zeros_like(spread)
    copies[0].wait()
    inner = []
    for wave in range(waves):
        copies[2 * wave + 1].wait()
        copies[2 * wave + 2].wait()

        def add_tile(tile, value):
            live = live_rows(rows[0, tile], (polars, height, side))
            planes = [
                jnp.where(live, field[wave, :, part, tile], jnp.zeros((), field.dtype))
                for part in range(2)
            ]
            planes = [plane.reshape(polars * height, side) for plane in planes]
            return value + dot(
                jnp.concatenate(planes, axis=1),
                jnp.concatenate(tile_kern(kern, wave, tile), axis=1),
                (1, 1),
            )

        zero = jnp.zeros((polars * height, 2 * focus), jnp.float32)
        inner.append(over_tiles(tiles, add_tile, zero))
    for wave in range(waves):
        for polar in range(polars):
            lanes = pl.ds(polar * 2 * focus, 2 * focus)
            terms = two_terms(inner[wave][polar * height : (polar + 1) * height])
            for index, term in enumerate(terms):
                spread[wave, pl.ds(index * side + first, height), lanes] = term
        own = tile_kern(kern, wave, tile_row)[0]
        both = dot(jnp.concatenate([own, own], axis=1), spread[wave], (1, 0))
        for polar in range(polars):
            lanes = slice(polar * 2 * focus, (polar + 1) * 2 * focus)
            straight, crossed = both[:focus, lanes], both[focus:, lanes]
            share[wave, polar] = (straight + swapped(crossed, focus, -1, 1)).astype(share.dtype)

    def put_count(tile, carry):
        counts[tile] = jnp.full(counts.shape[1:], rows[0, tile], jnp.int32)
        return carry

    over_tiles(tiles, put_count, 0)


def strip_kernel(field, kern, counts, own_kern, both_kern, strip_kern, *strips):
    waves, polars, _, tiles, height, side = field.shape
    blocks = side // height
    block = lax.axis_index("gy")
    tile_row = lax.axis_index("gx")
    for wave in range(waves):
        for part in range(2):
            turned = kern[wave, part, tile_row].astype(jnp.float32).T.astype(kern.dtype)
            own_kern[wave, pl.ds(part * side, side)] = jnp.concatenate([turned, turned], axis=1)

    def one_tile(tile, carry):
        live = live_rows(counts[tile, :1], (height, side))
        for wave in range(waves):
            parts = tile_kern(kern, wave, tile)
            both_kern[wave, tile] = jnp.concatenate(parts, axis=1)
            strip_kern[wave, tile] = side_by_side(*parts, block, blocks)
            for polar in range(polars):
                for distance, strip in enumerate(strips):
                    both = side_by_side(
                        field[wave, polar, 0, tile],
                        field[wave, polar, 1, tile],
                        block ^ distance,
                        blocks,
                    )
                    strip[wave, polar, tile] = jnp.where(live, both, jnp.zeros((), both.dtype))
        return carry

    over_tiles(tiles, one_tile, 0)


def twice(value):
    return jnp.concatenate([value, value], axis=0)


def crossed_kernel(scale, blocks, own_kern, strip_kern, target, *refs):
    strips, refs = refs[:blocks], refs[blocks:]
    shares, (powers, sides, crossed, rowside, whole, turned) = refs[:-6], refs[-6:]
    waves, polars, tiles, height, side = strips[0].shape
    focus = target.shape[1]
    block = lax.axis_index("gy")
    for wave in range(waves):
        focal = [
            total([share[wave, polar].astype(jnp.float32) for share in shares])
            for polar in range(polars)
        ]
        power = sum(value * value for value in focal)
        powers[wave] = power
        power = power + pltpu.roll(power, focus, 1)
        goal = target[wave]
        excess = power - jnp.concatenate([goal, goal], axis=1)
        source = jnp.concatenate([excess * value for value in focal], axis=1)
        terms = jnp.concatenate(two_terms(source), axis=0)
        rowside[wave] = dot(own_kern[wave], terms, (1, 0))
    near = []
    for wave in range(waves):
        near.append([])
        for distance in range(blocks):
            first = pl.multiple_of((block ^ distance) * height, height)
            parts = []
            for polar in range(polars):
                lanes = pl.ds(polar * 2 * focus, 2 * focus)
                straight = rowside[wave, pl.ds(first, height), lanes]
                across = rowside[wave, pl.ds(side + first, height), lanes]
                parts.append(straight + swapped(across, focus, 1, -1))
            terms = two_terms(jnp.concatenate(parts, axis=0))
            near[wave].append(jnp.concatenate(terms, axis=1))
        sides[wave] = near[wave][0]

    def add_tile(distance, carry):
        tile = lax.axis_index("gx") ^ distance
        for index, strip in enumerate(strips):
            value = jnp.zeros((height, side), jnp.float32)
            for wave in range(waves):
                back = dot(near[wave][index], twice(strip_kern[wave, tile]), (1, 0))
                back = back.reshape(polars, height, side)
                for polar in range(polars):
                    value += back[polar] * strip[wave, polar, tile].astype(jnp.float32)
            first = pl.multiple_of((block ^ index) * height, height)
            whole[distance, pl.ds(first, height)] = (
                value + pltpu.roll(value, side - height, 1)
            ) * scale
        turned[distance] = whole[distance].T
        own = turned[distance, pl.ds(pl.multiple_of(block * height, height), height)]
        crossed[distance] = own.astype(crossed.dtype)
        return carry

    over_tiles(tiles, add_tile, 0)


def straight_kernel(scale, field, counts, both_kern, sides, gradient):
    waves, polars, _, tiles, height, side = field.shape

    def add_tile(distance, carry):
        tile = lax.axis_index("gx") ^ distance
        term = jnp.zeros((height, side), jnp.float32)
        for wave in range(waves):
            back = dot(sides[wave], twice(both_kern[wave, tile]), (1, 0))
            back = back.reshape(polars, height, 2 * side)
            for polar in range(polars):
                for part in range(2):
                    plane = field[wave, polar, part, tile].astype(jnp.float32)
                    term += back[polar, :, part * side : (part + 1) * side] * plane
        live = live_rows(counts[tile, :1], (height, side))
        gradient[distance] = jnp.where(live, term * scale, 0.0)
        return carry

    over_tiles(tiles, add_tile, 0)


def call(kernel, out_shape, scratch, args, spaces):
    return pl.pallas_call(
        kernel,
        out_shape=out_shape,
        in_specs=[pl.BlockSpec(memory_space=space) for space in spaces],
        out_specs=[pl.BlockSpec(memory_space=pltpu.VMEM)] * len(out_shape),
        scratch_shapes=scratch,
        compiler_params=pltpu.CompilerParams(vmem_limit_bytes=VMEM),
    )(*args)


def pairs(count, distance):
    return [(device, device ^ distance) for device in range(count)]


def partners(value, axis, count):
    came = {d: lax.ppermute(value(d), axis, pairs(count, d)) for d in range(count - 1, 0, -1)}
    return [came[d] for d in range(1, count)]


def crosswise(value, mesh):
    count, cores = mesh.shape["gx"], mesh.shape["wa"]

    def routes(distance):
        return [
            (device * cores + core, (device ^ distance) * cores + cores - 1 - core)
            for device in range(count)
            for core in range(cores)
        ]

    came = {d: lax.ppermute(value(d), ("gx", "wa"), routes(d)) for d in range(count - 1, 0, -1)}
    return [came[d] for d in range(1, count)]


def total(terms):
    while len(terms) > 1:
        terms = [first + second for first, second in zip(terms[::2], terms[1::2])]
    return terms[0]


def rounded(value):
    return lax.reduce_precision(value, 8, 7)


def in_order(came, me):
    count = came.shape[0]
    rest = came.shape[1:]
    bit = 1
    while bit < count:
        split = came.reshape((count // (2 * bit), 2, bit) + rest)
        came = jnp.where((me & bit) != 0, split[:, ::-1], split).reshape((count,) + rest)
        bit *= 2
    return came


def make(mesh):
    count_x = mesh.shape["gx"]
    count_y = mesh.shape["gy"]

    def on_device(field, active_rows, kern, target):
        tile_row = lax.axis_index("gx")
        waves, polars = field.shape[0], field.shape[1]
        tiles = field.shape[4]
        rows_dev = field.shape[5]
        side = field.shape[6]
        focus = kern.shape[3]
        shape = (waves, polars, focus, 2 * focus)
        share, near_field, near_kern, counts = call(
            share_kernel,
            [
                jax.ShapeDtypeStruct(shape, jnp.bfloat16),
                jax.ShapeDtypeStruct(field.shape[:3] + field.shape[4:], field.dtype),
                jax.ShapeDtypeStruct(kern.shape, kern.dtype),
                jax.ShapeDtypeStruct((tiles, 8, side), jnp.int32),
            ],
            [
                pltpu.SMEM(active_rows.shape, jnp.int32),
                pltpu.VMEM((waves, 2 * side, polars * 2 * focus), jnp.bfloat16),
                pltpu.SemaphoreType.DMA((2 * waves + 1,)),
            ],
            [
                pltpu.with_memory_space_constraint(operand, pltpu.HBM)
                for operand in (active_rows, field, kern)
            ],
            [pltpu.HBM] * 3,
        )
        shares = [share] + partners(lambda d: share, "gy", count_y)
        share = total([term.astype(jnp.float32) for term in shares]).astype(jnp.bfloat16)
        strip_shape = (waves, polars, tiles, rows_dev, side)
        own_kern, both_kern, strip_kern, own_strip, *strips = call(
            strip_kernel,
            [
                jax.ShapeDtypeStruct((waves, 2 * side, 2 * focus), kern.dtype),
                jax.ShapeDtypeStruct((waves, tiles, 2 * focus, 2 * side), kern.dtype),
                jax.ShapeDtypeStruct((waves, tiles, 2 * focus, side), kern.dtype),
            ]
            + [jax.ShapeDtypeStruct(strip_shape, field.dtype)] * count_y,
            [],
            (near_field, near_kern, counts),
            [pltpu.VMEM] * 3,
        )
        strips = partners(lambda d: strips[d - 1], "gy", count_y)
        shares = [share] + partners(lambda d: share, "gx", count_x)
        shares = shares[::-1]
        shape = (tiles, rows_dev, side)
        scale = tiles * side / focus
        powers, sides, crossed = call(
            functools.partial(crossed_kernel, scale, count_y),
            [
                jax.ShapeDtypeStruct((waves, focus, 2 * focus), jnp.float32),
                jax.ShapeDtypeStruct((waves, polars * rows_dev, 4 * focus), jnp.bfloat16),
                jax.ShapeDtypeStruct(shape, jnp.bfloat16),
            ],
            [pltpu.VMEM((waves, 2 * side, polars * 2 * focus), jnp.float32)]
            + [pltpu.VMEM((tiles, side, side), jnp.float32)] * 2,
            (own_kern, strip_kern, target, own_strip, *strips, *shares),
            [pltpu.VMEM] * (3 + count_x + count_y),
        )
        (gradient,) = call(
            functools.partial(straight_kernel, scale),
            [jax.ShapeDtypeStruct(shape, jnp.float32)],
            [],
            (near_field, counts, both_kern, sides),
            [pltpu.VMEM] * 4,
        )
        came = [crossed[0]] + crosswise(lambda d: crossed[d], mesh)
        own = rounded(gradient + jnp.stack(came).astype(jnp.float32))
        other = lax.ppermute(own.astype(jnp.bfloat16), "wa", pairs(2, 1))
        design_grad = in_order(0.5 * (own + other.astype(jnp.float32)), tile_row)
        intensity = powers[:, :, :focus] + powers[:, :, focus:]
        return (design_grad[None], intensity)

    return on_device


def solution(mesh):
    placed = (
        P("wa", "cand", None, "gx", None, "gy", None),
        P("gx", None),
        P("wa", None, None, None, None),
        P("wa", None, None),
    )
    return jax.shard_map(
        make(mesh),
        mesh=mesh,
        in_specs=placed,
        out_specs=(P("gx", "cand", "gy", None), P("wa", "cand", None)),
        check_vma=False,
    )
```

```python
import functools

import jax
import jax.numpy as jnp
from jax import lax
from jax.experimental import pallas as pl
from jax.experimental.pallas import tpu as pltpu
from jax.sharding import PartitionSpec as P

VMEM = 16 * 2**20


def two_terms(value):
    high = value.astype(jnp.bfloat16)
    return high, (value - high.astype(jnp.float32)).astype(jnp.bfloat16)


def dot(first, second, over):
    return lax.dot_general(
        first, second, ((over[:1], over[1:]), ((), ())), preferred_element_type=jnp.float32
    )


def swapped(value, focus, left, right):
    lane = lax.broadcasted_iota(jnp.int32, value.shape, 1)
    sign = jnp.where(lane < focus, jnp.float32(left), jnp.float32(right))
    return pltpu.roll(value, focus, 1) * sign


def tile_kern(kern, wave, tile):
    real, imag = kern[wave, 0, tile], kern[wave, 1, tile]
    return jnp.concatenate([real, imag], axis=0), jnp.concatenate([-imag, real], axis=0)


def in_block(shape, block, width):
    lane = lax.broadcasted_iota(jnp.int32, shape, len(shape) - 1)
    return (lane >= block * width) & (lane < (block + 1) * width)


def side_by_side(first, second, block, blocks):
    width = first.shape[-1] // blocks
    first, second = first.astype(jnp.float32), second.astype(jnp.float32)
    beside = in_block(first.shape, lax.rem(block + 1, blocks), width)
    moved = jnp.where(beside, pltpu.roll(second, width, first.ndim - 1), 0.0)
    return jnp.where(in_block(first.shape, block, width), first, moved).astype(jnp.bfloat16)


def over_tiles(tiles, body, init):
    return lax.fori_loop(0, tiles, body, init, unroll=tiles <= 8)


def live_rows(count, shape):
    height = shape[-2]
    row = lax.axis_index("gy") * height + lax.broadcasted_iota(jnp.int32, shape, len(shape) - 2)
    return row < count


def share_kernel(rows_far, field_far, kern_far, share, field, kern, counts, rows, spread, arrived):
    waves, polars, _, tiles, height, side = field.shape
    focus = kern.shape[3]
    copies = [pltpu.make_async_copy(rows_far, rows, arrived.at[2 * waves])]
    for wave in range(waves):
        copies += [
            pltpu.make_async_copy(kern_far.at[wave], kern.at[wave], arrived.at[2 * wave]),
            pltpu.make_async_copy(
                field_far.at[wave, :, :, 0], field.at[wave], arrived.at[2 * wave + 1]
            ),
        ]
    for copy in copies:
        copy.start()
    tile_row = lax.axis_index("gx")
    first = pl.multiple_of(lax.axis_index("gy") * height, height)
    spread[...] = jnp.zeros_like(spread)
    copies[0].wait()
    inner = []
    for wave in range(waves):
        copies[2 * wave + 1].wait()
        copies[2 * wave + 2].wait()

        def add_tile(tile, value):
            live = live_rows(rows[0, tile], (polars, height, side))
            planes = [
                jnp.where(live, field[wave, :, part, tile], jnp.zeros((), field.dtype))
                for part in range(2)
            ]
            planes = [plane.reshape(polars * height, side) for plane in planes]
            return value + dot(
                jnp.concatenate(planes, axis=1),
                jnp.concatenate(tile_kern(kern, wave, tile), axis=1),
                (1, 1),
            )

        zero = jnp.zeros((polars * height, 2 * focus), jnp.float32)
        inner.append(over_tiles(tiles, add_tile, zero))
    for wave in range(waves):
        for polar in range(polars):
            lanes = pl.ds(polar * 2 * focus, 2 * focus)
            terms = two_terms(inner[wave][polar * height : (polar + 1) * height])
            for index, term in enumerate(terms):
                spread[wave, pl.ds(index * side + first, height), lanes] = term
        own = tile_kern(kern, wave, tile_row)[0]
        both = dot(jnp.concatenate([own, own], axis=1), spread[wave], (1, 0))
        for polar in range(polars):
            lanes = slice(polar * 2 * focus, (polar + 1) * 2 * focus)
            straight, crossed = both[:focus, lanes], both[focus:, lanes]
            share[wave, polar] = (straight + swapped(crossed, focus, -1, 1)).astype(share.dtype)

    def put_count(tile, carry):
        counts[tile] = jnp.full(counts.shape[1:], rows[0, tile], jnp.int32)
        return carry

    over_tiles(tiles, put_count, 0)


def strip_kernel(field, kern, counts, own_kern, both_kern, strip_kern, *strips):
    waves, polars, _, tiles, height, side = field.shape
    blocks = side // height
    block = lax.axis_index("gy")
    tile_row = lax.axis_index("gx")
    for wave in range(waves):
        for part in range(2):
            turned = kern[wave, part, tile_row].astype(jnp.float32).T.astype(kern.dtype)
            own_kern[wave, pl.ds(part * side, side)] = jnp.concatenate([turned, turned], axis=1)

    def one_tile(tile, carry):
        live = live_rows(counts[tile, :1], (height, side))
        for wave in range(waves):
            parts = tile_kern(kern, wave, tile)
            both_kern[wave, tile] = jnp.concatenate(parts, axis=1)
            strip_kern[wave, tile] = side_by_side(*parts, block, blocks)
            for polar in range(polars):
                for distance, strip in enumerate(strips):
                    both = side_by_side(
                        field[wave, polar, 0, tile],
                        field[wave, polar, 1, tile],
                        block ^ distance,
                        blocks,
                    )
                    strip[wave, polar, tile] = jnp.where(live, both, jnp.zeros((), both.dtype))
        return carry

    over_tiles(tiles, one_tile, 0)


def twice(value):
    return jnp.concatenate([value, value], axis=0)


def crossed_kernel(scale, blocks, own_kern, strip_kern, target, *refs):
    strips, refs = refs[:blocks], refs[blocks:]
    shares, (powers, sides, crossed, rowside, whole, turned) = refs[:-6], refs[-6:]
    waves, polars, tiles, height, side = strips[0].shape
    focus = target.shape[1]
    block = lax.axis_index("gy")
    for wave in range(waves):
        focal = [
            total([share[wave, polar].astype(jnp.float32) for share in shares])
            for polar in range(polars)
        ]
        power = sum(value * value for value in focal)
        powers[wave] = power
        power = power + pltpu.roll(power, focus, 1)
        goal = target[wave]
        excess = power - jnp.concatenate([goal, goal], axis=1)
        source = jnp.concatenate([excess * value for value in focal], axis=1)
        terms = jnp.concatenate(two_terms(source), axis=0)
        rowside[wave] = dot(own_kern[wave], terms, (1, 0))
    near = []
    for wave in range(waves):
        near.append([])
        for distance in range(blocks):
            first = pl.multiple_of((block ^ distance) * height, height)
            parts = []
            for polar in range(polars):
                lanes = pl.ds(polar * 2 * focus, 2 * focus)
                straight = rowside[wave, pl.ds(first, height), lanes]
                across = rowside[wave, pl.ds(side + first, height), lanes]
                parts.append(straight + swapped(across, focus, 1, -1))
            terms = two_terms(jnp.concatenate(parts, axis=0))
            near[wave].append(jnp.concatenate(terms, axis=1))
        sides[wave] = near[wave][0]

    def add_tile(distance, carry):
        tile = lax.axis_index("gx") ^ distance
        for index, strip in enumerate(strips):
            value = jnp.zeros((height, side), jnp.float32)
            for wave in range(waves):
                back = dot(near[wave][index], twice(strip_kern[wave, tile]), (1, 0))
                back = back.reshape(polars, height, side)
                for polar in range(polars):
                    value += back[polar] * strip[wave, polar, tile].astype(jnp.float32)
            first = pl.multiple_of((block ^ index) * height, height)
            whole[distance, pl.ds(first, height)] = (
                value + pltpu.roll(value, side - height, 1)
            ) * scale
        turned[distance] = whole[distance].T
        own = turned[distance, pl.ds(pl.multiple_of(block * height, height), height)]
        crossed[distance] = own.astype(crossed.dtype)
        return carry

    over_tiles(tiles, add_tile, 0)


def straight_kernel(scale, field, counts, both_kern, sides, gradient):
    waves, polars, _, tiles, height, side = field.shape

    def add_tile(distance, carry):
        tile = lax.axis_index("gx") ^ distance
        term = jnp.zeros((height, side), jnp.float32)
        for wave in range(waves):
            back = dot(sides[wave], twice(both_kern[wave, tile]), (1, 0))
            back = back.reshape(polars, height, 2 * side)
            for polar in range(polars):
                for part in range(2):
                    plane = field[wave, polar, part, tile].astype(jnp.float32)
                    term += back[polar, :, part * side : (part + 1) * side] * plane
        live = live_rows(counts[tile, :1], (height, side))
        gradient[distance] = jnp.where(live, term * scale, 0.0)
        return carry

    over_tiles(tiles, add_tile, 0)


def call(kernel, out_shape, scratch, args, spaces):
    return pl.pallas_call(
        kernel,
        out_shape=out_shape,
        in_specs=[pl.BlockSpec(memory_space=space) for space in spaces],
        out_specs=[pl.BlockSpec(memory_space=pltpu.VMEM)] * len(out_shape),
        scratch_shapes=scratch,
        compiler_params=pltpu.CompilerParams(vmem_limit_bytes=VMEM),
    )(*args)


def pairs(count, distance):
    return [(device, device ^ distance) for device in range(count)]


def partners(value, axis, count):
    came = {d: lax.ppermute(value(d), axis, pairs(count, d)) for d in range(count - 1, 0, -1)}
    return [came[d] for d in range(1, count)]


def crosswise(value, mesh):
    count, cores = mesh.shape["gx"], mesh.shape["wa"]

    def routes(distance):
        far = 2 * distance > count
        return [
            (
                device * cores + core,
                (device ^ distance) * cores + (cores - 1 - core if far else core),
            )
            for device in range(count)
            for core in range(cores)
        ]

    came = {d: lax.ppermute(value(d), ("gx", "wa"), routes(d)) for d in range(count - 1, 0, -1)}
    return [came[d] for d in range(1, count)]


def total(terms):
    while len(terms) > 1:
        terms = [first + second for first, second in zip(terms[::2], terms[1::2])]
    return terms[0]


def rounded(value):
    return lax.reduce_precision(value, 8, 7)


def in_order(came, me):
    count = came.shape[0]
    rest = came.shape[1:]
    bit = 1
    while bit < count:
        split = came.reshape((count // (2 * bit), 2, bit) + rest)
        came = jnp.where((me & bit) != 0, split[:, ::-1], split).reshape((count,) + rest)
        bit *= 2
    return came


def make(mesh):
    count_x = mesh.shape["gx"]
    count_y = mesh.shape["gy"]

    def on_device(field, active_rows, kern, target):
        tile_row = lax.axis_index("gx")
        waves, polars = field.shape[0], field.shape[1]
        tiles = field.shape[4]
        rows_dev = field.shape[5]
        side = field.shape[6]
        focus = kern.shape[3]
        shape = (waves, polars, focus, 2 * focus)
        share, near_field, near_kern, counts = call(
            share_kernel,
            [
                jax.ShapeDtypeStruct(shape, jnp.bfloat16),
                jax.ShapeDtypeStruct(field.shape[:3] + field.shape[4:], field.dtype),
                jax.ShapeDtypeStruct(kern.shape, kern.dtype),
                jax.ShapeDtypeStruct((tiles, 8, side), jnp.int32),
            ],
            [
                pltpu.SMEM(active_rows.shape, jnp.int32),
                pltpu.VMEM((waves, 2 * side, polars * 2 * focus), jnp.bfloat16),
                pltpu.SemaphoreType.DMA((2 * waves + 1,)),
            ],
            [
                pltpu.with_memory_space_constraint(operand, pltpu.HBM)
                for operand in (active_rows, field, kern)
            ],
            [pltpu.HBM] * 3,
        )
        shares = [share] + partners(lambda d: share, "gy", count_y)
        share = total([term.astype(jnp.float32) for term in shares]).astype(jnp.bfloat16)
        strip_shape = (waves, polars, tiles, rows_dev, side)
        own_kern, both_kern, strip_kern, own_strip, *strips = call(
            strip_kernel,
            [
                jax.ShapeDtypeStruct((waves, 2 * side, 2 * focus), kern.dtype),
                jax.ShapeDtypeStruct((waves, tiles, 2 * focus, 2 * side), kern.dtype),
                jax.ShapeDtypeStruct((waves, tiles, 2 * focus, side), kern.dtype),
            ]
            + [jax.ShapeDtypeStruct(strip_shape, field.dtype)] * count_y,
            [],
            (near_field, near_kern, counts),
            [pltpu.VMEM] * 3,
        )
        strips = partners(lambda d: strips[d - 1], "gy", count_y)
        shares = [share] + partners(lambda d: share, "gx", count_x)
        shares = shares[::-1]
        shape = (tiles, rows_dev, side)
        scale = tiles * side / focus
        powers, sides, crossed = call(
            functools.partial(crossed_kernel, scale, count_y),
            [
                jax.ShapeDtypeStruct((waves, focus, 2 * focus), jnp.float32),
                jax.ShapeDtypeStruct((waves, polars * rows_dev, 4 * focus), jnp.bfloat16),
                jax.ShapeDtypeStruct(shape, jnp.bfloat16),
            ],
            [pltpu.VMEM((waves, 2 * side, polars * 2 * focus), jnp.float32)]
            + [pltpu.VMEM((tiles, side, side), jnp.float32)] * 2,
            (own_kern, strip_kern, target, own_strip, *strips, *shares),
            [pltpu.VMEM] * (3 + count_x + count_y),
        )
        (gradient,) = call(
            functools.partial(straight_kernel, scale),
            [jax.ShapeDtypeStruct(shape, jnp.float32)],
            [],
            (near_field, counts, both_kern, sides),
            [pltpu.VMEM] * 4,
        )
        came = [crossed[0]] + crosswise(lambda d: crossed[d], mesh)
        own = rounded(gradient + jnp.stack(came).astype(jnp.float32))
        other = lax.ppermute(own.astype(jnp.bfloat16), "wa", pairs(2, 1))
        design_grad = in_order(0.5 * (own + other.astype(jnp.float32)), tile_row)
        intensity = powers[:, :, :focus] + powers[:, :, focus:]
        return (design_grad[None], intensity)

    return on_device


def solution(mesh):
    placed = (
        P("wa", "cand", None, "gx", None, "gy", None),
        P("gx", None),
        P("wa", None, None, None, None),
        P("wa", None, None),
    )
    return jax.shard_map(
        make(mesh),
        mesh=mesh,
        in_specs=placed,
        out_specs=(P("gx", "cand", "gy", None), P("wa", "cand", None)),
        check_vma=False,
    )
```

```python
import functools

import jax
import jax.numpy as jnp
from jax import lax
from jax.experimental import pallas as pl
from jax.experimental.pallas import tpu as pltpu
from jax.sharding import PartitionSpec as P

VMEM = 16 * 2**20


def two_terms(value):
    high = value.astype(jnp.bfloat16)
    return high, (value - high.astype(jnp.float32)).astype(jnp.bfloat16)


def dot(first, second, over):
    return lax.dot_general(
        first, second, ((over[:1], over[1:]), ((), ())), preferred_element_type=jnp.float32
    )


def swapped(value, focus, left, right):
    lane = lax.broadcasted_iota(jnp.int32, value.shape, 1)
    sign = jnp.where(lane < focus, jnp.float32(left), jnp.float32(right))
    return pltpu.roll(value, focus, 1) * sign


def tile_kern(kern, wave, tile):
    real, imag = kern[wave, 0, tile], kern[wave, 1, tile]
    return jnp.concatenate([real, imag], axis=0), jnp.concatenate([-imag, real], axis=0)


def in_block(shape, block, width):
    lane = lax.broadcasted_iota(jnp.int32, shape, len(shape) - 1)
    return (lane >= block * width) & (lane < (block + 1) * width)


def side_by_side(first, second, block, blocks):
    width = first.shape[-1] // blocks
    first, second = first.astype(jnp.float32), second.astype(jnp.float32)
    beside = in_block(first.shape, lax.rem(block + 1, blocks), width)
    moved = jnp.where(beside, pltpu.roll(second, width, first.ndim - 1), 0.0)
    return jnp.where(in_block(first.shape, block, width), first, moved).astype(jnp.bfloat16)


def over_tiles(tiles, body, init):
    return lax.fori_loop(0, tiles, body, init, unroll=tiles <= 8)


def live_rows(count, shape):
    height = shape[-2]
    row = lax.axis_index("gy") * height + lax.broadcasted_iota(jnp.int32, shape, len(shape) - 2)
    return row < count


def share_kernel(rows_far, field_far, kern_far, share, field, kern, counts, rows, spread, arrived):
    waves, polars, _, tiles, height, side = field.shape
    focus = kern.shape[3]
    copies = [pltpu.make_async_copy(rows_far, rows, arrived.at[2 * waves])]
    for wave in range(waves):
        copies += [
            pltpu.make_async_copy(kern_far.at[wave], kern.at[wave], arrived.at[2 * wave]),
            pltpu.make_async_copy(
                field_far.at[wave, :, :, 0], field.at[wave], arrived.at[2 * wave + 1]
            ),
        ]
    for copy in copies:
        copy.start()
    tile_row = lax.axis_index("gx")
    first = pl.multiple_of(lax.axis_index("gy") * height, height)
    spread[...] = jnp.zeros_like(spread)
    copies[0].wait()
    inner = []
    for wave in range(waves):
        copies[2 * wave + 1].wait()
        copies[2 * wave + 2].wait()

        def add_tile(tile, value):
            live = live_rows(rows[0, tile], (polars, height, side))
            planes = [
                jnp.where(live, field[wave, :, part, tile], jnp.zeros((), field.dtype))
                for part in range(2)
            ]
            planes = [plane.reshape(polars * height, side) for plane in planes]
            return value + dot(
                jnp.concatenate(planes, axis=1),
                jnp.concatenate(tile_kern(kern, wave, tile), axis=1),
                (1, 1),
            )

        zero = jnp.zeros((polars * height, 2 * focus), jnp.float32)
        inner.append(over_tiles(tiles, add_tile, zero))
    for wave in range(waves):
        for polar in range(polars):
            lanes = pl.ds(polar * 2 * focus, 2 * focus)
            terms = two_terms(inner[wave][polar * height : (polar + 1) * height])
            for index, term in enumerate(terms):
                spread[wave, pl.ds(index * side + first, height), lanes] = term
        own = tile_kern(kern, wave, tile_row)[0]
        both = dot(jnp.concatenate([own, own], axis=1), spread[wave], (1, 0))
        for polar in range(polars):
            lanes = slice(polar * 2 * focus, (polar + 1) * 2 * focus)
            straight, crossed = both[:focus, lanes], both[focus:, lanes]
            share[wave, polar] = (straight + swapped(crossed, focus, -1, 1)).astype(share.dtype)

    def put_count(tile, carry):
        counts[tile] = jnp.full(counts.shape[1:], rows[0, tile], jnp.int32)
        return carry

    over_tiles(tiles, put_count, 0)


def strip_kernel(field, kern, counts, own_kern, both_kern, strip_kern, *strips):
    waves, polars, _, tiles, height, side = field.shape
    blocks = side // height
    block = lax.axis_index("gy")
    tile_row = lax.axis_index("gx")
    for wave in range(waves):
        for part in range(2):
            turned = kern[wave, part, tile_row].astype(jnp.float32).T.astype(kern.dtype)
            own_kern[wave, pl.ds(part * side, side)] = jnp.concatenate([turned, turned], axis=1)

    def one_tile(tile, carry):
        live = live_rows(counts[tile, :1], (height, side))
        for wave in range(waves):
            parts = tile_kern(kern, wave, tile)
            both_kern[wave, tile] = jnp.concatenate(parts, axis=1)
            strip_kern[wave, tile] = side_by_side(*parts, block, blocks)
            for polar in range(polars):
                for distance, strip in enumerate(strips):
                    both = side_by_side(
                        field[wave, polar, 0, tile],
                        field[wave, polar, 1, tile],
                        block ^ distance,
                        blocks,
                    )
                    strip[wave, polar, tile] = jnp.where(live, both, jnp.zeros((), both.dtype))
        return carry

    over_tiles(tiles, one_tile, 0)


def twice(value):
    return jnp.concatenate([value, value], axis=0)


def crossed_kernel(scale, blocks, own_kern, strip_kern, target, *refs):
    strips, refs = refs[:blocks], refs[blocks:]
    shares, (powers, sides, crossed, rowside, whole, turned) = refs[:-6], refs[-6:]
    waves, polars, tiles, height, side = strips[0].shape
    focus = target.shape[1]
    block = lax.axis_index("gy")
    for wave in range(waves):
        focal = [
            total([share[wave, polar].astype(jnp.float32) for share in shares])
            for polar in range(polars)
        ]
        power = sum(value * value for value in focal)
        powers[wave] = power
        power = power + pltpu.roll(power, focus, 1)
        goal = target[wave]
        excess = power - jnp.concatenate([goal, goal], axis=1)
        source = jnp.concatenate([excess * value for value in focal], axis=1)
        terms = jnp.concatenate(two_terms(source), axis=0)
        rowside[wave] = dot(own_kern[wave], terms, (1, 0))
    near = []
    for wave in range(waves):
        near.append([])
        for distance in range(blocks):
            first = pl.multiple_of((block ^ distance) * height, height)
            parts = []
            for polar in range(polars):
                lanes = pl.ds(polar * 2 * focus, 2 * focus)
                straight = rowside[wave, pl.ds(first, height), lanes]
                across = rowside[wave, pl.ds(side + first, height), lanes]
                parts.append(straight + swapped(across, focus, 1, -1))
            terms = two_terms(jnp.concatenate(parts, axis=0))
            near[wave].append(jnp.concatenate(terms, axis=1))
        sides[wave] = near[wave][0]

    def add_tile(distance, carry):
        tile = lax.axis_index("gx") ^ distance
        for index, strip in enumerate(strips):
            value = jnp.zeros((height, side), jnp.float32)
            for wave in range(waves):
                back = dot(near[wave][index], twice(strip_kern[wave, tile]), (1, 0))
                back = back.reshape(polars, height, side)
                for polar in range(polars):
                    value += back[polar] * strip[wave, polar, tile].astype(jnp.float32)
            first = pl.multiple_of((block ^ index) * height, height)
            whole[distance, pl.ds(first, height)] = (
                value + pltpu.roll(value, side - height, 1)
            ) * scale
        turned[distance] = whole[distance].T
        own = turned[distance, pl.ds(pl.multiple_of(block * height, height), height)]
        crossed[distance] = own.astype(crossed.dtype)
        return carry

    over_tiles(tiles, add_tile, 0)


def straight_kernel(scale, field, counts, both_kern, sides, gradient):
    waves, polars, _, tiles, height, side = field.shape

    def add_tile(distance, carry):
        tile = lax.axis_index("gx") ^ distance
        term = jnp.zeros((height, side), jnp.float32)
        for wave in range(waves):
            back = dot(sides[wave], twice(both_kern[wave, tile]), (1, 0))
            back = back.reshape(polars, height, 2 * side)
            for polar in range(polars):
                for part in range(2):
                    plane = field[wave, polar, part, tile].astype(jnp.float32)
                    term += back[polar, :, part * side : (part + 1) * side] * plane
        live = live_rows(counts[tile, :1], (height, side))
        gradient[distance] = jnp.where(live, term * scale, 0.0)
        return carry

    over_tiles(tiles, add_tile, 0)


def call(kernel, out_shape, scratch, args, spaces):
    return pl.pallas_call(
        kernel,
        out_shape=out_shape,
        in_specs=[pl.BlockSpec(memory_space=space) for space in spaces],
        out_specs=[pl.BlockSpec(memory_space=pltpu.VMEM)] * len(out_shape),
        scratch_shapes=scratch,
        compiler_params=pltpu.CompilerParams(vmem_limit_bytes=VMEM),
    )(*args)


def pairs(count, distance):
    return [(device, device ^ distance) for device in range(count)]


def partners(value, axis, count):
    came = {d: lax.ppermute(value(d), axis, pairs(count, d)) for d in range(count - 1, 0, -1)}
    return [came[d] for d in range(1, count)]


def crosswise(value, mesh):
    count, cores = mesh.shape["gx"], mesh.shape["wa"]

    def routes(distance):
        odd = distance % 2 == 1
        return [
            (
                device * cores + core,
                (device ^ distance) * cores + (cores - 1 - core if odd else core),
            )
            for device in range(count)
            for core in range(cores)
        ]

    came = {d: lax.ppermute(value(d), ("gx", "wa"), routes(d)) for d in range(count - 1, 0, -1)}
    return [came[d] for d in range(1, count)]


def total(terms):
    while len(terms) > 1:
        terms = [first + second for first, second in zip(terms[::2], terms[1::2])]
    return terms[0]


def rounded(value):
    return lax.reduce_precision(value, 8, 7)


def in_order(came, me):
    count = came.shape[0]
    rest = came.shape[1:]
    bit = 1
    while bit < count:
        split = came.reshape((count // (2 * bit), 2, bit) + rest)
        came = jnp.where((me & bit) != 0, split[:, ::-1], split).reshape((count,) + rest)
        bit *= 2
    return came


def make(mesh):
    count_x = mesh.shape["gx"]
    count_y = mesh.shape["gy"]

    def on_device(field, active_rows, kern, target):
        tile_row = lax.axis_index("gx")
        waves, polars = field.shape[0], field.shape[1]
        tiles = field.shape[4]
        rows_dev = field.shape[5]
        side = field.shape[6]
        focus = kern.shape[3]
        shape = (waves, polars, focus, 2 * focus)
        share, near_field, near_kern, counts = call(
            share_kernel,
            [
                jax.ShapeDtypeStruct(shape, jnp.bfloat16),
                jax.ShapeDtypeStruct(field.shape[:3] + field.shape[4:], field.dtype),
                jax.ShapeDtypeStruct(kern.shape, kern.dtype),
                jax.ShapeDtypeStruct((tiles, 8, side), jnp.int32),
            ],
            [
                pltpu.SMEM(active_rows.shape, jnp.int32),
                pltpu.VMEM((waves, 2 * side, polars * 2 * focus), jnp.bfloat16),
                pltpu.SemaphoreType.DMA((2 * waves + 1,)),
            ],
            [
                pltpu.with_memory_space_constraint(operand, pltpu.HBM)
                for operand in (active_rows, field, kern)
            ],
            [pltpu.HBM] * 3,
        )
        shares = [share] + partners(lambda d: share, "gy", count_y)
        share = total([term.astype(jnp.float32) for term in shares]).astype(jnp.bfloat16)
        strip_shape = (waves, polars, tiles, rows_dev, side)
        own_kern, both_kern, strip_kern, own_strip, *strips = call(
            strip_kernel,
            [
                jax.ShapeDtypeStruct((waves, 2 * side, 2 * focus), kern.dtype),
                jax.ShapeDtypeStruct((waves, tiles, 2 * focus, 2 * side), kern.dtype),
                jax.ShapeDtypeStruct((waves, tiles, 2 * focus, side), kern.dtype),
            ]
            + [jax.ShapeDtypeStruct(strip_shape, field.dtype)] * count_y,
            [],
            (near_field, near_kern, counts),
            [pltpu.VMEM] * 3,
        )
        strips = partners(lambda d: strips[d - 1], "gy", count_y)
        shares = [share] + partners(lambda d: share, "gx", count_x)
        shares = shares[::-1]
        shape = (tiles, rows_dev, side)
        scale = tiles * side / focus
        powers, sides, crossed = call(
            functools.partial(crossed_kernel, scale, count_y),
            [
                jax.ShapeDtypeStruct((waves, focus, 2 * focus), jnp.float32),
                jax.ShapeDtypeStruct((waves, polars * rows_dev, 4 * focus), jnp.bfloat16),
                jax.ShapeDtypeStruct(shape, jnp.bfloat16),
            ],
            [pltpu.VMEM((waves, 2 * side, polars * 2 * focus), jnp.float32)]
            + [pltpu.VMEM((tiles, side, side), jnp.float32)] * 2,
            (own_kern, strip_kern, target, own_strip, *strips, *shares),
            [pltpu.VMEM] * (3 + count_x + count_y),
        )
        (gradient,) = call(
            functools.partial(straight_kernel, scale),
            [jax.ShapeDtypeStruct(shape, jnp.float32)],
            [],
            (near_field, counts, both_kern, sides),
            [pltpu.VMEM] * 4,
        )
        came = [crossed[0]] + crosswise(lambda d: crossed[d], mesh)
        own = rounded(gradient + jnp.stack(came).astype(jnp.float32))
        other = lax.ppermute(own.astype(jnp.bfloat16), "wa", pairs(2, 1))
        design_grad = in_order(0.5 * (own + other.astype(jnp.float32)), tile_row)
        intensity = powers[:, :, :focus] + powers[:, :, focus:]
        return (design_grad[None], intensity)

    return on_device


def solution(mesh):
    placed = (
        P("wa", "cand", None, "gx", None, "gy", None),
        P("gx", None),
        P("wa", None, None, None, None),
        P("wa", None, None),
    )
    return jax.shard_map(
        make(mesh),
        mesh=mesh,
        in_specs=placed,
        out_specs=(P("gx", "cand", "gy", None), P("wa", "cand", None)),
        check_vma=False,
    )
```

```python
import functools

import jax
import jax.numpy as jnp
from jax import lax
from jax.experimental import pallas as pl
from jax.experimental.pallas import tpu as pltpu
from jax.sharding import PartitionSpec as P

VMEM = 16 * 2**20


def two_terms(value):
    high = value.astype(jnp.bfloat16)
    return high, (value - high.astype(jnp.float32)).astype(jnp.bfloat16)


def dot(first, second, over):
    return lax.dot_general(
        first, second, ((over[:1], over[1:]), ((), ())), preferred_element_type=jnp.float32
    )


def swapped(value, focus, left, right):
    lane = lax.broadcasted_iota(jnp.int32, value.shape, 1)
    sign = jnp.where(lane < focus, jnp.float32(left), jnp.float32(right))
    return pltpu.roll(value, focus, 1) * sign


def tile_kern(kern, wave, tile):
    real, imag = kern[wave, 0, tile], kern[wave, 1, tile]
    return jnp.concatenate([real, imag], axis=0), jnp.concatenate([-imag, real], axis=0)


def in_block(shape, block, width):
    lane = lax.broadcasted_iota(jnp.int32, shape, len(shape) - 1)
    return (lane >= block * width) & (lane < (block + 1) * width)


def side_by_side(first, second, block, blocks):
    width = first.shape[-1] // blocks
    first, second = first.astype(jnp.float32), second.astype(jnp.float32)
    beside = in_block(first.shape, lax.rem(block + 1, blocks), width)
    moved = jnp.where(beside, pltpu.roll(second, width, first.ndim - 1), 0.0)
    return jnp.where(in_block(first.shape, block, width), first, moved).astype(jnp.bfloat16)


def over_tiles(tiles, body, init):
    return lax.fori_loop(0, tiles, body, init, unroll=tiles <= 8)


def live_rows(count, shape):
    height = shape[-2]
    row = lax.axis_index("gy") * height + lax.broadcasted_iota(jnp.int32, shape, len(shape) - 2)
    return row < count


def share_kernel(rows_far, field_far, kern_far, share, field, kern, counts, rows, spread, arrived):
    waves, polars, _, tiles, height, side = field.shape
    focus = kern.shape[3]
    copies = [pltpu.make_async_copy(rows_far, rows, arrived.at[2 * waves])]
    for wave in range(waves):
        copies += [
            pltpu.make_async_copy(kern_far.at[wave], kern.at[wave], arrived.at[2 * wave]),
            pltpu.make_async_copy(
                field_far.at[wave, :, :, 0], field.at[wave], arrived.at[2 * wave + 1]
            ),
        ]
    for copy in copies:
        copy.start()
    tile_row = lax.axis_index("gx")
    first = pl.multiple_of(lax.axis_index("gy") * height, height)
    spread[...] = jnp.zeros_like(spread)
    copies[0].wait()
    inner = []
    for wave in range(waves):
        copies[2 * wave + 1].wait()
        copies[2 * wave + 2].wait()

        def add_tile(tile, value):
            live = live_rows(rows[0, tile], (polars, height, side))
            planes = [
                jnp.where(live, field[wave, :, part, tile], jnp.zeros((), field.dtype))
                for part in range(2)
            ]
            planes = [plane.reshape(polars * height, side) for plane in planes]
            return value + dot(
                jnp.concatenate(planes, axis=1),
                jnp.concatenate(tile_kern(kern, wave, tile), axis=1),
                (1, 1),
            )

        zero = jnp.zeros((polars * height, 2 * focus), jnp.float32)
        inner.append(over_tiles(tiles, add_tile, zero))
    for wave in range(waves):
        for polar in range(polars):
            lanes = pl.ds(polar * 2 * focus, 2 * focus)
            terms = two_terms(inner[wave][polar * height : (polar + 1) * height])
            for index, term in enumerate(terms):
                spread[wave, pl.ds(index * side + first, height), lanes] = term
        own = tile_kern(kern, wave, tile_row)[0]
        both = dot(jnp.concatenate([own, own], axis=1), spread[wave], (1, 0))
        for polar in range(polars):
            lanes = slice(polar * 2 * focus, (polar + 1) * 2 * focus)
            straight, crossed = both[:focus, lanes], both[focus:, lanes]
            share[wave, polar] = (straight + swapped(crossed, focus, -1, 1)).astype(share.dtype)

    def put_count(tile, carry):
        counts[tile] = jnp.full(counts.shape[1:], rows[0, tile], jnp.int32)
        return carry

    over_tiles(tiles, put_count, 0)


def strip_kernel(field, kern, counts, own_kern, both_kern, strip_kern, *strips):
    waves, polars, _, tiles, height, side = field.shape
    blocks = side // height
    block = lax.axis_index("gy")
    tile_row = lax.axis_index("gx")
    for wave in range(waves):
        for part in range(2):
            turned = kern[wave, part, tile_row].astype(jnp.float32).T.astype(kern.dtype)
            own_kern[wave, pl.ds(part * side, side)] = jnp.concatenate([turned, turned], axis=1)

    def one_tile(tile, carry):
        live = live_rows(counts[tile, :1], (height, side))
        for wave in range(waves):
            parts = tile_kern(kern, wave, tile)
            both_kern[wave, tile] = jnp.concatenate(parts, axis=1)
            strip_kern[wave, tile] = side_by_side(*parts, block, blocks)
            for polar in range(polars):
                for distance, strip in enumerate(strips):
                    both = side_by_side(
                        field[wave, polar, 0, tile],
                        field[wave, polar, 1, tile],
                        block ^ distance,
                        blocks,
                    )
                    strip[wave, polar, tile] = jnp.where(live, both, jnp.zeros((), both.dtype))
        return carry

    over_tiles(tiles, one_tile, 0)


def twice(value):
    return jnp.concatenate([value, value], axis=0)


def crossed_kernel(scale, blocks, own_kern, strip_kern, target, *refs):
    strips, refs = refs[:blocks], refs[blocks:]
    shares, (powers, sides, crossed, rowside, whole, turned) = refs[:-6], refs[-6:]
    waves, polars, tiles, height, side = strips[0].shape
    focus = target.shape[1]
    block = lax.axis_index("gy")
    for wave in range(waves):
        focal = [
            total([share[wave, polar].astype(jnp.float32) for share in shares])
            for polar in range(polars)
        ]
        power = sum(value * value for value in focal)
        powers[wave] = power
        power = power + pltpu.roll(power, focus, 1)
        goal = target[wave]
        excess = power - jnp.concatenate([goal, goal], axis=1)
        source = jnp.concatenate([excess * value for value in focal], axis=1)
        terms = jnp.concatenate(two_terms(source), axis=0)
        rowside[wave] = dot(own_kern[wave], terms, (1, 0))
    near = []
    for wave in range(waves):
        near.append([])
        for distance in range(blocks):
            first = pl.multiple_of((block ^ distance) * height, height)
            parts = []
            for polar in range(polars):
                lanes = pl.ds(polar * 2 * focus, 2 * focus)
                straight = rowside[wave, pl.ds(first, height), lanes]
                across = rowside[wave, pl.ds(side + first, height), lanes]
                parts.append(straight + swapped(across, focus, 1, -1))
            terms = two_terms(jnp.concatenate(parts, axis=0))
            near[wave].append(jnp.concatenate(terms, axis=1))
        sides[wave] = near[wave][0]

    def add_tile(distance, carry):
        tile = lax.axis_index("gx") ^ distance
        for index, strip in enumerate(strips):
            value = jnp.zeros((height, side), jnp.float32)
            for wave in range(waves):
                back = dot(near[wave][index], twice(strip_kern[wave, tile]), (1, 0))
                back = back.reshape(polars, height, side)
                for polar in range(polars):
                    value += back[polar] * strip[wave, polar, tile].astype(jnp.float32)
            first = pl.multiple_of((block ^ index) * height, height)
            whole[distance, pl.ds(first, height)] = (
                value + pltpu.roll(value, side - height, 1)
            ) * scale
        turned[distance] = whole[distance].T
        own = turned[distance, pl.ds(pl.multiple_of(block * height, height), height)]
        crossed[distance] = own.astype(crossed.dtype)
        return carry

    over_tiles(tiles, add_tile, 0)


def straight_kernel(scale, field, counts, both_kern, sides, gradient):
    waves, polars, _, tiles, height, side = field.shape

    def add_tile(distance, carry):
        tile = lax.axis_index("gx") ^ distance
        term = jnp.zeros((height, side), jnp.float32)
        for wave in range(waves):
            back = dot(sides[wave], twice(both_kern[wave, tile]), (1, 0))
            back = back.reshape(polars, height, 2 * side)
            for polar in range(polars):
                for part in range(2):
                    plane = field[wave, polar, part, tile].astype(jnp.float32)
                    term += back[polar, :, part * side : (part + 1) * side] * plane
        live = live_rows(counts[tile, :1], (height, side))
        gradient[distance] = jnp.where(live, term * scale, 0.0)
        return carry

    over_tiles(tiles, add_tile, 0)


def call(kernel, out_shape, scratch, args, spaces):
    return pl.pallas_call(
        kernel,
        out_shape=out_shape,
        in_specs=[pl.BlockSpec(memory_space=space) for space in spaces],
        out_specs=[pl.BlockSpec(memory_space=pltpu.VMEM)] * len(out_shape),
        scratch_shapes=scratch,
        compiler_params=pltpu.CompilerParams(vmem_limit_bytes=VMEM),
    )(*args)


def pairs(count, distance):
    return [(device, device ^ distance) for device in range(count)]


def partners(value, axis, count):
    came = {d: lax.ppermute(value(d), axis, pairs(count, d)) for d in range(count - 1, 0, -1)}
    return [came[d] for d in range(1, count)]


def over_chips(value, distance, mesh, cross):
    count, cores = mesh.shape["gx"], mesh.shape["wa"]
    routes = [
        (device * cores + core, (device ^ distance) * cores + (cores - 1 - core if cross else core))
        for device in range(count)
        for core in range(cores)
    ]
    return lax.ppermute(value, ("gx", "wa"), routes)


def partners_by_way(value, mesh):
    count = mesh.shape["gx"]
    came = {}
    for distance in range(count - 1, 0, -1):
        far = 2 * distance > count
        came[distance] = over_chips(value, distance, mesh, far)
        if far:
            came[distance] = lax.ppermute(came[distance], "wa", pairs(2, 1))
    return [came[d] for d in range(1, count)]


def crosswise(value, mesh):
    count = mesh.shape["gx"]
    came = {d: over_chips(value(d), d, mesh, d % 2 == 1) for d in range(count - 1, 0, -1)}
    return [came[d] for d in range(1, count)]


def total(terms):
    while len(terms) > 1:
        terms = [first + second for first, second in zip(terms[::2], terms[1::2])]
    return terms[0]


def rounded(value):
    return lax.reduce_precision(value, 8, 7)


def in_order(came, me):
    count = came.shape[0]
    rest = came.shape[1:]
    bit = 1
    while bit < count:
        split = came.reshape((count // (2 * bit), 2, bit) + rest)
        came = jnp.where((me & bit) != 0, split[:, ::-1], split).reshape((count,) + rest)
        bit *= 2
    return came


def make(mesh):
    count_x = mesh.shape["gx"]
    count_y = mesh.shape["gy"]

    def on_device(field, active_rows, kern, target):
        tile_row = lax.axis_index("gx")
        waves, polars = field.shape[0], field.shape[1]
        tiles = field.shape[4]
        rows_dev = field.shape[5]
        side = field.shape[6]
        focus = kern.shape[3]
        shape = (waves, polars, focus, 2 * focus)
        share, near_field, near_kern, counts = call(
            share_kernel,
            [
                jax.ShapeDtypeStruct(shape, jnp.bfloat16),
                jax.ShapeDtypeStruct(field.shape[:3] + field.shape[4:], field.dtype),
                jax.ShapeDtypeStruct(kern.shape, kern.dtype),
                jax.ShapeDtypeStruct((tiles, 8, side), jnp.int32),
            ],
            [
                pltpu.SMEM(active_rows.shape, jnp.int32),
                pltpu.VMEM((waves, 2 * side, polars * 2 * focus), jnp.bfloat16),
                pltpu.SemaphoreType.DMA((2 * waves + 1,)),
            ],
            [
                pltpu.with_memory_space_constraint(operand, pltpu.HBM)
                for operand in (active_rows, field, kern)
            ],
            [pltpu.HBM] * 3,
        )
        shares = [share] + partners(lambda d: share, "gy", count_y)
        share = total([term.astype(jnp.float32) for term in shares]).astype(jnp.bfloat16)
        strip_shape = (waves, polars, tiles, rows_dev, side)
        own_kern, both_kern, strip_kern, own_strip, *strips = call(
            strip_kernel,
            [
                jax.ShapeDtypeStruct((waves, 2 * side, 2 * focus), kern.dtype),
                jax.ShapeDtypeStruct((waves, tiles, 2 * focus, 2 * side), kern.dtype),
                jax.ShapeDtypeStruct((waves, tiles, 2 * focus, side), kern.dtype),
            ]
            + [jax.ShapeDtypeStruct(strip_shape, field.dtype)] * count_y,
            [],
            (near_field, near_kern, counts),
            [pltpu.VMEM] * 3,
        )
        strips = partners(lambda d: strips[d - 1], "gy", count_y)
        shares = [share] + partners_by_way(share, mesh)
        shares = shares[::-1]
        shape = (tiles, rows_dev, side)
        scale = tiles * side / focus
        powers, sides, crossed = call(
            functools.partial(crossed_kernel, scale, count_y),
            [
                jax.ShapeDtypeStruct((waves, focus, 2 * focus), jnp.float32),
                jax.ShapeDtypeStruct((waves, polars * rows_dev, 4 * focus), jnp.bfloat16),
                jax.ShapeDtypeStruct(shape, jnp.bfloat16),
            ],
            [pltpu.VMEM((waves, 2 * side, polars * 2 * focus), jnp.float32)]
            + [pltpu.VMEM((tiles, side, side), jnp.float32)] * 2,
            (own_kern, strip_kern, target, own_strip, *strips, *shares),
            [pltpu.VMEM] * (3 + count_x + count_y),
        )
        (gradient,) = call(
            functools.partial(straight_kernel, scale),
            [jax.ShapeDtypeStruct(shape, jnp.float32)],
            [],
            (near_field, counts, both_kern, sides),
            [pltpu.VMEM] * 4,
        )
        came = [crossed[0]] + crosswise(lambda d: crossed[d], mesh)
        own = rounded(gradient + jnp.stack(came).astype(jnp.float32))
        other = lax.ppermute(own.astype(jnp.bfloat16), "wa", pairs(2, 1))
        design_grad = in_order(0.5 * (own + other.astype(jnp.float32)), tile_row)
        intensity = powers[:, :, :focus] + powers[:, :, focus:]
        return (design_grad[None], intensity)

    return on_device


def solution(mesh):
    placed = (
        P("wa", "cand", None, "gx", None, "gy", None),
        P("gx", None),
        P("wa", None, None, None, None),
        P("wa", None, None),
    )
    return jax.shard_map(
        make(mesh),
        mesh=mesh,
        in_specs=placed,
        out_specs=(P("gx", "cand", "gy", None), P("wa", "cand", None)),
        check_vma=False,
    )
```

```python
import functools
import math

import jax
import jax.numpy as jnp
from jax import lax
from jax.experimental import pallas as pl
from jax.experimental.pallas import tpu as pltpu
from jax.sharding import PartitionSpec as P

VMEM = 16 * 2**20


def two_terms(value):
    high = value.astype(jnp.bfloat16)
    return high, (value - high.astype(jnp.float32)).astype(jnp.bfloat16)


def dot(first, second, over):
    return lax.dot_general(
        first, second, ((over[:1], over[1:]), ((), ())), preferred_element_type=jnp.float32
    )


def swapped(value, focus, left, right):
    lane = lax.broadcasted_iota(jnp.int32, value.shape, 1)
    sign = jnp.where(lane < focus, jnp.float32(left), jnp.float32(right))
    return pltpu.roll(value, focus, 1) * sign


def tile_kern(kern, wave, tile):
    real, imag = kern[wave, 0, tile], kern[wave, 1, tile]
    return jnp.concatenate([real, imag], axis=0), jnp.concatenate([-imag, real], axis=0)


def in_block(shape, block, width):
    lane = lax.broadcasted_iota(jnp.int32, shape, len(shape) - 1)
    return (lane >= block * width) & (lane < (block + 1) * width)


def side_by_side(first, second, block, blocks):
    width = first.shape[-1] // blocks
    first, second = first.astype(jnp.float32), second.astype(jnp.float32)
    beside = in_block(first.shape, lax.rem(block + 1, blocks), width)
    moved = jnp.where(beside, pltpu.roll(second, width, first.ndim - 1), 0.0)
    return jnp.where(in_block(first.shape, block, width), first, moved).astype(jnp.bfloat16)


def over_tiles(tiles, body, init):
    return lax.fori_loop(0, tiles, body, init, unroll=tiles <= 8)


def live_rows(count, shape):
    height = shape[-2]
    row = lax.axis_index("gy") * height + lax.broadcasted_iota(jnp.int32, shape, len(shape) - 2)
    return row < count


def share_kernel(rows_far, field_far, kern_far, share, field, kern, counts, rows, spread, arrived):
    waves, polars, _, tiles, height, side = field.shape
    focus = kern.shape[3]
    copies = [pltpu.make_async_copy(rows_far, rows, arrived.at[2 * waves])]
    for wave in range(waves):
        copies += [
            pltpu.make_async_copy(kern_far.at[wave], kern.at[wave], arrived.at[2 * wave]),
            pltpu.make_async_copy(
                field_far.at[wave, :, :, 0], field.at[wave], arrived.at[2 * wave + 1]
            ),
        ]
    for copy in copies:
        copy.start()
    tile_row = lax.axis_index("gx")
    first = pl.multiple_of(lax.axis_index("gy") * height, height)
    spread[...] = jnp.zeros_like(spread)
    copies[0].wait()
    many = math.gcd(tiles, 4)
    inner = []
    for wave in range(waves):
        copies[2 * wave + 1].wait()
        copies[2 * wave + 2].wait()

        def add_tiles(group, value):
            planes = []
            parts = []
            for index in range(many):
                tile = group * many + index
                live = live_rows(rows[0, tile], (polars, height, side))
                for part in range(2):
                    plane = field[wave, :, part, tile]
                    plane = jnp.where(live, plane, jnp.zeros((), field.dtype))
                    planes.append(plane.reshape(polars * height, side))
                parts += tile_kern(kern, wave, tile)
            planes, parts = jnp.concatenate(planes, axis=1), jnp.concatenate(parts, axis=1)
            return value + dot(planes, parts, (1, 1))

        zero = jnp.zeros((polars * height, 2 * focus), jnp.float32)
        inner.append(over_tiles(tiles // many, add_tiles, zero))
    for wave in range(waves):
        for polar in range(polars):
            lanes = pl.ds(polar * 2 * focus, 2 * focus)
            terms = two_terms(inner[wave][polar * height : (polar + 1) * height])
            for index, term in enumerate(terms):
                spread[wave, pl.ds(index * side + first, height), lanes] = term
        own = tile_kern(kern, wave, tile_row)[0]
        both = dot(jnp.concatenate([own, own], axis=1), spread[wave], (1, 0))
        for polar in range(polars):
            lanes = slice(polar * 2 * focus, (polar + 1) * 2 * focus)
            straight, crossed = both[:focus, lanes], both[focus:, lanes]
            share[wave, polar] = (straight + swapped(crossed, focus, -1, 1)).astype(share.dtype)

    def put_count(tile, carry):
        counts[tile] = jnp.full(counts.shape[1:], rows[0, tile], jnp.int32)
        return carry

    over_tiles(tiles, put_count, 0)


def strip_kernel(field, kern, counts, target, goal, own_kern, both_kern, strip_kern, *strips):
    waves, polars, _, tiles, height, side = field.shape
    blocks = side // height
    block = lax.axis_index("gy")
    tile_row = lax.axis_index("gx")
    for wave in range(waves):
        goal[wave] = jnp.concatenate([target[wave], target[wave]], axis=1)
        own = [kern[wave, part, tile_row].astype(jnp.float32).T for part in range(2)]
        own_kern[wave] = jnp.concatenate(own + own, axis=1).astype(kern.dtype)

    def one_tile(tile, carry):
        live = live_rows(counts[tile, :1], (height, side))
        for wave in range(waves):
            parts = tile_kern(kern, wave, tile)
            both_kern[wave, tile] = jnp.concatenate(parts, axis=1)
            strip_kern[wave, tile] = side_by_side(*parts, block, blocks)
            for polar in range(polars):
                for distance, strip in enumerate(strips):
                    both = side_by_side(
                        field[wave, polar, 0, tile],
                        field[wave, polar, 1, tile],
                        block ^ distance,
                        blocks,
                    )
                    strip[wave, polar, tile] = jnp.where(live, both, jnp.zeros((), both.dtype))
        return carry

    over_tiles(tiles, one_tile, 0)


def twice(value):
    return jnp.concatenate([value, value], axis=0)


def crossed_kernel(scale, blocks, own_kern, strip_kern, goal, *refs):
    strips, refs = refs[:blocks], refs[blocks:]
    shares, (powers, sides, crossed) = refs[:-3], refs[-3:]
    waves, polars, tiles, height, side = strips[0].shape
    focus = goal.shape[1]
    block = lax.axis_index("gy")
    near = []
    for wave in range(waves):
        focal = [
            total([share[wave, polar].astype(jnp.float32) for share in shares])
            for polar in range(polars)
        ]
        power = sum(value * value for value in focal)
        powers[wave] = power
        power = power + pltpu.roll(power, focus, 1)
        excess = power - goal[wave]
        source = [excess * value for value in focal]
        upright = jnp.concatenate(source, axis=1)
        turned = jnp.concatenate([swapped(value, focus, 1, -1) for value in source], axis=1)
        terms = two_terms(jnp.concatenate([upright, turned], axis=0))
        rowside = dot(own_kern[wave], jnp.concatenate(terms, axis=0), (1, 0))
        near.append([])
        for index in range(blocks):
            rows = rowside[index * height : (index + 1) * height]
            rows = [
                rows[:, polar * 2 * focus : (polar + 1) * 2 * focus] for polar in range(polars)
            ]
            terms = two_terms(jnp.concatenate(rows, axis=0))
            near[wave].append(jnp.concatenate(terms, axis=1))
        own = near[wave][0]
        for index in range(1, blocks):
            own = jnp.where(block == index, near[wave][index], own)
        sides[wave] = own
    lane = lax.broadcasted_iota(jnp.int32, (height, 2 * side), 1)
    row = lax.broadcasted_iota(jnp.int32, (height, 2 * side), 0)
    pick = jnp.where(lax.rem(lane, height) == row, 1.0, 0.0).astype(jnp.bfloat16)

    def add_tile(distance, carry):
        tile = lax.axis_index("gx") ^ distance
        values = []
        for index in range(blocks):
            value = jnp.zeros((height, side), jnp.float32)
            for wave in range(waves):
                back = dot(near[wave][index], twice(strip_kern[wave, tile]), (1, 0))
                back = back.reshape(polars, height, side)
                for polar in range(polars):
                    strip = strips[0][wave, polar, tile]
                    for apart in range(1, blocks):
                        other = strips[apart][wave, polar, tile]
                        strip = jnp.where((block ^ apart) == index, other, strip)
                    value += back[polar] * strip.astype(jnp.float32)
            values.append(value)
        terms = jnp.concatenate(two_terms(jnp.concatenate(values, axis=0)), axis=1)
        crossed[distance] = (dot(pick, terms, (1, 1)) * scale).astype(crossed.dtype)
        return carry

    over_tiles(tiles, add_tile, 0)


def straight_kernel(scale, field, counts, both_kern, sides, gradient):
    waves, polars, _, tiles, height, side = field.shape

    def add_tile(distance, carry):
        tile = lax.axis_index("gx") ^ distance
        term = jnp.zeros((height, side), jnp.float32)
        for wave in range(waves):
            back = dot(sides[wave], twice(both_kern[wave, tile]), (1, 0))
            back = back.reshape(polars, height, 2 * side)
            for polar in range(polars):
                for part in range(2):
                    plane = field[wave, polar, part, tile].astype(jnp.float32)
                    term += back[polar, :, part * side : (part + 1) * side] * plane
        live = live_rows(counts[tile, :1], (height, side))
        gradient[distance] = jnp.where(live, term * scale, 0.0)
        return carry

    over_tiles(tiles, add_tile, 0)


def call(kernel, out_shape, scratch, args, spaces):
    return pl.pallas_call(
        kernel,
        out_shape=out_shape,
        in_specs=[pl.BlockSpec(memory_space=space) for space in spaces],
        out_specs=[pl.BlockSpec(memory_space=pltpu.VMEM)] * len(out_shape),
        scratch_shapes=scratch,
        compiler_params=pltpu.CompilerParams(vmem_limit_bytes=VMEM),
    )(*args)


def pairs(count, distance):
    return [(device, device ^ distance) for device in range(count)]


def partners(value, axis, count):
    came = {d: lax.ppermute(value(d), axis, pairs(count, d)) for d in range(count - 1, 0, -1)}
    return [came[d] for d in range(1, count)]


def crosswise(value, mesh):
    count, cores = mesh.shape["gx"], mesh.shape["wa"]

    def routes(distance):
        odd = distance % 2 == 1
        return [
            (
                device * cores + core,
                (device ^ distance) * cores + (cores - 1 - core if odd else core),
            )
            for device in range(count)
            for core in range(cores)
        ]

    came = {d: lax.ppermute(value(d), ("gx", "wa"), routes(d)) for d in range(count - 1, 0, -1)}
    return [came[d] for d in range(1, count)]


def total(terms):
    while len(terms) > 1:
        terms = [first + second for first, second in zip(terms[::2], terms[1::2])]
    return terms[0]


def rounded(value):
    return lax.reduce_precision(value, 8, 7)


def in_order(came, me):
    count = came.shape[0]
    rest = came.shape[1:]
    bit = 1
    while bit < count:
        split = came.reshape((count // (2 * bit), 2, bit) + rest)
        came = jnp.where((me & bit) != 0, split[:, ::-1], split).reshape((count,) + rest)
        bit *= 2
    return came


def make(mesh):
    count_x = mesh.shape["gx"]
    count_y = mesh.shape["gy"]

    def on_device(field, active_rows, kern, target):
        tile_row = lax.axis_index("gx")
        waves, polars = field.shape[0], field.shape[1]
        tiles = field.shape[4]
        rows_dev = field.shape[5]
        side = field.shape[6]
        focus = kern.shape[3]
        shape = (waves, polars, focus, 2 * focus)
        share, near_field, near_kern, counts = call(
            share_kernel,
            [
                jax.ShapeDtypeStruct(shape, jnp.bfloat16),
                jax.ShapeDtypeStruct(field.shape[:3] + field.shape[4:], field.dtype),
                jax.ShapeDtypeStruct(kern.shape, kern.dtype),
                jax.ShapeDtypeStruct((tiles, 8, side), jnp.int32),
            ],
            [
                pltpu.SMEM(active_rows.shape, jnp.int32),
                pltpu.VMEM((waves, 2 * side, polars * 2 * focus), jnp.bfloat16),
                pltpu.SemaphoreType.DMA((2 * waves + 1,)),
            ],
            [
                pltpu.with_memory_space_constraint(operand, pltpu.HBM)
                for operand in (active_rows, field, kern)
            ],
            [pltpu.HBM] * 3,
        )
        shares = [share] + partners(lambda d: share, "gy", count_y)
        share = total([term.astype(jnp.float32) for term in shares]).astype(jnp.bfloat16)
        strip_shape = (waves, polars, tiles, rows_dev, side)
        goal, own_kern, both_kern, strip_kern, own_strip, *strips = call(
            strip_kernel,
            [
                jax.ShapeDtypeStruct((waves, focus, 2 * focus), target.dtype),
                jax.ShapeDtypeStruct((waves, side, 4 * focus), kern.dtype),
                jax.ShapeDtypeStruct((waves, tiles, 2 * focus, 2 * side), kern.dtype),
                jax.ShapeDtypeStruct((waves, tiles, 2 * focus, side), kern.dtype),
            ]
            + [jax.ShapeDtypeStruct(strip_shape, field.dtype)] * count_y,
            [],
            (near_field, near_kern, counts, target),
            [pltpu.VMEM] * 4,
        )
        strips = partners(lambda d: strips[d - 1], "gy", count_y)
        shares = [share] + partners(lambda d: share, "gx", count_x)
        shares = shares[::-1]
        shape = (tiles, rows_dev, side)
        scale = tiles * side / focus
        powers, sides, crossed = call(
            functools.partial(crossed_kernel, scale, count_y),
            [
                jax.ShapeDtypeStruct((waves, focus, 2 * focus), jnp.float32),
                jax.ShapeDtypeStruct((waves, polars * rows_dev, 4 * focus), jnp.bfloat16),
                jax.ShapeDtypeStruct(shape, jnp.bfloat16),
            ],
            [],
            (own_kern, strip_kern, goal, own_strip, *strips, *shares),
            [pltpu.VMEM] * (3 + count_x + count_y),
        )
        (gradient,) = call(
            functools.partial(straight_kernel, scale),
            [jax.ShapeDtypeStruct(shape, jnp.float32)],
            [],
            (near_field, counts, both_kern, sides),
            [pltpu.VMEM] * 4,
        )
        came = [crossed[0]] + crosswise(lambda d: crossed[d], mesh)
        own = rounded(gradient + jnp.stack(came).astype(jnp.float32))
        other = lax.ppermute(own.astype(jnp.bfloat16), "wa", pairs(2, 1))
        design_grad = in_order(0.5 * (own + other.astype(jnp.float32)), tile_row)
        intensity = powers[:, :, :focus] + powers[:, :, focus:]
        return (design_grad[None], intensity)

    return on_device


def solution(mesh):
    placed = (
        P("wa", "cand", None, "gx", None, "gy", None),
        P("gx", None),
        P("wa", None, None, None, None),
        P("wa", None, None),
    )
    return jax.shard_map(
        make(mesh),
        mesh=mesh,
        in_specs=placed,
        out_specs=(P("gx", "cand", "gy", None), P("wa", "cand", None)),
        check_vma=False,
    )
```

```python
import functools

import jax
import jax.numpy as jnp
from jax import lax
from jax.experimental import pallas as pl
from jax.experimental.pallas import tpu as pltpu
from jax.sharding import PartitionSpec as P

VMEM = 16 * 2**20


def two_terms(value):
    high = value.astype(jnp.bfloat16)
    return high, (value - high.astype(jnp.float32)).astype(jnp.bfloat16)


def dot(first, second, over):
    return lax.dot_general(
        first, second, ((over[:1], over[1:]), ((), ())), preferred_element_type=jnp.float32
    )


def swapped(value, focus, left, right):
    lane = lax.broadcasted_iota(jnp.int32, value.shape, 1)
    sign = jnp.where(lane < focus, jnp.float32(left), jnp.float32(right))
    return pltpu.roll(value, focus, 1) * sign


def tile_kern(kern, wave, tile):
    real, imag = kern[wave, 0, tile], kern[wave, 1, tile]
    return jnp.concatenate([real, imag], axis=0), jnp.concatenate([-imag, real], axis=0)


def in_block(shape, block, width):
    lane = lax.broadcasted_iota(jnp.int32, shape, len(shape) - 1)
    return (lane >= block * width) & (lane < (block + 1) * width)


def side_by_side(first, second, block, blocks):
    width = first.shape[-1] // blocks
    first, second = first.astype(jnp.float32), second.astype(jnp.float32)
    beside = in_block(first.shape, lax.rem(block + 1, blocks), width)
    moved = jnp.where(beside, pltpu.roll(second, width, first.ndim - 1), 0.0)
    return jnp.where(in_block(first.shape, block, width), first, moved).astype(jnp.bfloat16)


def over_tiles(tiles, body, init):
    return lax.fori_loop(0, tiles, body, init, unroll=tiles <= 8)


def live_rows(count, shape):
    height = shape[-2]
    row = lax.axis_index("gy") * height + lax.broadcasted_iota(jnp.int32, shape, len(shape) - 2)
    return row < count


def share_kernel(rows_far, field_far, kern_far, share, field, kern, counts, rows, spread, arrived):
    waves, polars, _, tiles, height, side = field.shape
    focus = kern.shape[3]
    copies = [pltpu.make_async_copy(rows_far, rows, arrived.at[2 * waves])]
    for wave in range(waves):
        copies += [
            pltpu.make_async_copy(kern_far.at[wave], kern.at[wave], arrived.at[2 * wave]),
            pltpu.make_async_copy(
                field_far.at[wave, :, :, 0], field.at[wave], arrived.at[2 * wave + 1]
            ),
        ]
    for copy in copies:
        copy.start()
    tile_row = lax.axis_index("gx")
    first = pl.multiple_of(lax.axis_index("gy") * height, height)
    spread[...] = jnp.zeros_like(spread)
    copies[0].wait()
    inner = []
    for wave in range(waves):
        copies[2 * wave + 1].wait()
        copies[2 * wave + 2].wait()

        def add_tile(tile, value):
            live = live_rows(rows[0, tile], (polars, height, side))
            planes = [
                jnp.where(live, field[wave, :, part, tile], jnp.zeros((), field.dtype))
                for part in range(2)
            ]
            planes = [plane.reshape(polars * height, side) for plane in planes]
            return value + dot(
                jnp.concatenate(planes, axis=1),
                jnp.concatenate(tile_kern(kern, wave, tile), axis=1),
                (1, 1),
            )

        zero = jnp.zeros((polars * height, 2 * focus), jnp.float32)
        inner.append(over_tiles(tiles, add_tile, zero))
    for wave in range(waves):
        for polar in range(polars):
            lanes = pl.ds(polar * 2 * focus, 2 * focus)
            terms = two_terms(inner[wave][polar * height : (polar + 1) * height])
            for index, term in enumerate(terms):
                spread[wave, pl.ds(index * side + first, height), lanes] = term
        own = tile_kern(kern, wave, tile_row)[0]
        both = dot(jnp.concatenate([own, own], axis=1), spread[wave], (1, 0))
        for polar in range(polars):
            lanes = slice(polar * 2 * focus, (polar + 1) * 2 * focus)
            straight, crossed = both[:focus, lanes], both[focus:, lanes]
            share[wave, polar] = (straight + swapped(crossed, focus, -1, 1)).astype(share.dtype)

    def put_count(tile, carry):
        counts[tile] = jnp.full(counts.shape[1:], rows[0, tile], jnp.int32)
        return carry

    over_tiles(tiles, put_count, 0)


def strip_kernel(field, kern, counts, own_kern, both_kern, strip_kern, *strips):
    waves, polars, _, tiles, height, side = field.shape
    blocks = side // height
    block = lax.axis_index("gy")
    tile_row = lax.axis_index("gx")
    for wave in range(waves):
        for part in range(2):
            turned = kern[wave, part, tile_row].astype(jnp.float32).T.astype(kern.dtype)
            own_kern[wave, pl.ds(part * side, side)] = jnp.concatenate([turned, turned], axis=1)

    def one_tile(tile, carry):
        live = live_rows(counts[tile, :1], (height, side))
        for wave in range(waves):
            parts = tile_kern(kern, wave, tile)
            both_kern[wave, tile] = jnp.concatenate(parts, axis=1)
            strip_kern[wave, tile] = side_by_side(*parts, block, blocks)
            for polar in range(polars):
                for distance, strip in enumerate(strips):
                    both = side_by_side(
                        field[wave, polar, 0, tile],
                        field[wave, polar, 1, tile],
                        block ^ distance,
                        blocks,
                    )
                    strip[wave, polar, tile] = jnp.where(live, both, jnp.zeros((), both.dtype))
        return carry

    over_tiles(tiles, one_tile, 0)


def twice(value):
    return jnp.concatenate([value, value], axis=0)


def crossed_kernel(scale, blocks, own_kern, strip_kern, target, *refs):
    strips, refs = refs[:blocks], refs[blocks:]
    shares, (powers, sides, crossed, rowside, whole, turned) = refs[:-6], refs[-6:]
    waves, polars, tiles, height, side = strips[0].shape
    focus = target.shape[1]
    block = lax.axis_index("gy")
    for wave in range(waves):
        focal = [
            total([share[wave, polar].astype(jnp.float32) for share in shares])
            for polar in range(polars)
        ]
        power = sum(value * value for value in focal)
        powers[wave] = power
        power = power + pltpu.roll(power, focus, 1)
        goal = target[wave]
        excess = power - jnp.concatenate([goal, goal], axis=1)
        source = jnp.concatenate([excess * value for value in focal], axis=1)
        terms = jnp.concatenate(two_terms(source), axis=0)
        rowside[wave] = dot(own_kern[wave], terms, (1, 0))
    near = []
    for wave in range(waves):
        near.append([])
        for distance in range(blocks):
            first = pl.multiple_of((block ^ distance) * height, height)
            parts = []
            for polar in range(polars):
                lanes = pl.ds(polar * 2 * focus, 2 * focus)
                straight = rowside[wave, pl.ds(first, height), lanes]
                across = rowside[wave, pl.ds(side + first, height), lanes]
                parts.append(straight + swapped(across, focus, 1, -1))
            terms = two_terms(jnp.concatenate(parts, axis=0))
            near[wave].append(jnp.concatenate(terms, axis=1))
        sides[wave] = near[wave][0]

    def add_tile(distance, carry):
        tile = lax.axis_index("gx") ^ distance
        for index, strip in enumerate(strips):
            value = jnp.zeros((height, side), jnp.float32)
            for wave in range(waves):
                back = dot(near[wave][index], twice(strip_kern[wave, tile]), (1, 0))
                back = back.reshape(polars, height, side)
                for polar in range(polars):
                    value += back[polar] * strip[wave, polar, tile].astype(jnp.float32)
            first = pl.multiple_of((block ^ index) * height, height)
            whole[distance, pl.ds(first, height)] = (
                value + pltpu.roll(value, side - height, 1)
            ) * scale
        turned[distance] = whole[distance].T
        own = turned[distance, pl.ds(pl.multiple_of(block * height, height), height)]
        crossed[distance] = own.astype(crossed.dtype)
        return carry

    over_tiles(tiles, add_tile, 0)


def straight_kernel(scale, field, counts, both_kern, sides, gradient):
    waves, polars, _, tiles, height, side = field.shape

    def add_tile(distance, carry):
        tile = lax.axis_index("gx") ^ distance
        term = jnp.zeros((height, side), jnp.float32)
        for wave in range(waves):
            back = dot(sides[wave], twice(both_kern[wave, tile]), (1, 0))
            back = back.reshape(polars, height, 2 * side)
            for polar in range(polars):
                for part in range(2):
                    plane = field[wave, polar, part, tile].astype(jnp.float32)
                    term += back[polar, :, part * side : (part + 1) * side] * plane
        live = live_rows(counts[tile, :1], (height, side))
        gradient[distance] = jnp.where(live, term * scale, 0.0)
        return carry

    over_tiles(tiles, add_tile, 0)


def call(kernel, out_shape, scratch, args, spaces):
    return pl.pallas_call(
        kernel,
        out_shape=out_shape,
        in_specs=[pl.BlockSpec(memory_space=space) for space in spaces],
        out_specs=[pl.BlockSpec(memory_space=pltpu.VMEM)] * len(out_shape),
        scratch_shapes=scratch,
        compiler_params=pltpu.CompilerParams(vmem_limit_bytes=VMEM),
    )(*args)


def pairs(count, distance):
    return [(device, device ^ distance) for device in range(count)]


def partners(value, axis, count):
    came = {d: lax.ppermute(value(d), axis, pairs(count, d)) for d in range(count - 1, 0, -1)}
    return [came[d] for d in range(1, count)]


def crosswise(value, mesh):
    count, cores = mesh.shape["gx"], mesh.shape["wa"]

    def routes(distance):
        far = 2 * distance > count
        return [
            (
                device * cores + core,
                (device ^ distance) * cores + (cores - 1 - core if far else core),
            )
            for device in range(count)
            for core in range(cores)
        ]

    came = {d: lax.ppermute(value(d), ("gx", "wa"), routes(d)) for d in range(count - 1, 0, -1)}
    return [came[d] for d in range(1, count)]


def total(terms):
    while len(terms) > 1:
        terms = [first + second for first, second in zip(terms[::2], terms[1::2])]
    return terms[0]


def rounded(value):
    return lax.reduce_precision(value, 8, 7)


def in_order(came, me):
    count = came.shape[0]
    rest = came.shape[1:]
    bit = 1
    while bit < count:
        split = came.reshape((count // (2 * bit), 2, bit) + rest)
        came = jnp.where((me & bit) != 0, split[:, ::-1], split).reshape((count,) + rest)
        bit *= 2
    return came


def make(mesh):
    count_x = mesh.shape["gx"]
    count_y = mesh.shape["gy"]

    def on_device(field, active_rows, kern, target):
        tile_row = lax.axis_index("gx")
        waves, polars = field.shape[0], field.shape[1]
        tiles = field.shape[4]
        rows_dev = field.shape[5]
        side = field.shape[6]
        focus = kern.shape[3]
        shape = (waves, polars, focus, 2 * focus)
        share, near_field, near_kern, counts = call(
            share_kernel,
            [
                jax.ShapeDtypeStruct(shape, jnp.bfloat16),
                jax.ShapeDtypeStruct(field.shape[:3] + field.shape[4:], field.dtype),
                jax.ShapeDtypeStruct(kern.shape, kern.dtype),
                jax.ShapeDtypeStruct((tiles, 8, side), jnp.int32),
            ],
            [
                pltpu.SMEM(active_rows.shape, jnp.int32),
                pltpu.VMEM((waves, 2 * side, polars * 2 * focus), jnp.bfloat16),
                pltpu.SemaphoreType.DMA((2 * waves + 1,)),
            ],
            [
                pltpu.with_memory_space_constraint(operand, pltpu.HBM)
                for operand in (active_rows, field, kern)
            ],
            [pltpu.HBM] * 3,
        )
        shares = [share] + partners(lambda d: share, "gy", count_y)
        share = total([term.astype(jnp.float32) for term in shares]).astype(jnp.bfloat16)
        strip_shape = (waves, polars, tiles, rows_dev, side)
        own_kern, both_kern, strip_kern, own_strip, *strips = call(
            strip_kernel,
            [
                jax.ShapeDtypeStruct((waves, 2 * side, 2 * focus), kern.dtype),
                jax.ShapeDtypeStruct((waves, tiles, 2 * focus, 2 * side), kern.dtype),
                jax.ShapeDtypeStruct((waves, tiles, 2 * focus, side), kern.dtype),
            ]
            + [jax.ShapeDtypeStruct(strip_shape, field.dtype)] * count_y,
            [],
            (near_field, near_kern, counts),
            [pltpu.VMEM] * 3,
        )
        strips = partners(lambda d: strips[d - 1], "gy", count_y)
        shares = [share] + partners(lambda d: share, "gx", count_x)
        shares = shares[:2] + shares[:1:-1]
        shape = (tiles, rows_dev, side)
        scale = tiles * side / focus
        powers, sides, crossed = call(
            functools.partial(crossed_kernel, scale, count_y),
            [
                jax.ShapeDtypeStruct((waves, focus, 2 * focus), jnp.float32),
                jax.ShapeDtypeStruct((waves, polars * rows_dev, 4 * focus), jnp.bfloat16),
                jax.ShapeDtypeStruct(shape, jnp.bfloat16),
            ],
            [pltpu.VMEM((waves, 2 * side, polars * 2 * focus), jnp.float32)]
            + [pltpu.VMEM((tiles, side, side), jnp.float32)] * 2,
            (own_kern, strip_kern, target, own_strip, *strips, *shares),
            [pltpu.VMEM] * (3 + count_x + count_y),
        )
        (gradient,) = call(
            functools.partial(straight_kernel, scale),
            [jax.ShapeDtypeStruct(shape, jnp.float32)],
            [],
            (near_field, counts, both_kern, sides),
            [pltpu.VMEM] * 4,
        )
        came = [crossed[0]] + crosswise(lambda d: crossed[d], mesh)
        own = rounded(gradient + jnp.stack(came).astype(jnp.float32))
        other = lax.ppermute(own.astype(jnp.bfloat16), "wa", pairs(2, 1))
        design_grad = in_order(0.5 * (own + other.astype(jnp.float32)), tile_row)
        intensity = powers[:, :, :focus] + powers[:, :, focus:]
        return (design_grad[None], intensity)

    return on_device


def solution(mesh):
    placed = (
        P("wa", "cand", None, "gx", None, "gy", None),
        P("gx", None),
        P("wa", None, None, None, None),
        P("wa", None, None),
    )
    return jax.shard_map(
        make(mesh),
        mesh=mesh,
        in_specs=placed,
        out_specs=(P("gx", "cand", "gy", None), P("wa", "cand", None)),
        check_vma=False,
    )
```

```python
import functools
import math

import jax
import jax.numpy as jnp
from jax import lax
from jax.experimental import pallas as pl
from jax.experimental.pallas import tpu as pltpu
from jax.sharding import PartitionSpec as P

VMEM = 16 * 2**20


def two_terms(value):
    high = value.astype(jnp.bfloat16)
    return high, (value - high.astype(jnp.float32)).astype(jnp.bfloat16)


def dot(first, second, over):
    return lax.dot_general(
        first, second, ((over[:1], over[1:]), ((), ())), preferred_element_type=jnp.float32
    )


def swapped(value, focus, left, right):
    lane = lax.broadcasted_iota(jnp.int32, value.shape, 1)
    sign = jnp.where(lane < focus, jnp.float32(left), jnp.float32(right))
    return pltpu.roll(value, focus, 1) * sign


def tile_kern(kern, wave, tile):
    real, imag = kern[wave, 0, tile], kern[wave, 1, tile]
    return jnp.concatenate([real, imag], axis=0), jnp.concatenate([-imag, real], axis=0)


def in_block(shape, block, width):
    lane = lax.broadcasted_iota(jnp.int32, shape, len(shape) - 1)
    return (lane >= block * width) & (lane < (block + 1) * width)


def side_by_side(first, second, block, blocks):
    width = first.shape[-1] // blocks
    first, second = first.astype(jnp.float32), second.astype(jnp.float32)
    beside = in_block(first.shape, lax.rem(block + 1, blocks), width)
    moved = jnp.where(beside, pltpu.roll(second, width, first.ndim - 1), 0.0)
    return jnp.where(in_block(first.shape, block, width), first, moved).astype(jnp.bfloat16)


def over_tiles(tiles, body, init):
    return lax.fori_loop(0, tiles, body, init, unroll=tiles <= 8)


def live_rows(count, shape):
    height = shape[-2]
    row = lax.axis_index("gy") * height + lax.broadcasted_iota(jnp.int32, shape, len(shape) - 2)
    return row < count


def share_kernel(rows_far, field_far, kern_far, share, field, kern, counts, rows, spread, arrived):
    waves, polars, _, tiles, height, side = field.shape
    focus = kern.shape[3]
    copies = [pltpu.make_async_copy(rows_far, rows, arrived.at[2 * waves])]
    for wave in range(waves):
        copies += [
            pltpu.make_async_copy(kern_far.at[wave], kern.at[wave], arrived.at[2 * wave]),
            pltpu.make_async_copy(
                field_far.at[wave, :, :, 0], field.at[wave], arrived.at[2 * wave + 1]
            ),
        ]
    for copy in copies:
        copy.start()
    tile_row = lax.axis_index("gx")
    first = pl.multiple_of(lax.axis_index("gy") * height, height)
    spread[...] = jnp.zeros_like(spread)
    copies[0].wait()
    many = math.gcd(tiles, 4)
    inner = []
    for wave in range(waves):
        copies[2 * wave + 1].wait()
        copies[2 * wave + 2].wait()

        def add_tiles(group, value):
            planes = []
            parts = []
            for index in range(many):
                tile = group * many + index
                live = live_rows(rows[0, tile], (polars, height, side))
                pair = []
                for part in range(2):
                    plane = field[wave, :, part, tile]
                    plane = jnp.where(live, plane, jnp.zeros((), field.dtype))
                    pair.append(plane.reshape(polars * height, side))
                planes.append(jnp.concatenate(pair, axis=0))
                pair = [kern[wave, part, tile] for part in range(2)]
                parts.append(jnp.concatenate(pair, axis=0))
            planes, parts = jnp.concatenate(planes, axis=1), jnp.concatenate(parts, axis=1)
            return value + dot(planes, parts, (1, 1))

        zero = jnp.zeros((2 * polars * height, 2 * focus), jnp.float32)
        value = over_tiles(tiles // many, add_tiles, zero)
        real, imag = value[: polars * height], value[polars * height :]
        inner.append(real + swapped(imag, focus, -1, 1))
    for wave in range(waves):
        for polar in range(polars):
            lanes = pl.ds(polar * 2 * focus, 2 * focus)
            terms = two_terms(inner[wave][polar * height : (polar + 1) * height])
            for index, term in enumerate(terms):
                spread[wave, pl.ds(index * side + first, height), lanes] = term
        own = tile_kern(kern, wave, tile_row)[0]
        both = dot(jnp.concatenate([own, own], axis=1), spread[wave], (1, 0))
        for polar in range(polars):
            lanes = slice(polar * 2 * focus, (polar + 1) * 2 * focus)
            straight, crossed = both[:focus, lanes], both[focus:, lanes]
            share[wave, polar] = (straight + swapped(crossed, focus, -1, 1)).astype(share.dtype)

    def put_count(tile, carry):
        counts[tile] = jnp.full(counts.shape[1:], rows[0, tile], jnp.int32)
        return carry

    over_tiles(tiles, put_count, 0)


def strip_kernel(field, kern, counts, own_kern, both_kern, strip_kern, *strips):
    waves, polars, _, tiles, height, side = field.shape
    blocks = side // height
    block = lax.axis_index("gy")
    tile_row = lax.axis_index("gx")
    for wave in range(waves):
        for part in range(2):
            turned = kern[wave, part, tile_row].astype(jnp.float32).T.astype(kern.dtype)
            own_kern[wave, pl.ds(part * side, side)] = jnp.concatenate([turned, turned], axis=1)

    def one_tile(tile, carry):
        live = live_rows(counts[tile, :1], (height, side))
        for wave in range(waves):
            parts = tile_kern(kern, wave, tile)
            both_kern[wave, tile] = jnp.concatenate(parts, axis=1)
            strip_kern[wave, tile] = side_by_side(*parts, block, blocks)
            for polar in range(polars):
                for distance, strip in enumerate(strips):
                    both = side_by_side(
                        field[wave, polar, 0, tile],
                        field[wave, polar, 1, tile],
                        block ^ distance,
                        blocks,
                    )
                    strip[wave, polar, tile] = jnp.where(live, both, jnp.zeros((), both.dtype))
        return carry

    over_tiles(tiles, one_tile, 0)


def twice(value):
    return jnp.concatenate([value, value], axis=0)


def crossed_kernel(scale, blocks, own_kern, strip_kern, target, *refs):
    strips, refs = refs[:blocks], refs[blocks:]
    shares, (powers, sides, crossed, rowside, whole, turned) = refs[:-6], refs[-6:]
    waves, polars, tiles, height, side = strips[0].shape
    focus = target.shape[1]
    block = lax.axis_index("gy")
    for wave in range(waves):
        focal = [
            total([share[wave, polar].astype(jnp.float32) for share in shares])
            for polar in range(polars)
        ]
        power = sum(value * value for value in focal)
        powers[wave] = power
        power = power + pltpu.roll(power, focus, 1)
        goal = target[wave]
        excess = power - jnp.concatenate([goal, goal], axis=1)
        source = jnp.concatenate([excess * value for value in focal], axis=1)
        terms = jnp.concatenate(two_terms(source), axis=0)
        rowside[wave] = dot(own_kern[wave], terms, (1, 0))
    near = []
    for wave in range(waves):
        near.append([])
        for distance in range(blocks):
            first = pl.multiple_of((block ^ distance) * height, height)
            parts = []
            for polar in range(polars):
                lanes = pl.ds(polar * 2 * focus, 2 * focus)
                straight = rowside[wave, pl.ds(first, height), lanes]
                across = rowside[wave, pl.ds(side + first, height), lanes]
                parts.append(straight + swapped(across, focus, 1, -1))
            terms = two_terms(jnp.concatenate(parts, axis=0))
            near[wave].append(jnp.concatenate(terms, axis=1))
        sides[wave] = near[wave][0]

    def add_tile(distance, carry):
        tile = lax.axis_index("gx") ^ distance
        for index, strip in enumerate(strips):
            value = jnp.zeros((height, side), jnp.float32)
            for wave in range(waves):
                back = dot(near[wave][index], twice(strip_kern[wave, tile]), (1, 0))
                back = back.reshape(polars, height, side)
                for polar in range(polars):
                    value += back[polar] * strip[wave, polar, tile].astype(jnp.float32)
            first = pl.multiple_of((block ^ index) * height, height)
            whole[distance, pl.ds(first, height)] = (
                value + pltpu.roll(value, side - height, 1)
            ) * scale
        turned[distance] = whole[distance].T
        own = turned[distance, pl.ds(pl.multiple_of(block * height, height), height)]
        crossed[distance] = own.astype(crossed.dtype)
        return carry

    over_tiles(tiles, add_tile, 0)


def straight_kernel(scale, field, counts, both_kern, sides, gradient):
    waves, polars, _, tiles, height, side = field.shape

    def add_tile(distance, carry):
        tile = lax.axis_index("gx") ^ distance
        term = jnp.zeros((height, side), jnp.float32)
        for wave in range(waves):
            back = dot(sides[wave], twice(both_kern[wave, tile]), (1, 0))
            back = back.reshape(polars, height, 2 * side)
            for polar in range(polars):
                for part in range(2):
                    plane = field[wave, polar, part, tile].astype(jnp.float32)
                    term += back[polar, :, part * side : (part + 1) * side] * plane
        live = live_rows(counts[tile, :1], (height, side))
        gradient[distance] = jnp.where(live, term * scale, 0.0)
        return carry

    over_tiles(tiles, add_tile, 0)


def call(kernel, out_shape, scratch, args, spaces):
    return pl.pallas_call(
        kernel,
        out_shape=out_shape,
        in_specs=[pl.BlockSpec(memory_space=space) for space in spaces],
        out_specs=[pl.BlockSpec(memory_space=pltpu.VMEM)] * len(out_shape),
        scratch_shapes=scratch,
        compiler_params=pltpu.CompilerParams(vmem_limit_bytes=VMEM),
    )(*args)


def pairs(count, distance):
    return [(device, device ^ distance) for device in range(count)]


def partners(value, axis, count):
    came = {d: lax.ppermute(value(d), axis, pairs(count, d)) for d in range(count - 1, 0, -1)}
    return [came[d] for d in range(1, count)]


def crosswise(value, mesh):
    count, cores = mesh.shape["gx"], mesh.shape["wa"]

    def routes(distance):
        odd = distance % 2 == 1
        return [
            (
                device * cores + core,
                (device ^ distance) * cores + (cores - 1 - core if odd else core),
            )
            for device in range(count)
            for core in range(cores)
        ]

    came = {d: lax.ppermute(value(d), ("gx", "wa"), routes(d)) for d in range(count - 1, 0, -1)}
    return [came[d] for d in range(1, count)]


def total(terms):
    while len(terms) > 1:
        terms = [first + second for first, second in zip(terms[::2], terms[1::2])]
    return terms[0]


def rounded(value):
    return lax.reduce_precision(value, 8, 7)


def in_order(came, me):
    count = came.shape[0]
    rest = came.shape[1:]
    bit = 1
    while bit < count:
        split = came.reshape((count // (2 * bit), 2, bit) + rest)
        came = jnp.where((me & bit) != 0, split[:, ::-1], split).reshape((count,) + rest)
        bit *= 2
    return came


def make(mesh):
    count_x = mesh.shape["gx"]
    count_y = mesh.shape["gy"]

    def on_device(field, active_rows, kern, target):
        tile_row = lax.axis_index("gx")
        waves, polars = field.shape[0], field.shape[1]
        tiles = field.shape[4]
        rows_dev = field.shape[5]
        side = field.shape[6]
        focus = kern.shape[3]
        shape = (waves, polars, focus, 2 * focus)
        share, near_field, near_kern, counts = call(
            share_kernel,
            [
                jax.ShapeDtypeStruct(shape, jnp.bfloat16),
                jax.ShapeDtypeStruct(field.shape[:3] + field.shape[4:], field.dtype),
                jax.ShapeDtypeStruct(kern.shape, kern.dtype),
                jax.ShapeDtypeStruct((tiles, 8, side), jnp.int32),
            ],
            [
                pltpu.SMEM(active_rows.shape, jnp.int32),
                pltpu.VMEM((waves, 2 * side, polars * 2 * focus), jnp.bfloat16),
                pltpu.SemaphoreType.DMA((2 * waves + 1,)),
            ],
            [
                pltpu.with_memory_space_constraint(operand, pltpu.HBM)
                for operand in (active_rows, field, kern)
            ],
            [pltpu.HBM] * 3,
        )
        shares = [share] + partners(lambda d: share, "gy", count_y)
        share = total([term.astype(jnp.float32) for term in shares]).astype(jnp.bfloat16)
        strip_shape = (waves, polars, tiles, rows_dev, side)
        own_kern, both_kern, strip_kern, own_strip, *strips = call(
            strip_kernel,
            [
                jax.ShapeDtypeStruct((waves, 2 * side, 2 * focus), kern.dtype),
                jax.ShapeDtypeStruct((waves, tiles, 2 * focus, 2 * side), kern.dtype),
                jax.ShapeDtypeStruct((waves, tiles, 2 * focus, side), kern.dtype),
            ]
            + [jax.ShapeDtypeStruct(strip_shape, field.dtype)] * count_y,
            [],
            (near_field, near_kern, counts),
            [pltpu.VMEM] * 3,
        )
        strips = partners(lambda d: strips[d - 1], "gy", count_y)
        shares = [share] + partners(lambda d: share, "gx", count_x)
        shares = shares[::-1]
        shape = (tiles, rows_dev, side)
        scale = tiles * side / focus
        powers, sides, crossed = call(
            functools.partial(crossed_kernel, scale, count_y),
            [
                jax.ShapeDtypeStruct((waves, focus, 2 * focus), jnp.float32),
                jax.ShapeDtypeStruct((waves, polars * rows_dev, 4 * focus), jnp.bfloat16),
                jax.ShapeDtypeStruct(shape, jnp.bfloat16),
            ],
            [pltpu.VMEM((waves, 2 * side, polars * 2 * focus), jnp.float32)]
            + [pltpu.VMEM((tiles, side, side), jnp.float32)] * 2,
            (own_kern, strip_kern, target, own_strip, *strips, *shares),
            [pltpu.VMEM] * (3 + count_x + count_y),
        )
        (gradient,) = call(
            functools.partial(straight_kernel, scale),
            [jax.ShapeDtypeStruct(shape, jnp.float32)],
            [],
            (near_field, counts, both_kern, sides),
            [pltpu.VMEM] * 4,
        )
        came = [crossed[0]] + crosswise(lambda d: crossed[d], mesh)
        own = rounded(gradient + jnp.stack(came).astype(jnp.float32))
        other = lax.ppermute(own.astype(jnp.bfloat16), "wa", pairs(2, 1))
        design_grad = in_order(0.5 * (own + other.astype(jnp.float32)), tile_row)
        intensity = powers[:, :, :focus] + powers[:, :, focus:]
        return (design_grad[None], intensity)

    return on_device


def solution(mesh):
    placed = (
        P("wa", "cand", None, "gx", None, "gy", None),
        P("gx", None),
        P("wa", None, None, None, None),
        P("wa", None, None),
    )
    return jax.shard_map(
        make(mesh),
        mesh=mesh,
        in_specs=placed,
        out_specs=(P("gx", "cand", "gy", None), P("wa", "cand", None)),
        check_vma=False,
    )
```

```python
import functools

import jax
import jax.numpy as jnp
from jax import lax
from jax.experimental import pallas as pl
from jax.experimental.pallas import tpu as pltpu
from jax.sharding import PartitionSpec as P

VMEM = 16 * 2**20


def two_terms(value):
    high = value.astype(jnp.bfloat16)
    return high, (value - high.astype(jnp.float32)).astype(jnp.bfloat16)


def dot(first, second, over):
    return lax.dot_general(
        first, second, ((over[:1], over[1:]), ((), ())), preferred_element_type=jnp.float32
    )


def swapped(value, focus, left, right):
    lane = lax.broadcasted_iota(jnp.int32, value.shape, 1)
    sign = jnp.where(lane < focus, jnp.float32(left), jnp.float32(right))
    return pltpu.roll(value, focus, 1) * sign


def tile_kern(kern, wave, tile):
    real, imag = kern[wave, 0, tile], kern[wave, 1, tile]
    return jnp.concatenate([real, imag], axis=0), jnp.concatenate([-imag, real], axis=0)


def in_block(shape, block, width):
    lane = lax.broadcasted_iota(jnp.int32, shape, len(shape) - 1)
    return (lane >= block * width) & (lane < (block + 1) * width)


def side_by_side(first, second, block, blocks):
    width = first.shape[-1] // blocks
    first, second = first.astype(jnp.float32), second.astype(jnp.float32)
    beside = in_block(first.shape, lax.rem(block + 1, blocks), width)
    moved = jnp.where(beside, pltpu.roll(second, width, first.ndim - 1), 0.0)
    return jnp.where(in_block(first.shape, block, width), first, moved).astype(jnp.bfloat16)


def over_tiles(tiles, body, init):
    return lax.fori_loop(0, tiles, body, init, unroll=tiles <= 8)


def live_rows(count, shape):
    height = shape[-2]
    row = lax.axis_index("gy") * height + lax.broadcasted_iota(jnp.int32, shape, len(shape) - 2)
    return row < count


def one_block(value, block, blocks):
    width = value.shape[1] // blocks
    picked = value[:, :width]
    for index in range(1, blocks):
        picked = jnp.where(block == index, value[:, index * width : (index + 1) * width], picked)
    return picked


def share_kernel(rows_far, field_far, kern_far, share, field, kern, counts, rows, arrived):
    waves, polars, _, tiles, height, side = field.shape
    focus = kern.shape[3]
    copies = {
        0: pltpu.make_async_copy(rows_far, rows, arrived.at[0]),
    }
    for wave in range(waves):
        for part in range(2):
            copies["kern", wave, part] = pltpu.make_async_copy(
                kern_far.at[wave, part], kern.at[wave, part], arrived.at[len(copies)]
            )
        for polar in range(polars):
            copies["field", wave, polar] = pltpu.make_async_copy(
                field_far.at[wave, polar, :, 0], field.at[wave, polar], arrived.at[len(copies)]
            )
    for copy in copies.values():
        copy.start()
    tile_row = lax.axis_index("gx")
    block = lax.axis_index("gy")
    copies[0].wait()
    inner = []
    own = []
    for wave in range(waves):
        for part in range(2):
            copies["kern", wave, part].wait()
        value = jnp.concatenate([kern[wave, part, tile_row] for part in range(2)], axis=0)
        value = one_block(value.astype(jnp.float32), block, side // height)
        own.append(jnp.concatenate([value, value], axis=1).astype(kern.dtype))
        for polar in range(polars):
            copies["field", wave, polar].wait()

        def add_tile(tile, value):
            live = live_rows(rows[0, tile], (polars, height, side))
            planes = [
                jnp.where(live, field[wave, :, part, tile], jnp.zeros((), field.dtype))
                for part in range(2)
            ]
            planes = [plane.reshape(polars * height, side) for plane in planes]
            return value + dot(
                jnp.concatenate(planes, axis=1),
                jnp.concatenate(tile_kern(kern, wave, tile), axis=1),
                (1, 1),
            )

        zero = jnp.zeros((polars * height, 2 * focus), jnp.float32)
        inner.append(over_tiles(tiles, add_tile, zero))
    for wave in range(waves):
        value = [
            inner[wave][polar * height : (polar + 1) * height] for polar in range(polars)
        ]
        terms = jnp.concatenate(two_terms(jnp.concatenate(value, axis=1)), axis=0)
        both = dot(own[wave], terms, (1, 0))
        for polar in range(polars):
            lanes = slice(polar * 2 * focus, (polar + 1) * 2 * focus)
            straight, crossed = both[:focus, lanes], both[focus:, lanes]
            share[wave, polar] = (straight + swapped(crossed, focus, -1, 1)).astype(share.dtype)

    def put_count(tile, carry):
        counts[tile] = jnp.full(counts.shape[1:], rows[0, tile], jnp.int32)
        return carry

    over_tiles(tiles, put_count, 0)


def strip_kernel(field, kern, counts, own_kern, both_kern, strip_kern, *strips):
    waves, polars, _, tiles, height, side = field.shape
    blocks = side // height
    block = lax.axis_index("gy")
    tile_row = lax.axis_index("gx")
    for wave in range(waves):
        for part in range(2):
            turned = kern[wave, part, tile_row].astype(jnp.float32).T.astype(kern.dtype)
            own_kern[wave, pl.ds(part * side, side)] = jnp.concatenate([turned, turned], axis=1)

    def one_tile(tile, carry):
        live = live_rows(counts[tile, :1], (height, side))
        for wave in range(waves):
            parts = tile_kern(kern, wave, tile)
            both_kern[wave, tile] = jnp.concatenate(parts, axis=1)
            strip_kern[wave, tile] = side_by_side(*parts, block, blocks)
            for polar in range(polars):
                for distance, strip in enumerate(strips):
                    both = side_by_side(
                        field[wave, polar, 0, tile],
                        field[wave, polar, 1, tile],
                        block ^ distance,
                        blocks,
                    )
                    strip[wave, polar, tile] = jnp.where(live, both, jnp.zeros((), both.dtype))
        return carry

    over_tiles(tiles, one_tile, 0)


def twice(value):
    return jnp.concatenate([value, value], axis=0)


def crossed_kernel(scale, blocks, own_kern, strip_kern, target, *refs):
    strips, refs = refs[:blocks], refs[blocks:]
    shares, (powers, sides, crossed, rowside, whole, turned) = refs[:-6], refs[-6:]
    waves, polars, tiles, height, side = strips[0].shape
    focus = target.shape[1]
    block = lax.axis_index("gy")
    for wave in range(waves):
        focal = [
            total([share[wave, polar].astype(jnp.float32) for share in shares])
            for polar in range(polars)
        ]
        power = sum(value * value for value in focal)
        powers[wave] = power
        power = power + pltpu.roll(power, focus, 1)
        goal = target[wave]
        excess = power - jnp.concatenate([goal, goal], axis=1)
        source = jnp.concatenate([excess * value for value in focal], axis=1)
        terms = jnp.concatenate(two_terms(source), axis=0)
        rowside[wave] = dot(own_kern[wave], terms, (1, 0))
    near = []
    for wave in range(waves):
        near.append([])
        for distance in range(blocks):
            first = pl.multiple_of((block ^ distance) * height, height)
            parts = []
            for polar in range(polars):
                lanes = pl.ds(polar * 2 * focus, 2 * focus)
                straight = rowside[wave, pl.ds(first, height), lanes]
                across = rowside[wave, pl.ds(side + first, height), lanes]
                parts.append(straight + swapped(across, focus, 1, -1))
            terms = two_terms(jnp.concatenate(parts, axis=0))
            near[wave].append(jnp.concatenate(terms, axis=1))
        sides[wave] = near[wave][0]

    def add_tile(distance, carry):
        tile = lax.axis_index("gx") ^ distance
        for index, strip in enumerate(strips):
            value = jnp.zeros((height, side), jnp.float32)
            for wave in range(waves):
                back = dot(near[wave][index], twice(strip_kern[wave, tile]), (1, 0))
                back = back.reshape(polars, height, side)
                for polar in range(polars):
                    value += back[polar] * strip[wave, polar, tile].astype(jnp.float32)
            first = pl.multiple_of((block ^ index) * height, height)
            whole[distance, pl.ds(first, height)] = (
                value + pltpu.roll(value, side - height, 1)
            ) * scale
        turned[distance] = whole[distance].T
        own = turned[distance, pl.ds(pl.multiple_of(block * height, height), height)]
        crossed[distance] = own.astype(crossed.dtype)
        return carry

    over_tiles(tiles, add_tile, 0)


def straight_kernel(scale, field, counts, both_kern, sides, gradient):
    waves, polars, _, tiles, height, side = field.shape

    def add_tile(distance, carry):
        tile = lax.axis_index("gx") ^ distance
        term = jnp.zeros((height, side), jnp.float32)
        for wave in range(waves):
            back = dot(sides[wave], twice(both_kern[wave, tile]), (1, 0))
            back = back.reshape(polars, height, 2 * side)
            for polar in range(polars):
                for part in range(2):
                    plane = field[wave, polar, part, tile].astype(jnp.float32)
                    term += back[polar, :, part * side : (part + 1) * side] * plane
        live = live_rows(counts[tile, :1], (height, side))
        gradient[distance] = jnp.where(live, term * scale, 0.0)
        return carry

    over_tiles(tiles, add_tile, 0)


def call(kernel, out_shape, scratch, args, spaces):
    return pl.pallas_call(
        kernel,
        out_shape=out_shape,
        in_specs=[pl.BlockSpec(memory_space=space) for space in spaces],
        out_specs=[pl.BlockSpec(memory_space=pltpu.VMEM)] * len(out_shape),
        scratch_shapes=scratch,
        compiler_params=pltpu.CompilerParams(vmem_limit_bytes=VMEM),
    )(*args)


def pairs(count, distance):
    return [(device, device ^ distance) for device in range(count)]


def partners(value, axis, count):
    came = {d: lax.ppermute(value(d), axis, pairs(count, d)) for d in range(count - 1, 0, -1)}
    return [came[d] for d in range(1, count)]


def crosswise(value, mesh):
    count, cores = mesh.shape["gx"], mesh.shape["wa"]

    def routes(distance):
        odd = distance % 2 == 1
        return [
            (
                device * cores + core,
                (device ^ distance) * cores + (cores - 1 - core if odd else core),
            )
            for device in range(count)
            for core in range(cores)
        ]

    came = {d: lax.ppermute(value(d), ("gx", "wa"), routes(d)) for d in range(count - 1, 0, -1)}
    return [came[d] for d in range(1, count)]


def total(terms):
    while len(terms) > 1:
        terms = [first + second for first, second in zip(terms[::2], terms[1::2])]
    return terms[0]


def rounded(value):
    return lax.reduce_precision(value, 8, 7)


def in_order(came, me):
    count = came.shape[0]
    rest = came.shape[1:]
    bit = 1
    while bit < count:
        split = came.reshape((count // (2 * bit), 2, bit) + rest)
        came = jnp.where((me & bit) != 0, split[:, ::-1], split).reshape((count,) + rest)
        bit *= 2
    return came


def make(mesh):
    count_x = mesh.shape["gx"]
    count_y = mesh.shape["gy"]

    def on_device(field, active_rows, kern, target):
        tile_row = lax.axis_index("gx")
        waves, polars = field.shape[0], field.shape[1]
        tiles = field.shape[4]
        rows_dev = field.shape[5]
        side = field.shape[6]
        focus = kern.shape[3]
        shape = (waves, polars, focus, 2 * focus)
        share, near_field, near_kern, counts = call(
            share_kernel,
            [
                jax.ShapeDtypeStruct(shape, jnp.bfloat16),
                jax.ShapeDtypeStruct(field.shape[:3] + field.shape[4:], field.dtype),
                jax.ShapeDtypeStruct(kern.shape, kern.dtype),
                jax.ShapeDtypeStruct((tiles, 8, side), jnp.int32),
            ],
            [
                pltpu.SMEM(active_rows.shape, jnp.int32),
                pltpu.SemaphoreType.DMA(((2 + polars) * waves + 1,)),
            ],
            [
                pltpu.with_memory_space_constraint(operand, pltpu.HBM)
                for operand in (active_rows, field, kern)
            ],
            [pltpu.HBM] * 3,
        )
        shares = [share] + partners(lambda d: share, "gy", count_y)
        share = total([term.astype(jnp.float32) for term in shares]).astype(jnp.bfloat16)
        strip_shape = (waves, polars, tiles, rows_dev, side)
        own_kern, both_kern, strip_kern, own_strip, *strips = call(
            strip_kernel,
            [
                jax.ShapeDtypeStruct((waves, 2 * side, 2 * focus), kern.dtype),
                jax.ShapeDtypeStruct((waves, tiles, 2 * focus, 2 * side), kern.dtype),
                jax.ShapeDtypeStruct((waves, tiles, 2 * focus, side), kern.dtype),
            ]
            + [jax.ShapeDtypeStruct(strip_shape, field.dtype)] * count_y,
            [],
            (near_field, near_kern, counts),
            [pltpu.VMEM] * 3,
        )
        strips = partners(lambda d: strips[d - 1], "gy", count_y)
        shares = [share] + partners(lambda d: share, "gx", count_x)
        shares = shares[::-1]
        shape = (tiles, rows_dev, side)
        scale = tiles * side / focus
        powers, sides, crossed = call(
            functools.partial(crossed_kernel, scale, count_y),
            [
                jax.ShapeDtypeStruct((waves, focus, 2 * focus), jnp.float32),
                jax.ShapeDtypeStruct((waves, polars * rows_dev, 4 * focus), jnp.bfloat16),
                jax.ShapeDtypeStruct(shape, jnp.bfloat16),
            ],
            [pltpu.VMEM((waves, 2 * side, polars * 2 * focus), jnp.float32)]
            + [pltpu.VMEM((tiles, side, side), jnp.float32)] * 2,
            (own_kern, strip_kern, target, own_strip, *strips, *shares),
            [pltpu.VMEM] * (3 + count_x + count_y),
        )
        (gradient,) = call(
            functools.partial(straight_kernel, scale),
            [jax.ShapeDtypeStruct(shape, jnp.float32)],
            [],
            (near_field, counts, both_kern, sides),
            [pltpu.VMEM] * 4,
        )
        came = [crossed[0]] + crosswise(lambda d: crossed[d], mesh)
        own = rounded(gradient + jnp.stack(came).astype(jnp.float32))
        other = lax.ppermute(own.astype(jnp.bfloat16), "wa", pairs(2, 1))
        design_grad = in_order(0.5 * (own + other.astype(jnp.float32)), tile_row)
        intensity = powers[:, :, :focus] + powers[:, :, focus:]
        return (design_grad[None], intensity)

    return on_device


def solution(mesh):
    placed = (
        P("wa", "cand", None, "gx", None, "gy", None),
        P("gx", None),
        P("wa", None, None, None, None),
        P("wa", None, None),
    )
    return jax.shard_map(
        make(mesh),
        mesh=mesh,
        in_specs=placed,
        out_specs=(P("gx", "cand", "gy", None), P("wa", "cand", None)),
        check_vma=False,
    )
```

```python
import functools

import jax
import jax.numpy as jnp
from jax import lax
from jax.experimental import pallas as pl
from jax.experimental.pallas import tpu as pltpu
from jax.sharding import PartitionSpec as P

VMEM = 16 * 2**20


def two_terms(value):
    high = value.astype(jnp.bfloat16)
    return high, (value - high.astype(jnp.float32)).astype(jnp.bfloat16)


def dot(first, second, over):
    return lax.dot_general(
        first, second, ((over[:1], over[1:]), ((), ())), preferred_element_type=jnp.float32
    )


def swapped(value, focus, left, right):
    lane = lax.broadcasted_iota(jnp.int32, value.shape, 1)
    sign = jnp.where(lane < focus, jnp.float32(left), jnp.float32(right))
    return pltpu.roll(value, focus, 1) * sign


def tile_kern(kern, wave, tile):
    real, imag = kern[wave, 0, tile], kern[wave, 1, tile]
    return jnp.concatenate([real, imag], axis=0), jnp.concatenate([-imag, real], axis=0)


def in_block(shape, block, width):
    lane = lax.broadcasted_iota(jnp.int32, shape, len(shape) - 1)
    return (lane >= block * width) & (lane < (block + 1) * width)


def side_by_side(first, second, block, blocks):
    width = first.shape[-1] // blocks
    first, second = first.astype(jnp.float32), second.astype(jnp.float32)
    beside = in_block(first.shape, lax.rem(block + 1, blocks), width)
    moved = jnp.where(beside, pltpu.roll(second, width, first.ndim - 1), 0.0)
    return jnp.where(in_block(first.shape, block, width), first, moved).astype(jnp.bfloat16)


def over_tiles(tiles, body, init):
    return lax.fori_loop(0, tiles, body, init, unroll=tiles <= 8)


def live_rows(count, shape):
    height = shape[-2]
    row = lax.axis_index("gy") * height + lax.broadcasted_iota(jnp.int32, shape, len(shape) - 2)
    return row < count


def share_kernel(rows_far, field_far, kern_far, share, field, kern, counts, rows, spread, arrived):
    waves, polars, _, tiles, height, side = field.shape
    focus = kern.shape[3]
    copies = [pltpu.make_async_copy(rows_far, rows, arrived.at[2 * waves])]
    for wave in range(waves):
        copies += [
            pltpu.make_async_copy(kern_far.at[wave], kern.at[wave], arrived.at[2 * wave]),
            pltpu.make_async_copy(
                field_far.at[wave, :, :, 0], field.at[wave], arrived.at[2 * wave + 1]
            ),
        ]
    for copy in copies:
        copy.start()
    tile_row = lax.axis_index("gx")
    first = pl.multiple_of(lax.axis_index("gy") * height, height)
    spread[...] = jnp.zeros_like(spread)
    copies[0].wait()
    inner = []
    for wave in range(waves):
        copies[2 * wave + 1].wait()
        copies[2 * wave + 2].wait()

        def add_tile(tile, value):
            live = live_rows(rows[0, tile], (polars, height, side))
            planes = [
                jnp.where(live, field[wave, :, part, tile], jnp.zeros((), field.dtype))
                for part in range(2)
            ]
            planes = [plane.reshape(polars * height, side) for plane in planes]
            return value + dot(
                jnp.concatenate(planes, axis=1),
                jnp.concatenate(tile_kern(kern, wave, tile), axis=1),
                (1, 1),
            )

        zero = jnp.zeros((polars * height, 2 * focus), jnp.float32)
        inner.append(over_tiles(tiles, add_tile, zero))
    for wave in range(waves):
        for polar in range(polars):
            lanes = pl.ds(polar * 2 * focus, 2 * focus)
            terms = two_terms(inner[wave][polar * height : (polar + 1) * height])
            for index, term in enumerate(terms):
                spread[wave, pl.ds(index * side + first, height), lanes] = term
        own = tile_kern(kern, wave, tile_row)[0]
        both = dot(jnp.concatenate([own, own], axis=1), spread[wave], (1, 0))
        for polar in range(polars):
            lanes = slice(polar * 2 * focus, (polar + 1) * 2 * focus)
            straight, crossed = both[:focus, lanes], both[focus:, lanes]
            share[wave, polar] = (straight + swapped(crossed, focus, -1, 1)).astype(share.dtype)

    def put_count(tile, carry):
        counts[tile] = jnp.full(counts.shape[1:], rows[0, tile], jnp.int32)
        return carry

    over_tiles(tiles, put_count, 0)


def strip_kernel(field, kern, counts, own_kern, both_kern, strip_kern, *strips):
    waves, polars, _, tiles, height, side = field.shape
    blocks = side // height
    block = lax.axis_index("gy")
    tile_row = lax.axis_index("gx")
    for wave in range(waves):
        for part in range(2):
            turned = kern[wave, part, tile_row].astype(jnp.float32).T.astype(kern.dtype)
            own_kern[wave, pl.ds(part * side, side)] = jnp.concatenate([turned, turned], axis=1)

    def one_tile(tile, carry):
        live = live_rows(counts[tile, :1], (height, side))
        for wave in range(waves):
            parts = tile_kern(kern, wave, tile)
            both_kern[wave, tile] = jnp.concatenate(parts, axis=1)
            strip_kern[wave, tile] = side_by_side(*parts, block, blocks)
            for polar in range(polars):
                for distance, strip in enumerate(strips):
                    both = side_by_side(
                        field[wave, polar, 0, tile],
                        field[wave, polar, 1, tile],
                        block ^ distance,
                        blocks,
                    )
                    strip[wave, polar, tile] = jnp.where(live, both, jnp.zeros((), both.dtype))
        return carry

    over_tiles(tiles, one_tile, 0)


def twice(value):
    return jnp.concatenate([value, value], axis=0)


def crossed_kernel(scale, blocks, own_kern, strip_kern, target, *refs):
    strips, refs = refs[:blocks], refs[blocks:]
    shares, (powers, sides, crossed, rowside, whole) = refs[:-5], refs[-5:]
    waves, polars, tiles, height, side = strips[0].shape
    focus = target.shape[1]
    block = lax.axis_index("gy")
    for wave in range(waves):
        focal = [
            total([share[wave, polar].astype(jnp.float32) for share in shares])
            for polar in range(polars)
        ]
        power = sum(value * value for value in focal)
        powers[wave] = power
        power = power + pltpu.roll(power, focus, 1)
        goal = target[wave]
        excess = power - jnp.concatenate([goal, goal], axis=1)
        source = jnp.concatenate([excess * value for value in focal], axis=1)
        terms = jnp.concatenate(two_terms(source), axis=0)
        rowside[wave] = dot(own_kern[wave], terms, (1, 0))
    near = []
    for wave in range(waves):
        near.append([])
        for distance in range(blocks):
            first = pl.multiple_of((block ^ distance) * height, height)
            parts = []
            for polar in range(polars):
                lanes = pl.ds(polar * 2 * focus, 2 * focus)
                straight = rowside[wave, pl.ds(first, height), lanes]
                across = rowside[wave, pl.ds(side + first, height), lanes]
                parts.append(straight + swapped(across, focus, 1, -1))
            terms = two_terms(jnp.concatenate(parts, axis=0))
            near[wave].append(jnp.concatenate(terms, axis=1))
        sides[wave] = near[wave][0]

    lane = lax.broadcasted_iota(jnp.int32, (height, side), 1)
    row = lax.broadcasted_iota(jnp.int32, (height, side), 0)
    pick = jnp.where(lane == row + block * height, 1.0, 0.0).astype(whole.dtype)

    def add_tile(distance, carry):
        tile = lax.axis_index("gx") ^ distance
        for index, strip in enumerate(strips):
            value = jnp.zeros((height, side), jnp.float32)
            for wave in range(waves):
                back = dot(near[wave][index], twice(strip_kern[wave, tile]), (1, 0))
                back = back.reshape(polars, height, side)
                for polar in range(polars):
                    value += back[polar] * strip[wave, polar, tile].astype(jnp.float32)
            first = pl.multiple_of((block ^ index) * height, height)
            value = (value + pltpu.roll(value, side - height, 1)) * scale
            whole[distance, pl.ds(first, height)] = value.astype(whole.dtype)
        crossed[distance] = dot(pick, whole[distance], (1, 1)).astype(crossed.dtype)
        return carry

    over_tiles(tiles, add_tile, 0)


def straight_kernel(scale, field, counts, both_kern, sides, gradient):
    waves, polars, _, tiles, height, side = field.shape

    def add_tile(distance, carry):
        tile = lax.axis_index("gx") ^ distance
        term = jnp.zeros((height, side), jnp.float32)
        for wave in range(waves):
            back = dot(sides[wave], twice(both_kern[wave, tile]), (1, 0))
            back = back.reshape(polars, height, 2 * side)
            for polar in range(polars):
                for part in range(2):
                    plane = field[wave, polar, part, tile].astype(jnp.float32)
                    term += back[polar, :, part * side : (part + 1) * side] * plane
        live = live_rows(counts[tile, :1], (height, side))
        gradient[distance] = jnp.where(live, term * scale, 0.0)
        return carry

    over_tiles(tiles, add_tile, 0)


def call(kernel, out_shape, scratch, args, spaces):
    return pl.pallas_call(
        kernel,
        out_shape=out_shape,
        in_specs=[pl.BlockSpec(memory_space=space) for space in spaces],
        out_specs=[pl.BlockSpec(memory_space=pltpu.VMEM)] * len(out_shape),
        scratch_shapes=scratch,
        compiler_params=pltpu.CompilerParams(vmem_limit_bytes=VMEM),
    )(*args)


def pairs(count, distance):
    return [(device, device ^ distance) for device in range(count)]


def partners(value, axis, count):
    came = {d: lax.ppermute(value(d), axis, pairs(count, d)) for d in range(count - 1, 0, -1)}
    return [came[d] for d in range(1, count)]


def crosswise(value, mesh):
    count, cores = mesh.shape["gx"], mesh.shape["wa"]

    def routes(distance):
        odd = distance % 2 == 1
        return [
            (
                device * cores + core,
                (device ^ distance) * cores + (cores - 1 - core if odd else core),
            )
            for device in range(count)
            for core in range(cores)
        ]

    came = {d: lax.ppermute(value(d), ("gx", "wa"), routes(d)) for d in range(count - 1, 0, -1)}
    return [came[d] for d in range(1, count)]


def total(terms):
    while len(terms) > 1:
        terms = [first + second for first, second in zip(terms[::2], terms[1::2])]
    return terms[0]


def rounded(value):
    return lax.reduce_precision(value, 8, 7)


def in_order(came, me):
    count = came.shape[0]
    rest = came.shape[1:]
    bit = 1
    while bit < count:
        split = came.reshape((count // (2 * bit), 2, bit) + rest)
        came = jnp.where((me & bit) != 0, split[:, ::-1], split).reshape((count,) + rest)
        bit *= 2
    return came


def make(mesh):
    count_x = mesh.shape["gx"]
    count_y = mesh.shape["gy"]

    def on_device(field, active_rows, kern, target):
        tile_row = lax.axis_index("gx")
        waves, polars = field.shape[0], field.shape[1]
        tiles = field.shape[4]
        rows_dev = field.shape[5]
        side = field.shape[6]
        focus = kern.shape[3]
        shape = (waves, polars, focus, 2 * focus)
        share, near_field, near_kern, counts = call(
            share_kernel,
            [
                jax.ShapeDtypeStruct(shape, jnp.bfloat16),
                jax.ShapeDtypeStruct(field.shape[:3] + field.shape[4:], field.dtype),
                jax.ShapeDtypeStruct(kern.shape, kern.dtype),
                jax.ShapeDtypeStruct((tiles, 8, side), jnp.int32),
            ],
            [
                pltpu.SMEM(active_rows.shape, jnp.int32),
                pltpu.VMEM((waves, 2 * side, polars * 2 * focus), jnp.bfloat16),
                pltpu.SemaphoreType.DMA((2 * waves + 1,)),
            ],
            [
                pltpu.with_memory_space_constraint(operand, pltpu.HBM)
                for operand in (active_rows, field, kern)
            ],
            [pltpu.HBM] * 3,
        )
        shares = [share] + partners(lambda d: share, "gy", count_y)
        share = total([term.astype(jnp.float32) for term in shares]).astype(jnp.bfloat16)
        strip_shape = (waves, polars, tiles, rows_dev, side)
        own_kern, both_kern, strip_kern, own_strip, *strips = call(
            strip_kernel,
            [
                jax.ShapeDtypeStruct((waves, 2 * side, 2 * focus), kern.dtype),
                jax.ShapeDtypeStruct((waves, tiles, 2 * focus, 2 * side), kern.dtype),
                jax.ShapeDtypeStruct((waves, tiles, 2 * focus, side), kern.dtype),
            ]
            + [jax.ShapeDtypeStruct(strip_shape, field.dtype)] * count_y,
            [],
            (near_field, near_kern, counts),
            [pltpu.VMEM] * 3,
        )
        strips = partners(lambda d: strips[d - 1], "gy", count_y)
        shares = [share] + partners(lambda d: share, "gx", count_x)
        shares = shares[::-1]
        shape = (tiles, rows_dev, side)
        scale = tiles * side / focus
        powers, sides, crossed = call(
            functools.partial(crossed_kernel, scale, count_y),
            [
                jax.ShapeDtypeStruct((waves, focus, 2 * focus), jnp.float32),
                jax.ShapeDtypeStruct((waves, polars * rows_dev, 4 * focus), jnp.bfloat16),
                jax.ShapeDtypeStruct(shape, jnp.bfloat16),
            ],
            [pltpu.VMEM((waves, 2 * side, polars * 2 * focus), jnp.float32)]
            + [pltpu.VMEM((tiles, side, side), jnp.bfloat16)],
            (own_kern, strip_kern, target, own_strip, *strips, *shares),
            [pltpu.VMEM] * (3 + count_x + count_y),
        )
        (gradient,) = call(
            functools.partial(straight_kernel, scale),
            [jax.ShapeDtypeStruct(shape, jnp.float32)],
            [],
            (near_field, counts, both_kern, sides),
            [pltpu.VMEM] * 4,
        )
        came = [crossed[0]] + crosswise(lambda d: crossed[d], mesh)
        own = rounded(gradient + jnp.stack(came).astype(jnp.float32))
        other = lax.ppermute(own.astype(jnp.bfloat16), "wa", pairs(2, 1))
        design_grad = in_order(0.5 * (own + other.astype(jnp.float32)), tile_row)
        intensity = powers[:, :, :focus] + powers[:, :, focus:]
        return (design_grad[None], intensity)

    return on_device


def solution(mesh):
    placed = (
        P("wa", "cand", None, "gx", None, "gy", None),
        P("gx", None),
        P("wa", None, None, None, None),
        P("wa", None, None),
    )
    return jax.shard_map(
        make(mesh),
        mesh=mesh,
        in_specs=placed,
        out_specs=(P("gx", "cand", "gy", None), P("wa", "cand", None)),
        check_vma=False,
    )
```

```python
import functools

import jax
import jax.numpy as jnp
from jax import lax
from jax.experimental import pallas as pl
from jax.experimental.pallas import tpu as pltpu
from jax.sharding import PartitionSpec as P

VMEM = 16 * 2**20


def two_terms(value):
    high = value.astype(jnp.bfloat16)
    return high, (value - high.astype(jnp.float32)).astype(jnp.bfloat16)


def dot(first, second, over):
    return lax.dot_general(
        first, second, ((over[:1], over[1:]), ((), ())), preferred_element_type=jnp.float32
    )


def swapped(value, focus, left, right):
    lane = lax.broadcasted_iota(jnp.int32, value.shape, 1)
    sign = jnp.where(lane < focus, jnp.float32(left), jnp.float32(right))
    return pltpu.roll(value, focus, 1) * sign


def tile_kern(kern, wave, tile):
    real, imag = kern[wave, 0, tile], kern[wave, 1, tile]
    return jnp.concatenate([real, imag], axis=0), jnp.concatenate([-imag, real], axis=0)


def in_block(shape, block, width):
    lane = lax.broadcasted_iota(jnp.int32, shape, len(shape) - 1)
    return (lane >= block * width) & (lane < (block + 1) * width)


def side_by_side(first, second, block, blocks):
    width = first.shape[-1] // blocks
    first, second = first.astype(jnp.float32), second.astype(jnp.float32)
    beside = in_block(first.shape, lax.rem(block + 1, blocks), width)
    moved = jnp.where(beside, pltpu.roll(second, width, first.ndim - 1), 0.0)
    return jnp.where(in_block(first.shape, block, width), first, moved).astype(jnp.bfloat16)


def over_tiles(tiles, body, init):
    return lax.fori_loop(0, tiles, body, init, unroll=tiles <= 8)


def live_rows(count, shape):
    height = shape[-2]
    row = lax.axis_index("gy") * height + lax.broadcasted_iota(jnp.int32, shape, len(shape) - 2)
    return row < count


def share_kernel(rows_far, field_far, kern_far, share, field, kern, counts, rows, spread, arrived):
    waves, polars, _, tiles, height, side = field.shape
    focus = kern.shape[3]
    copies = [pltpu.make_async_copy(rows_far, rows, arrived.at[2 * waves])]
    for wave in range(waves):
        copies += [
            pltpu.make_async_copy(kern_far.at[wave], kern.at[wave], arrived.at[2 * wave]),
            pltpu.make_async_copy(
                field_far.at[wave, :, :, 0], field.at[wave], arrived.at[2 * wave + 1]
            ),
        ]
    for copy in copies:
        copy.start()
    tile_row = lax.axis_index("gx")
    first = pl.multiple_of(lax.axis_index("gy") * height, height)
    spread[...] = jnp.zeros_like(spread)
    copies[0].wait()
    inner = []
    for wave in range(waves):
        copies[2 * wave + 1].wait()
        copies[2 * wave + 2].wait()

        def add_tile(tile, value):
            live = live_rows(rows[0, tile], (polars, height, side))
            planes = [
                jnp.where(live, field[wave, :, part, tile], jnp.zeros((), field.dtype))
                for part in range(2)
            ]
            planes = [plane.reshape(polars * height, side) for plane in planes]
            return value + dot(
                jnp.concatenate(planes, axis=1),
                jnp.concatenate(tile_kern(kern, wave, tile), axis=1),
                (1, 1),
            )

        zero = jnp.zeros((polars * height, 2 * focus), jnp.float32)
        inner.append(over_tiles(tiles, add_tile, zero))
    for wave in range(waves):
        for polar in range(polars):
            lanes = pl.ds(polar * 2 * focus, 2 * focus)
            terms = two_terms(inner[wave][polar * height : (polar + 1) * height])
            for index, term in enumerate(terms):
                spread[wave, pl.ds(index * side + first, height), lanes] = term
        own = tile_kern(kern, wave, tile_row)[0]
        both = dot(jnp.concatenate([own, own], axis=1), spread[wave], (1, 0))
        for polar in range(polars):
            lanes = slice(polar * 2 * focus, (polar + 1) * 2 * focus)
            straight, crossed = both[:focus, lanes], both[focus:, lanes]
            share[wave, polar] = (straight + swapped(crossed, focus, -1, 1)).astype(share.dtype)

    def put_count(tile, carry):
        counts[tile] = jnp.full(counts.shape[1:], rows[0, tile], jnp.int32)
        return carry

    over_tiles(tiles, put_count, 0)


def strip_kernel(field, kern, counts, own_kern, both_kern, strip_kern, *strips):
    waves, polars, _, tiles, height, side = field.shape
    blocks = side // height
    block = lax.axis_index("gy")
    tile_row = lax.axis_index("gx")
    for wave in range(waves):
        for part in range(2):
            turned = kern[wave, part, tile_row].astype(jnp.float32).T.astype(kern.dtype)
            own_kern[wave, pl.ds(part * side, side)] = jnp.concatenate([turned, turned], axis=1)

    def one_tile(tile, carry):
        live = live_rows(counts[tile, :1], (height, side))
        for wave in range(waves):
            parts = tile_kern(kern, wave, tile)
            both_kern[wave, tile] = jnp.concatenate(parts, axis=1)
            strip_kern[wave, tile] = side_by_side(*parts, block, blocks)
            for polar in range(polars):
                for distance, strip in enumerate(strips):
                    both = side_by_side(
                        field[wave, polar, 0, tile],
                        field[wave, polar, 1, tile],
                        block ^ distance,
                        blocks,
                    )
                    strip[wave, polar, tile] = jnp.where(live, both, jnp.zeros((), both.dtype))
        return carry

    over_tiles(tiles, one_tile, 0)


def twice(value):
    return jnp.concatenate([value, value], axis=0)


def crossed_kernel(scale, blocks, own_kern, strip_kern, target, *refs):
    strips, refs = refs[:blocks], refs[blocks:]
    shares, (powers, sides, crossed, rowside, whole) = refs[:-5], refs[-5:]
    waves, polars, tiles, height, side = strips[0].shape
    focus = target.shape[1]
    block = lax.axis_index("gy")
    for wave in range(waves):
        focal = [
            total([share[wave, polar].astype(jnp.float32) for share in shares])
            for polar in range(polars)
        ]
        power = sum(value * value for value in focal)
        powers[wave] = power
        power = power + pltpu.roll(power, focus, 1)
        goal = target[wave]
        excess = power - jnp.concatenate([goal, goal], axis=1)
        source = jnp.concatenate([excess * value for value in focal], axis=1)
        terms = jnp.concatenate(two_terms(source), axis=0)
        rowside[wave] = dot(own_kern[wave], terms, (1, 0))
    near = []
    for wave in range(waves):
        near.append([])
        for distance in range(blocks):
            first = pl.multiple_of((block ^ distance) * height, height)
            parts = []
            for polar in range(polars):
                lanes = pl.ds(polar * 2 * focus, 2 * focus)
                straight = rowside[wave, pl.ds(first, height), lanes]
                across = rowside[wave, pl.ds(side + first, height), lanes]
                parts.append(straight + swapped(across, focus, 1, -1))
            terms = two_terms(jnp.concatenate(parts, axis=0))
            near[wave].append(jnp.concatenate(terms, axis=1))
        sides[wave] = near[wave][0]

    lane = lax.broadcasted_iota(jnp.int32, (height, side), 1)

    def add_tiles(group, carry):
        for index, strip in enumerate(strips):
            rows = None
            for at in range(blocks):
                tile = lax.axis_index("gx") ^ (group * blocks + at)
                value = jnp.zeros((height, side), jnp.float32)
                for wave in range(waves):
                    back = dot(near[wave][index], twice(strip_kern[wave, tile]), (1, 0))
                    back = back.reshape(polars, height, side)
                    for polar in range(polars):
                        value += back[polar] * strip[wave, polar, tile].astype(jnp.float32)
                value = sum(pltpu.roll(value, turn * height, 1) for turn in range(blocks))
                rows = value if rows is None else jnp.where(lane < at * height, rows, value)
            first = pl.multiple_of((block ^ index) * height, height)
            whole[group, pl.ds(first, height)] = rows * scale
        turned = whole[group].T
        for at in range(blocks):
            own = turned[at * height : (at + 1) * height]
            crossed[group * blocks + at] = own.astype(crossed.dtype)
        return carry

    over_tiles(tiles // blocks, add_tiles, 0)


def straight_kernel(scale, field, counts, both_kern, sides, gradient):
    waves, polars, _, tiles, height, side = field.shape

    def add_tile(distance, carry):
        tile = lax.axis_index("gx") ^ distance
        term = jnp.zeros((height, side), jnp.float32)
        for wave in range(waves):
            back = dot(sides[wave], twice(both_kern[wave, tile]), (1, 0))
            back = back.reshape(polars, height, 2 * side)
            for polar in range(polars):
                for part in range(2):
                    plane = field[wave, polar, part, tile].astype(jnp.float32)
                    term += back[polar, :, part * side : (part + 1) * side] * plane
        live = live_rows(counts[tile, :1], (height, side))
        gradient[distance] = jnp.where(live, term * scale, 0.0)
        return carry

    over_tiles(tiles, add_tile, 0)


def call(kernel, out_shape, scratch, args, spaces):
    return pl.pallas_call(
        kernel,
        out_shape=out_shape,
        in_specs=[pl.BlockSpec(memory_space=space) for space in spaces],
        out_specs=[pl.BlockSpec(memory_space=pltpu.VMEM)] * len(out_shape),
        scratch_shapes=scratch,
        compiler_params=pltpu.CompilerParams(vmem_limit_bytes=VMEM),
    )(*args)


def pairs(count, distance):
    return [(device, device ^ distance) for device in range(count)]


def partners(value, axis, count):
    came = {d: lax.ppermute(value(d), axis, pairs(count, d)) for d in range(count - 1, 0, -1)}
    return [came[d] for d in range(1, count)]


def crosswise(value, mesh):
    count, cores = mesh.shape["gx"], mesh.shape["wa"]

    def routes(distance):
        odd = distance % 2 == 1
        return [
            (
                device * cores + core,
                (device ^ distance) * cores + (cores - 1 - core if odd else core),
            )
            for device in range(count)
            for core in range(cores)
        ]

    came = {d: lax.ppermute(value(d), ("gx", "wa"), routes(d)) for d in range(count - 1, 0, -1)}
    return [came[d] for d in range(1, count)]


def total(terms):
    while len(terms) > 1:
        terms = [first + second for first, second in zip(terms[::2], terms[1::2])]
    return terms[0]


def rounded(value):
    return lax.reduce_precision(value, 8, 7)


def in_order(came, me):
    count = came.shape[0]
    rest = came.shape[1:]
    bit = 1
    while bit < count:
        split = came.reshape((count // (2 * bit), 2, bit) + rest)
        came = jnp.where((me & bit) != 0, split[:, ::-1], split).reshape((count,) + rest)
        bit *= 2
    return came


def make(mesh):
    count_x = mesh.shape["gx"]
    count_y = mesh.shape["gy"]

    def on_device(field, active_rows, kern, target):
        tile_row = lax.axis_index("gx")
        waves, polars = field.shape[0], field.shape[1]
        tiles = field.shape[4]
        rows_dev = field.shape[5]
        side = field.shape[6]
        focus = kern.shape[3]
        shape = (waves, polars, focus, 2 * focus)
        share, near_field, near_kern, counts = call(
            share_kernel,
            [
                jax.ShapeDtypeStruct(shape, jnp.bfloat16),
                jax.ShapeDtypeStruct(field.shape[:3] + field.shape[4:], field.dtype),
                jax.ShapeDtypeStruct(kern.shape, kern.dtype),
                jax.ShapeDtypeStruct((tiles, 8, side), jnp.int32),
            ],
            [
                pltpu.SMEM(active_rows.shape, jnp.int32),
                pltpu.VMEM((waves, 2 * side, polars * 2 * focus), jnp.bfloat16),
                pltpu.SemaphoreType.DMA((2 * waves + 1,)),
            ],
            [
                pltpu.with_memory_space_constraint(operand, pltpu.HBM)
                for operand in (active_rows, field, kern)
            ],
            [pltpu.HBM] * 3,
        )
        shares = [share] + partners(lambda d: share, "gy", count_y)
        share = total([term.astype(jnp.float32) for term in shares]).astype(jnp.bfloat16)
        strip_shape = (waves, polars, tiles, rows_dev, side)
        own_kern, both_kern, strip_kern, own_strip, *strips = call(
            strip_kernel,
            [
                jax.ShapeDtypeStruct((waves, 2 * side, 2 * focus), kern.dtype),
                jax.ShapeDtypeStruct((waves, tiles, 2 * focus, 2 * side), kern.dtype),
                jax.ShapeDtypeStruct((waves, tiles, 2 * focus, side), kern.dtype),
            ]
            + [jax.ShapeDtypeStruct(strip_shape, field.dtype)] * count_y,
            [],
            (near_field, near_kern, counts),
            [pltpu.VMEM] * 3,
        )
        strips = partners(lambda d: strips[d - 1], "gy", count_y)
        shares = [share] + partners(lambda d: share, "gx", count_x)
        shares = shares[::-1]
        shape = (tiles, rows_dev, side)
        scale = tiles * side / focus
        powers, sides, crossed = call(
            functools.partial(crossed_kernel, scale, count_y),
            [
                jax.ShapeDtypeStruct((waves, focus, 2 * focus), jnp.float32),
                jax.ShapeDtypeStruct((waves, polars * rows_dev, 4 * focus), jnp.bfloat16),
                jax.ShapeDtypeStruct(shape, jnp.bfloat16),
            ],
            [pltpu.VMEM((waves, 2 * side, polars * 2 * focus), jnp.float32)]
            + [pltpu.VMEM((tiles // count_y, side, side), jnp.float32)],
            (own_kern, strip_kern, target, own_strip, *strips, *shares),
            [pltpu.VMEM] * (3 + count_x + count_y),
        )
        (gradient,) = call(
            functools.partial(straight_kernel, scale),
            [jax.ShapeDtypeStruct(shape, jnp.float32)],
            [],
            (near_field, counts, both_kern, sides),
            [pltpu.VMEM] * 4,
        )
        came = [crossed[0]] + crosswise(lambda d: crossed[d], mesh)
        own = rounded(gradient + jnp.stack(came).astype(jnp.float32))
        other = lax.ppermute(own.astype(jnp.bfloat16), "wa", pairs(2, 1))
        design_grad = in_order(0.5 * (own + other.astype(jnp.float32)), tile_row)
        intensity = powers[:, :, :focus] + powers[:, :, focus:]
        return (design_grad[None], intensity)

    return on_device


def solution(mesh):
    placed = (
        P("wa", "cand", None, "gx", None, "gy", None),
        P("gx", None),
        P("wa", None, None, None, None),
        P("wa", None, None),
    )
    return jax.shard_map(
        make(mesh),
        mesh=mesh,
        in_specs=placed,
        out_specs=(P("gx", "cand", "gy", None), P("wa", "cand", None)),
        check_vma=False,
    )
```

```python
import functools

import jax
import jax.numpy as jnp
from jax import lax
from jax.experimental import pallas as pl
from jax.experimental.pallas import tpu as pltpu
from jax.sharding import PartitionSpec as P

VMEM = 16 * 2**20


def two_terms(value):
    high = value.astype(jnp.bfloat16)
    return high, (value - high.astype(jnp.float32)).astype(jnp.bfloat16)


def dot(first, second, over):
    return lax.dot_general(
        first, second, ((over[:1], over[1:]), ((), ())), preferred_element_type=jnp.float32
    )


def tile_kern(kern, wave, tile):
    real, imag = kern[wave, 0, tile], kern[wave, 1, tile]
    return jnp.concatenate([real, imag], axis=0), jnp.concatenate([-imag, real], axis=0)


def one_block(value, block, blocks):
    width = value.shape[1] // blocks
    picked = value[:, :width]
    for index in range(1, blocks):
        picked = jnp.where(block == index, value[:, index * width : (index + 1) * width], picked)
    return picked


def turn(value):
    width = value.shape[1]
    row = lax.broadcasted_iota(jnp.int32, (width, width), 0)
    column = lax.broadcasted_iota(jnp.int32, (width, width), 1)
    unit = jnp.where(row == column, 1.0, 0.0).astype(value.dtype)
    return dot(unit, value, (1, 1)).astype(value.dtype)


def twice(value, axis):
    return jnp.concatenate([value, value], axis=axis)


def diagonal(value, count):
    zero = jnp.zeros_like(value)
    rows = [
        jnp.concatenate([value if index == other else zero for other in range(count)], axis=1)
        for index in range(count)
    ]
    return jnp.concatenate(rows, axis=0)


def over_tiles(tiles, body, init):
    return lax.fori_loop(0, tiles, body, init, unroll=tiles <= 8)


def live_rows(count, shape):
    height = shape[-2]
    row = lax.axis_index("gy") * height + lax.broadcasted_iota(jnp.int32, shape, len(shape) - 2)
    return row < count


def share_kernel(rows_far, field_far, kern_far, share, field, kern, counts, rows, arrived):
    waves, polars, _, tiles, height, side = field.shape
    focus = kern.shape[3]
    copies = [pltpu.make_async_copy(rows_far, rows, arrived.at[2 * waves])]
    for wave in range(waves):
        copies += [
            pltpu.make_async_copy(kern_far.at[wave], kern.at[wave], arrived.at[2 * wave]),
            pltpu.make_async_copy(
                field_far.at[wave, :, :, 0], field.at[wave], arrived.at[2 * wave + 1]
            ),
        ]
    for copy in copies:
        copy.start()
    tile_row = lax.axis_index("gx")
    block = lax.axis_index("gy")
    copies[0].wait()
    inner = []
    own = []
    for wave in range(waves):
        copies[2 * wave + 1].wait()
        parts = []
        for part in range(2):
            value = kern[wave, part, tile_row].astype(jnp.float32)
            parts.append(diagonal(one_block(value, block, side // height), polars))
        own.append(twice(jnp.concatenate(parts, axis=0).astype(kern.dtype), 1))
        copies[2 * wave + 2].wait()

        def add_tile(tile, value):
            live = live_rows(rows[0, tile], (polars, height, side))
            planes = [
                jnp.where(live, field[wave, :, part, tile], jnp.zeros((), field.dtype))
                for part in range(2)
            ]
            planes = [plane.reshape(polars * height, side) for plane in planes]
            return value + dot(
                jnp.concatenate(tile_kern(kern, wave, tile), axis=1),
                jnp.concatenate(planes, axis=1),
                (1, 1),
            )

        zero = jnp.zeros((2 * focus, polars * height), jnp.float32)
        inner.append(over_tiles(tiles, add_tile, zero))
    for wave in range(waves):
        both = dot(jnp.concatenate(two_terms(inner[wave]), axis=1), own[wave], (1, 1))
        real, imag = both[:, : polars * focus], both[:, polars * focus :]
        focal = [real[:focus] - imag[focus:], real[focus:] + imag[:focus]]
        share[wave] = jnp.concatenate(focal, axis=0).astype(share.dtype)

    def put_count(tile, carry):
        counts[tile] = jnp.full(counts.shape[1:], rows[0, tile], jnp.int32)
        return carry

    over_tiles(tiles, put_count, 0)


def turned_strip(planes, block, blocks):
    rows = [
        jnp.concatenate([one_block(plane, block, blocks) for plane in pair], axis=1)
        for pair in planes
    ]
    return turn(jnp.concatenate(rows, axis=0).astype(jnp.bfloat16))


def live_planes(field, counts, wave, tile):
    polars, height, side = field.shape[1], field.shape[4], field.shape[5]
    live = live_rows(counts[tile, :1], (height, side))
    return [
        [
            jnp.where(live, field[wave, polar, part, tile].astype(jnp.float32), 0.0)
            for part in range(2)
        ]
        for polar in range(polars)
    ]


def strip_kernel(field, counts, *strips):
    waves, _, _, tiles, height, side = field.shape
    blocks = side // height
    block = lax.axis_index("gy")

    def one_tile(tile, carry):
        for wave in range(waves):
            planes = live_planes(field, counts, wave, tile)
            for distance, strip in enumerate(strips, 1):
                strip[wave, tile] = turned_strip(planes, block ^ distance, blocks)
        return carry

    over_tiles(tiles, one_tile, 0)


def layout_kernel(field, kern, counts, target, goal, row_kern, turn_kern, both_kern, own_strip):
    waves, polars, _, tiles, height, side = field.shape
    blocks = side // height
    block = lax.axis_index("gy")
    tile_row = lax.axis_index("gx")
    for wave in range(waves):
        goal[wave] = jnp.concatenate([target[wave].T] * polars, axis=1)
        for part in range(2):
            value = kern[wave, part, tile_row].astype(jnp.float32)
            columns = [
                diagonal(one_block(value, block ^ distance, blocks), polars)
                for distance in range(blocks)
            ]
            rows = pl.ds(part * polars * value.shape[0], polars * value.shape[0])
            row_kern[wave, rows] = jnp.concatenate(columns, axis=1).astype(kern.dtype)

    def one_tile(tile, carry):
        for wave in range(waves):
            parts = tile_kern(kern, wave, tile)
            both_kern[wave, tile] = jnp.concatenate(parts, axis=1)
            parts = [one_block(part.astype(jnp.float32), block, blocks) for part in parts]
            turned = turn(jnp.concatenate(parts, axis=1).astype(kern.dtype))
            turn_kern[wave, tile] = twice(turned, 1)
            planes = live_planes(field, counts, wave, tile)
            own_strip[wave, tile] = turned_strip(planes, block, blocks)
        return carry

    over_tiles(tiles, one_tile, 0)


def crossed_kernel(scale, blocks, row_kern, turn_kern, goal, *refs):
    strips, refs = refs[:blocks], refs[blocks:]
    shares, (intensity, near, crossed) = refs[:-3], refs[-3:]
    waves, tiles, height, width = strips[0].shape
    height = height // 2
    polars = width // height
    focus = goal.shape[1]
    block = lax.axis_index("gy")
    sides = []
    for wave in range(waves):
        focal = total([share[wave].astype(jnp.float32) for share in shares])
        real, imag = focal[:focus], focal[focus:]
        power = real * real + imag * imag
        power = sum(pltpu.roll(power, polar * focus, 1) for polar in range(polars))
        intensity[wave] = power
        excess = power - goal[wave]
        real, imag = excess * real, excess * imag
        upright = jnp.concatenate([real, imag], axis=0)
        turned = jnp.concatenate([imag, -real], axis=0)
        terms = two_terms(jnp.concatenate([upright, turned], axis=1))
        row = dot(jnp.concatenate(terms, axis=1), twice(row_kern[wave], 0), (1, 0))
        sides.append(jnp.concatenate(two_terms(row), axis=0))
        near[wave] = sides[wave]

    def add_tile(distance, carry):
        tile = lax.axis_index("gx") ^ distance
        value = jnp.zeros((2 * height, blocks * width), jnp.float32)
        for wave in range(waves):
            back = dot(turn_kern[wave, tile], sides[wave], (1, 0))
            strip = jnp.concatenate([strip[wave, tile] for strip in strips], axis=1)
            value += back * strip.astype(jnp.float32)
        value = (value[:height] + value[height:]) * scale
        parts = []
        for apart in range(blocks):
            part = value[:, apart * width : (apart + 1) * width]
            parts.append(sum(part[:, at * height : (at + 1) * height] for at in range(polars)))
        columns = []
        for index in range(blocks):
            column = parts[0]
            for apart in range(1, blocks):
                column = jnp.where((block ^ apart) == index, parts[apart], column)
            columns.append(column)
        crossed[distance] = jnp.concatenate(columns, axis=1).astype(crossed.dtype)
        return carry

    over_tiles(tiles, add_tile, 0)


def straight_kernel(scale, field, counts, both_kern, near, gradient):
    waves, polars, _, tiles, height, side = field.shape
    sides = []
    for wave in range(waves):
        sides.append(turn(near[wave, :, : polars * height]))

    def add_tile(distance, carry):
        tile = lax.axis_index("gx") ^ distance
        term = jnp.zeros((height, side), jnp.float32)
        for wave in range(waves):
            back = dot(sides[wave], twice(both_kern[wave, tile], 0), (1, 0))
            back = back.reshape(polars, height, 2 * side)
            for polar in range(polars):
                for part in range(2):
                    plane = field[wave, polar, part, tile].astype(jnp.float32)
                    term += back[polar, :, part * side : (part + 1) * side] * plane
        live = live_rows(counts[tile, :1], (height, side))
        gradient[distance] = jnp.where(live, term * scale, 0.0)
        return carry

    over_tiles(tiles, add_tile, 0)


def call(kernel, out_shape, scratch, args, spaces):
    return pl.pallas_call(
        kernel,
        out_shape=out_shape,
        in_specs=[pl.BlockSpec(memory_space=space) for space in spaces],
        out_specs=[pl.BlockSpec(memory_space=pltpu.VMEM)] * len(out_shape),
        scratch_shapes=scratch,
        compiler_params=pltpu.CompilerParams(vmem_limit_bytes=VMEM),
    )(*args)


def pairs(count, distance):
    return [(device, device ^ distance) for device in range(count)]


def partners(value, axis, count):
    came = {d: lax.ppermute(value(d), axis, pairs(count, d)) for d in range(count - 1, 0, -1)}
    return [came[d] for d in range(1, count)]


def crosswise(value, mesh):
    count, cores = mesh.shape["gx"], mesh.shape["wa"]

    def routes(distance):
        odd = distance % 2 == 1
        return [
            (
                device * cores + core,
                (device ^ distance) * cores + (cores - 1 - core if odd else core),
            )
            for device in range(count)
            for core in range(cores)
        ]

    came = {d: lax.ppermute(value(d), ("gx", "wa"), routes(d)) for d in range(count - 1, 0, -1)}
    return [came[d] for d in range(1, count)]


def total(terms):
    while len(terms) > 1:
        terms = [first + second for first, second in zip(terms[::2], terms[1::2])]
    return terms[0]


def rounded(value):
    return lax.reduce_precision(value, 8, 7)


def in_order(came, me):
    count = came.shape[0]
    rest = came.shape[1:]
    bit = 1
    while bit < count:
        split = came.reshape((count // (2 * bit), 2, bit) + rest)
        came = jnp.where((me & bit) != 0, split[:, ::-1], split).reshape((count,) + rest)
        bit *= 2
    return came


def make(mesh):
    count_x = mesh.shape["gx"]
    count_y = mesh.shape["gy"]

    def on_device(field, active_rows, kern, target):
        tile_row = lax.axis_index("gx")
        waves, polars = field.shape[0], field.shape[1]
        tiles = field.shape[4]
        rows_dev = field.shape[5]
        side = field.shape[6]
        focus = kern.shape[3]
        shape = (waves, 2 * focus, polars * focus)
        share, near_field, near_kern, counts = call(
            share_kernel,
            [
                jax.ShapeDtypeStruct(shape, jnp.bfloat16),
                jax.ShapeDtypeStruct(field.shape[:3] + field.shape[4:], field.dtype),
                jax.ShapeDtypeStruct(kern.shape, kern.dtype),
                jax.ShapeDtypeStruct((tiles, 8, side), jnp.int32),
            ],
            [
                pltpu.SMEM(active_rows.shape, jnp.int32),
                pltpu.SemaphoreType.DMA((2 * waves + 1,)),
            ],
            [
                pltpu.with_memory_space_constraint(operand, pltpu.HBM)
                for operand in (active_rows, field, kern)
            ],
            [pltpu.HBM] * 3,
        )
        shares = [share] + partners(lambda d: share, "gy", count_y)
        share = total([term.astype(jnp.float32) for term in shares]).astype(jnp.bfloat16)
        strip_shape = (waves, tiles, 2 * rows_dev, polars * rows_dev)
        strips = call(
            strip_kernel,
            [jax.ShapeDtypeStruct(strip_shape, field.dtype)] * (count_y - 1),
            [],
            (near_field, counts),
            [pltpu.VMEM] * 2,
        )
        strips = partners(lambda d: strips[d - 1], "gy", count_y)
        shares = [share] + partners(lambda d: share, "gx", count_x)
        shares = shares[::-1]
        shape = (tiles, rows_dev, side)
        goal, row_kern, turn_kern, both_kern, own_strip = call(
            layout_kernel,
            [
                jax.ShapeDtypeStruct((waves, focus, polars * focus), target.dtype),
                jax.ShapeDtypeStruct((waves, 2 * polars * focus, polars * side), kern.dtype),
                jax.ShapeDtypeStruct((waves, tiles, 2 * rows_dev, 4 * focus), kern.dtype),
                jax.ShapeDtypeStruct((waves, tiles, 2 * focus, 2 * side), kern.dtype),
                jax.ShapeDtypeStruct(strip_shape, field.dtype),
            ],
            [],
            (near_field, near_kern, counts, target),
            [pltpu.VMEM] * 4,
        )
        scale = tiles * side / focus
        power, near, crossed = call(
            functools.partial(crossed_kernel, scale, count_y),
            [
                jax.ShapeDtypeStruct((waves, focus, polars * focus), jnp.float32),
                jax.ShapeDtypeStruct((waves, 4 * focus, polars * side), jnp.bfloat16),
                jax.ShapeDtypeStruct(shape, jnp.bfloat16),
            ],
            [],
            (row_kern, turn_kern, goal, own_strip, *strips, *shares),
            [pltpu.VMEM] * (3 + count_x + count_y),
        )
        (gradient,) = call(
            functools.partial(straight_kernel, scale),
            [jax.ShapeDtypeStruct(shape, jnp.float32)],
            [],
            (near_field, counts, both_kern, near),
            [pltpu.VMEM] * 4,
        )
        came = [crossed[0]] + crosswise(lambda d: crossed[d], mesh)
        own = rounded(gradient + jnp.stack(came).astype(jnp.float32))
        other = lax.ppermute(own.astype(jnp.bfloat16), "wa", pairs(2, 1))
        design_grad = in_order(0.5 * (own + other.astype(jnp.float32)), tile_row)
        intensity = jnp.swapaxes(power[:, :, :focus], 1, 2)
        return (design_grad[None], intensity)

    return on_device


def solution(mesh):
    placed = (
        P("wa", "cand", None, "gx", None, "gy", None),
        P("gx", None),
        P("wa", None, None, None, None),
        P("wa", None, None),
    )
    return jax.shard_map(
        make(mesh),
        mesh=mesh,
        in_specs=placed,
        out_specs=(P("gx", "cand", "gy", None), P("wa", "cand", None)),
        check_vma=False,
    )
```

```python
import functools

import jax
import jax.numpy as jnp
from jax import lax
from jax.experimental import pallas as pl
from jax.experimental.pallas import tpu as pltpu
from jax.sharding import PartitionSpec as P

VMEM = 16 * 2**20


def two_terms(value):
    high = value.astype(jnp.bfloat16)
    return high, (value - high.astype(jnp.float32)).astype(jnp.bfloat16)


def dot(first, second, over):
    return lax.dot_general(
        first, second, ((over[:1], over[1:]), ((), ())), preferred_element_type=jnp.float32
    )


def tile_kern(kern, wave, tile):
    real, imag = kern[wave, 0, tile], kern[wave, 1, tile]
    return jnp.concatenate([real, imag], axis=0), jnp.concatenate([-imag, real], axis=0)


def one_block(value, block, blocks):
    width = value.shape[1] // blocks
    picked = value[:, :width]
    for index in range(1, blocks):
        picked = jnp.where(block == index, value[:, index * width : (index + 1) * width], picked)
    return picked


def turn(value):
    width = value.shape[1]
    row = lax.broadcasted_iota(jnp.int32, (width, width), 0)
    column = lax.broadcasted_iota(jnp.int32, (width, width), 1)
    unit = jnp.where(row == column, 1.0, 0.0).astype(value.dtype)
    return dot(unit, value, (1, 1)).astype(value.dtype)


def twice(value, axis):
    return jnp.concatenate([value, value], axis=axis)


def diagonal(value, count):
    zero = jnp.zeros_like(value)
    rows = [
        jnp.concatenate([value if index == other else zero for other in range(count)], axis=1)
        for index in range(count)
    ]
    return jnp.concatenate(rows, axis=0)


def over_tiles(tiles, body, init):
    return lax.fori_loop(0, tiles, body, init, unroll=tiles <= 8)


def live_rows(count, shape):
    height = shape[-2]
    row = lax.axis_index("gy") * height + lax.broadcasted_iota(jnp.int32, shape, len(shape) - 2)
    return row < count


def share_kernel(rows_far, field_far, kern_far, share, field, kern, counts, rows, arrived):
    waves, polars, _, tiles, height, side = field.shape
    focus = kern.shape[3]
    copies = [pltpu.make_async_copy(rows_far, rows, arrived.at[2 * waves])]
    copies += [
        pltpu.make_async_copy(kern_far.at[wave], kern.at[wave], arrived.at[wave])
        for wave in range(waves)
    ]
    copies += [
        pltpu.make_async_copy(
            field_far.at[wave, :, :, 0], field.at[wave], arrived.at[waves + wave]
        )
        for wave in range(waves)
    ]
    for copy in copies:
        copy.start()
    tile_row = lax.axis_index("gx")
    block = lax.axis_index("gy")
    copies[0].wait()
    own = []
    for wave in range(waves):
        copies[1 + wave].wait()
        parts = []
        for part in range(2):
            value = kern[wave, part, tile_row].astype(jnp.float32)
            parts.append(diagonal(one_block(value, block, side // height), polars))
        own.append(twice(jnp.concatenate(parts, axis=0).astype(kern.dtype), 1))
    inner = []
    for wave in range(waves):
        copies[1 + waves + wave].wait()

        def add_tile(tile, value):
            live = live_rows(rows[0, tile], (polars, height, side))
            planes = [
                jnp.where(live, field[wave, :, part, tile], jnp.zeros((), field.dtype))
                for part in range(2)
            ]
            planes = [plane.reshape(polars * height, side) for plane in planes]
            return value + dot(
                jnp.concatenate(tile_kern(kern, wave, tile), axis=1),
                jnp.concatenate(planes, axis=1),
                (1, 1),
            )

        zero = jnp.zeros((2 * focus, polars * height), jnp.float32)
        inner.append(over_tiles(tiles, add_tile, zero))
    for wave in range(waves):
        both = dot(jnp.concatenate(two_terms(inner[wave]), axis=1), own[wave], (1, 1))
        real, imag = both[:, : polars * focus], both[:, polars * focus :]
        focal = [real[:focus] - imag[focus:], real[focus:] + imag[:focus]]
        share[wave] = jnp.concatenate(focal, axis=0).astype(share.dtype)

    def put_count(tile, carry):
        counts[tile] = jnp.full(counts.shape[1:], rows[0, tile], jnp.int32)
        return carry

    over_tiles(tiles, put_count, 0)


def turned_strip(planes, block, blocks):
    rows = [
        jnp.concatenate([one_block(plane, block, blocks) for plane in pair], axis=1)
        for pair in planes
    ]
    return turn(jnp.concatenate(rows, axis=0).astype(jnp.bfloat16))


def live_planes(field, counts, wave, tile):
    polars, height, side = field.shape[1], field.shape[4], field.shape[5]
    live = live_rows(counts[tile, :1], (height, side))
    return [
        [
            jnp.where(live, field[wave, polar, part, tile].astype(jnp.float32), 0.0)
            for part in range(2)
        ]
        for polar in range(polars)
    ]


def strip_kernel(field, counts, *strips):
    waves, _, _, tiles, height, side = field.shape
    blocks = side // height
    block = lax.axis_index("gy")

    def one_tile(tile, carry):
        for wave in range(waves):
            planes = live_planes(field, counts, wave, tile)
            for distance, strip in enumerate(strips, 1):
                strip[wave, tile] = turned_strip(planes, block ^ distance, blocks)
        return carry

    over_tiles(tiles, one_tile, 0)


def layout_kernel(field, kern, counts, target, goal, row_kern, turn_kern, both_kern, own_strip):
    waves, polars, _, tiles, height, side = field.shape
    blocks = side // height
    block = lax.axis_index("gy")
    tile_row = lax.axis_index("gx")
    for wave in range(waves):
        goal[wave] = jnp.concatenate([target[wave].T] * polars, axis=1)
        for part in range(2):
            value = kern[wave, part, tile_row].astype(jnp.float32)
            columns = [
                diagonal(one_block(value, block ^ distance, blocks), polars)
                for distance in range(blocks)
            ]
            rows = pl.ds(part * polars * value.shape[0], polars * value.shape[0])
            row_kern[wave, rows] = jnp.concatenate(columns, axis=1).astype(kern.dtype)

    def one_tile(tile, carry):
        for wave in range(waves):
            parts = tile_kern(kern, wave, tile)
            both_kern[wave, tile] = jnp.concatenate(parts, axis=1)
            parts = [one_block(part.astype(jnp.float32), block, blocks) for part in parts]
            turned = turn(jnp.concatenate(parts, axis=1).astype(kern.dtype))
            turn_kern[wave, tile] = twice(turned, 1)
            planes = live_planes(field, counts, wave, tile)
            own_strip[wave, tile] = turned_strip(planes, block, blocks)
        return carry

    over_tiles(tiles, one_tile, 0)


def crossed_kernel(scale, blocks, row_kern, turn_kern, goal, *refs):
    strips, refs = refs[:blocks], refs[blocks:]
    shares, (intensity, near, crossed) = refs[:-3], refs[-3:]
    waves, tiles, height, width = strips[0].shape
    height = height // 2
    polars = width // height
    focus = goal.shape[1]
    block = lax.axis_index("gy")
    sides = []
    for wave in range(waves):
        focal = total([share[wave].astype(jnp.float32) for share in shares])
        real, imag = focal[:focus], focal[focus:]
        power = real * real + imag * imag
        power = sum(pltpu.roll(power, polar * focus, 1) for polar in range(polars))
        intensity[wave] = power
        excess = power - goal[wave]
        real, imag = excess * real, excess * imag
        upright = jnp.concatenate([real, imag], axis=0)
        turned = jnp.concatenate([imag, -real], axis=0)
        terms = two_terms(jnp.concatenate([upright, turned], axis=1))
        row = dot(jnp.concatenate(terms, axis=1), twice(row_kern[wave], 0), (1, 0))
        sides.append(jnp.concatenate(two_terms(row), axis=0))
        near[wave] = sides[wave]

    def add_tile(distance, carry):
        tile = lax.axis_index("gx") ^ distance
        value = jnp.zeros((2 * height, blocks * width), jnp.float32)
        for wave in range(waves):
            back = dot(turn_kern[wave, tile], sides[wave], (1, 0))
            strip = jnp.concatenate([strip[wave, tile] for strip in strips], axis=1)
            value += back * strip.astype(jnp.float32)
        value = (value[:height] + value[height:]) * scale
        parts = []
        for apart in range(blocks):
            part = value[:, apart * width : (apart + 1) * width]
            parts.append(sum(part[:, at * height : (at + 1) * height] for at in range(polars)))
        columns = []
        for index in range(blocks):
            column = parts[0]
            for apart in range(1, blocks):
                column = jnp.where((block ^ apart) == index, parts[apart], column)
            columns.append(column)
        crossed[distance] = jnp.concatenate(columns, axis=1).astype(crossed.dtype)
        return carry

    over_tiles(tiles, add_tile, 0)


def straight_kernel(scale, field, counts, both_kern, near, gradient):
    waves, polars, _, tiles, height, side = field.shape
    sides = []
    for wave in range(waves):
        sides.append(turn(near[wave, :, : polars * height]))

    def add_tile(distance, carry):
        tile = lax.axis_index("gx") ^ distance
        term = jnp.zeros((height, side), jnp.float32)
        for wave in range(waves):
            back = dot(sides[wave], twice(both_kern[wave, tile], 0), (1, 0))
            back = back.reshape(polars, height, 2 * side)
            for polar in range(polars):
                for part in range(2):
                    plane = field[wave, polar, part, tile].astype(jnp.float32)
                    term += back[polar, :, part * side : (part + 1) * side] * plane
        live = live_rows(counts[tile, :1], (height, side))
        gradient[distance] = jnp.where(live, term * scale, 0.0)
        return carry

    over_tiles(tiles, add_tile, 0)


def call(kernel, out_shape, scratch, args, spaces):
    return pl.pallas_call(
        kernel,
        out_shape=out_shape,
        in_specs=[pl.BlockSpec(memory_space=space) for space in spaces],
        out_specs=[pl.BlockSpec(memory_space=pltpu.VMEM)] * len(out_shape),
        scratch_shapes=scratch,
        compiler_params=pltpu.CompilerParams(vmem_limit_bytes=VMEM),
    )(*args)


def pairs(count, distance):
    return [(device, device ^ distance) for device in range(count)]


def partners(value, axis, count):
    came = {d: lax.ppermute(value(d), axis, pairs(count, d)) for d in range(count - 1, 0, -1)}
    return [came[d] for d in range(1, count)]


def crosswise(value, mesh):
    count, cores = mesh.shape["gx"], mesh.shape["wa"]

    def routes(distance):
        odd = distance % 2 == 1
        return [
            (
                device * cores + core,
                (device ^ distance) * cores + (cores - 1 - core if odd else core),
            )
            for device in range(count)
            for core in range(cores)
        ]

    came = {d: lax.ppermute(value(d), ("gx", "wa"), routes(d)) for d in range(count - 1, 0, -1)}
    return [came[d] for d in range(1, count)]


def total(terms):
    while len(terms) > 1:
        terms = [first + second for first, second in zip(terms[::2], terms[1::2])]
    return terms[0]


def rounded(value):
    return lax.reduce_precision(value, 8, 7)


def in_order(came, me):
    count = came.shape[0]
    rest = came.shape[1:]
    bit = 1
    while bit < count:
        split = came.reshape((count // (2 * bit), 2, bit) + rest)
        came = jnp.where((me & bit) != 0, split[:, ::-1], split).reshape((count,) + rest)
        bit *= 2
    return came


def make(mesh):
    count_x = mesh.shape["gx"]
    count_y = mesh.shape["gy"]

    def on_device(field, active_rows, kern, target):
        tile_row = lax.axis_index("gx")
        waves, polars = field.shape[0], field.shape[1]
        tiles = field.shape[4]
        rows_dev = field.shape[5]
        side = field.shape[6]
        focus = kern.shape[3]
        shape = (waves, 2 * focus, polars * focus)
        share, near_field, near_kern, counts = call(
            share_kernel,
            [
                jax.ShapeDtypeStruct(shape, jnp.bfloat16),
                jax.ShapeDtypeStruct(field.shape[:3] + field.shape[4:], field.dtype),
                jax.ShapeDtypeStruct(kern.shape, kern.dtype),
                jax.ShapeDtypeStruct((tiles, 8, side), jnp.int32),
            ],
            [
                pltpu.SMEM(active_rows.shape, jnp.int32),
                pltpu.SemaphoreType.DMA((2 * waves + 1,)),
            ],
            [
                pltpu.with_memory_space_constraint(operand, pltpu.HBM)
                for operand in (active_rows, field, kern)
            ],
            [pltpu.HBM] * 3,
        )
        shares = [share] + partners(lambda d: share, "gy", count_y)
        share = total([term.astype(jnp.float32) for term in shares]).astype(jnp.bfloat16)
        strip_shape = (waves, tiles, 2 * rows_dev, polars * rows_dev)
        strips = call(
            strip_kernel,
            [jax.ShapeDtypeStruct(strip_shape, field.dtype)] * (count_y - 1),
            [],
            (near_field, counts),
            [pltpu.VMEM] * 2,
        )
        strips = partners(lambda d: strips[d - 1], "gy", count_y)
        shares = [share] + partners(lambda d: share, "gx", count_x)
        shares = shares[::-1]
        shape = (tiles, rows_dev, side)
        goal, row_kern, turn_kern, both_kern, own_strip = call(
            layout_kernel,
            [
                jax.ShapeDtypeStruct((waves, focus, polars * focus), target.dtype),
                jax.ShapeDtypeStruct((waves, 2 * polars * focus, polars * side), kern.dtype),
                jax.ShapeDtypeStruct((waves, tiles, 2 * rows_dev, 4 * focus), kern.dtype),
                jax.ShapeDtypeStruct((waves, tiles, 2 * focus, 2 * side), kern.dtype),
                jax.ShapeDtypeStruct(strip_shape, field.dtype),
            ],
            [],
            (near_field, near_kern, counts, target),
            [pltpu.VMEM] * 4,
        )
        scale = tiles * side / focus
        power, near, crossed = call(
            functools.partial(crossed_kernel, scale, count_y),
            [
                jax.ShapeDtypeStruct((waves, focus, polars * focus), jnp.float32),
                jax.ShapeDtypeStruct((waves, 4 * focus, polars * side), jnp.bfloat16),
                jax.ShapeDtypeStruct(shape, jnp.bfloat16),
            ],
            [],
            (row_kern, turn_kern, goal, own_strip, *strips, *shares),
            [pltpu.VMEM] * (3 + count_x + count_y),
        )
        (gradient,) = call(
            functools.partial(straight_kernel, scale),
            [jax.ShapeDtypeStruct(shape, jnp.float32)],
            [],
            (near_field, counts, both_kern, near),
            [pltpu.VMEM] * 4,
        )
        came = [crossed[0]] + crosswise(lambda d: crossed[d], mesh)
        own = rounded(gradient + jnp.stack(came).astype(jnp.float32))
        other = lax.ppermute(own.astype(jnp.bfloat16), "wa", pairs(2, 1))
        design_grad = in_order(0.5 * (own + other.astype(jnp.float32)), tile_row)
        intensity = jnp.swapaxes(power[:, :, :focus], 1, 2)
        return (design_grad[None], intensity)

    return on_device


def solution(mesh):
    placed = (
        P("wa", "cand", None, "gx", None, "gy", None),
        P("gx", None),
        P("wa", None, None, None, None),
        P("wa", None, None),
    )
    return jax.shard_map(
        make(mesh),
        mesh=mesh,
        in_specs=placed,
        out_specs=(P("gx", "cand", "gy", None), P("wa", "cand", None)),
        check_vma=False,
    )
```

```python
import functools

import jax
import jax.numpy as jnp
from jax import lax
from jax.experimental import pallas as pl
from jax.experimental.pallas import tpu as pltpu
from jax.sharding import PartitionSpec as P

VMEM = 16 * 2**20


def two_terms(value):
    high = value.astype(jnp.bfloat16)
    return high, (value - high.astype(jnp.float32)).astype(jnp.bfloat16)


def dot(first, second, over):
    return lax.dot_general(
        first, second, ((over[:1], over[1:]), ((), ())), preferred_element_type=jnp.float32
    )


def tile_kern(kern, wave, tile):
    real, imag = kern[wave, 0, tile], kern[wave, 1, tile]
    return jnp.concatenate([real, imag], axis=0), jnp.concatenate([-imag, real], axis=0)


def one_block(value, block, blocks):
    width = value.shape[1] // blocks
    picked = value[:, :width]
    for index in range(1, blocks):
        picked = jnp.where(block == index, value[:, index * width : (index + 1) * width], picked)
    return picked


def turn(value):
    width = value.shape[1]
    row = lax.broadcasted_iota(jnp.int32, (width, width), 0)
    column = lax.broadcasted_iota(jnp.int32, (width, width), 1)
    unit = jnp.where(row == column, 1.0, 0.0).astype(value.dtype)
    return dot(unit, value, (1, 1)).astype(value.dtype)


def twice(value, axis):
    return jnp.concatenate([value, value], axis=axis)


def diagonal(value, count):
    zero = jnp.zeros_like(value)
    rows = [
        jnp.concatenate([value if index == other else zero for other in range(count)], axis=1)
        for index in range(count)
    ]
    return jnp.concatenate(rows, axis=0)


def over_tiles(tiles, body, init):
    return lax.fori_loop(0, tiles, body, init, unroll=tiles <= 8)


def live_rows(count, shape):
    height = shape[-2]
    row = lax.axis_index("gy") * height + lax.broadcasted_iota(jnp.int32, shape, len(shape) - 2)
    return row < count


def share_kernel(rows_far, field_far, kern_far, share, field, kern, counts, rows, arrived):
    waves, polars, _, tiles, height, side = field.shape
    focus = kern.shape[3]
    copies = [pltpu.make_async_copy(rows_far, rows, arrived.at[2 * waves])]
    for wave in range(waves):
        copies += [
            pltpu.make_async_copy(kern_far.at[wave], kern.at[wave], arrived.at[2 * wave]),
            pltpu.make_async_copy(
                field_far.at[wave, :, :, 0], field.at[wave], arrived.at[2 * wave + 1]
            ),
        ]
    for copy in copies:
        copy.start()
    tile_row = lax.axis_index("gx")
    block = lax.axis_index("gy")
    copies[0].wait()

    def put_count(tile, carry):
        at = lax.broadcasted_iota(jnp.int32, rows.shape, 1)
        count = jnp.sum(jnp.where(at == tile, rows[...], 0), axis=1, keepdims=True)
        counts[tile] = jnp.broadcast_to(count, counts.shape[1:])
        return carry

    over_tiles(tiles, put_count, 0)
    inner = []
    own = []
    for wave in range(waves):
        copies[2 * wave + 1].wait()
        parts = []
        for part in range(2):
            value = kern[wave, part, tile_row].astype(jnp.float32)
            parts.append(diagonal(one_block(value, block, side // height), polars))
        own.append(twice(jnp.concatenate(parts, axis=0).astype(kern.dtype), 1))
        copies[2 * wave + 2].wait()

        def add_tile(tile, value):
            live = live_rows(counts[tile, :1], (polars, height, side))
            planes = [
                jnp.where(live, field[wave, :, part, tile], jnp.zeros((), field.dtype))
                for part in range(2)
            ]
            planes = [plane.reshape(polars * height, side) for plane in planes]
            return value + dot(
                jnp.concatenate(tile_kern(kern, wave, tile), axis=1),
                jnp.concatenate(planes, axis=1),
                (1, 1),
            )

        zero = jnp.zeros((2 * focus, polars * height), jnp.float32)
        inner.append(over_tiles(tiles, add_tile, zero))
    for wave in range(waves):
        both = dot(jnp.concatenate(two_terms(inner[wave]), axis=1), own[wave], (1, 1))
        real, imag = both[:, : polars * focus], both[:, polars * focus :]
        focal = [real[:focus] - imag[focus:], real[focus:] + imag[:focus]]
        share[wave] = jnp.concatenate(focal, axis=0).astype(share.dtype)


def turned_strip(planes, block, blocks):
    rows = [
        jnp.concatenate([one_block(plane, block, blocks) for plane in pair], axis=1)
        for pair in planes
    ]
    return turn(jnp.concatenate(rows, axis=0).astype(jnp.bfloat16))


def live_planes(field, counts, wave, tile):
    polars, height, side = field.shape[1], field.shape[4], field.shape[5]
    live = live_rows(counts[tile, :1], (height, side))
    return [
        [
            jnp.where(live, field[wave, polar, part, tile].astype(jnp.float32), 0.0)
            for part in range(2)
        ]
        for polar in range(polars)
    ]


def strip_kernel(field, counts, *strips):
    waves, _, _, tiles, height, side = field.shape
    blocks = side // height
    block = lax.axis_index("gy")

    def one_tile(tile, carry):
        for wave in range(waves):
            planes = live_planes(field, counts, wave, tile)
            for distance, strip in enumerate(strips, 1):
                strip[wave, tile] = turned_strip(planes, block ^ distance, blocks)
        return carry

    over_tiles(tiles, one_tile, 0)


def layout_kernel(field, kern, counts, target, goal, row_kern, turn_kern, both_kern, own_strip):
    waves, polars, _, tiles, height, side = field.shape
    blocks = side // height
    block = lax.axis_index("gy")
    tile_row = lax.axis_index("gx")
    for wave in range(waves):
        goal[wave] = jnp.concatenate([target[wave].T] * polars, axis=1)
        for part in range(2):
            value = kern[wave, part, tile_row].astype(jnp.float32)
            columns = [
                diagonal(one_block(value, block ^ distance, blocks), polars)
                for distance in range(blocks)
            ]
            rows = pl.ds(part * polars * value.shape[0], polars * value.shape[0])
            row_kern[wave, rows] = jnp.concatenate(columns, axis=1).astype(kern.dtype)

    def one_tile(tile, carry):
        for wave in range(waves):
            parts = tile_kern(kern, wave, tile)
            both_kern[wave, tile] = jnp.concatenate(parts, axis=1)
            parts = [one_block(part.astype(jnp.float32), block, blocks) for part in parts]
            turned = turn(jnp.concatenate(parts, axis=1).astype(kern.dtype))
            turn_kern[wave, tile] = twice(turned, 1)
            planes = live_planes(field, counts, wave, tile)
            own_strip[wave, tile] = turned_strip(planes, block, blocks)
        return carry

    over_tiles(tiles, one_tile, 0)


def crossed_kernel(scale, blocks, row_kern, turn_kern, goal, *refs):
    strips, refs = refs[:blocks], refs[blocks:]
    shares, (intensity, near, crossed) = refs[:-3], refs[-3:]
    waves, tiles, height, width = strips[0].shape
    height = height // 2
    polars = width // height
    focus = goal.shape[1]
    block = lax.axis_index("gy")
    sides = []
    for wave in range(waves):
        focal = total([share[wave].astype(jnp.float32) for share in shares])
        real, imag = focal[:focus], focal[focus:]
        power = real * real + imag * imag
        power = sum(pltpu.roll(power, polar * focus, 1) for polar in range(polars))
        intensity[wave] = power
        excess = power - goal[wave]
        real, imag = excess * real, excess * imag
        upright = jnp.concatenate([real, imag], axis=0)
        turned = jnp.concatenate([imag, -real], axis=0)
        terms = two_terms(jnp.concatenate([upright, turned], axis=1))
        row = dot(jnp.concatenate(terms, axis=1), twice(row_kern[wave], 0), (1, 0))
        sides.append(jnp.concatenate(two_terms(row), axis=0))
        near[wave] = sides[wave]

    def add_tile(distance, carry):
        tile = lax.axis_index("gx") ^ distance
        value = jnp.zeros((2 * height, blocks * width), jnp.float32)
        for wave in range(waves):
            back = dot(turn_kern[wave, tile], sides[wave], (1, 0))
            strip = jnp.concatenate([strip[wave, tile] for strip in strips], axis=1)
            value += back * strip.astype(jnp.float32)
        value = (value[:height] + value[height:]) * scale
        parts = []
        for apart in range(blocks):
            part = value[:, apart * width : (apart + 1) * width]
            parts.append(sum(part[:, at * height : (at + 1) * height] for at in range(polars)))
        columns = []
        for index in range(blocks):
            column = parts[0]
            for apart in range(1, blocks):
                column = jnp.where((block ^ apart) == index, parts[apart], column)
            columns.append(column)
        crossed[distance] = jnp.concatenate(columns, axis=1).astype(crossed.dtype)
        return carry

    over_tiles(tiles, add_tile, 0)


def straight_kernel(scale, field, counts, both_kern, near, gradient):
    waves, polars, _, tiles, height, side = field.shape
    sides = []
    for wave in range(waves):
        sides.append(turn(near[wave, :, : polars * height]))

    def add_tile(distance, carry):
        tile = lax.axis_index("gx") ^ distance
        term = jnp.zeros((height, side), jnp.float32)
        for wave in range(waves):
            back = dot(sides[wave], twice(both_kern[wave, tile], 0), (1, 0))
            back = back.reshape(polars, height, 2 * side)
            for polar in range(polars):
                for part in range(2):
                    plane = field[wave, polar, part, tile].astype(jnp.float32)
                    term += back[polar, :, part * side : (part + 1) * side] * plane
        live = live_rows(counts[tile, :1], (height, side))
        gradient[distance] = jnp.where(live, term * scale, 0.0)
        return carry

    over_tiles(tiles, add_tile, 0)


def call(kernel, out_shape, scratch, args, spaces):
    return pl.pallas_call(
        kernel,
        out_shape=out_shape,
        in_specs=[pl.BlockSpec(memory_space=space) for space in spaces],
        out_specs=[pl.BlockSpec(memory_space=pltpu.VMEM)] * len(out_shape),
        scratch_shapes=scratch,
        compiler_params=pltpu.CompilerParams(vmem_limit_bytes=VMEM),
    )(*args)


def pairs(count, distance):
    return [(device, device ^ distance) for device in range(count)]


def partners(value, axis, count):
    came = {d: lax.ppermute(value(d), axis, pairs(count, d)) for d in range(count - 1, 0, -1)}
    return [came[d] for d in range(1, count)]


def crosswise(value, mesh):
    count, cores = mesh.shape["gx"], mesh.shape["wa"]

    def routes(distance):
        odd = distance % 2 == 1
        return [
            (
                device * cores + core,
                (device ^ distance) * cores + (cores - 1 - core if odd else core),
            )
            for device in range(count)
            for core in range(cores)
        ]

    came = {d: lax.ppermute(value(d), ("gx", "wa"), routes(d)) for d in range(count - 1, 0, -1)}
    return [came[d] for d in range(1, count)]


def total(terms):
    while len(terms) > 1:
        terms = [first + second for first, second in zip(terms[::2], terms[1::2])]
    return terms[0]


def rounded(value):
    return lax.reduce_precision(value, 8, 7)


def in_order(came, me):
    count = came.shape[0]
    rest = came.shape[1:]
    bit = 1
    while bit < count:
        split = came.reshape((count // (2 * bit), 2, bit) + rest)
        came = jnp.where((me & bit) != 0, split[:, ::-1], split).reshape((count,) + rest)
        bit *= 2
    return came


def make(mesh):
    count_x = mesh.shape["gx"]
    count_y = mesh.shape["gy"]

    def on_device(field, active_rows, kern, target):
        tile_row = lax.axis_index("gx")
        waves, polars = field.shape[0], field.shape[1]
        tiles = field.shape[4]
        rows_dev = field.shape[5]
        side = field.shape[6]
        focus = kern.shape[3]
        shape = (waves, 2 * focus, polars * focus)
        share, near_field, near_kern, counts = call(
            share_kernel,
            [
                jax.ShapeDtypeStruct(shape, jnp.bfloat16),
                jax.ShapeDtypeStruct(field.shape[:3] + field.shape[4:], field.dtype),
                jax.ShapeDtypeStruct(kern.shape, kern.dtype),
                jax.ShapeDtypeStruct((tiles, 8, side), jnp.int32),
            ],
            [
                pltpu.VMEM(active_rows.shape, jnp.int32),
                pltpu.SemaphoreType.DMA((2 * waves + 1,)),
            ],
            [
                pltpu.with_memory_space_constraint(operand, pltpu.HBM)
                for operand in (active_rows, field, kern)
            ],
            [pltpu.HBM] * 3,
        )
        shares = [share] + partners(lambda d: share, "gy", count_y)
        share = total([term.astype(jnp.float32) for term in shares]).astype(jnp.bfloat16)
        strip_shape = (waves, tiles, 2 * rows_dev, polars * rows_dev)
        strips = call(
            strip_kernel,
            [jax.ShapeDtypeStruct(strip_shape, field.dtype)] * (count_y - 1),
            [],
            (near_field, counts),
            [pltpu.VMEM] * 2,
        )
        strips = partners(lambda d: strips[d - 1], "gy", count_y)
        shares = [share] + partners(lambda d: share, "gx", count_x)
        shares = shares[::-1]
        shape = (tiles, rows_dev, side)
        goal, row_kern, turn_kern, both_kern, own_strip = call(
            layout_kernel,
            [
                jax.ShapeDtypeStruct((waves, focus, polars * focus), target.dtype),
                jax.ShapeDtypeStruct((waves, 2 * polars * focus, polars * side), kern.dtype),
                jax.ShapeDtypeStruct((waves, tiles, 2 * rows_dev, 4 * focus), kern.dtype),
                jax.ShapeDtypeStruct((waves, tiles, 2 * focus, 2 * side), kern.dtype),
                jax.ShapeDtypeStruct(strip_shape, field.dtype),
            ],
            [],
            (near_field, near_kern, counts, target),
            [pltpu.VMEM] * 4,
        )
        scale = tiles * side / focus
        power, near, crossed = call(
            functools.partial(crossed_kernel, scale, count_y),
            [
                jax.ShapeDtypeStruct((waves, focus, polars * focus), jnp.float32),
                jax.ShapeDtypeStruct((waves, 4 * focus, polars * side), jnp.bfloat16),
                jax.ShapeDtypeStruct(shape, jnp.bfloat16),
            ],
            [],
            (row_kern, turn_kern, goal, own_strip, *strips, *shares),
            [pltpu.VMEM] * (3 + count_x + count_y),
        )
        (gradient,) = call(
            functools.partial(straight_kernel, scale),
            [jax.ShapeDtypeStruct(shape, jnp.float32)],
            [],
            (near_field, counts, both_kern, near),
            [pltpu.VMEM] * 4,
        )
        came = [crossed[0]] + crosswise(lambda d: crossed[d], mesh)
        own = rounded(gradient + jnp.stack(came).astype(jnp.float32))
        other = lax.ppermute(own.astype(jnp.bfloat16), "wa", pairs(2, 1))
        design_grad = in_order(0.5 * (own + other.astype(jnp.float32)), tile_row)
        intensity = jnp.swapaxes(power[:, :, :focus], 1, 2)
        return (design_grad[None], intensity)

    return on_device


def solution(mesh):
    placed = (
        P("wa", "cand", None, "gx", None, "gy", None),
        P("gx", None),
        P("wa", None, None, None, None),
        P("wa", None, None),
    )
    return jax.shard_map(
        make(mesh),
        mesh=mesh,
        in_specs=placed,
        out_specs=(P("gx", "cand", "gy", None), P("wa", "cand", None)),
        check_vma=False,
    )
```

```python
import functools

import jax
import jax.numpy as jnp
from jax import lax
from jax.experimental import pallas as pl
from jax.experimental.pallas import tpu as pltpu
from jax.sharding import PartitionSpec as P

VMEM = 16 * 2**20


def two_terms(value):
    high = value.astype(jnp.bfloat16)
    return high, (value - high.astype(jnp.float32)).astype(jnp.bfloat16)


def dot(first, second, over):
    return lax.dot_general(
        first, second, ((over[:1], over[1:]), ((), ())), preferred_element_type=jnp.float32
    )


def tile_kern(kern, wave, tile):
    real, imag = kern[wave, 0, tile], kern[wave, 1, tile]
    return jnp.concatenate([real, imag], axis=0), jnp.concatenate([-imag, real], axis=0)


def one_block(value, block, blocks):
    width = value.shape[1] // blocks
    picked = value[:, :width]
    for index in range(1, blocks):
        picked = jnp.where(block == index, value[:, index * width : (index + 1) * width], picked)
    return picked


def turn(value):
    width = value.shape[1]
    row = lax.broadcasted_iota(jnp.int32, (width, width), 0)
    column = lax.broadcasted_iota(jnp.int32, (width, width), 1)
    unit = jnp.where(row == column, 1.0, 0.0).astype(value.dtype)
    return dot(unit, value, (1, 1)).astype(value.dtype)


def twice(value, axis):
    return jnp.concatenate([value, value], axis=axis)


def diagonal(value, count):
    zero = jnp.zeros_like(value)
    rows = [
        jnp.concatenate([value if index == other else zero for other in range(count)], axis=1)
        for index in range(count)
    ]
    return jnp.concatenate(rows, axis=0)


def over_tiles(tiles, body, init):
    return lax.fori_loop(0, tiles, body, init, unroll=tiles <= 8)


def live_rows(count, shape):
    height = shape[-2]
    row = lax.axis_index("gy") * height + lax.broadcasted_iota(jnp.int32, shape, len(shape) - 2)
    return row < count


def share_kernel(rows_far, field_far, kern_far, share, field, kern, counts, rows, arrived):
    waves, polars, _, tiles, height, side = field.shape
    focus = kern.shape[3]
    copies = [pltpu.make_async_copy(rows_far, rows, arrived.at[2 * waves])]
    copies += [
        pltpu.make_async_copy(kern_far.at[wave], kern.at[wave], arrived.at[wave])
        for wave in range(waves)
    ]
    copies += [
        pltpu.make_async_copy(
            field_far.at[wave, :, :, 0], field.at[wave], arrived.at[waves + wave]
        )
        for wave in range(waves)
    ]
    for copy in copies:
        copy.start()
    tile_row = lax.axis_index("gx")
    block = lax.axis_index("gy")
    copies[0].wait()

    def put_count(tile, carry):
        at = lax.broadcasted_iota(jnp.int32, rows.shape, 1)
        count = jnp.sum(jnp.where(at == tile, rows[...], 0), axis=1, keepdims=True)
        counts[tile] = jnp.broadcast_to(count, counts.shape[1:])
        return carry

    over_tiles(tiles, put_count, 0)
    own = []
    for wave in range(waves):
        copies[1 + wave].wait()
        parts = []
        for part in range(2):
            value = kern[wave, part, tile_row].astype(jnp.float32)
            parts.append(diagonal(one_block(value, block, side // height).T, polars))
        own.append(twice(jnp.concatenate(parts, axis=1).astype(kern.dtype), 0))
    inner = []
    for wave in range(waves):
        copies[1 + waves + wave].wait()

        def add_tile(tile, value):
            live = live_rows(counts[tile, :1], (polars, height, side))
            planes = [
                jnp.where(live, field[wave, :, part, tile], jnp.zeros((), field.dtype))
                for part in range(2)
            ]
            planes = [plane.reshape(polars * height, side) for plane in planes]
            return value + dot(
                jnp.concatenate(tile_kern(kern, wave, tile), axis=1),
                jnp.concatenate(planes, axis=1),
                (1, 1),
            )

        zero = jnp.zeros((2 * focus, polars * height), jnp.float32)
        inner.append(over_tiles(tiles, add_tile, zero))
    for wave in range(waves):
        both = dot(jnp.concatenate(two_terms(inner[wave]), axis=1), own[wave], (1, 0))
        real, imag = both[:, : polars * focus], both[:, polars * focus :]
        focal = [real[:focus] - imag[focus:], real[focus:] + imag[:focus]]
        share[wave] = jnp.concatenate(focal, axis=0).astype(share.dtype)


def turned_strip(planes, block, blocks):
    rows = [
        jnp.concatenate([one_block(plane, block, blocks) for plane in pair], axis=1)
        for pair in planes
    ]
    return turn(jnp.concatenate(rows, axis=0).astype(jnp.bfloat16))


def live_planes(field, counts, wave, tile):
    polars, height, side = field.shape[1], field.shape[4], field.shape[5]
    live = live_rows(counts[tile, :1], (height, side))
    return [
        [
            jnp.where(live, field[wave, polar, part, tile].astype(jnp.float32), 0.0)
            for part in range(2)
        ]
        for polar in range(polars)
    ]


def strip_kernel(field, counts, *strips):
    waves, _, _, tiles, height, side = field.shape
    blocks = side // height
    block = lax.axis_index("gy")

    def one_tile(tile, carry):
        for wave in range(waves):
            planes = live_planes(field, counts, wave, tile)
            for distance, strip in enumerate(strips, 1):
                strip[wave, tile] = turned_strip(planes, block ^ distance, blocks)
        return carry

    over_tiles(tiles, one_tile, 0)


def layout_kernel(field, kern, counts, target, goal, row_kern, turn_kern, both_kern, own_strip):
    waves, polars, _, tiles, height, side = field.shape
    blocks = side // height
    block = lax.axis_index("gy")
    tile_row = lax.axis_index("gx")
    for wave in range(waves):
        goal[wave] = jnp.concatenate([target[wave].T] * polars, axis=1)
        for part in range(2):
            value = kern[wave, part, tile_row].astype(jnp.float32)
            columns = [
                diagonal(one_block(value, block ^ distance, blocks), polars)
                for distance in range(blocks)
            ]
            rows = pl.ds(part * polars * value.shape[0], polars * value.shape[0])
            row_kern[wave, rows] = jnp.concatenate(columns, axis=1).astype(kern.dtype)

    def one_tile(tile, carry):
        for wave in range(waves):
            parts = tile_kern(kern, wave, tile)
            both_kern[wave, tile] = jnp.concatenate(parts, axis=1)
            parts = [one_block(part.astype(jnp.float32), block, blocks) for part in parts]
            turned = turn(jnp.concatenate(parts, axis=1).astype(kern.dtype))
            turn_kern[wave, tile] = twice(turned, 1)
            planes = live_planes(field, counts, wave, tile)
            own_strip[wave, tile] = turned_strip(planes, block, blocks)
        return carry

    over_tiles(tiles, one_tile, 0)


def crossed_kernel(scale, blocks, row_kern, turn_kern, goal, *refs):
    strips, refs = refs[:blocks], refs[blocks:]
    shares, (intensity, near, crossed) = refs[:-3], refs[-3:]
    waves, tiles, height, width = strips[0].shape
    height = height // 2
    polars = width // height
    focus = goal.shape[1]
    block = lax.axis_index("gy")
    sides = []
    for wave in range(waves):
        focal = total([share[wave].astype(jnp.float32) for share in shares])
        real, imag = focal[:focus], focal[focus:]
        power = real * real + imag * imag
        power = sum(pltpu.roll(power, polar * focus, 1) for polar in range(polars))
        intensity[wave] = power
        excess = power - goal[wave]
        real, imag = excess * real, excess * imag
        upright = jnp.concatenate([real, imag], axis=0)
        turned = jnp.concatenate([imag, -real], axis=0)
        terms = two_terms(jnp.concatenate([upright, turned], axis=1))
        row = dot(jnp.concatenate(terms, axis=1), twice(row_kern[wave], 0), (1, 0))
        sides.append(jnp.concatenate(two_terms(row), axis=0))
        near[wave] = sides[wave]

    def add_tile(distance, carry):
        tile = lax.axis_index("gx") ^ distance
        value = jnp.zeros((2 * height, blocks * width), jnp.float32)
        for wave in range(waves):
            back = dot(turn_kern[wave, tile], sides[wave], (1, 0))
            strip = jnp.concatenate([strip[wave, tile] for strip in strips], axis=1)
            value += back * strip.astype(jnp.float32)
        value = (value[:height] + value[height:]) * scale
        parts = []
        for apart in range(blocks):
            part = value[:, apart * width : (apart + 1) * width]
            parts.append(sum(part[:, at * height : (at + 1) * height] for at in range(polars)))
        columns = []
        for index in range(blocks):
            column = parts[0]
            for apart in range(1, blocks):
                column = jnp.where((block ^ apart) == index, parts[apart], column)
            columns.append(column)
        crossed[distance] = jnp.concatenate(columns, axis=1).astype(crossed.dtype)
        return carry

    over_tiles(tiles, add_tile, 0)


def straight_kernel(scale, field, counts, both_kern, near, gradient):
    waves, polars, _, tiles, height, side = field.shape
    sides = []
    for wave in range(waves):
        sides.append(turn(near[wave, :, : polars * height]))

    def add_tile(distance, carry):
        tile = lax.axis_index("gx") ^ distance
        term = jnp.zeros((height, side), jnp.float32)
        for wave in range(waves):
            back = dot(sides[wave], twice(both_kern[wave, tile], 0), (1, 0))
            back = back.reshape(polars, height, 2 * side)
            for polar in range(polars):
                for part in range(2):
                    plane = field[wave, polar, part, tile].astype(jnp.float32)
                    term += back[polar, :, part * side : (part + 1) * side] * plane
        live = live_rows(counts[tile, :1], (height, side))
        gradient[distance] = jnp.where(live, term * scale, 0.0)
        return carry

    over_tiles(tiles, add_tile, 0)


def call(kernel, out_shape, scratch, args, spaces):
    return pl.pallas_call(
        kernel,
        out_shape=out_shape,
        in_specs=[pl.BlockSpec(memory_space=space) for space in spaces],
        out_specs=[pl.BlockSpec(memory_space=pltpu.VMEM)] * len(out_shape),
        scratch_shapes=scratch,
        compiler_params=pltpu.CompilerParams(vmem_limit_bytes=VMEM),
    )(*args)


def pairs(count, distance):
    return [(device, device ^ distance) for device in range(count)]


def partners(value, axis, count):
    came = {d: lax.ppermute(value(d), axis, pairs(count, d)) for d in range(count - 1, 0, -1)}
    return [came[d] for d in range(1, count)]


def crosswise(value, mesh):
    count, cores = mesh.shape["gx"], mesh.shape["wa"]

    def routes(distance):
        odd = distance % 2 == 1
        return [
            (
                device * cores + core,
                (device ^ distance) * cores + (cores - 1 - core if odd else core),
            )
            for device in range(count)
            for core in range(cores)
        ]

    came = {d: lax.ppermute(value(d), ("gx", "wa"), routes(d)) for d in range(count - 1, 0, -1)}
    return [came[d] for d in range(1, count)]


def total(terms):
    while len(terms) > 1:
        terms = [first + second for first, second in zip(terms[::2], terms[1::2])]
    return terms[0]


def rounded(value):
    return lax.reduce_precision(value, 8, 7)


def in_order(came, me):
    count = came.shape[0]
    rest = came.shape[1:]
    bit = 1
    while bit < count:
        split = came.reshape((count // (2 * bit), 2, bit) + rest)
        came = jnp.where((me & bit) != 0, split[:, ::-1], split).reshape((count,) + rest)
        bit *= 2
    return came


def make(mesh):
    count_x = mesh.shape["gx"]
    count_y = mesh.shape["gy"]

    def on_device(field, active_rows, kern, target):
        tile_row = lax.axis_index("gx")
        waves, polars = field.shape[0], field.shape[1]
        tiles = field.shape[4]
        rows_dev = field.shape[5]
        side = field.shape[6]
        focus = kern.shape[3]
        shape = (waves, 2 * focus, polars * focus)
        share, near_field, near_kern, counts = call(
            share_kernel,
            [
                jax.ShapeDtypeStruct(shape, jnp.bfloat16),
                jax.ShapeDtypeStruct(field.shape[:3] + field.shape[4:], field.dtype),
                jax.ShapeDtypeStruct(kern.shape, kern.dtype),
                jax.ShapeDtypeStruct((tiles, 8, side), jnp.int32),
            ],
            [
                pltpu.VMEM(active_rows.shape, jnp.int32),
                pltpu.SemaphoreType.DMA((2 * waves + 1,)),
            ],
            [
                pltpu.with_memory_space_constraint(operand, pltpu.HBM)
                for operand in (active_rows, field, kern)
            ],
            [pltpu.HBM] * 3,
        )
        shares = [share] + partners(lambda d: share, "gy", count_y)
        share = total([term.astype(jnp.float32) for term in shares]).astype(jnp.bfloat16)
        strip_shape = (waves, tiles, 2 * rows_dev, polars * rows_dev)
        strips = call(
            strip_kernel,
            [jax.ShapeDtypeStruct(strip_shape, field.dtype)] * (count_y - 1),
            [],
            (near_field, counts),
            [pltpu.VMEM] * 2,
        )
        strips = partners(lambda d: strips[d - 1], "gy", count_y)
        shares = [share] + partners(lambda d: share, "gx", count_x)
        shares = shares[::-1]
        shape = (tiles, rows_dev, side)
        goal, row_kern, turn_kern, both_kern, own_strip = call(
            layout_kernel,
            [
                jax.ShapeDtypeStruct((waves, focus, polars * focus), target.dtype),
                jax.ShapeDtypeStruct((waves, 2 * polars * focus, polars * side), kern.dtype),
                jax.ShapeDtypeStruct((waves, tiles, 2 * rows_dev, 4 * focus), kern.dtype),
                jax.ShapeDtypeStruct((waves, tiles, 2 * focus, 2 * side), kern.dtype),
                jax.ShapeDtypeStruct(strip_shape, field.dtype),
            ],
            [],
            (near_field, near_kern, counts, target),
            [pltpu.VMEM] * 4,
        )
        scale = tiles * side / focus
        power, near, crossed = call(
            functools.partial(crossed_kernel, scale, count_y),
            [
                jax.ShapeDtypeStruct((waves, focus, polars * focus), jnp.float32),
                jax.ShapeDtypeStruct((waves, 4 * focus, polars * side), jnp.bfloat16),
                jax.ShapeDtypeStruct(shape, jnp.bfloat16),
            ],
            [],
            (row_kern, turn_kern, goal, own_strip, *strips, *shares),
            [pltpu.VMEM] * (3 + count_x + count_y),
        )
        (gradient,) = call(
            functools.partial(straight_kernel, scale),
            [jax.ShapeDtypeStruct(shape, jnp.float32)],
            [],
            (near_field, counts, both_kern, near),
            [pltpu.VMEM] * 4,
        )
        came = [crossed[0]] + crosswise(lambda d: crossed[d], mesh)
        own = rounded(gradient + jnp.stack(came).astype(jnp.float32))
        other = lax.ppermute(own.astype(jnp.bfloat16), "wa", pairs(2, 1))
        design_grad = in_order(0.5 * (own + other.astype(jnp.float32)), tile_row)
        intensity = jnp.swapaxes(power[:, :, :focus], 1, 2)
        return (design_grad[None], intensity)

    return on_device


def solution(mesh):
    placed = (
        P("wa", "cand", None, "gx", None, "gy", None),
        P("gx", None),
        P("wa", None, None, None, None),
        P("wa", None, None),
    )
    return jax.shard_map(
        make(mesh),
        mesh=mesh,
        in_specs=placed,
        out_specs=(P("gx", "cand", "gy", None), P("wa", "cand", None)),
        check_vma=False,
    )
```

```python
import functools

import jax
import jax.numpy as jnp
from jax import lax
from jax.experimental import pallas as pl
from jax.experimental.pallas import tpu as pltpu
from jax.sharding import PartitionSpec as P

VMEM = 16 * 2**20


def two_terms(value):
    high = value.astype(jnp.bfloat16)
    return high, (value - high.astype(jnp.float32)).astype(jnp.bfloat16)


def dot(first, second, over):
    return lax.dot_general(
        first, second, ((over[:1], over[1:]), ((), ())), preferred_element_type=jnp.float32
    )


def tile_kern(kern, wave, tile):
    real, imag = kern[wave, 0, tile], kern[wave, 1, tile]
    return jnp.concatenate([real, imag], axis=0), jnp.concatenate([-imag, real], axis=0)


def one_block(value, block, blocks):
    width = value.shape[1] // blocks
    picked = value[:, :width]
    for index in range(1, blocks):
        picked = jnp.where(block == index, value[:, index * width : (index + 1) * width], picked)
    return picked


def turn(value):
    width = value.shape[1]
    row = lax.broadcasted_iota(jnp.int32, (width, width), 0)
    column = lax.broadcasted_iota(jnp.int32, (width, width), 1)
    unit = jnp.where(row == column, 1.0, 0.0).astype(value.dtype)
    return dot(unit, value, (1, 1)).astype(value.dtype)


def twice(value, axis):
    return jnp.concatenate([value, value], axis=axis)


def diagonal(value, count):
    zero = jnp.zeros_like(value)
    rows = [
        jnp.concatenate([value if index == other else zero for other in range(count)], axis=1)
        for index in range(count)
    ]
    return jnp.concatenate(rows, axis=0)


def over_tiles(tiles, body, init):
    return lax.fori_loop(0, tiles, body, init, unroll=tiles <= 8)


def live_rows(count, shape):
    height = shape[-2]
    row = lax.axis_index("gy") * height + lax.broadcasted_iota(jnp.int32, shape, len(shape) - 2)
    return row < count


def share_kernel(rows_far, field_far, kern_far, share, field, kern, counts, rows, arrived):
    waves, polars, _, tiles, height, side = field.shape
    focus = kern.shape[3]
    copies = [pltpu.make_async_copy(rows_far, rows, arrived.at[2 * waves])]
    for wave in range(waves):
        copies += [
            pltpu.make_async_copy(kern_far.at[wave], kern.at[wave], arrived.at[2 * wave]),
            pltpu.make_async_copy(
                field_far.at[wave, :, :, 0], field.at[wave], arrived.at[2 * wave + 1]
            ),
        ]
    for copy in copies:
        copy.start()
    tile_row = lax.axis_index("gx")
    block = lax.axis_index("gy")
    copies[0].wait()

    def put_count(tile, carry):
        at = lax.broadcasted_iota(jnp.int32, rows.shape, 1)
        count = jnp.sum(jnp.where(at == tile, rows[...], 0), axis=1, keepdims=True)
        counts[tile] = jnp.broadcast_to(count, counts.shape[1:])
        return carry

    over_tiles(tiles, put_count, 0)
    row = lax.broadcasted_iota(jnp.int32, (2 * focus, polars * height), 1)
    row = block * height + lax.rem(row, height)
    inner = []
    own = []
    for wave in range(waves):
        copies[2 * wave + 1].wait()
        parts = []
        for part in range(2):
            value = kern[wave, part, tile_row].astype(jnp.float32)
            parts.append(diagonal(one_block(value, block, side // height), polars))
        own.append(twice(jnp.concatenate(parts, axis=0).astype(kern.dtype), 1))
        copies[2 * wave + 2].wait()

        def add_tile(tile, value):
            planes = [field[wave, :, part, tile] for part in range(2)]
            planes = [plane.reshape(polars * height, side) for plane in planes]
            product = dot(
                jnp.concatenate(tile_kern(kern, wave, tile), axis=1),
                jnp.concatenate(planes, axis=1),
                (1, 1),
            )
            count = jnp.broadcast_to(counts[tile, :1, : polars * height], product.shape)
            return value + jnp.where(row < count, product, 0.0)

        zero = jnp.zeros((2 * focus, polars * height), jnp.float32)
        inner.append(over_tiles(tiles, add_tile, zero))
    for wave in range(waves):
        both = dot(jnp.concatenate(two_terms(inner[wave]), axis=1), own[wave], (1, 1))
        real, imag = both[:, : polars * focus], both[:, polars * focus :]
        focal = [real[:focus] - imag[focus:], real[focus:] + imag[:focus]]
        share[wave] = jnp.concatenate(focal, axis=0).astype(share.dtype)


def turned_strip(planes, block, blocks):
    rows = [
        jnp.concatenate([one_block(plane, block, blocks) for plane in pair], axis=1)
        for pair in planes
    ]
    return turn(jnp.concatenate(rows, axis=0).astype(jnp.bfloat16))


def live_planes(field, counts, wave, tile):
    polars, height, side = field.shape[1], field.shape[4], field.shape[5]
    live = live_rows(counts[tile, :1], (height, side))
    return [
        [
            jnp.where(live, field[wave, polar, part, tile].astype(jnp.float32), 0.0)
            for part in range(2)
        ]
        for polar in range(polars)
    ]


def strip_kernel(field, counts, *strips):
    waves, _, _, tiles, height, side = field.shape
    blocks = side // height
    block = lax.axis_index("gy")

    def one_tile(tile, carry):
        for wave in range(waves):
            planes = live_planes(field, counts, wave, tile)
            for distance, strip in enumerate(strips, 1):
                strip[wave, tile] = turned_strip(planes, block ^ distance, blocks)
        return carry

    over_tiles(tiles, one_tile, 0)


def layout_kernel(field, kern, counts, target, goal, row_kern, turn_kern, both_kern, own_strip):
    waves, polars, _, tiles, height, side = field.shape
    blocks = side // height
    block = lax.axis_index("gy")
    tile_row = lax.axis_index("gx")
    for wave in range(waves):
        goal[wave] = jnp.concatenate([target[wave].T] * polars, axis=1)
        for part in range(2):
            value = kern[wave, part, tile_row].astype(jnp.float32)
            columns = [
                diagonal(one_block(value, block ^ distance, blocks), polars)
                for distance in range(blocks)
            ]
            rows = pl.ds(part * polars * value.shape[0], polars * value.shape[0])
            row_kern[wave, rows] = jnp.concatenate(columns, axis=1).astype(kern.dtype)

    def one_tile(tile, carry):
        for wave in range(waves):
            parts = tile_kern(kern, wave, tile)
            both_kern[wave, tile] = jnp.concatenate(parts, axis=1)
            parts = [one_block(part.astype(jnp.float32), block, blocks) for part in parts]
            turned = turn(jnp.concatenate(parts, axis=1).astype(kern.dtype))
            turn_kern[wave, tile] = twice(turned, 1)
            planes = live_planes(field, counts, wave, tile)
            own_strip[wave, tile] = turned_strip(planes, block, blocks)
        return carry

    over_tiles(tiles, one_tile, 0)


def crossed_kernel(scale, blocks, row_kern, turn_kern, goal, *refs):
    strips, refs = refs[:blocks], refs[blocks:]
    shares, (intensity, near, crossed) = refs[:-3], refs[-3:]
    waves, tiles, height, width = strips[0].shape
    height = height // 2
    polars = width // height
    focus = goal.shape[1]
    block = lax.axis_index("gy")
    sides = []
    for wave in range(waves):
        focal = total([share[wave].astype(jnp.float32) for share in shares])
        real, imag = focal[:focus], focal[focus:]
        power = real * real + imag * imag
        power = sum(pltpu.roll(power, polar * focus, 1) for polar in range(polars))
        intensity[wave] = power
        excess = power - goal[wave]
        real, imag = excess * real, excess * imag
        upright = jnp.concatenate([real, imag], axis=0)
        turned = jnp.concatenate([imag, -real], axis=0)
        terms = two_terms(jnp.concatenate([upright, turned], axis=1))
        row = dot(jnp.concatenate(terms, axis=1), twice(row_kern[wave], 0), (1, 0))
        sides.append(jnp.concatenate(two_terms(row), axis=0))
        near[wave] = sides[wave]

    def add_tile(distance, carry):
        tile = lax.axis_index("gx") ^ distance
        value = jnp.zeros((2 * height, blocks * width), jnp.float32)
        for wave in range(waves):
            back = dot(turn_kern[wave, tile], sides[wave], (1, 0))
            strip = jnp.concatenate([strip[wave, tile] for strip in strips], axis=1)
            value += back * strip.astype(jnp.float32)
        value = (value[:height] + value[height:]) * scale
        parts = []
        for apart in range(blocks):
            part = value[:, apart * width : (apart + 1) * width]
            parts.append(sum(part[:, at * height : (at + 1) * height] for at in range(polars)))
        columns = []
        for index in range(blocks):
            column = parts[0]
            for apart in range(1, blocks):
                column = jnp.where((block ^ apart) == index, parts[apart], column)
            columns.append(column)
        crossed[distance] = jnp.concatenate(columns, axis=1).astype(crossed.dtype)
        return carry

    over_tiles(tiles, add_tile, 0)


def straight_kernel(scale, field, counts, both_kern, near, gradient):
    waves, polars, _, tiles, height, side = field.shape
    sides = []
    for wave in range(waves):
        sides.append(turn(near[wave, :, : polars * height]))

    def add_tile(distance, carry):
        tile = lax.axis_index("gx") ^ distance
        term = jnp.zeros((height, side), jnp.float32)
        for wave in range(waves):
            back = dot(sides[wave], twice(both_kern[wave, tile], 0), (1, 0))
            back = back.reshape(polars, height, 2 * side)
            for polar in range(polars):
                for part in range(2):
                    plane = field[wave, polar, part, tile].astype(jnp.float32)
                    term += back[polar, :, part * side : (part + 1) * side] * plane
        live = live_rows(counts[tile, :1], (height, side))
        gradient[distance] = jnp.where(live, term * scale, 0.0)
        return carry

    over_tiles(tiles, add_tile, 0)


def call(kernel, out_shape, scratch, args, spaces):
    return pl.pallas_call(
        kernel,
        out_shape=out_shape,
        in_specs=[pl.BlockSpec(memory_space=space) for space in spaces],
        out_specs=[pl.BlockSpec(memory_space=pltpu.VMEM)] * len(out_shape),
        scratch_shapes=scratch,
        compiler_params=pltpu.CompilerParams(vmem_limit_bytes=VMEM),
    )(*args)


def pairs(count, distance):
    return [(device, device ^ distance) for device in range(count)]


def partners(value, axis, count):
    came = {d: lax.ppermute(value(d), axis, pairs(count, d)) for d in range(count - 1, 0, -1)}
    return [came[d] for d in range(1, count)]


def crosswise(value, mesh):
    count, cores = mesh.shape["gx"], mesh.shape["wa"]

    def routes(distance):
        odd = distance % 2 == 1
        return [
            (
                device * cores + core,
                (device ^ distance) * cores + (cores - 1 - core if odd else core),
            )
            for device in range(count)
            for core in range(cores)
        ]

    came = {d: lax.ppermute(value(d), ("gx", "wa"), routes(d)) for d in range(count - 1, 0, -1)}
    return [came[d] for d in range(1, count)]


def total(terms):
    while len(terms) > 1:
        terms = [first + second for first, second in zip(terms[::2], terms[1::2])]
    return terms[0]


def rounded(value):
    return lax.reduce_precision(value, 8, 7)


def in_order(came, me):
    count = came.shape[0]
    rest = came.shape[1:]
    bit = 1
    while bit < count:
        split = came.reshape((count // (2 * bit), 2, bit) + rest)
        came = jnp.where((me & bit) != 0, split[:, ::-1], split).reshape((count,) + rest)
        bit *= 2
    return came


def make(mesh):
    count_x = mesh.shape["gx"]
    count_y = mesh.shape["gy"]

    def on_device(field, active_rows, kern, target):
        tile_row = lax.axis_index("gx")
        waves, polars = field.shape[0], field.shape[1]
        tiles = field.shape[4]
        rows_dev = field.shape[5]
        side = field.shape[6]
        focus = kern.shape[3]
        shape = (waves, 2 * focus, polars * focus)
        share, near_field, near_kern, counts = call(
            share_kernel,
            [
                jax.ShapeDtypeStruct(shape, jnp.bfloat16),
                jax.ShapeDtypeStruct(field.shape[:3] + field.shape[4:], field.dtype),
                jax.ShapeDtypeStruct(kern.shape, kern.dtype),
                jax.ShapeDtypeStruct((tiles, 8, side), jnp.int32),
            ],
            [
                pltpu.VMEM(active_rows.shape, jnp.int32),
                pltpu.SemaphoreType.DMA((2 * waves + 1,)),
            ],
            [
                pltpu.with_memory_space_constraint(operand, pltpu.HBM)
                for operand in (active_rows, field, kern)
            ],
            [pltpu.HBM] * 3,
        )
        shares = [share] + partners(lambda d: share, "gy", count_y)
        share = total([term.astype(jnp.float32) for term in shares]).astype(jnp.bfloat16)
        strip_shape = (waves, tiles, 2 * rows_dev, polars * rows_dev)
        strips = call(
            strip_kernel,
            [jax.ShapeDtypeStruct(strip_shape, field.dtype)] * (count_y - 1),
            [],
            (near_field, counts),
            [pltpu.VMEM] * 2,
        )
        strips = partners(lambda d: strips[d - 1], "gy", count_y)
        shares = [share] + partners(lambda d: share, "gx", count_x)
        shares = shares[::-1]
        shape = (tiles, rows_dev, side)
        goal, row_kern, turn_kern, both_kern, own_strip = call(
            layout_kernel,
            [
                jax.ShapeDtypeStruct((waves, focus, polars * focus), target.dtype),
                jax.ShapeDtypeStruct((waves, 2 * polars * focus, polars * side), kern.dtype),
                jax.ShapeDtypeStruct((waves, tiles, 2 * rows_dev, 4 * focus), kern.dtype),
                jax.ShapeDtypeStruct((waves, tiles, 2 * focus, 2 * side), kern.dtype),
                jax.ShapeDtypeStruct(strip_shape, field.dtype),
            ],
            [],
            (near_field, near_kern, counts, target),
            [pltpu.VMEM] * 4,
        )
        scale = tiles * side / focus
        power, near, crossed = call(
            functools.partial(crossed_kernel, scale, count_y),
            [
                jax.ShapeDtypeStruct((waves, focus, polars * focus), jnp.float32),
                jax.ShapeDtypeStruct((waves, 4 * focus, polars * side), jnp.bfloat16),
                jax.ShapeDtypeStruct(shape, jnp.bfloat16),
            ],
            [],
            (row_kern, turn_kern, goal, own_strip, *strips, *shares),
            [pltpu.VMEM] * (3 + count_x + count_y),
        )
        (gradient,) = call(
            functools.partial(straight_kernel, scale),
            [jax.ShapeDtypeStruct(shape, jnp.float32)],
            [],
            (near_field, counts, both_kern, near),
            [pltpu.VMEM] * 4,
        )
        came = [crossed[0]] + crosswise(lambda d: crossed[d], mesh)
        own = rounded(gradient + jnp.stack(came).astype(jnp.float32))
        other = lax.ppermute(own.astype(jnp.bfloat16), "wa", pairs(2, 1))
        design_grad = in_order(0.5 * (own + other.astype(jnp.float32)), tile_row)
        intensity = jnp.swapaxes(power[:, :, :focus], 1, 2)
        return (design_grad[None], intensity)

    return on_device


def solution(mesh):
    placed = (
        P("wa", "cand", None, "gx", None, "gy", None),
        P("gx", None),
        P("wa", None, None, None, None),
        P("wa", None, None),
    )
    return jax.shard_map(
        make(mesh),
        mesh=mesh,
        in_specs=placed,
        out_specs=(P("gx", "cand", "gy", None), P("wa", "cand", None)),
        check_vma=False,
    )
```

```python
import functools

import jax
import jax.numpy as jnp
from jax import lax
from jax.experimental import pallas as pl
from jax.experimental.pallas import tpu as pltpu
from jax.sharding import PartitionSpec as P

VMEM = 16 * 2**20


def two_terms(value):
    high = value.astype(jnp.bfloat16)
    return high, (value - high.astype(jnp.float32)).astype(jnp.bfloat16)


def dot(first, second, over):
    return lax.dot_general(
        first, second, ((over[:1], over[1:]), ((), ())), preferred_element_type=jnp.float32
    )


def tile_kern(kern, wave, tile):
    real, imag = kern[wave, 0, tile], kern[wave, 1, tile]
    return jnp.concatenate([real, imag], axis=0), jnp.concatenate([-imag, real], axis=0)


def one_block(value, block, blocks):
    width = value.shape[1] // blocks
    picked = value[:, :width]
    for index in range(1, blocks):
        picked = jnp.where(block == index, value[:, index * width : (index + 1) * width], picked)
    return picked


def turn(value):
    width = value.shape[1]
    row = lax.broadcasted_iota(jnp.int32, (width, width), 0)
    column = lax.broadcasted_iota(jnp.int32, (width, width), 1)
    unit = jnp.where(row == column, 1.0, 0.0).astype(value.dtype)
    return dot(unit, value, (1, 1)).astype(value.dtype)


def twice(value, axis):
    return jnp.concatenate([value, value], axis=axis)


def diagonal(value, count):
    zero = jnp.zeros_like(value)
    rows = [
        jnp.concatenate([value if index == other else zero for other in range(count)], axis=1)
        for index in range(count)
    ]
    return jnp.concatenate(rows, axis=0)


def over_tiles(tiles, body, init):
    return lax.fori_loop(0, tiles, body, init, unroll=tiles <= 8)


def live_rows(count, shape):
    height = shape[-2]
    row = lax.axis_index("gy") * height + lax.broadcasted_iota(jnp.int32, shape, len(shape) - 2)
    return row < count


def share_kernel(rows_far, field_far, kern_far, share, field, kern, counts, rows, arrived):
    waves, polars, _, tiles, height, side = field.shape
    focus = kern.shape[3]
    copies = [pltpu.make_async_copy(rows_far, rows, arrived.at[2 * waves])]
    for wave in range(waves):
        copies += [
            pltpu.make_async_copy(kern_far.at[wave], kern.at[wave], arrived.at[2 * wave]),
            pltpu.make_async_copy(
                field_far.at[wave, :, :, 0], field.at[wave], arrived.at[2 * wave + 1]
            ),
        ]
    for copy in copies:
        copy.start()
    tile_row = lax.axis_index("gx")
    block = lax.axis_index("gy")
    copies[0].wait()

    def put_count(tile, carry):
        at = lax.broadcasted_iota(jnp.int32, rows.shape, 1)
        count = jnp.sum(jnp.where(at == tile, rows[...], 0), axis=1, keepdims=True)
        counts[tile] = jnp.broadcast_to(count, counts.shape[1:])
        return carry

    over_tiles(tiles, put_count, 0)
    row = lax.broadcasted_iota(jnp.int32, (2 * focus, polars * height), 1)
    row = block * height + lax.rem(row, height)
    inner = []
    own = []
    for wave in range(waves):
        copies[2 * wave + 1].wait()
        parts = []
        for part in range(2):
            value = kern[wave, part, tile_row].astype(jnp.float32)
            parts.append(diagonal(one_block(value, block, side // height), polars))
        own.append(twice(jnp.concatenate(parts, axis=0).astype(kern.dtype), 1))
        copies[2 * wave + 2].wait()

        def add_tile(tile, value):
            planes = [field[wave, :, part, tile] for part in range(2)]
            planes = [plane.reshape(polars * height, side) for plane in planes]
            product = dot(
                jnp.concatenate(tile_kern(kern, wave, tile), axis=1),
                jnp.concatenate(planes, axis=1),
                (1, 1),
            )
            count = jnp.broadcast_to(counts[tile, :1, : polars * height], product.shape)
            return value + jnp.where(row < count, product, 0.0)

        zero = jnp.zeros((2 * focus, polars * height), jnp.float32)
        inner.append(over_tiles(tiles, add_tile, zero))
    for wave in range(waves):
        both = dot(jnp.concatenate(two_terms(inner[wave]), axis=1), own[wave], (1, 1))
        real, imag = both[:, : polars * focus], both[:, polars * focus :]
        focal = [real[:focus] - imag[focus:], real[focus:] + imag[:focus]]
        share[wave] = jnp.concatenate(focal, axis=0).astype(share.dtype)


def turned_strip(planes, block, blocks):
    rows = [
        jnp.concatenate([one_block(plane, block, blocks) for plane in pair], axis=1)
        for pair in planes
    ]
    return turn(jnp.concatenate(rows, axis=0).astype(jnp.bfloat16))


def live_planes(field, counts, wave, tile):
    polars, height, side = field.shape[1], field.shape[4], field.shape[5]
    live = live_rows(counts[tile, :1], (height, side))
    return [
        [
            jnp.where(live, field[wave, polar, part, tile].astype(jnp.float32), 0.0)
            for part in range(2)
        ]
        for polar in range(polars)
    ]


def strip_kernel(field, counts, *strips):
    waves, _, _, tiles, height, side = field.shape
    blocks = side // height
    block = lax.axis_index("gy")

    def one_tile(tile, carry):
        for wave in range(waves):
            planes = live_planes(field, counts, wave, tile)
            for distance, strip in enumerate(strips, 1):
                strip[wave, tile] = turned_strip(planes, block ^ distance, blocks)
        return carry

    over_tiles(tiles, one_tile, 0)


def layout_kernel(field, kern, counts, target, goal, row_kern, turn_kern, both_kern, own_strip):
    waves, polars, _, tiles, height, side = field.shape
    blocks = side // height
    block = lax.axis_index("gy")
    tile_row = lax.axis_index("gx")
    for wave in range(waves):
        goal[wave] = jnp.concatenate([target[wave].T] * polars, axis=1)
        for part in range(2):
            value = kern[wave, part, tile_row].astype(jnp.float32)
            columns = [
                diagonal(one_block(value, block ^ distance, blocks), polars)
                for distance in range(blocks)
            ]
            rows = pl.ds(part * polars * value.shape[0], polars * value.shape[0])
            row_kern[wave, rows] = jnp.concatenate(columns, axis=1).astype(kern.dtype)

    def one_tile(tile, carry):
        for wave in range(waves):
            parts = tile_kern(kern, wave, tile)
            both_kern[wave, tile] = jnp.concatenate(parts, axis=1)
            parts = [one_block(part.astype(jnp.float32), block, blocks) for part in parts]
            turned = turn(jnp.concatenate(parts, axis=1).astype(kern.dtype))
            turn_kern[wave, tile] = twice(turned, 1)
            planes = live_planes(field, counts, wave, tile)
            own_strip[wave, tile] = turned_strip(planes, block, blocks)
        return carry

    over_tiles(tiles, one_tile, 0)


def crossed_kernel(scale, blocks, row_kern, turn_kern, goal, *refs):
    strips, refs = refs[:blocks], refs[blocks:]
    shares, (intensity, near, crossed) = refs[:-3], refs[-3:]
    waves, tiles, height, width = strips[0].shape
    height = height // 2
    polars = width // height
    focus = goal.shape[1]
    block = lax.axis_index("gy")
    sides = []
    for wave in range(waves):
        focal = total([share[wave].astype(jnp.float32) for share in shares])
        real, imag = focal[:focus], focal[focus:]
        power = real * real + imag * imag
        power = sum(pltpu.roll(power, polar * focus, 1) for polar in range(polars))
        intensity[wave] = power
        excess = power - goal[wave]
        real, imag = excess * real, excess * imag
        upright = jnp.concatenate([real, imag], axis=0)
        turned = jnp.concatenate([imag, -real], axis=0)
        terms = two_terms(jnp.concatenate([upright, turned], axis=1))
        row = dot(jnp.concatenate(terms, axis=1), twice(row_kern[wave], 0), (1, 0))
        sides.append(jnp.concatenate(two_terms(row), axis=0))
        near[wave] = sides[wave]

    def add_tile(distance, carry):
        tile = lax.axis_index("gx") ^ distance
        value = jnp.zeros((2 * height, blocks * width), jnp.float32)
        for wave in range(waves):
            back = dot(turn_kern[wave, tile], sides[wave], (1, 0))
            strip = jnp.concatenate([strip[wave, tile] for strip in strips], axis=1)
            value += back * strip.astype(jnp.float32)
        value = (value[:height] + value[height:]) * scale
        parts = []
        for apart in range(blocks):
            part = value[:, apart * width : (apart + 1) * width]
            parts.append(sum(part[:, at * height : (at + 1) * height] for at in range(polars)))
        columns = []
        for index in range(blocks):
            column = parts[0]
            for apart in range(1, blocks):
                column = jnp.where((block ^ apart) == index, parts[apart], column)
            columns.append(column)
        crossed[distance] = jnp.concatenate(columns, axis=1).astype(crossed.dtype)
        return carry

    over_tiles(tiles, add_tile, 0)


def straight_kernel(scale, field, counts, both_kern, near, gradient):
    waves, polars, _, tiles, height, side = field.shape
    sides = []
    for wave in range(waves):
        sides.append(turn(near[wave, :, : polars * height]))

    def add_tile(distance, carry):
        tile = lax.axis_index("gx") ^ distance
        term = jnp.zeros((height, side), jnp.float32)
        for wave in range(waves):
            back = dot(sides[wave], twice(both_kern[wave, tile], 0), (1, 0))
            back = back.reshape(polars, height, 2 * side)
            for polar in range(polars):
                for part in range(2):
                    plane = field[wave, polar, part, tile].astype(jnp.float32)
                    term += back[polar, :, part * side : (part + 1) * side] * plane
        live = live_rows(counts[tile, :1], (height, side))
        gradient[distance] = jnp.where(live, term * scale, 0.0)
        return carry

    over_tiles(tiles, add_tile, 0)


def call(kernel, out_shape, scratch, args, spaces):
    return pl.pallas_call(
        kernel,
        out_shape=out_shape,
        in_specs=[pl.BlockSpec(memory_space=space) for space in spaces],
        out_specs=[pl.BlockSpec(memory_space=pltpu.VMEM)] * len(out_shape),
        scratch_shapes=scratch,
        compiler_params=pltpu.CompilerParams(vmem_limit_bytes=VMEM),
    )(*args)


def pairs(count, distance):
    return [(device, device ^ distance) for device in range(count)]


def partners(value, axis, count):
    came = {d: lax.ppermute(value(d), axis, pairs(count, d)) for d in range(count - 1, 0, -1)}
    return [came[d] for d in range(1, count)]


def crosswise(value, mesh):
    count, cores = mesh.shape["gx"], mesh.shape["wa"]

    def routes(distance):
        odd = distance % 2 == 1
        return [
            (
                device * cores + core,
                (device ^ distance) * cores + (cores - 1 - core if odd else core),
            )
            for device in range(count)
            for core in range(cores)
        ]

    came = {d: lax.ppermute(value(d), ("gx", "wa"), routes(d)) for d in range(count - 1, 0, -1)}
    return [came[d] for d in range(1, count)]


def total(terms):
    while len(terms) > 1:
        terms = [first + second for first, second in zip(terms[::2], terms[1::2])]
    return terms[0]


def rounded(value):
    return lax.reduce_precision(value, 8, 7)


def in_order(came, me):
    count = came.shape[0]
    rest = came.shape[1:]
    bit = 1
    while bit < count:
        split = came.reshape((count // (2 * bit), 2, bit) + rest)
        came = jnp.where((me & bit) != 0, split[:, ::-1], split).reshape((count,) + rest)
        bit *= 2
    return came


def make(mesh):
    count_x = mesh.shape["gx"]
    count_y = mesh.shape["gy"]

    def on_device(field, active_rows, kern, target):
        tile_row = lax.axis_index("gx")
        waves, polars = field.shape[0], field.shape[1]
        tiles = field.shape[4]
        rows_dev = field.shape[5]
        side = field.shape[6]
        focus = kern.shape[3]
        shape = (waves, 2 * focus, polars * focus)
        share, near_field, near_kern, counts = call(
            share_kernel,
            [
                jax.ShapeDtypeStruct(shape, jnp.bfloat16),
                jax.ShapeDtypeStruct(field.shape[:3] + field.shape[4:], field.dtype),
                jax.ShapeDtypeStruct(kern.shape, kern.dtype),
                jax.ShapeDtypeStruct((tiles, 8, side), jnp.int32),
            ],
            [
                pltpu.VMEM(active_rows.shape, jnp.int32),
                pltpu.SemaphoreType.DMA((2 * waves + 1,)),
            ],
            [
                pltpu.with_memory_space_constraint(operand, pltpu.HBM)
                for operand in (active_rows, field, kern)
            ],
            [pltpu.HBM] * 3,
        )
        shares = [share] + partners(lambda d: share, "gy", count_y)
        share = total([term.astype(jnp.float32) for term in shares]).astype(jnp.bfloat16)
        strip_shape = (waves, tiles, 2 * rows_dev, polars * rows_dev)
        strips = call(
            strip_kernel,
            [jax.ShapeDtypeStruct(strip_shape, field.dtype)] * (count_y - 1),
            [],
            (near_field, counts),
            [pltpu.VMEM] * 2,
        )
        strips = partners(lambda d: strips[d - 1], "gy", count_y)
        shares = [share] + partners(lambda d: share, "gx", count_x)
        shares = shares[::-1]
        shape = (tiles, rows_dev, side)
        goal, row_kern, turn_kern, both_kern, own_strip = call(
            layout_kernel,
            [
                jax.ShapeDtypeStruct((waves, focus, polars * focus), target.dtype),
                jax.ShapeDtypeStruct((waves, 2 * polars * focus, polars * side), kern.dtype),
                jax.ShapeDtypeStruct((waves, tiles, 2 * rows_dev, 4 * focus), kern.dtype),
                jax.ShapeDtypeStruct((waves, tiles, 2 * focus, 2 * side), kern.dtype),
                jax.ShapeDtypeStruct(strip_shape, field.dtype),
            ],
            [],
            (near_field, near_kern, counts, target),
            [pltpu.VMEM] * 4,
        )
        scale = tiles * side / focus
        power, near, crossed = call(
            functools.partial(crossed_kernel, scale, count_y),
            [
                jax.ShapeDtypeStruct((waves, focus, polars * focus), jnp.float32),
                jax.ShapeDtypeStruct((waves, 4 * focus, polars * side), jnp.bfloat16),
                jax.ShapeDtypeStruct(shape, jnp.bfloat16),
            ],
            [],
            (row_kern, turn_kern, goal, own_strip, *strips, *shares),
            [pltpu.VMEM] * (3 + count_x + count_y),
        )
        (gradient,) = call(
            functools.partial(straight_kernel, scale),
            [jax.ShapeDtypeStruct(shape, jnp.float32)],
            [],
            (near_field, counts, both_kern, near),
            [pltpu.VMEM] * 4,
        )
        came = [crossed[0]] + crosswise(lambda d: crossed[d], mesh)
        own = rounded(in_order(gradient + jnp.stack(came).astype(jnp.float32), tile_row))
        other = lax.ppermute(own.astype(jnp.bfloat16), "wa", pairs(2, 1))
        design_grad = 0.5 * (own + other.astype(jnp.float32))
        intensity = jnp.swapaxes(power[:, :, :focus], 1, 2)
        return (design_grad[None], intensity)

    return on_device


def solution(mesh):
    placed = (
        P("wa", "cand", None, "gx", None, "gy", None),
        P("gx", None),
        P("wa", None, None, None, None),
        P("wa", None, None),
    )
    return jax.shard_map(
        make(mesh),
        mesh=mesh,
        in_specs=placed,
        out_specs=(P("gx", "cand", "gy", None), P("wa", "cand", None)),
        check_vma=False,
    )
```

```python
import functools

import jax
import jax.numpy as jnp
from jax import lax
from jax.experimental import pallas as pl
from jax.experimental.pallas import tpu as pltpu
from jax.sharding import PartitionSpec as P

VMEM = 16 * 2**20


def two_terms(value):
    high = value.astype(jnp.bfloat16)
    return high, (value - high.astype(jnp.float32)).astype(jnp.bfloat16)


def dot(first, second, over):
    return lax.dot_general(
        first, second, ((over[:1], over[1:]), ((), ())), preferred_element_type=jnp.float32
    )


def tile_kern(kern, wave, tile):
    real, imag = kern[wave, 0, tile], kern[wave, 1, tile]
    return jnp.concatenate([real, imag], axis=0), jnp.concatenate([-imag, real], axis=0)


def one_block(value, block, blocks):
    width = value.shape[1] // blocks
    picked = value[:, :width]
    for index in range(1, blocks):
        picked = jnp.where(block == index, value[:, index * width : (index + 1) * width], picked)
    return picked


def turn(value):
    width = value.shape[1]
    row = lax.broadcasted_iota(jnp.int32, (width, width), 0)
    column = lax.broadcasted_iota(jnp.int32, (width, width), 1)
    unit = jnp.where(row == column, 1.0, 0.0).astype(value.dtype)
    return dot(unit, value, (1, 1)).astype(value.dtype)


def twice(value, axis):
    return jnp.concatenate([value, value], axis=axis)


def diagonal(value, count):
    zero = jnp.zeros_like(value)
    rows = [
        jnp.concatenate([value if index == other else zero for other in range(count)], axis=1)
        for index in range(count)
    ]
    return jnp.concatenate(rows, axis=0)


def over_tiles(tiles, body, init):
    return lax.fori_loop(0, tiles, body, init, unroll=tiles <= 8)


def live_rows(count, shape):
    height = shape[-2]
    row = lax.axis_index("gy") * height + lax.broadcasted_iota(jnp.int32, shape, len(shape) - 2)
    return row < count


def share_kernel(rows_far, field_far, kern_far, share, field, kern, counts, rows, arrived):
    waves, polars, _, tiles, height, side = field.shape
    focus = kern.shape[3]
    copies = [pltpu.make_async_copy(rows_far, rows, arrived.at[2 * waves])]
    for wave in range(waves):
        copies += [
            pltpu.make_async_copy(kern_far.at[wave], kern.at[wave], arrived.at[2 * wave]),
            pltpu.make_async_copy(
                field_far.at[wave, :, :, 0], field.at[wave], arrived.at[2 * wave + 1]
            ),
        ]
    for copy in copies:
        copy.start()
    tile_row = lax.axis_index("gx")
    block = lax.axis_index("gy")
    copies[0].wait()

    def put_count(tile, carry):
        at = lax.broadcasted_iota(jnp.int32, rows.shape, 1)
        count = jnp.sum(jnp.where(at == tile, rows[...], 0), axis=1, keepdims=True)
        counts[tile] = jnp.broadcast_to(count, counts.shape[1:])
        return carry

    over_tiles(tiles, put_count, 0)
    row = lax.broadcasted_iota(jnp.int32, (2 * focus, polars * height), 1)
    row = block * height + lax.rem(row, height)
    inner = []
    for wave in range(waves):
        copies[2 * wave + 1].wait()
        copies[2 * wave + 2].wait()

        def add_tile(tile, value):
            planes = [field[wave, :, part, tile] for part in range(2)]
            planes = [plane.reshape(polars * height, side) for plane in planes]
            product = dot(
                jnp.concatenate(tile_kern(kern, wave, tile), axis=1),
                jnp.concatenate(planes, axis=1),
                (1, 1),
            )
            count = jnp.broadcast_to(counts[tile, :1, : polars * height], product.shape)
            return value + jnp.where(row < count, product, 0.0)

        zero = jnp.zeros((2 * focus, polars * height), jnp.float32)
        inner.append(over_tiles(tiles, add_tile, zero))
    own = []
    for wave in range(waves):
        parts = []
        for part in range(2):
            value = kern[wave, part, tile_row].astype(jnp.float32)
            parts.append(diagonal(one_block(value, block, side // height), polars))
        own.append(twice(jnp.concatenate(parts, axis=0).astype(kern.dtype), 1))
    for wave in range(waves):
        both = dot(jnp.concatenate(two_terms(inner[wave]), axis=1), own[wave], (1, 1))
        real, imag = both[:, : polars * focus], both[:, polars * focus :]
        focal = [real[:focus] - imag[focus:], real[focus:] + imag[:focus]]
        share[wave] = jnp.concatenate(focal, axis=0).astype(share.dtype)


def turned_strip(planes, block, blocks):
    rows = [
        jnp.concatenate([one_block(plane, block, blocks) for plane in pair], axis=1)
        for pair in planes
    ]
    return turn(jnp.concatenate(rows, axis=0).astype(jnp.bfloat16))


def live_planes(field, counts, wave, tile):
    polars, height, side = field.shape[1], field.shape[4], field.shape[5]
    live = live_rows(counts[tile, :1], (height, side))
    return [
        [
            jnp.where(live, field[wave, polar, part, tile].astype(jnp.float32), 0.0)
            for part in range(2)
        ]
        for polar in range(polars)
    ]


def strip_kernel(field, counts, *strips):
    waves, _, _, tiles, height, side = field.shape
    blocks = side // height
    block = lax.axis_index("gy")

    def one_tile(tile, carry):
        for wave in range(waves):
            planes = live_planes(field, counts, wave, tile)
            for distance, strip in enumerate(strips, 1):
                strip[wave, tile] = turned_strip(planes, block ^ distance, blocks)
        return carry

    over_tiles(tiles, one_tile, 0)


def layout_kernel(field, kern, counts, target, goal, row_kern, turn_kern, both_kern, own_strip):
    waves, polars, _, tiles, height, side = field.shape
    blocks = side // height
    block = lax.axis_index("gy")
    tile_row = lax.axis_index("gx")
    for wave in range(waves):
        goal[wave] = jnp.concatenate([target[wave].T] * polars, axis=1)
        for part in range(2):
            value = kern[wave, part, tile_row].astype(jnp.float32)
            columns = [
                diagonal(one_block(value, block ^ distance, blocks), polars)
                for distance in range(blocks)
            ]
            rows = pl.ds(part * polars * value.shape[0], polars * value.shape[0])
            row_kern[wave, rows] = jnp.concatenate(columns, axis=1).astype(kern.dtype)

    def one_tile(tile, carry):
        for wave in range(waves):
            parts = tile_kern(kern, wave, tile)
            both_kern[wave, tile] = jnp.concatenate(parts, axis=1)
            parts = [one_block(part.astype(jnp.float32), block, blocks) for part in parts]
            turned = turn(jnp.concatenate(parts, axis=1).astype(kern.dtype))
            turn_kern[wave, tile] = twice(turned, 1)
            planes = live_planes(field, counts, wave, tile)
            own_strip[wave, tile] = turned_strip(planes, block, blocks)
        return carry

    over_tiles(tiles, one_tile, 0)


def crossed_kernel(scale, blocks, row_kern, turn_kern, goal, *refs):
    strips, refs = refs[:blocks], refs[blocks:]
    shares, (intensity, near, crossed) = refs[:-3], refs[-3:]
    waves, tiles, height, width = strips[0].shape
    height = height // 2
    polars = width // height
    focus = goal.shape[1]
    block = lax.axis_index("gy")
    sides = []
    for wave in range(waves):
        focal = total([share[wave].astype(jnp.float32) for share in shares])
        real, imag = focal[:focus], focal[focus:]
        power = real * real + imag * imag
        power = sum(pltpu.roll(power, polar * focus, 1) for polar in range(polars))
        intensity[wave] = power
        excess = power - goal[wave]
        real, imag = excess * real, excess * imag
        upright = jnp.concatenate([real, imag], axis=0)
        turned = jnp.concatenate([imag, -real], axis=0)
        terms = two_terms(jnp.concatenate([upright, turned], axis=1))
        row = dot(jnp.concatenate(terms, axis=1), twice(row_kern[wave], 0), (1, 0))
        sides.append(jnp.concatenate(two_terms(row), axis=0))
        near[wave] = sides[wave]

    def add_tile(distance, carry):
        tile = lax.axis_index("gx") ^ distance
        value = jnp.zeros((2 * height, blocks * width), jnp.float32)
        for wave in range(waves):
            back = dot(turn_kern[wave, tile], sides[wave], (1, 0))
            strip = jnp.concatenate([strip[wave, tile] for strip in strips], axis=1)
            value += back * strip.astype(jnp.float32)
        value = (value[:height] + value[height:]) * scale
        parts = []
        for apart in range(blocks):
            part = value[:, apart * width : (apart + 1) * width]
            parts.append(sum(part[:, at * height : (at + 1) * height] for at in range(polars)))
        columns = []
        for index in range(blocks):
            column = parts[0]
            for apart in range(1, blocks):
                column = jnp.where((block ^ apart) == index, parts[apart], column)
            columns.append(column)
        crossed[distance] = jnp.concatenate(columns, axis=1).astype(crossed.dtype)
        return carry

    over_tiles(tiles, add_tile, 0)


def straight_kernel(scale, field, counts, both_kern, near, gradient):
    waves, polars, _, tiles, height, side = field.shape
    sides = []
    for wave in range(waves):
        sides.append(turn(near[wave, :, : polars * height]))

    def add_tile(distance, carry):
        tile = lax.axis_index("gx") ^ distance
        term = jnp.zeros((height, side), jnp.float32)
        for wave in range(waves):
            back = dot(sides[wave], twice(both_kern[wave, tile], 0), (1, 0))
            back = back.reshape(polars, height, 2 * side)
            for polar in range(polars):
                for part in range(2):
                    plane = field[wave, polar, part, tile].astype(jnp.float32)
                    term += back[polar, :, part * side : (part + 1) * side] * plane
        live = live_rows(counts[tile, :1], (height, side))
        gradient[distance] = jnp.where(live, term * scale, 0.0)
        return carry

    over_tiles(tiles, add_tile, 0)


def call(kernel, out_shape, scratch, args, spaces):
    return pl.pallas_call(
        kernel,
        out_shape=out_shape,
        in_specs=[pl.BlockSpec(memory_space=space) for space in spaces],
        out_specs=[pl.BlockSpec(memory_space=pltpu.VMEM)] * len(out_shape),
        scratch_shapes=scratch,
        compiler_params=pltpu.CompilerParams(vmem_limit_bytes=VMEM),
    )(*args)


def pairs(count, distance):
    return [(device, device ^ distance) for device in range(count)]


def partners(value, axis, count):
    came = {d: lax.ppermute(value(d), axis, pairs(count, d)) for d in range(count - 1, 0, -1)}
    return [came[d] for d in range(1, count)]


def crosswise(value, mesh):
    count, cores = mesh.shape["gx"], mesh.shape["wa"]

    def routes(distance):
        odd = distance % 2 == 1
        return [
            (
                device * cores + core,
                (device ^ distance) * cores + (cores - 1 - core if odd else core),
            )
            for device in range(count)
            for core in range(cores)
        ]

    came = {d: lax.ppermute(value(d), ("gx", "wa"), routes(d)) for d in range(count - 1, 0, -1)}
    return [came[d] for d in range(1, count)]


def total(terms):
    while len(terms) > 1:
        terms = [first + second for first, second in zip(terms[::2], terms[1::2])]
    return terms[0]


def rounded(value):
    return lax.reduce_precision(value, 8, 7)


def in_order(came, me):
    count = came.shape[0]
    rest = came.shape[1:]
    bit = 1
    while bit < count:
        split = came.reshape((count // (2 * bit), 2, bit) + rest)
        came = jnp.where((me & bit) != 0, split[:, ::-1], split).reshape((count,) + rest)
        bit *= 2
    return came


def make(mesh):
    count_x = mesh.shape["gx"]
    count_y = mesh.shape["gy"]

    def on_device(field, active_rows, kern, target):
        tile_row = lax.axis_index("gx")
        waves, polars = field.shape[0], field.shape[1]
        tiles = field.shape[4]
        rows_dev = field.shape[5]
        side = field.shape[6]
        focus = kern.shape[3]
        shape = (waves, 2 * focus, polars * focus)
        share, near_field, near_kern, counts = call(
            share_kernel,
            [
                jax.ShapeDtypeStruct(shape, jnp.bfloat16),
                jax.ShapeDtypeStruct(field.shape[:3] + field.shape[4:], field.dtype),
                jax.ShapeDtypeStruct(kern.shape, kern.dtype),
                jax.ShapeDtypeStruct((tiles, 8, side), jnp.int32),
            ],
            [
                pltpu.VMEM(active_rows.shape, jnp.int32),
                pltpu.SemaphoreType.DMA((2 * waves + 1,)),
            ],
            [
                pltpu.with_memory_space_constraint(operand, pltpu.HBM)
                for operand in (active_rows, field, kern)
            ],
            [pltpu.HBM] * 3,
        )
        shares = [share] + partners(lambda d: share, "gy", count_y)
        share = total([term.astype(jnp.float32) for term in shares]).astype(jnp.bfloat16)
        strip_shape = (waves, tiles, 2 * rows_dev, polars * rows_dev)
        strips = call(
            strip_kernel,
            [jax.ShapeDtypeStruct(strip_shape, field.dtype)] * (count_y - 1),
            [],
            (near_field, counts),
            [pltpu.VMEM] * 2,
        )
        strips = partners(lambda d: strips[d - 1], "gy", count_y)
        shares = [share] + partners(lambda d: share, "gx", count_x)
        shares = shares[::-1]
        shape = (tiles, rows_dev, side)
        goal, row_kern, turn_kern, both_kern, own_strip = call(
            layout_kernel,
            [
                jax.ShapeDtypeStruct((waves, focus, polars * focus), target.dtype),
                jax.ShapeDtypeStruct((waves, 2 * polars * focus, polars * side), kern.dtype),
                jax.ShapeDtypeStruct((waves, tiles, 2 * rows_dev, 4 * focus), kern.dtype),
                jax.ShapeDtypeStruct((waves, tiles, 2 * focus, 2 * side), kern.dtype),
                jax.ShapeDtypeStruct(strip_shape, field.dtype),
            ],
            [],
            (near_field, near_kern, counts, target),
            [pltpu.VMEM] * 4,
        )
        scale = tiles * side / focus
        power, near, crossed = call(
            functools.partial(crossed_kernel, scale, count_y),
            [
                jax.ShapeDtypeStruct((waves, focus, polars * focus), jnp.float32),
                jax.ShapeDtypeStruct((waves, 4 * focus, polars * side), jnp.bfloat16),
                jax.ShapeDtypeStruct(shape, jnp.bfloat16),
            ],
            [],
            (row_kern, turn_kern, goal, own_strip, *strips, *shares),
            [pltpu.VMEM] * (3 + count_x + count_y),
        )
        (gradient,) = call(
            functools.partial(straight_kernel, scale),
            [jax.ShapeDtypeStruct(shape, jnp.float32)],
            [],
            (near_field, counts, both_kern, near),
            [pltpu.VMEM] * 4,
        )
        came = [crossed[0]] + crosswise(lambda d: crossed[d], mesh)
        own = rounded(in_order(gradient + jnp.stack(came).astype(jnp.float32), tile_row))
        other = lax.ppermute(own.astype(jnp.bfloat16), "wa", pairs(2, 1))
        design_grad = 0.5 * (own + other.astype(jnp.float32))
        intensity = jnp.swapaxes(power[:, :, :focus], 1, 2)
        return (design_grad[None], intensity)

    return on_device


def solution(mesh):
    placed = (
        P("wa", "cand", None, "gx", None, "gy", None),
        P("gx", None),
        P("wa", None, None, None, None),
        P("wa", None, None),
    )
    return jax.shard_map(
        make(mesh),
        mesh=mesh,
        in_specs=placed,
        out_specs=(P("gx", "cand", "gy", None), P("wa", "cand", None)),
        check_vma=False,
    )
```

```python
import functools

import jax
import jax.numpy as jnp
from jax import lax
from jax.experimental import pallas as pl
from jax.experimental.pallas import tpu as pltpu
from jax.sharding import PartitionSpec as P

VMEM = 16 * 2**20


def two_terms(value):
    high = value.astype(jnp.bfloat16)
    return high, (value - high.astype(jnp.float32)).astype(jnp.bfloat16)


def dot(first, second, over):
    return lax.dot_general(
        first, second, ((over[:1], over[1:]), ((), ())), preferred_element_type=jnp.float32
    )


def tile_kern(kern, wave, tile):
    real, imag = kern[wave, 0, tile], kern[wave, 1, tile]
    return jnp.concatenate([real, imag], axis=0), jnp.concatenate([-imag, real], axis=0)


def one_block(value, block, blocks):
    width = value.shape[1] // blocks
    picked = value[:, :width]
    for index in range(1, blocks):
        picked = jnp.where(block == index, value[:, index * width : (index + 1) * width], picked)
    return picked


def turn(value):
    width = value.shape[1]
    row = lax.broadcasted_iota(jnp.int32, (width, width), 0)
    column = lax.broadcasted_iota(jnp.int32, (width, width), 1)
    unit = jnp.where(row == column, 1.0, 0.0).astype(value.dtype)
    return dot(unit, value, (1, 1)).astype(value.dtype)


def twice(value, axis):
    return jnp.concatenate([value, value], axis=axis)


def diagonal(value, count):
    zero = jnp.zeros_like(value)
    rows = [
        jnp.concatenate([value if index == other else zero for other in range(count)], axis=1)
        for index in range(count)
    ]
    return jnp.concatenate(rows, axis=0)


def over_tiles(tiles, body, init):
    return lax.fori_loop(0, tiles, body, init, unroll=tiles <= 8)


def live_rows(count, shape):
    height = shape[-2]
    row = lax.axis_index("gy") * height + lax.broadcasted_iota(jnp.int32, shape, len(shape) - 2)
    return row < count


def share_kernel(rows_far, field_far, kern_far, share, field, kern, counts, rows, arrived):
    waves, polars, _, tiles, height, side = field.shape
    focus = kern.shape[3]
    copies = [pltpu.make_async_copy(rows_far, rows, arrived.at[2 * waves])]
    for wave in range(waves):
        copies += [
            pltpu.make_async_copy(kern_far.at[wave], kern.at[wave], arrived.at[2 * wave]),
            pltpu.make_async_copy(
                field_far.at[wave, :, :, 0], field.at[wave], arrived.at[2 * wave + 1]
            ),
        ]
    for copy in copies:
        copy.start()
    tile_row = lax.axis_index("gx")
    block = lax.axis_index("gy")
    copies[0].wait()

    def put_count(tile, carry):
        at = lax.broadcasted_iota(jnp.int32, rows.shape, 1)
        count = jnp.sum(jnp.where(at == tile, rows[...], 0), axis=1, keepdims=True)
        counts[tile] = jnp.broadcast_to(count, counts.shape[1:])
        return carry

    over_tiles(tiles, put_count, 0)
    row = lax.broadcasted_iota(jnp.int32, (2 * focus, polars * height), 1)
    row = block * height + lax.rem(row, height)
    for copy in copies[1:]:
        copy.wait()
    inner = []
    for wave in range(waves):

        def add_tile(tile, value):
            planes = [field[wave, :, part, tile] for part in range(2)]
            planes = [plane.reshape(polars * height, side) for plane in planes]
            product = dot(
                jnp.concatenate(tile_kern(kern, wave, tile), axis=1),
                jnp.concatenate(planes, axis=1),
                (1, 1),
            )
            count = jnp.broadcast_to(counts[tile, :1, : polars * height], product.shape)
            return value + jnp.where(row < count, product, 0.0)

        zero = jnp.zeros((2 * focus, polars * height), jnp.float32)
        inner.append(over_tiles(tiles, add_tile, zero))
    own = []
    for wave in range(waves):
        parts = []
        for part in range(2):
            value = kern[wave, part, tile_row].astype(jnp.float32)
            parts.append(diagonal(one_block(value, block, side // height), polars))
        own.append(twice(jnp.concatenate(parts, axis=0).astype(kern.dtype), 1))
    for wave in range(waves):
        both = dot(jnp.concatenate(two_terms(inner[wave]), axis=1), own[wave], (1, 1))
        real, imag = both[:, : polars * focus], both[:, polars * focus :]
        focal = [real[:focus] - imag[focus:], real[focus:] + imag[:focus]]
        share[wave] = jnp.concatenate(focal, axis=0).astype(share.dtype)


def turned_strip(planes, block, blocks):
    rows = [
        jnp.concatenate([one_block(plane, block, blocks) for plane in pair], axis=1)
        for pair in planes
    ]
    return turn(jnp.concatenate(rows, axis=0).astype(jnp.bfloat16))


def live_planes(field, counts, wave, tile):
    polars, height, side = field.shape[1], field.shape[4], field.shape[5]
    live = live_rows(counts[tile, :1], (height, side))
    return [
        [
            jnp.where(live, field[wave, polar, part, tile].astype(jnp.float32), 0.0)
            for part in range(2)
        ]
        for polar in range(polars)
    ]


def strip_kernel(field, counts, *strips):
    waves, _, _, tiles, height, side = field.shape
    blocks = side // height
    block = lax.axis_index("gy")

    def one_tile(tile, carry):
        for wave in range(waves):
            planes = live_planes(field, counts, wave, tile)
            for distance, strip in enumerate(strips, 1):
                strip[wave, tile] = turned_strip(planes, block ^ distance, blocks)
        return carry

    over_tiles(tiles, one_tile, 0)


def layout_kernel(field, kern, counts, target, goal, row_kern, turn_kern, both_kern, own_strip):
    waves, polars, _, tiles, height, side = field.shape
    blocks = side // height
    block = lax.axis_index("gy")
    tile_row = lax.axis_index("gx")
    for wave in range(waves):
        goal[wave] = jnp.concatenate([target[wave].T] * polars, axis=1)
        for part in range(2):
            value = kern[wave, part, tile_row].astype(jnp.float32)
            columns = [
                diagonal(one_block(value, block ^ distance, blocks), polars)
                for distance in range(blocks)
            ]
            rows = pl.ds(part * polars * value.shape[0], polars * value.shape[0])
            row_kern[wave, rows] = jnp.concatenate(columns, axis=1).astype(kern.dtype)

    def one_tile(tile, carry):
        for wave in range(waves):
            parts = tile_kern(kern, wave, tile)
            both_kern[wave, tile] = jnp.concatenate(parts, axis=1)
            parts = [one_block(part.astype(jnp.float32), block, blocks) for part in parts]
            turned = turn(jnp.concatenate(parts, axis=1).astype(kern.dtype))
            turn_kern[wave, tile] = twice(turned, 1)
            planes = live_planes(field, counts, wave, tile)
            own_strip[wave, tile] = turned_strip(planes, block, blocks)
        return carry

    over_tiles(tiles, one_tile, 0)


def crossed_kernel(scale, blocks, row_kern, turn_kern, goal, *refs):
    strips, refs = refs[:blocks], refs[blocks:]
    shares, (intensity, near, crossed) = refs[:-3], refs[-3:]
    waves, tiles, height, width = strips[0].shape
    height = height // 2
    polars = width // height
    focus = goal.shape[1]
    block = lax.axis_index("gy")
    sides = []
    for wave in range(waves):
        focal = total([share[wave].astype(jnp.float32) for share in shares])
        real, imag = focal[:focus], focal[focus:]
        power = real * real + imag * imag
        power = sum(pltpu.roll(power, polar * focus, 1) for polar in range(polars))
        intensity[wave] = power
        excess = power - goal[wave]
        real, imag = excess * real, excess * imag
        upright = jnp.concatenate([real, imag], axis=0)
        turned = jnp.concatenate([imag, -real], axis=0)
        terms = two_terms(jnp.concatenate([upright, turned], axis=1))
        row = dot(jnp.concatenate(terms, axis=1), twice(row_kern[wave], 0), (1, 0))
        sides.append(jnp.concatenate(two_terms(row), axis=0))
        near[wave] = sides[wave]

    def add_tile(distance, carry):
        tile = lax.axis_index("gx") ^ distance
        value = jnp.zeros((2 * height, blocks * width), jnp.float32)
        for wave in range(waves):
            back = dot(turn_kern[wave, tile], sides[wave], (1, 0))
            strip = jnp.concatenate([strip[wave, tile] for strip in strips], axis=1)
            value += back * strip.astype(jnp.float32)
        value = (value[:height] + value[height:]) * scale
        parts = []
        for apart in range(blocks):
            part = value[:, apart * width : (apart + 1) * width]
            parts.append(sum(part[:, at * height : (at + 1) * height] for at in range(polars)))
        columns = []
        for index in range(blocks):
            column = parts[0]
            for apart in range(1, blocks):
                column = jnp.where((block ^ apart) == index, parts[apart], column)
            columns.append(column)
        crossed[distance] = jnp.concatenate(columns, axis=1).astype(crossed.dtype)
        return carry

    over_tiles(tiles, add_tile, 0)


def straight_kernel(scale, field, counts, both_kern, near, gradient):
    waves, polars, _, tiles, height, side = field.shape
    sides = []
    for wave in range(waves):
        sides.append(turn(near[wave, :, : polars * height]))

    def add_tile(distance, carry):
        tile = lax.axis_index("gx") ^ distance
        term = jnp.zeros((height, side), jnp.float32)
        for wave in range(waves):
            back = dot(sides[wave], twice(both_kern[wave, tile], 0), (1, 0))
            back = back.reshape(polars, height, 2 * side)
            for polar in range(polars):
                for part in range(2):
                    plane = field[wave, polar, part, tile].astype(jnp.float32)
                    term += back[polar, :, part * side : (part + 1) * side] * plane
        live = live_rows(counts[tile, :1], (height, side))
        gradient[distance] = jnp.where(live, term * scale, 0.0)
        return carry

    over_tiles(tiles, add_tile, 0)


def call(kernel, out_shape, scratch, args, spaces):
    return pl.pallas_call(
        kernel,
        out_shape=out_shape,
        in_specs=[pl.BlockSpec(memory_space=space) for space in spaces],
        out_specs=[pl.BlockSpec(memory_space=pltpu.VMEM)] * len(out_shape),
        scratch_shapes=scratch,
        compiler_params=pltpu.CompilerParams(vmem_limit_bytes=VMEM),
    )(*args)


def pairs(count, distance):
    return [(device, device ^ distance) for device in range(count)]


def partners(value, axis, count):
    came = {d: lax.ppermute(value(d), axis, pairs(count, d)) for d in range(count - 1, 0, -1)}
    return [came[d] for d in range(1, count)]


def crosswise(value, mesh):
    count, cores = mesh.shape["gx"], mesh.shape["wa"]

    def routes(distance):
        odd = distance % 2 == 1
        return [
            (
                device * cores + core,
                (device ^ distance) * cores + (cores - 1 - core if odd else core),
            )
            for device in range(count)
            for core in range(cores)
        ]

    came = {d: lax.ppermute(value(d), ("gx", "wa"), routes(d)) for d in range(count - 1, 0, -1)}
    return [came[d] for d in range(1, count)]


def total(terms):
    while len(terms) > 1:
        terms = [first + second for first, second in zip(terms[::2], terms[1::2])]
    return terms[0]


def rounded(value):
    return lax.reduce_precision(value, 8, 7)


def in_order(came, me):
    count = came.shape[0]
    rest = came.shape[1:]
    bit = 1
    while bit < count:
        split = came.reshape((count // (2 * bit), 2, bit) + rest)
        came = jnp.where((me & bit) != 0, split[:, ::-1], split).reshape((count,) + rest)
        bit *= 2
    return came


def make(mesh):
    count_x = mesh.shape["gx"]
    count_y = mesh.shape["gy"]

    def on_device(field, active_rows, kern, target):
        tile_row = lax.axis_index("gx")
        waves, polars = field.shape[0], field.shape[1]
        tiles = field.shape[4]
        rows_dev = field.shape[5]
        side = field.shape[6]
        focus = kern.shape[3]
        shape = (waves, 2 * focus, polars * focus)
        share, near_field, near_kern, counts = call(
            share_kernel,
            [
                jax.ShapeDtypeStruct(shape, jnp.bfloat16),
                jax.ShapeDtypeStruct(field.shape[:3] + field.shape[4:], field.dtype),
                jax.ShapeDtypeStruct(kern.shape, kern.dtype),
                jax.ShapeDtypeStruct((tiles, 8, side), jnp.int32),
            ],
            [
                pltpu.VMEM(active_rows.shape, jnp.int32),
                pltpu.SemaphoreType.DMA((2 * waves + 1,)),
            ],
            [
                pltpu.with_memory_space_constraint(operand, pltpu.HBM)
                for operand in (active_rows, field, kern)
            ],
            [pltpu.HBM] * 3,
        )
        shares = [share] + partners(lambda d: share, "gy", count_y)
        share = total([term.astype(jnp.float32) for term in shares]).astype(jnp.bfloat16)
        strip_shape = (waves, tiles, 2 * rows_dev, polars * rows_dev)
        strips = call(
            strip_kernel,
            [jax.ShapeDtypeStruct(strip_shape, field.dtype)] * (count_y - 1),
            [],
            (near_field, counts),
            [pltpu.VMEM] * 2,
        )
        strips = partners(lambda d: strips[d - 1], "gy", count_y)
        shares = [share] + partners(lambda d: share, "gx", count_x)
        shares = shares[::-1]
        shape = (tiles, rows_dev, side)
        goal, row_kern, turn_kern, both_kern, own_strip = call(
            layout_kernel,
            [
                jax.ShapeDtypeStruct((waves, focus, polars * focus), target.dtype),
                jax.ShapeDtypeStruct((waves, 2 * polars * focus, polars * side), kern.dtype),
                jax.ShapeDtypeStruct((waves, tiles, 2 * rows_dev, 4 * focus), kern.dtype),
                jax.ShapeDtypeStruct((waves, tiles, 2 * focus, 2 * side), kern.dtype),
                jax.ShapeDtypeStruct(strip_shape, field.dtype),
            ],
            [],
            (near_field, near_kern, counts, target),
            [pltpu.VMEM] * 4,
        )
        scale = tiles * side / focus
        power, near, crossed = call(
            functools.partial(crossed_kernel, scale, count_y),
            [
                jax.ShapeDtypeStruct((waves, focus, polars * focus), jnp.float32),
                jax.ShapeDtypeStruct((waves, 4 * focus, polars * side), jnp.bfloat16),
                jax.ShapeDtypeStruct(shape, jnp.bfloat16),
            ],
            [],
            (row_kern, turn_kern, goal, own_strip, *strips, *shares),
            [pltpu.VMEM] * (3 + count_x + count_y),
        )
        (gradient,) = call(
            functools.partial(straight_kernel, scale),
            [jax.ShapeDtypeStruct(shape, jnp.float32)],
            [],
            (near_field, counts, both_kern, near),
            [pltpu.VMEM] * 4,
        )
        came = [crossed[0]] + crosswise(lambda d: crossed[d], mesh)
        own = rounded(in_order(gradient + jnp.stack(came).astype(jnp.float32), tile_row))
        other = lax.ppermute(own.astype(jnp.bfloat16), "wa", pairs(2, 1))
        design_grad = 0.5 * (own + other.astype(jnp.float32))
        intensity = jnp.swapaxes(power[:, :, :focus], 1, 2)
        return (design_grad[None], intensity)

    return on_device


def solution(mesh):
    placed = (
        P("wa", "cand", None, "gx", None, "gy", None),
        P("gx", None),
        P("wa", None, None, None, None),
        P("wa", None, None),
    )
    return jax.shard_map(
        make(mesh),
        mesh=mesh,
        in_specs=placed,
        out_specs=(P("gx", "cand", "gy", None), P("wa", "cand", None)),
        check_vma=False,
    )
```

```python
import functools

import jax
import jax.numpy as jnp
from jax import lax
from jax.experimental import pallas as pl
from jax.experimental.pallas import tpu as pltpu
from jax.sharding import PartitionSpec as P

VMEM = 16 * 2**20


def two_terms(value):
    high = value.astype(jnp.bfloat16)
    return high, (value - high.astype(jnp.float32)).astype(jnp.bfloat16)


def dot(first, second, over):
    return lax.dot_general(
        first, second, ((over[:1], over[1:]), ((), ())), preferred_element_type=jnp.float32
    )


def tile_kern(kern, wave, tile):
    real, imag = kern[wave, 0, tile], kern[wave, 1, tile]
    return jnp.concatenate([real, imag], axis=0), jnp.concatenate([-imag, real], axis=0)


def one_block(value, block, blocks):
    width = value.shape[1] // blocks
    picked = value[:, :width]
    for index in range(1, blocks):
        picked = jnp.where(block == index, value[:, index * width : (index + 1) * width], picked)
    return picked


def turn(value):
    width = value.shape[1]
    row = lax.broadcasted_iota(jnp.int32, (width, width), 0)
    column = lax.broadcasted_iota(jnp.int32, (width, width), 1)
    unit = jnp.where(row == column, 1.0, 0.0).astype(value.dtype)
    return dot(unit, value, (1, 1)).astype(value.dtype)


def twice(value, axis):
    return jnp.concatenate([value, value], axis=axis)


def diagonal(value, count):
    zero = jnp.zeros_like(value)
    rows = [
        jnp.concatenate([value if index == other else zero for other in range(count)], axis=1)
        for index in range(count)
    ]
    return jnp.concatenate(rows, axis=0)


def over_tiles(tiles, body, init):
    return lax.fori_loop(0, tiles, body, init, unroll=tiles <= 8)


def live_rows(count, shape):
    height = shape[-2]
    row = lax.axis_index("gy") * height + lax.broadcasted_iota(jnp.int32, shape, len(shape) - 2)
    return row < count


def share_kernel(rows_far, field_far, kern_far, share, field, kern, counts, rows, arrived):
    waves, polars, _, tiles, height, side = field.shape
    focus = kern.shape[3]
    copies = [
        pltpu.make_async_copy(rows_far, rows, arrived.at[0]),
        pltpu.make_async_copy(kern_far, kern, arrived.at[1]),
        pltpu.make_async_copy(field_far.at[:, :, :, 0], field, arrived.at[2]),
    ]
    for copy in copies:
        copy.start()
    tile_row = lax.axis_index("gx")
    block = lax.axis_index("gy")
    copies[0].wait()

    def put_count(tile, carry):
        at = lax.broadcasted_iota(jnp.int32, rows.shape, 1)
        count = jnp.sum(jnp.where(at == tile, rows[...], 0), axis=1, keepdims=True)
        counts[tile] = jnp.broadcast_to(count, counts.shape[1:])
        return carry

    over_tiles(tiles, put_count, 0)
    row = lax.broadcasted_iota(jnp.int32, (2 * focus, polars * height), 1)
    row = block * height + lax.rem(row, height)
    for copy in copies[1:]:
        copy.wait()
    inner = []
    for wave in range(waves):

        def add_tile(tile, value):
            planes = [field[wave, :, part, tile] for part in range(2)]
            planes = [plane.reshape(polars * height, side) for plane in planes]
            product = dot(
                jnp.concatenate(tile_kern(kern, wave, tile), axis=1),
                jnp.concatenate(planes, axis=1),
                (1, 1),
            )
            count = jnp.broadcast_to(counts[tile, :1, : polars * height], product.shape)
            return value + jnp.where(row < count, product, 0.0)

        zero = jnp.zeros((2 * focus, polars * height), jnp.float32)
        inner.append(over_tiles(tiles, add_tile, zero))
    own = []
    for wave in range(waves):
        parts = []
        for part in range(2):
            value = kern[wave, part, tile_row].astype(jnp.float32)
            parts.append(diagonal(one_block(value, block, side // height), polars))
        own.append(twice(jnp.concatenate(parts, axis=0).astype(kern.dtype), 1))
    for wave in range(waves):
        both = dot(jnp.concatenate(two_terms(inner[wave]), axis=1), own[wave], (1, 1))
        real, imag = both[:, : polars * focus], both[:, polars * focus :]
        focal = [real[:focus] - imag[focus:], real[focus:] + imag[:focus]]
        share[wave] = jnp.concatenate(focal, axis=0).astype(share.dtype)


def turned_strip(planes, block, blocks):
    rows = [
        jnp.concatenate([one_block(plane, block, blocks) for plane in pair], axis=1)
        for pair in planes
    ]
    return turn(jnp.concatenate(rows, axis=0).astype(jnp.bfloat16))


def live_planes(field, counts, wave, tile):
    polars, height, side = field.shape[1], field.shape[4], field.shape[5]
    live = live_rows(counts[tile, :1], (height, side))
    return [
        [
            jnp.where(live, field[wave, polar, part, tile].astype(jnp.float32), 0.0)
            for part in range(2)
        ]
        for polar in range(polars)
    ]


def strip_kernel(field, counts, *strips):
    waves, _, _, tiles, height, side = field.shape
    blocks = side // height
    block = lax.axis_index("gy")

    def one_tile(tile, carry):
        for wave in range(waves):
            planes = live_planes(field, counts, wave, tile)
            for distance, strip in enumerate(strips, 1):
                strip[wave, tile] = turned_strip(planes, block ^ distance, blocks)
        return carry

    over_tiles(tiles, one_tile, 0)


def layout_kernel(field, kern, counts, target, goal, row_kern, turn_kern, both_kern, own_strip):
    waves, polars, _, tiles, height, side = field.shape
    blocks = side // height
    block = lax.axis_index("gy")
    tile_row = lax.axis_index("gx")
    for wave in range(waves):
        goal[wave] = jnp.concatenate([target[wave].T] * polars, axis=1)
        for part in range(2):
            value = kern[wave, part, tile_row].astype(jnp.float32)
            columns = [
                diagonal(one_block(value, block ^ distance, blocks), polars)
                for distance in range(blocks)
            ]
            rows = pl.ds(part * polars * value.shape[0], polars * value.shape[0])
            row_kern[wave, rows] = jnp.concatenate(columns, axis=1).astype(kern.dtype)

    def one_tile(tile, carry):
        for wave in range(waves):
            parts = tile_kern(kern, wave, tile)
            both_kern[wave, tile] = jnp.concatenate(parts, axis=1)
            parts = [one_block(part.astype(jnp.float32), block, blocks) for part in parts]
            turned = turn(jnp.concatenate(parts, axis=1).astype(kern.dtype))
            turn_kern[wave, tile] = twice(turned, 1)
            planes = live_planes(field, counts, wave, tile)
            own_strip[wave, tile] = turned_strip(planes, block, blocks)
        return carry

    over_tiles(tiles, one_tile, 0)


def crossed_kernel(scale, blocks, row_kern, turn_kern, goal, *refs):
    strips, refs = refs[:blocks], refs[blocks:]
    shares, (intensity, near, crossed) = refs[:-3], refs[-3:]
    waves, tiles, height, width = strips[0].shape
    height = height // 2
    polars = width // height
    focus = goal.shape[1]
    block = lax.axis_index("gy")
    sides = []
    for wave in range(waves):
        focal = total([share[wave].astype(jnp.float32) for share in shares])
        real, imag = focal[:focus], focal[focus:]
        power = real * real + imag * imag
        power = sum(pltpu.roll(power, polar * focus, 1) for polar in range(polars))
        intensity[wave] = power
        excess = power - goal[wave]
        real, imag = excess * real, excess * imag
        upright = jnp.concatenate([real, imag], axis=0)
        turned = jnp.concatenate([imag, -real], axis=0)
        terms = two_terms(jnp.concatenate([upright, turned], axis=1))
        row = dot(jnp.concatenate(terms, axis=1), twice(row_kern[wave], 0), (1, 0))
        sides.append(jnp.concatenate(two_terms(row), axis=0))
        near[wave] = sides[wave]

    def add_tile(distance, carry):
        tile = lax.axis_index("gx") ^ distance
        value = jnp.zeros((2 * height, blocks * width), jnp.float32)
        for wave in range(waves):
            back = dot(turn_kern[wave, tile], sides[wave], (1, 0))
            strip = jnp.concatenate([strip[wave, tile] for strip in strips], axis=1)
            value += back * strip.astype(jnp.float32)
        value = (value[:height] + value[height:]) * scale
        parts = []
        for apart in range(blocks):
            part = value[:, apart * width : (apart + 1) * width]
            parts.append(sum(part[:, at * height : (at + 1) * height] for at in range(polars)))
        columns = []
        for index in range(blocks):
            column = parts[0]
            for apart in range(1, blocks):
                column = jnp.where((block ^ apart) == index, parts[apart], column)
            columns.append(column)
        crossed[distance] = jnp.concatenate(columns, axis=1).astype(crossed.dtype)
        return carry

    over_tiles(tiles, add_tile, 0)


def straight_kernel(scale, field, counts, both_kern, near, gradient):
    waves, polars, _, tiles, height, side = field.shape
    sides = []
    for wave in range(waves):
        sides.append(turn(near[wave, :, : polars * height]))

    def add_tile(distance, carry):
        tile = lax.axis_index("gx") ^ distance
        term = jnp.zeros((height, side), jnp.float32)
        for wave in range(waves):
            back = dot(sides[wave], twice(both_kern[wave, tile], 0), (1, 0))
            back = back.reshape(polars, height, 2 * side)
            for polar in range(polars):
                for part in range(2):
                    plane = field[wave, polar, part, tile].astype(jnp.float32)
                    term += back[polar, :, part * side : (part + 1) * side] * plane
        live = live_rows(counts[tile, :1], (height, side))
        gradient[distance] = jnp.where(live, term * scale, 0.0)
        return carry

    over_tiles(tiles, add_tile, 0)


def call(kernel, out_shape, scratch, args, spaces):
    return pl.pallas_call(
        kernel,
        out_shape=out_shape,
        in_specs=[pl.BlockSpec(memory_space=space) for space in spaces],
        out_specs=[pl.BlockSpec(memory_space=pltpu.VMEM)] * len(out_shape),
        scratch_shapes=scratch,
        compiler_params=pltpu.CompilerParams(vmem_limit_bytes=VMEM),
    )(*args)


def pairs(count, distance):
    return [(device, device ^ distance) for device in range(count)]


def partners(value, axis, count):
    came = {d: lax.ppermute(value(d), axis, pairs(count, d)) for d in range(count - 1, 0, -1)}
    return [came[d] for d in range(1, count)]


def crosswise(value, mesh):
    count, cores = mesh.shape["gx"], mesh.shape["wa"]

    def routes(distance):
        odd = distance % 2 == 1
        return [
            (
                device * cores + core,
                (device ^ distance) * cores + (cores - 1 - core if odd else core),
            )
            for device in range(count)
            for core in range(cores)
        ]

    came = {d: lax.ppermute(value(d), ("gx", "wa"), routes(d)) for d in range(count - 1, 0, -1)}
    return [came[d] for d in range(1, count)]


def total(terms):
    while len(terms) > 1:
        terms = [first + second for first, second in zip(terms[::2], terms[1::2])]
    return terms[0]


def rounded(value):
    return lax.reduce_precision(value, 8, 7)


def in_order(came, me):
    count = came.shape[0]
    rest = came.shape[1:]
    bit = 1
    while bit < count:
        split = came.reshape((count // (2 * bit), 2, bit) + rest)
        came = jnp.where((me & bit) != 0, split[:, ::-1], split).reshape((count,) + rest)
        bit *= 2
    return came


def make(mesh):
    count_x = mesh.shape["gx"]
    count_y = mesh.shape["gy"]

    def on_device(field, active_rows, kern, target):
        tile_row = lax.axis_index("gx")
        waves, polars = field.shape[0], field.shape[1]
        tiles = field.shape[4]
        rows_dev = field.shape[5]
        side = field.shape[6]
        focus = kern.shape[3]
        shape = (waves, 2 * focus, polars * focus)
        share, near_field, near_kern, counts = call(
            share_kernel,
            [
                jax.ShapeDtypeStruct(shape, jnp.bfloat16),
                jax.ShapeDtypeStruct(field.shape[:3] + field.shape[4:], field.dtype),
                jax.ShapeDtypeStruct(kern.shape, kern.dtype),
                jax.ShapeDtypeStruct((tiles, 8, side), jnp.int32),
            ],
            [
                pltpu.VMEM(active_rows.shape, jnp.int32),
                pltpu.SemaphoreType.DMA((3,)),
            ],
            [
                pltpu.with_memory_space_constraint(operand, pltpu.HBM)
                for operand in (active_rows, field, kern)
            ],
            [pltpu.HBM] * 3,
        )
        shares = [share] + partners(lambda d: share, "gy", count_y)
        share = total([term.astype(jnp.float32) for term in shares]).astype(jnp.bfloat16)
        strip_shape = (waves, tiles, 2 * rows_dev, polars * rows_dev)
        strips = call(
            strip_kernel,
            [jax.ShapeDtypeStruct(strip_shape, field.dtype)] * (count_y - 1),
            [],
            (near_field, counts),
            [pltpu.VMEM] * 2,
        )
        strips = partners(lambda d: strips[d - 1], "gy", count_y)
        shares = [share] + partners(lambda d: share, "gx", count_x)
        shares = shares[::-1]
        shape = (tiles, rows_dev, side)
        goal, row_kern, turn_kern, both_kern, own_strip = call(
            layout_kernel,
            [
                jax.ShapeDtypeStruct((waves, focus, polars * focus), target.dtype),
                jax.ShapeDtypeStruct((waves, 2 * polars * focus, polars * side), kern.dtype),
                jax.ShapeDtypeStruct((waves, tiles, 2 * rows_dev, 4 * focus), kern.dtype),
                jax.ShapeDtypeStruct((waves, tiles, 2 * focus, 2 * side), kern.dtype),
                jax.ShapeDtypeStruct(strip_shape, field.dtype),
            ],
            [],
            (near_field, near_kern, counts, target),
            [pltpu.VMEM] * 4,
        )
        scale = tiles * side / focus
        power, near, crossed = call(
            functools.partial(crossed_kernel, scale, count_y),
            [
                jax.ShapeDtypeStruct((waves, focus, polars * focus), jnp.float32),
                jax.ShapeDtypeStruct((waves, 4 * focus, polars * side), jnp.bfloat16),
                jax.ShapeDtypeStruct(shape, jnp.bfloat16),
            ],
            [],
            (row_kern, turn_kern, goal, own_strip, *strips, *shares),
            [pltpu.VMEM] * (3 + count_x + count_y),
        )
        (gradient,) = call(
            functools.partial(straight_kernel, scale),
            [jax.ShapeDtypeStruct(shape, jnp.float32)],
            [],
            (near_field, counts, both_kern, near),
            [pltpu.VMEM] * 4,
        )
        came = [crossed[0]] + crosswise(lambda d: crossed[d], mesh)
        own = rounded(in_order(gradient + jnp.stack(came).astype(jnp.float32), tile_row))
        other = lax.ppermute(own.astype(jnp.bfloat16), "wa", pairs(2, 1))
        design_grad = 0.5 * (own + other.astype(jnp.float32))
        intensity = jnp.swapaxes(power[:, :, :focus], 1, 2)
        return (design_grad[None], intensity)

    return on_device


def solution(mesh):
    placed = (
        P("wa", "cand", None, "gx", None, "gy", None),
        P("gx", None),
        P("wa", None, None, None, None),
        P("wa", None, None),
    )
    return jax.shard_map(
        make(mesh),
        mesh=mesh,
        in_specs=placed,
        out_specs=(P("gx", "cand", "gy", None), P("wa", "cand", None)),
        check_vma=False,
    )
```
